32 devices in a mesh: seq: 8 (over z, y), head: 4 (over x, core).
Axes of the slice: x: 2, y: 2, z: 4, core: 2. Of those that a mesh axis runs over, the one named last changes fastest.
Arguments:
- short_input: bfloat16 [2, 512, 768], P(None, 'seq'), may hold values from -6 to 6
- long_input: bfloat16 [2, 1024, 768], P(None, 'seq'), may hold values from -6 to 6
- short_cotangent: bfloat16 [2, 512, 768], P(None, 'seq'), may hold values from -6 to 6
- long_cotangent: bfloat16 [2, 1024, 768], P(None, 'seq'), may hold values from -6 to 6
- short_lengths: int32 [2], replicated, may hold values from 256 to 512, as said below
- long_lengths: int32 [2], replicated, may hold values from 512 to 1024, as said below
- proj_weight: bfloat16 [3, 768, 768], P(None, 'seq', 'head'), may hold values from -0.3125 to 0.3125
- out_weight: bfloat16 [768, 768], P('head', 'seq'), may hold values from -1.5 to 1.5
- conv_taps: bfloat16 [9, 768], P(None, ('head', 'seq')), may hold values from -3 to 3
- attention_gain: bfloat16 [768], P('seq'), may hold values from 0.25 to 1.75
- up_weight: bfloat16 [768, 3072], P('seq', 'head'), may hold values from -0.21875 to 0.21875
- down_weight: bfloat16 [3072, 768], P('head', 'seq'), may hold values from -0.109375 to 0.109375
- feed_gain: bfloat16 [768], P('seq'), may hold values from 0.25 to 1.75
Outputs:
- short_output: bfloat16 [2, 512, 768], P(None, 'seq')
- long_output: bfloat16 [2, 1024, 768], P(None, 'seq')
- short_input_grad: float32 [2, 512, 768], P(None, 'seq')
- long_input_grad: float32 [2, 1024, 768], P(None, 'seq')
- proj_weight_grad: float32 [3, 768, 768], P(None, 'seq', 'head')
- out_weight_grad: float32 [768, 768], P('head', 'seq')
- conv_taps_grad: float32 [9, 768], P(None, ('head', 'seq'))
- attention_gain_grad: float32 [768], P('seq')
- up_weight_grad: float32 [768, 3072], P('seq', 'head')
- down_weight_grad: float32 [3072, 768], P('head', 'seq')
- feed_gain_grad: float32 [768], P('seq')
The draws below stay inside these ranges and needn't reach their ends.
Inputs may be any that keep to these rules, and one draw needn't show every extreme that they name: `short_lengths`: one sequence of every draw, which one drawn from the seed, has all 512 positions; the others have fewer. `long_lengths`: one sequence of every draw, which one drawn from the seed, has all 1024 positions; the others have fewer.
All inputs are finite; a program needn't handle non-finite values.
Results may differ from the reference program's by a relative error of at most 0.023.
Values may be sent and summed in bfloat16 or wider, within the bound.
No kernel may reach another device: no remote copies, remote signals or barrier semaphores. Data moves between devices by JAX's collectives and lax.ppermute only.
A program may use at most 128 MiB of HBM per device.

```python
import jax
import jax.numpy as jnp
from jax import lax

D = 768
HEADS = 12
FF = 3072
HEAD_DIM = 64
SHORT_SEQS = 2
LONG_SEQS = 2
SHORT_LEN = 512
LONG_LEN = 1024


def draw_short_lengths(key, part):
    key = jax.random.fold_in(key, 11)
    first_key, second_key = jax.random.split(key)
    drawn = jax.random.randint(first_key, (SHORT_SEQS,), SHORT_LEN // 2, SHORT_LEN)
    chosen = jax.random.randint(second_key, (), 0, SHORT_SEQS)
    return jnp.where(jnp.arange(SHORT_SEQS) == chosen, SHORT_LEN, drawn).astype(jnp.int32)


def draw_long_lengths(key, part):
    key = jax.random.fold_in(key, 12)
    first_key, second_key = jax.random.split(key)
    drawn = jax.random.randint(first_key, (LONG_SEQS,), LONG_LEN // 2, LONG_LEN)
    chosen = jax.random.randint(second_key, (), 0, LONG_SEQS)
    return jnp.where(jnp.arange(LONG_SEQS) == chosen, LONG_LEN, drawn).astype(jnp.int32)


def spiked(values, key, source, target, parts, factor):
    def block_of(axis_at):
        return (jnp.arange(values.shape[axis_at]) // (values.shape[axis_at] // parts)).reshape((-1,) + (1,) * (values.ndim - 1 - axis_at))

    near = jax.random.permutation(key, parts)[block_of(target)]
    far = (block_of(target) + parts // 2) % parts
    return jnp.where((block_of(source) == near) | (block_of(source) == far), factor * values, values)


def level_of(stream_key, dims, pieces, smallest, largest):
    def one(axis_at, parts):
        draws = jax.random.uniform(jax.random.fold_in(jax.random.fold_in(stream_key, 6), axis_at), (parts,), jnp.float32, smallest / len(pieces), largest / len(pieces))
        return jnp.repeat(jnp.exp(draws), dims[axis_at] // parts).reshape((-1,) + (1,) * (len(dims) - axis_at - 1))

    level = one(*pieces[0])
    for cut in pieces[1:]:
        level = level * one(*cut)
    return level


def scatter_about(own_key, extent, spread, most, cuts=(), kind=jnp.bfloat16):
    loudness = level_of(own_key, extent, cuts, -0.22, 0.18) if cuts else 1.0
    values = jax.random.normal(own_key, extent, jnp.float32) * spread * loudness
    return jnp.minimum(jnp.maximum(values, -most), most).astype(kind)


def gaussian_with(own_key, extent, deviation, most, shards, heavy, kind=jnp.bfloat16):
    entries = deviation * jax.random.normal(own_key, extent, jnp.float32)
    if shards:
        entries = entries * level_of(own_key, extent, shards, -0.22, 0.18)
    return jnp.clip(spiked(entries, jax.random.fold_in(own_key, 3), *heavy), -most, most).astype(kind)


def setup_inputs(seed: int = 0) -> dict:
    keys = jax.random.split(jax.random.key(seed), 14)
    return {
        "short_input": scatter_about(keys[0], (SHORT_SEQS, SHORT_LEN, D), 1.0, 6.0, ((1, 8),)),
        "long_input": scatter_about(keys[1], (LONG_SEQS, LONG_LEN, D), 1.0, 6.0, ((1, 8),)),
        "short_cotangent": gaussian_with(keys[2], (SHORT_SEQS, SHORT_LEN, D), 1.0, 6.0, ((1, 8),), (1, 2, 8, 2.0)),
        "long_cotangent": gaussian_with(keys[3], (LONG_SEQS, LONG_LEN, D), 1.0, 6.0, ((1, 8),), (1, 2, 8, 2.0)),
        "short_lengths": draw_short_lengths(jax.random.fold_in(keys[13], 71), 0),
        "long_lengths": draw_long_lengths(jax.random.fold_in(keys[13], 71), 0),
        "proj_weight": scatter_about(keys[6], (3, D, D), (D // 2) ** -0.5, 0.3125, ((1, 8), (2, 4))),
        "out_weight": scatter_about(keys[7], (D, D), (D // 48) ** -0.5, 1.5, ((0, 4), (1, 8))),
        "conv_taps": scatter_about(keys[8], (9, D), 0.6, 3.0, ((1, 32),)),
        "attention_gain": jnp.clip(1.0 + 0.15 * jax.random.normal(keys[9], (D,), jnp.float32), 0.25, 1.75).astype(jnp.bfloat16),
        "up_weight": scatter_about(keys[10], (D, FF), D ** -0.5, 0.21875, ((0, 8), (1, 4))),
        "down_weight": scatter_about(keys[11], (FF, D), FF ** -0.5, 0.109375, ((0, 4), (1, 8))),
        "feed_gain": jnp.clip(1.0 + 0.15 * jax.random.normal(keys[12], (D,), jnp.float32), 0.25, 1.75).astype(jnp.bfloat16),
    }


norm_eps = 1e-06
mask_fill = -1e+30
highest = lax.Precision.HIGHEST

@jax.custom_vjp
def low(v):
    return lax.optimization_barrier(v.astype(jnp.bfloat16)).astype(jnp.float32)

@jax.custom_vjp
def low_back(v):
    return v

def low_keep(v):
    return (low(v), None)

def low_pass(kept, grad):
    return (grad,)

def back_keep(v):
    return (v, None)

def back_low(kept, grad):
    return (low(grad),)
low.defvjp(low_keep, low_pass)
low_back.defvjp(back_keep, back_low)

def rms_norm(values_in, gain_row):
    inv_root = lax.rsqrt(lax.optimization_barrier(jnp.mean(values_in * values_in, axis=-1, keepdims=True)) + norm_eps)
    return values_in * inv_root * gain_row

def attend(queries, key_rows, values, length):
    seq_len = queries.shape[0]
    block_size = 512 if seq_len % 512 == 0 else seq_len
    block_count = seq_len // block_size
    key_pos = jnp.arange(seq_len, dtype=jnp.int32)

    def one_block(block_index):
        first_row = block_index * block_size
        query_block = lax.dynamic_slice_in_dim(queries, first_row, block_size, 0)
        raw_scores = jnp.einsum('qhe,khe->hqk', query_block, key_rows, precision=highest) * HEAD_DIM ** (-0.5)
        scores = low_back(raw_scores)
        query_pos = first_row + jnp.arange(block_size, dtype=jnp.int32)
        allowed = jnp.logical_and(key_pos[None, :] <= query_pos[:, None], key_pos[None, :] < length)
        scores = jnp.where(allowed[None], scores, mask_fill)
        top_row = lax.optimization_barrier(jnp.max(scores, axis=-1, keepdims=True))
        exp_terms = jnp.where(allowed[None], jnp.exp(scores - top_row), 0.0)
        row_total = lax.optimization_barrier(jnp.sum(exp_terms, axis=-1, keepdims=True))
        weighted = jnp.einsum('hqk,khe->qhe', low(exp_terms), values, precision=highest)
        return weighted / jnp.transpose(row_total, (1, 0, 2))
    result = lax.map(jax.checkpoint(one_block), jnp.arange(block_count, dtype=jnp.int32))
    return result.reshape(seq_len, queries.shape[1], queries.shape[2])

def sequence_forward(inputs, length, params):
    proj_weight, out_weight, conv_taps, attention_gain, up_weight, down_weight, feed_gain = params
    seq_len = inputs.shape[0]
    normed = low(rms_norm(inputs, attention_gain))
    mixed_qkv = low_back(low(jnp.einsum('td,cde->cte', normed, proj_weight, precision=highest)))
    padded = jnp.pad(mixed_qkv, ((0, 0), (2, 0), (0, 0)))
    tap_table = conv_taps.reshape(3, 3, D)
    conved = tap_table[:, 0:1, :] * padded[:, 2:, :] + tap_table[:, 1:2, :] * padded[:, 1:-1, :] + tap_table[:, 2:3, :] * padded[:, :-2, :]
    conv_out = low(conved).reshape(3, seq_len, HEADS, HEAD_DIM)
    attention = attend(conv_out[0], conv_out[1], conv_out[2], length).reshape(seq_len, D)
    attention_low = low_back(low(attention))
    mid_residual = inputs + low_back(jnp.dot(attention_low, out_weight, precision=highest))
    normed_ffn = low(rms_norm(mid_residual, feed_gain))
    up_proj = low_back(jnp.dot(normed_ffn, up_weight, precision=highest))
    squared = low(jnp.square(jax.nn.relu(up_proj)))
    return mid_residual + low_back(jnp.dot(squared, down_weight, precision=highest))

def sub_batch(inputs, lengths, params):

    def one_sequence(seq_pair):
        return sequence_forward(seq_pair[0], seq_pair[1], params)
    return lax.map(one_sequence, (inputs, lengths))

def masked(cotangent, lengths, seq_len):
    valid_rows = jnp.arange(seq_len, dtype=jnp.int32)[None, :] < lengths[:, None]
    return jnp.where(valid_rows[:, :, None], cotangent.astype(jnp.float32), 0.0)

def reference(short_input, long_input, short_cotangent, long_cotangent, short_lengths, long_lengths, proj_weight, out_weight, conv_taps, attention_gain, up_weight, down_weight, feed_gain):
    params = tuple((weight_arr.astype(jnp.float32) for weight_arr in (proj_weight, out_weight, conv_taps, attention_gain, up_weight, down_weight, feed_gain)))

    def forward(short_in, long_in, *weights):
        return (sub_batch(short_in, short_lengths, weights), sub_batch(long_in, long_lengths, weights))
    outputs, pull_back = jax.vjp(forward, short_input.astype(jnp.float32), long_input.astype(jnp.float32), *params)
    gradients = pull_back((masked(short_cotangent, short_lengths, SHORT_LEN), masked(long_cotangent, long_lengths, LONG_LEN)))
    return (outputs[0].astype(jnp.bfloat16), outputs[1].astype(jnp.bfloat16), gradients[0], gradients[1], gradients[2], gradients[3], gradients[4], gradients[5], gradients[6], gradients[7], gradients[8])
```

```python
import functools

import jax
import jax.numpy as jnp
import numpy as np
from jax import lax
from jax.experimental import pallas as pl
from jax.experimental.pallas import tpu as pltpu
from jax.sharding import PartitionSpec as P

HEAD_DIM = 64


norm_eps = 1e-06
mask_fill = -1e30
block_limit = 2048


def passed_along(block, axis, distance):
    devices = range(lax.axis_size(axis))
    route = [((i - distance) % len(devices), i) for i in devices]
    return lax.ppermute(block, axis, route)


def shifted(array, axis, by):
    peers = lax.axis_size(axis)
    pairs = [(i, i + by) for i in range(peers) if 0 <= i + by < peers]
    return lax.ppermute(array, axis, pairs)


def block_rows(row_count):
    size_rows = min(row_count, block_limit)
    while row_count % size_rows != 0:
        size_rows = size_rows - 1
    return size_rows


def norm_forward(values_in, gain_row):
    inv_root = lax.rsqrt(jnp.mean(values_in * values_in, axis=-1, keepdims=True) + norm_eps)
    return (values_in * inv_root * gain_row, inv_root)


def norm_backward(values_in, inv_root, gain_row, grad_in):
    weighted = grad_in * gain_row
    inner_mean = jnp.mean(weighted * values_in, axis=-1, keepdims=True)
    grad_values = inv_root * weighted - values_in * inv_root * inv_root * inv_root * inner_mean
    grad_gain = jnp.sum(grad_in * values_in * inv_root, axis=(0, 1))
    return (grad_values, grad_gain)


def allowed_mask(query_pos, key_pos, lengths):
    causal = key_pos[None, :] <= query_pos[:, None]
    inside = key_pos[None, :] < lengths[:, None]
    return jnp.logical_and(causal[None, None], inside[:, None, None, :])


def block_scores(query_rows, key_rows, query_pos, key_pos, lengths):
    allowed = allowed_mask(query_pos, key_pos, lengths)
    raw_scores = jnp.einsum(
        "bqhe,bkhe->bhqk", query_rows, key_rows, preferred_element_type=jnp.float32
    ) * HEAD_DIM ** (-0.5)
    return (jnp.where(allowed, raw_scores, mask_fill), allowed)


def block_grads(
    query_rows, grad_rows, log_rows, delta_rows, key_rows, value_rows, query_pos, key_pos, lengths
):
    scores, allowed = block_scores(query_rows, key_rows, query_pos, key_pos, lengths)
    prob_rows = jnp.where(
        allowed, jnp.exp(scores - jnp.transpose(log_rows, (0, 2, 1))[..., None]), 0.0
    )
    grad_probs = jnp.einsum(
        "bqhe,bkhe->bhqk", grad_rows, value_rows, preferred_element_type=jnp.float32
    )
    grad_scores = (
        prob_rows * (grad_probs - jnp.transpose(delta_rows, (0, 2, 1))[..., None])
    ).astype(jnp.bfloat16)
    grad_query = jnp.einsum(
        "bhqk,bkhe->bqhe", grad_scores, key_rows, preferred_element_type=jnp.float32
    ) * HEAD_DIM ** (-0.5)
    grad_key = jnp.einsum(
        "bhqk,bqhe->bkhe", grad_scores, query_rows, preferred_element_type=jnp.float32
    ) * HEAD_DIM ** (-0.5)
    grad_value = jnp.einsum(
        "bhqk,bqhe->bkhe",
        prob_rows.astype(jnp.bfloat16),
        grad_rows,
        preferred_element_type=jnp.float32,
    )
    return (grad_query, grad_key, grad_value)


def attend_forward(queries, keys_here, values_here, query_pos, lengths):
    seq_count, span_rows, head_count, head_width = queries.shape
    initial = (
        jnp.full((seq_count, head_count, span_rows), mask_fill, jnp.float32),
        jnp.zeros((seq_count, head_count, span_rows), jnp.float32),
        jnp.zeros((seq_count, span_rows, head_count, head_width), jnp.float32),
    )
    key_piece = lax.all_gather(keys_here, "seq", axis=1, tiled=True)
    value_piece = lax.all_gather(values_here, "seq", axis=1, tiled=True)
    row_count = key_piece.shape[1]
    size_rows = block_rows(row_count)

    def one_block(block_index, carried_state):
        running_top, running_sum, acc_rows = carried_state
        offset = block_index * size_rows
        key_rows = lax.dynamic_slice_in_dim(key_piece, offset, size_rows, 1)
        value_rows = lax.dynamic_slice_in_dim(value_piece, offset, size_rows, 1)
        key_pos = offset + jnp.arange(size_rows, dtype=jnp.int32)
        scores, allowed = block_scores(queries, key_rows, query_pos, key_pos, lengths)
        new_top = jnp.maximum(running_top, jnp.max(scores, axis=-1))
        exp_terms = jnp.where(allowed, jnp.exp(scores - new_top[..., None]), 0.0)
        shrink = jnp.exp(running_top - new_top)
        running_sum = running_sum * shrink + jnp.sum(exp_terms, axis=-1)
        acc_rows = acc_rows * jnp.transpose(shrink, (0, 2, 1))[..., None] + jnp.einsum(
            "bhqk,bkhe->bqhe",
            exp_terms.astype(jnp.bfloat16),
            value_rows,
            preferred_element_type=jnp.float32,
        )
        return (new_top, running_sum, acc_rows)

    running_top, running_sum, acc_rows = lax.fori_loop(
        0, row_count // size_rows, one_block, initial
    )
    attention = acc_rows / jnp.transpose(running_sum, (0, 2, 1))[..., None]
    log_totals = jnp.transpose(running_top + jnp.log(running_sum), (0, 2, 1))
    return (attention, log_totals)


def pass_sums(grad_keys, grad_values):
    return (
        passed_along(grad_keys.astype(jnp.bfloat16), "seq", 1).astype(grad_keys.dtype),
        passed_along(grad_values.astype(jnp.bfloat16), "seq", 1).astype(grad_values.dtype),
    )


def attend_backward(
    queries, keys_here, values_here, grad_attention, log_totals, delta_rows, query_pos, lengths
):
    seq_count, span_rows, head_count, head_width = queries.shape
    zeros_local = jnp.zeros(queries.shape, jnp.float32)
    seq_size = lax.axis_size("seq")
    my_index = lax.axis_index("seq")
    local_pos = jnp.arange(span_rows, dtype=jnp.int32)

    def step_grads(step, key_piece, value_piece):
        anchor = jnp.mod(my_index - step, seq_size)
        key_pos = anchor * span_rows + local_pos
        return block_grads(
            queries,
            grad_attention,
            log_totals,
            delta_rows,
            key_piece,
            value_piece,
            query_pos,
            key_pos,
            lengths,
        )

    def cycle_step(step, state):
        key_piece, value_piece, grad_keys, grad_values, grad_query = state
        query_part, key_part, value_part = step_grads(step, key_piece, value_piece)
        key_piece, value_piece = shifted((key_piece, value_piece), "seq", 1)
        grad_keys, grad_values = pass_sums(grad_keys + key_part, grad_values + value_part)
        return (key_piece, value_piece, grad_keys, grad_values, grad_query + query_part)

    final_state = lax.fori_loop(
        0, seq_size - 1, cycle_step, (keys_here, values_here, zeros_local, zeros_local, zeros_local)
    )
    key_piece, value_piece, grad_keys, grad_values, grad_query = final_state
    query_part, key_part, value_part = step_grads(seq_size - 1, key_piece, value_piece)
    grad_key, grad_value = pass_sums(grad_keys + key_part, grad_values + value_part)
    grad_query = grad_query + query_part
    return (grad_query, grad_key, grad_value)


def micro_batch(inputs, cotangent, lengths, weights):
    proj_full, out_full, taps_full, attend_gain, up_full, down_full, ffn_gain = weights
    seq_count, span_rows, model_width = inputs.shape
    local_width = proj_full.shape[2]
    heads_here = local_width // HEAD_DIM
    query_pos = lax.axis_index("seq") * span_rows + jnp.arange(span_rows, dtype=jnp.int32)
    valid_rows = (query_pos[None, :] < lengths[:, None])[..., None]
    residual_in = inputs.astype(jnp.float32)
    normed, inv_first = norm_forward(residual_in, attend_gain)
    normed_low = normed.astype(jnp.bfloat16)
    mixed_qkv = jnp.einsum(
        "btd,cde->cbte", normed_low, proj_full, preferred_element_type=jnp.float32
    ).astype(jnp.bfloat16)
    borrowed = shifted(mixed_qkv[:, :, span_rows - 2 :, :], "seq", 1)
    extended = jnp.concatenate([borrowed, mixed_qkv], axis=2).astype(jnp.float32)
    tap_table = taps_full.astype(jnp.float32).reshape(3, 3, local_width)
    tap_now = tap_table[:, 0][:, None, None, :]
    tap_one = tap_table[:, 1][:, None, None, :]
    tap_two = tap_table[:, 2][:, None, None, :]
    conved = (
        tap_now * extended[:, :, 2:]
        + tap_one * extended[:, :, 1:-1]
        + tap_two * extended[:, :, :-2]
    )
    conv_out = conved.astype(jnp.bfloat16).reshape(3, seq_count, span_rows, heads_here, HEAD_DIM)
    queries, keys_here, values_here = (conv_out[0], conv_out[1], conv_out[2])
    attention, log_totals = attend_forward(queries, keys_here, values_here, query_pos, lengths)
    attention_low = attention.astype(jnp.bfloat16).reshape(seq_count, span_rows, local_width)
    attend_part = jnp.einsum(
        "bte,ed->btd", attention_low, out_full, preferred_element_type=jnp.float32
    )
    mid_residual = residual_in + lax.psum(attend_part.astype(jnp.bfloat16), "head").astype(
        jnp.float32
    )
    normed_ffn, inv_second = norm_forward(mid_residual, ffn_gain)
    normed_ffn_low = normed_ffn.astype(jnp.bfloat16)
    up_proj = jnp.einsum("btd,df->btf", normed_ffn_low, up_full, preferred_element_type=jnp.float32)
    relu_up = jnp.maximum(up_proj, 0.0)
    squared = (relu_up * relu_up).astype(jnp.bfloat16)
    ffn_part = jnp.einsum("btf,fd->btd", squared, down_full, preferred_element_type=jnp.float32)
    output = (
        mid_residual + lax.psum(ffn_part.astype(jnp.bfloat16), "head").astype(jnp.float32)
    ).astype(jnp.bfloat16)
    grad_out = jnp.where(valid_rows, cotangent.astype(jnp.float32), 0.0)
    grad_out_low = grad_out.astype(jnp.bfloat16)
    down_term = jnp.einsum("btf,btd->fd", squared, grad_out_low, preferred_element_type=jnp.float32)
    grad_squared = jnp.einsum(
        "btd,fd->btf", grad_out_low, down_full, preferred_element_type=jnp.float32
    )
    grad_up = (grad_squared * 2.0 * relu_up).astype(jnp.bfloat16)
    up_term = jnp.einsum("btd,btf->df", normed_ffn_low, grad_up, preferred_element_type=jnp.float32)
    grad_normed_ffn = lax.psum(
        jnp.einsum("btf,df->btd", grad_up, up_full, preferred_element_type=jnp.float32).astype(
            jnp.bfloat16
        ),
        "head",
    ).astype(jnp.float32)
    grad_through, feed_term = norm_backward(mid_residual, inv_second, ffn_gain, grad_normed_ffn)
    grad_mid = grad_out + grad_through
    grad_mid_low = grad_mid.astype(jnp.bfloat16)
    out_term = jnp.einsum(
        "bte,btd->ed", attention_low, grad_mid_low, preferred_element_type=jnp.float32
    )
    grad_attention = jnp.einsum(
        "btd,ed->bte", grad_mid_low, out_full, preferred_element_type=jnp.float32
    )
    grad_attention = grad_attention.astype(jnp.bfloat16).reshape(
        seq_count, span_rows, heads_here, HEAD_DIM
    )
    delta_rows = jnp.einsum("bqhe,bqhe->bqh", grad_attention.astype(jnp.float32), attention)
    grad_query, grad_key, grad_value = attend_backward(
        queries, keys_here, values_here, grad_attention, log_totals, delta_rows, query_pos, lengths
    )
    grad_conv = jnp.stack([grad_query, grad_key, grad_value]).reshape(
        3, seq_count, span_rows, local_width
    )
    taps_term = jnp.stack(
        [
            jnp.sum(grad_conv * extended[:, :, 2:], axis=(1, 2)),
            jnp.sum(grad_conv * extended[:, :, 1:-1], axis=(1, 2)),
            jnp.sum(grad_conv * extended[:, :, :-2], axis=(1, 2)),
        ],
        axis=1,
    ).reshape(9, local_width)
    full_grad = jnp.pad(grad_conv, ((0, 0), (0, 0), (2, 2), (0, 0)))
    grad_extended = (
        tap_now * full_grad[:, :, 0 : span_rows + 2]
        + tap_one * full_grad[:, :, 1 : span_rows + 3]
        + tap_two * full_grad[:, :, 2 : span_rows + 4]
    )
    returned = shifted(grad_extended[:, :, :2], "seq", -1)
    grad_mixed = jnp.concatenate(
        [grad_extended[:, :, 2:span_rows], grad_extended[:, :, span_rows:] + returned], axis=2
    ).astype(jnp.bfloat16)
    proj_term = jnp.einsum(
        "btd,cbte->cde", normed_low, grad_mixed, preferred_element_type=jnp.float32
    )
    grad_normed = lax.psum(
        jnp.einsum(
            "cbte,cde->btd", grad_mixed, proj_full, preferred_element_type=jnp.float32
        ).astype(jnp.bfloat16),
        "head",
    ).astype(jnp.float32)
    grad_first, attention_term = norm_backward(residual_in, inv_first, attend_gain, grad_normed)
    grad_input = grad_mid + grad_first
    return (
        output,
        grad_input,
        (proj_term, out_term, taps_term, attention_term, up_term, down_term, feed_term),
    )


def ring_shards(
    short_input,
    long_input,
    short_cotangent,
    long_cotangent,
    short_lengths,
    long_lengths,
    proj_weight,
    out_weight,
    conv_taps,
    attention_gain,
    up_weight,
    down_weight,
    feed_gain,
):
    proj_full, out_full, taps_full, attend_gain = (
        lax.all_gather(proj_weight, "seq", axis=1, tiled=True),
        lax.all_gather(out_weight, "seq", axis=1, tiled=True),
        lax.all_gather(conv_taps, "seq", axis=1, tiled=True),
        lax.all_gather(attention_gain, "seq", axis=0, tiled=True),
    )
    up_full, down_full, ffn_gain = (
        lax.all_gather(up_weight, "seq", axis=0, tiled=True),
        lax.all_gather(down_weight, "seq", axis=1, tiled=True),
        lax.all_gather(feed_gain, "seq", axis=0, tiled=True),
    )
    weights = (
        proj_full,
        out_full,
        taps_full,
        attend_gain.astype(jnp.float32),
        up_full,
        down_full,
        ffn_gain.astype(jnp.float32),
    )
    short_output, short_input_grad, short_terms = micro_batch(
        short_input, short_cotangent, short_lengths, weights
    )
    long_output, long_input_grad, long_terms = micro_batch(
        long_input, long_cotangent, long_lengths, weights
    )
    summed = tuple(
        (first_term + second_term for first_term, second_term in zip(short_terms, long_terms))
    )
    reduced = (
        lax.psum_scatter(summed[0], "seq", scatter_dimension=1, tiled=True),
        lax.psum_scatter(summed[1], "seq", scatter_dimension=1, tiled=True),
        lax.psum_scatter(summed[2], "seq", scatter_dimension=1, tiled=True),
        lax.psum_scatter(summed[3], "seq", scatter_dimension=0, tiled=True),
        lax.psum_scatter(summed[4], "seq", scatter_dimension=0, tiled=True),
        lax.psum_scatter(summed[5], "seq", scatter_dimension=1, tiled=True),
        lax.psum_scatter(summed[6], "seq", scatter_dimension=0, tiled=True),
    )
    return (
        short_output,
        long_output,
        short_input_grad,
        long_input_grad,
        reduced[0],
        reduced[1],
        reduced[2],
        reduced[3],
        reduced[4],
        reduced[5],
        reduced[6],
    )


LANES = 128
NT = (((1,), (1,)), ((), ()))
TN = (((0,), (0,)), ((), ()))
F32 = jnp.float32
BF16 = jnp.bfloat16


def dot(a, b, dims=(((1,), (0,)), ((), ()))):
    return lax.dot_general(a, b, dims, preferred_element_type=F32)


def in_vmem(body, outs, scalars, arrays, scratch=(), limit_mib=16):
    return pl.pallas_call(
        body,
        out_shape=[
            pltpu.HBM(*out[:2]) if len(out) == 3 else jax.ShapeDtypeStruct(*out) for out in outs
        ],
        in_specs=[pl.BlockSpec(memory_space=pltpu.SMEM)] * len(scalars)
        + [pl.BlockSpec(memory_space=pltpu.VMEM)] * len(arrays),
        out_specs=[pl.BlockSpec(memory_space=pltpu.VMEM)] * len(outs),
        scratch_shapes=[pltpu.VMEM(shape, kind) for shape, kind in scratch],
        compiler_params=pltpu.CompilerParams(vmem_limit_bytes=limit_mib * 1024 * 1024),
        cost_estimate=pl.CostEstimate(flops=0, bytes_accessed=0, transcendentals=0),
    )(*scalars, *arrays)


def far(*arrays):
    return tuple(pltpu.with_memory_space_constraint(array, pltpu.HBM) for array in arrays)


def after(array, *others):
    return lax.optimization_barrier((array, *others))[0]


def exchange(array, axis, mask):
    size = lax.axis_size(axis)
    return lax.ppermute(array, axis, [(i, i ^ mask) for i in range(size)])


def add_low(a, b):
    return (a.astype(F32) + b.astype(F32)).astype(BF16)


def shift_back(rows, by):
    index = lax.broadcasted_iota(jnp.int32, rows.shape, 0)
    return jnp.where(index >= by, pltpu.roll(rows, by, axis=0), 0.0)


def shift_ahead(rows, by):
    count = rows.shape[0]
    index = lax.broadcasted_iota(jnp.int32, rows.shape, 0)
    return jnp.where(index < count - by, pltpu.roll(rows, count - by, axis=0), 0.0)


def fold(rows):
    half = rows.shape[0] // 2
    return jnp.concatenate([rows[:half], rows[half:]], axis=1)


def unfold(rows):
    return jnp.concatenate([rows[:, :HEAD_DIM], rows[:, HEAD_DIM:]], axis=0)


def pack_proj_body(proj, gain, packed):
    rows = proj.shape[1]
    for c in range(3):
        packed[c * rows : (c + 1) * rows, :] = proj[c, :, :LANES]
    narrow = jnp.concatenate([proj[c, :, LANES:] for c in range(3)], axis=0)
    packed[3 * rows : 9 * rows // 2, :] = fold(narrow)
    gain_row = gain[...].astype(F32).reshape(1, rows)
    gain_row = jnp.concatenate([gain_row, jnp.zeros((1, LANES - rows), F32)], axis=1)
    packed[9 * rows // 2 :, :] = jnp.broadcast_to(gain_row, (16, LANES)).astype(BF16)


def unpack_proj(packed, rows):
    narrow = unfold(packed[3 * rows : 9 * rows // 2, :])
    return [
        (packed[c * rows : (c + 1) * rows, :], narrow[c * rows : (c + 1) * rows, :])
        for c in range(3)
    ]


def narrow_pack(block, store):
    groups = block.shape[0] // 16
    for g in range(groups):
        rows = block[16 * g : 16 * g + 16, :]
        store(0, LANES * g, rows[:, :LANES])
        tail = rows[:, LANES:]
        store(16, LANES * g, jnp.concatenate([tail, jnp.zeros_like(tail)], axis=1))


def pack_ffn_body(up, down, out, gain, packed):
    rows = up.shape[0]
    gain_column = gain[...].astype(F32).reshape(1, rows).T
    packed[:rows, :] = (up[...].astype(F32) * gain_column).astype(BF16)
    packed[rows : 2 * rows, :] = down[...]

    def store(row, lane, value):
        packed[2 * rows + row : 2 * rows + row + 16, lane : lane + LANES] = value

    narrow_pack(out[...].astype(F32).T.astype(BF16), store)


def place_ffn_body(place, *refs):
    parts = refs[:8]
    up, down, out = refs[8:]
    rows = up.shape[0] // 8
    for i in range(8):
        first = pl.multiple_of(jnp.bitwise_xor(place[0], i) * rows, rows)
        part = parts[i]
        up[pl.ds(first, rows), :] = part[:rows, :]
        down[pl.ds(first, rows), :] = part[rows : 2 * rows, :]
        for g in range(rows // 16):
            at = pl.ds(pl.multiple_of(first + 16 * g, 16), 16)
            lanes = slice(LANES * g, LANES * g + LANES)
            out[at, :LANES] = part[2 * rows : 2 * rows + 16, lanes]
            out[at, LANES:] = part[2 * rows + 16 : 2 * rows + 32, LANES * g : LANES * g + HEAD_DIM]


def project_body(place, *refs):
    parts = refs[:8]
    long_in, short_in, taps, send, normed, weight, gain, gain_rows = refs[8:]
    seqs, long_rows, _ = long_in.shape
    rows = long_rows + short_in.shape[1]
    for i in range(8):
        packed = parts[i][...]
        shard = weight.shape[1] // 8
        owner = jnp.bitwise_xor(place[0], i)
        gain_rows[pl.ds(owner, 1), :] = packed[9 * shard // 2 :, :].astype(F32)[:1]
        first = pl.multiple_of(owner * shard, shard)
        for c, (wide, narrow) in enumerate(unpack_proj(packed, shard)):
            weight[c, pl.ds(first, shard), :LANES] = wide
            weight[c, pl.ds(first, shard), LANES:] = narrow
    gain[...] = jnp.concatenate([gain_rows[j : j + 1, :shard] for j in range(8)], axis=1)
    for b in range(seqs):
        values = jnp.concatenate([long_in[b], short_in[b]], axis=0).astype(F32)
        root = lax.rsqrt(jnp.mean(values * values, axis=-1, keepdims=True) + norm_eps)
        normed[b * rows : (b + 1) * rows, :] = (values * root * gain[...]).astype(BF16)
    mixed = [dot(normed[...], weight[c]).astype(BF16) for c in range(3)]
    tap_rows = jnp.concatenate(
        [taps[...], jnp.zeros((16 - taps.shape[0], taps.shape[1]), BF16)], axis=0
    )
    tap_rows = jnp.concatenate(
        [tap_rows, jnp.zeros((16, LANES - taps.shape[1]), BF16)], axis=1
    )
    half = rows // 2
    for dest in range(8):
        if dest < 3 * seqs:
            e, b = dest // seqs, dest % seqs
            lanes = slice(e * HEAD_DIM, (e + 1) * HEAD_DIM)
            q, k, v = [m[b * rows : (b + 1) * rows, lanes] for m in mixed]
            send[dest, :rows, :] = jnp.concatenate([k, v], axis=1)
            send[dest, rows : rows + half, :] = fold(q)
        else:
            send[dest, : rows + half, :] = jnp.zeros((rows + half, LANES), BF16)
        send[dest, rows + half :, :] = tap_rows


def head_taps(place, came, rows, seqs):
    first = rows + rows // 2
    width = 3 * HEAD_DIM // 8
    whole = jnp.concatenate(
        [came[j, first:, :].astype(F32)[:, :width] for j in range(8)], axis=1
    )
    e = place[0] // seqs
    mine = whole[:, :HEAD_DIM]
    for other in (1, 2):
        mine = jnp.where(
            e == other, whole[:, other * HEAD_DIM : (other + 1) * HEAD_DIM], mine
        )
    taps_q = [mine[m : m + 1, :] for m in range(3)]
    taps_kv = [
        jnp.concatenate([mine[3 + m : 4 + m, :], mine[6 + m : 7 + m, :]], axis=1) for m in range(3)
    ]
    return taps_q, taps_kv


def own_pair(came, long_rows, rows):
    q_rows = [unfold(came[j, rows : rows + rows // 2, :]) for j in range(8)]
    result = []
    for part in (slice(0, long_rows), slice(long_rows, rows)):
        q = jnp.concatenate([piece[part] for piece in q_rows], axis=0).astype(F32)
        kv = jnp.concatenate([came[j, part, :] for j in range(8)], axis=0).astype(F32)
        result.append((q, kv))
    return result


def convolve(rows, taps):
    return taps[0] * rows + taps[1] * shift_back(rows, 1) + taps[2] * shift_back(rows, 2)


def attend_body(
    long_rows, seqs, place, long_lengths, short_lengths, came, send, q_all, kv_all, att_t, log_row, kept
):
    rows = (came.shape[1] - 16) * 2 // 3
    kept[...] = came[...]
    taps_q, taps_kv = head_taps(place, came, rows, seqs)
    b = place[0] % seqs
    first = 0
    results = []
    for lengths, (q_mixed, kv_mixed) in zip(
        (long_lengths, short_lengths), own_pair(came, long_rows, rows)
    ):
        count = q_mixed.shape[0]
        block = min(256, count)
        length = lengths[b]
        q = (convolve(q_mixed, taps_q).astype(BF16).astype(F32) * HEAD_DIM ** (-0.5)).astype(BF16)
        kv = convolve(kv_mixed, taps_kv).astype(BF16)
        kv_t = kv.astype(F32).T.astype(BF16)
        q_all[first : first + count, :] = q
        kv_all[first : first + count, :] = kv
        k = kv[:, :HEAD_DIM]
        v_t = kv_t[HEAD_DIM:, :]
        pieces = []
        for start in range(0, count, block):
            stop = start + block
            scores = dot(k[:stop], q[start:stop], NT)
            key_pos = lax.broadcasted_iota(jnp.int32, scores.shape, 0)
            query_pos = lax.broadcasted_iota(jnp.int32, scores.shape, 1) + start
            allowed = jnp.logical_and(key_pos <= query_pos, key_pos < length)
            scores = jnp.where(allowed, scores, mask_fill)
            top = jnp.max(scores, axis=0, keepdims=True)
            terms = jnp.exp(scores - top)
            total = jnp.sum(terms, axis=0, keepdims=True)
            out_t = dot(v_t[:, :stop], terms.astype(BF16)) / total
            att_t[:, first + start : first + stop] = out_t
            log_row[:, first + start : first + stop] = top + jnp.log(total)
            pieces.append(out_t.T.astype(BF16))
        results.append(jnp.concatenate(pieces, axis=0))
        first += count
    short_rows = rows - long_rows
    for j in range(8):
        mine = jnp.concatenate(
            [
                results[0][j * long_rows : (j + 1) * long_rows],
                results[1][j * short_rows : (j + 1) * short_rows],
            ],
            axis=0,
        )
        send[j, :, :] = fold(mine)


def pair_rows(came, seqs):
    columns = []
    for e in range(3):
        columns.append(
            jnp.concatenate([unfold(came[seqs * e + b]) for b in range(seqs)], axis=0)
        )
    return jnp.concatenate(columns, axis=1)


def feed_body(
    long_rows,
    place,
    long_lengths,
    short_lengths,
    att_0,
    att_1,
    att_2,
    att_3,
    out_0,
    out_1,
    out_2,
    out_3,
    long_in,
    short_in,
    long_cot,
    short_cot,
    up,
    down,
    mid_ref,
    normed_ref,
    squared_ref,
    grad_up_ref,
    grad_out_ref,
    att_ref,
    keep,
    send,
    scratch,
    sums,
):
    seqs = long_in.shape[0]
    rows = long_rows + short_in.shape[1]
    att_ref[...] = pair_rows(att_0, seqs)
    sums[place[1]] = dot(att_ref[...], out_0[...], NT)
    for i, att, out in ((1, att_1, out_1), (2, att_2, out_2), (3, att_3, out_3)):
        sums[jnp.bitwise_xor(place[1], i)] = dot(pair_rows(att, seqs), out[...], NT)
    for b in range(seqs):
        at = slice(b * rows, (b + 1) * rows)
        residual = jnp.concatenate([long_in[b], short_in[b]], axis=0).astype(F32)
        mid = residual + ((sums[0, at, :] + sums[1, at, :]) + (sums[2, at, :] + sums[3, at, :]))
        mid_ref[at, :] = mid
        root = lax.rsqrt(jnp.mean(mid * mid, axis=-1, keepdims=True) + norm_eps)
        normed_ref[at, :] = (mid * root).astype(BF16)
        for cot, lengths, first, count in (
            (long_cot, long_lengths, b * rows, long_rows),
            (short_cot, short_lengths, b * rows + long_rows, rows - long_rows),
        ):
            value = cot[b]
            position = lax.broadcasted_iota(jnp.int32, value.shape, 0) + place[0] * count
            grad_out_ref[first : first + count, :] = jnp.where(
                position < lengths[b], value.astype(F32), 0.0
            ).astype(BF16)
    relu = jnp.maximum(dot(normed_ref[...], up[...]), 0.0)
    squared_ref[...] = (relu * relu).astype(BF16)
    grad_squared = dot(grad_out_ref[...], down[...])
    grad_up_ref[...] = (grad_squared * 2.0 * relu).astype(BF16)
    scratch[...] = dot(grad_up_ref[...], up[...], NT).astype(BF16)
    split_halves(place, scratch, keep, send)


def split_halves(place, whole, keep, send):
    half = whole.shape[0] // 2
    core = place[1] % 2
    keep[...] = whole[pl.ds(pl.multiple_of(core * half, half), half), :]
    send[...] = whole[pl.ds(pl.multiple_of((1 - core) * half, half), half), :]


def join_halves(place, whole, own, other):
    half = own.shape[0]
    core = place[1] % 2
    whole[pl.ds(pl.multiple_of(core * half, half), half), :] = own[...].astype(whole.dtype)
    whole[pl.ds(pl.multiple_of((1 - core) * half, half), half), :] = other[...].astype(whole.dtype)


def split_y(place, blocks, keep, send):
    y = place[0] % 2
    for z in range(4):
        keep[z] = blocks[2 * z + y]
        send[z] = blocks[2 * z + 1 - y]


def feed_terms_body(
    place, normed, squared, grad_up, grad_out, down, f_keep, f_send, keep, send, scratch, blocks
):
    scratch[...] = dot(squared[...], down[...], NT).astype(BF16)
    split_halves(place, scratch, f_keep, f_send)
    rows = down.shape[0] // 8
    up_term = dot(normed[...], grad_up[...], TN).astype(BF16)
    down_term = dot(grad_out[...], squared[...], TN).astype(BF16)
    for s in range(8):
        blocks[s, :rows, :] = up_term[s * rows : (s + 1) * rows]
        blocks[s, rows:, :] = down_term[s * rows : (s + 1) * rows]
    split_y(place, blocks, keep, send)


def middle_body(place, own, other, mid_ref, grad_out, out, grad_mid_ref, low_ref, send, scratch):
    join_halves(place, scratch, own, other)
    seqs = 2
    rows = mid_ref.shape[0] // seqs
    for b in range(seqs):
        at = slice(b * rows, (b + 1) * rows)
        mid = mid_ref[at, :]
        weighted = scratch[at, :]
        root = lax.rsqrt(jnp.mean(mid * mid, axis=-1, keepdims=True) + norm_eps)
        inner = jnp.mean(weighted * mid, axis=-1, keepdims=True)
        grad_mid = grad_out[at, :].astype(F32) + (
            root * weighted - mid * (root * root * root * inner)
        )
        grad_mid_ref[at, :] = grad_mid
        low_ref[at, :] = grad_mid.astype(BF16)
    grad_att = dot(low_ref[...], out[...]).astype(BF16)
    for dest in range(8):
        if dest < 3 * seqs:
            e, b = dest // seqs, dest % seqs
            send[dest] = fold(
                grad_att[b * rows : (b + 1) * rows, e * HEAD_DIM : (e + 1) * HEAD_DIM]
            )
        else:
            send[dest] = jnp.zeros_like(send[dest])


def out_term_body(place, low, att, keep, send, blocks):
    term = dot(low[...], att[...], TN).astype(BF16)
    rows = term.shape[0] // 8
    for s in range(8):

        def store(row, lane, value):
            blocks[s, row : row + 16, lane : lane + LANES] = value

        narrow_pack(term[s * rows : (s + 1) * rows], store)
    split_y(place, blocks, keep, send)


def attend_back_body(
    long_rows,
    seqs,
    place,
    long_lengths,
    short_lengths,
    came,
    q_all,
    kv_all,
    att_t,
    log_row,
    grad_came,
    send,
):
    rows = (came.shape[1] - 16) * 2 // 3
    short_rows = rows - long_rows
    taps_q, taps_kv = head_taps(place, came, rows, seqs)
    b = place[0] % seqs
    e = place[0] // seqs
    grads = [unfold(grad_came[j]) for j in range(8)]
    first = 0
    terms_q = [0.0, 0.0, 0.0]
    terms_kv = [0.0, 0.0, 0.0]
    results = []
    for lengths, part, (q_mixed, kv_mixed) in zip(
        (long_lengths, short_lengths),
        (slice(0, long_rows), slice(long_rows, rows)),
        own_pair(came, long_rows, rows),
    ):
        count = q_mixed.shape[0]
        block = min(256, count)
        length = lengths[b]
        at = slice(first, first + count)
        grad = jnp.concatenate([g[part] for g in grads], axis=0)
        q = q_all[at, :]
        kv = kv_all[at, :]
        kv_t = kv.astype(F32).T.astype(BF16)
        delta = jnp.sum(grad.astype(F32).T * att_t[:, at], axis=0, keepdims=True)
        log_total = log_row[:, at]
        k, v = kv[:, :HEAD_DIM], kv[:, HEAD_DIM:]
        k_t = kv_t[:HEAD_DIM, :]
        grad_q = None
        grad_kv = []
        for start in range(0, count, block):
            stop = start + block
            scores = dot(k[start:stop], q[start:], NT)
            key_pos = lax.broadcasted_iota(jnp.int32, scores.shape, 0)
            query_pos = lax.broadcasted_iota(jnp.int32, scores.shape, 1)
            allowed = jnp.logical_and(key_pos <= query_pos, key_pos + start < length)
            prob = jnp.where(allowed, jnp.exp(scores - log_total[:, start:]), 0.0)
            grad_prob = dot(v[start:stop], grad[start:], NT)
            grad_scores = (prob * (grad_prob - delta[:, start:])).astype(BF16)
            grad_k = dot(grad_scores, q[start:])
            grad_v = dot(prob.astype(BF16), grad[start:])
            grad_kv.append(jnp.concatenate([grad_k, grad_v], axis=1))
            part_q = dot(k_t[:, start:stop], grad_scores)
            if start == 0:
                grad_q = part_q
            else:
                grad_q = jnp.concatenate(
                    [grad_q[:, :start], grad_q[:, start:] + part_q], axis=1
                )
        grad_q = grad_q.T * HEAD_DIM ** (-0.5)
        grad_kv = jnp.concatenate(grad_kv, axis=0)
        pair = []
        for grad_conv, mixed, taps, terms in (
            (grad_q, q_mixed, taps_q, terms_q),
            (grad_kv, kv_mixed, taps_kv, terms_kv),
        ):
            for m in range(3):
                back = mixed if m == 0 else shift_back(mixed, m)
                terms[m] = terms[m] + jnp.sum(grad_conv * back, axis=0, keepdims=True)
            pair.append(
                (
                    taps[0] * grad_conv
                    + taps[1] * shift_ahead(grad_conv, 1)
                    + taps[2] * shift_ahead(grad_conv, 2)
                ).astype(BF16)
            )
        results.append(pair)
        first += count
    table = jnp.concatenate(
        terms_q
        + [t[:, :HEAD_DIM] for t in terms_kv]
        + [t[:, HEAD_DIM:] for t in terms_kv]
        + [jnp.zeros((7, HEAD_DIM), F32)],
        axis=0,
    )
    table = jnp.concatenate([jnp.where(e == i, table, 0.0) for i in range(3)], axis=1)
    width = 3 * HEAD_DIM // 8
    for j in range(8):
        mine = [
            jnp.concatenate(
                [
                    results[0][i][j * long_rows : (j + 1) * long_rows],
                    results[1][i][j * short_rows : (j + 1) * short_rows],
                ],
                axis=0,
            )
            for i in range(2)
        ]
        send[j, :rows, :] = mine[1]
        send[j, rows : rows + rows // 2, :] = fold(mine[0])
        send[j, rows + rows // 2 :, :] = jnp.concatenate(
            [table[:, j * width : (j + 1) * width], jnp.zeros((16, LANES - width), F32)], axis=1
        ).astype(BF16)


def project_back_body(
    place, came, normed, weight, keep, send, keep_w, send_w, taps, scratch, grad_mixed, blocks
):
    seqs = 2
    rows = (came.shape[1] - 16) * 2 // 3
    for e in range(3):
        for b in range(seqs):
            j = seqs * e + b
            at = slice(b * rows, (b + 1) * rows)
            lanes = slice(e * HEAD_DIM, (e + 1) * HEAD_DIM)
            grad_mixed[0, at, lanes] = unfold(came[j, rows : rows + rows // 2, :])
            grad_mixed[1, at, lanes] = came[j, :rows, :HEAD_DIM]
            grad_mixed[2, at, lanes] = came[j, :rows, HEAD_DIM:]
    total = came[0, rows + rows // 2 :, :].astype(F32)
    for j in range(1, 3 * seqs):
        total = total + came[j, rows + rows // 2 :, :].astype(F32)
    taps[...] = total[: taps.shape[0], : taps.shape[1]]
    shard = weight.shape[1] // 8
    terms = [dot(normed[...], grad_mixed[c], TN).astype(BF16) for c in range(3)]
    for s in range(8):
        at = slice(s * shard, (s + 1) * shard)
        for c in range(3):
            blocks[s, c * shard : (c + 1) * shard, :] = terms[c][at, :LANES]
        blocks[s, 3 * shard :, :] = fold(
            jnp.concatenate([terms[c][at, LANES:] for c in range(3)], axis=0)
        )
    split_y(place, blocks, keep, send)
    total = dot(grad_mixed[0], weight[0], NT)
    for c in (1, 2):
        total = total + dot(grad_mixed[c], weight[c], NT)
    scratch[...] = total.astype(BF16)
    split_halves(place, scratch, keep_w, send_w)


def input_grad_body(
    place, own, other, grad_mid, gain, long_in, short_in, long_out, short_out, scratch
):
    join_halves(place, scratch, own, other)
    seqs, long_rows, _ = long_in.shape
    rows = long_rows + short_in.shape[1]
    for b in range(seqs):
        at = slice(b * rows, (b + 1) * rows)
        values = jnp.concatenate([long_in[b], short_in[b]], axis=0).astype(F32)
        weighted = scratch[at, :] * gain[...]
        root = lax.rsqrt(jnp.mean(values * values, axis=-1, keepdims=True) + norm_eps)
        inner = jnp.mean(weighted * values, axis=-1, keepdims=True)
        grad = grad_mid[at, :] + (root * weighted - values * (root * root * root * inner))
        long_out[b] = grad[:long_rows]
        short_out[b] = grad[long_rows:]


def scatter_z_body(place, *refs):
    count = (len(refs) - 4) // 2
    outs = refs[2 * count :]
    z = place[0] // 2
    for i in range(4):
        block = jnp.bitwise_xor(z, i)
        first = 0
        for a in range(count):
            keep, came = refs[2 * a], refs[2 * a + 1]
            rows = keep.shape[1]
            outs[i][first : first + rows, :] = (
                keep[block].astype(F32) + came[block].astype(F32)
            ).astype(BF16)
            first += rows


def sum_blocks(blocks):
    return (blocks[0][...].astype(F32) + blocks[1][...].astype(F32)) + (
        blocks[2][...].astype(F32) + blocks[3][...].astype(F32)
    )


def proj_grad_body(b0, b1, b2, b3, proj, gain, grad, gain_grad):
    total = sum_blocks((b0, b1, b2, b3))
    rows = proj.shape[1]
    column = 0.0
    for c, (wide, narrow) in enumerate(unpack_proj(total, rows)):
        term = jnp.concatenate([wide, narrow], axis=1)
        column = column + jnp.sum(term * proj[c].astype(F32), axis=1, keepdims=True)
        grad[c] = term
    gain_grad[...] = column.T / gain[...].astype(F32).reshape(1, rows)


def ffn_grad_body(b0, b1, b2, b3, up, gain, up_grad, down_grad, out_grad, gain_grad):
    total = sum_blocks((b0, b1, b2, b3))
    rows = up.shape[0]
    raw = total[:rows]
    gain_grad[...] = jnp.sum(raw * up[...].astype(F32), axis=1, keepdims=True).T
    up_grad[...] = raw * gain[...].astype(F32).reshape(1, rows).T
    down_grad[...] = total[rows : 2 * rows]
    wide = total[2 * rows : 2 * rows + 16]
    narrow = total[2 * rows + 16 :]
    out = jnp.concatenate(
        [
            jnp.concatenate(
                [
                    wide[:, LANES * g : LANES * (g + 1)],
                    narrow[:, LANES * g : LANES * g + HEAD_DIM],
                ],
                axis=1,
            )
            for g in range(rows // 16)
        ],
        axis=0,
    )
    out_grad[...] = out.T


def pair_shards(
    short_input,
    long_input,
    short_cotangent,
    long_cotangent,
    short_lengths,
    long_lengths,
    proj_weight,
    out_weight,
    conv_taps,
    attention_gain,
    up_weight,
    down_weight,
    feed_gain,
):
    seqs, long_rows, width = long_input.shape
    short_rows = short_input.shape[1]
    rows = long_rows + short_rows
    tokens = seqs * rows
    shard = proj_weight.shape[1]
    local = proj_weight.shape[2]
    hidden = up_weight.shape[1]
    long_len, short_len = 8 * long_rows, 8 * short_rows
    total_len = long_len + short_len
    place = jnp.stack([lax.axis_index("seq"), lax.axis_index("head")]).astype(jnp.int32)
    packed_rows = shard * 9 // 2
    chunk = rows + rows // 2 + 16
    down_t = down_weight.T

    (proj_packed,) = in_vmem(
        pack_proj_body, [((packed_rows + 16, LANES), BF16)], (), (proj_weight, attention_gain)
    )
    proj_z = [proj_packed] + [exchange(proj_packed, "seq", mask) for mask in (2, 4, 6)]
    proj_parts = []
    for piece in proj_z:
        proj_parts += [piece, exchange(piece, "seq", 1)]
    (ffn_packed,) = in_vmem(
        pack_ffn_body,
        [((2 * shard + 32, hidden), BF16)],
        (),
        far(up_weight, down_t, out_weight) + (feed_gain,),
    )
    send, normed, proj_full, gain = in_vmem(
        project_body,
        [
            ((8, chunk, LANES), BF16),
            ((tokens, width), BF16, "far"),
            ((3, width, local), BF16, "far"),
            ((1, width), F32, "far"),
        ],
        (place,),
        (*proj_parts, *far(long_input, short_input, conv_taps)),
        scratch=[((8, LANES), F32)],
    )
    came = lax.all_to_all(send, "seq", 0, 0, tiled=True)
    ffn_0 = after(ffn_packed, *proj_z)
    ffn_2 = exchange(ffn_0, "seq", 2)
    ffn_4 = exchange(ffn_0, "seq", 4)
    ffn_1 = exchange(ffn_0, "seq", 1)
    att_send, q_all, kv_all, att_t, log_row, mixed = in_vmem(
        functools.partial(attend_body, long_rows, seqs),
        [
            ((8, rows // 2, LANES), BF16),
            ((total_len, HEAD_DIM), BF16, "far"),
            ((total_len, 2 * HEAD_DIM), BF16, "far"),
            ((HEAD_DIM, total_len), F32, "far"),
            ((1, total_len), F32, "far"),
            ((8, chunk, LANES), BF16, "far"),
        ],
        (place, long_lengths, short_lengths),
        (came,),
    )
    att_0 = lax.all_to_all(att_send, "seq", 0, 0, tiled=True)
    ffn_2, ffn_4 = after(ffn_2, att_send), after(ffn_4, att_send)
    ffn_6 = exchange(ffn_4, "seq", 2)
    ffn_3 = exchange(ffn_2, "seq", 1)
    ffn_5 = exchange(ffn_4, "seq", 1)
    ffn_7 = exchange(ffn_6, "seq", 1)
    up_full, down_full, out_full = in_vmem(
        place_ffn_body,
        [
            ((width, hidden), BF16, "far"),
            ((width, hidden), BF16, "far"),
            ((width, local), BF16, "far"),
        ],
        (place,),
        far(ffn_0, ffn_1, ffn_2, ffn_3, ffn_4, ffn_5, ffn_6, ffn_7),
    )
    out_2 = exchange(out_full, "head", 2)
    out_1 = exchange(out_full, "head", 1)
    out_3 = exchange(out_2, "head", 1)
    att_2 = exchange(att_0, "head", 2)
    att_1 = exchange(att_0, "head", 1)
    att_3 = exchange(att_2, "head", 1)
    mid, normed_ffn, squared, grad_up, grad_out, att, keep, send = in_vmem(
        functools.partial(feed_body, long_rows),
        [
            ((tokens, width), F32, "far"),
            ((tokens, width), BF16, "far"),
            ((tokens, hidden), BF16, "far"),
            ((tokens, hidden), BF16, "far"),
            ((tokens, width), BF16, "far"),
            ((tokens, local), BF16, "far"),
            ((tokens // 2, width), BF16),
            ((tokens // 2, width), BF16),
        ],
        (place, long_lengths, short_lengths),
        (att_0, att_1, att_2, att_3)
        + far(
            out_full,
            out_1,
            out_2,
            out_3,
            long_input,
            short_input,
            long_cotangent,
            short_cotangent,
            up_full,
            down_full,
        ),
        scratch=[((tokens, width), BF16), ((4, tokens, width), F32)],
        limit_mib=32,
    )
    half = add_low(keep, exchange(send, "head", 1))
    f_keep, f_send, ffn_keep, ffn_send = in_vmem(
        feed_terms_body,
        [
            ((tokens // 2, width), BF16, "far"),
            ((tokens // 2, width), BF16, "far"),
            ((4, 2 * shard, hidden), BF16, "far"),
            ((4, 2 * shard, hidden), BF16, "far"),
        ],
        (place,),
        far(normed_ffn, squared, grad_up, grad_out, down_full),
        scratch=[((tokens, width), BF16), ((8, 2 * shard, hidden), BF16)],
        limit_mib=32,
    )
    ffn_came = exchange(ffn_send, "seq", 1)
    own = add_low(half, after(exchange(half, "head", 2), ffn_send))
    other = exchange(own, "head", 1)
    grad_mid, grad_mid_low, send = in_vmem(
        middle_body,
        [
            ((tokens, width), F32, "far"),
            ((tokens, width), BF16, "far"),
            ((8, rows // 2, LANES), BF16),
        ],
        (place,),
        (own, other) + far(mid, grad_out, out_full),
        scratch=[((tokens, width), F32)],
    )
    grad_came = lax.all_to_all(send, "seq", 0, 0, tiled=True)
    out_keep, out_send = in_vmem(
        out_term_body,
        [((4, 32, hidden), BF16, "far"), ((4, 32, hidden), BF16, "far")],
        (place,),
        far(grad_mid_low, att),
        scratch=[((8, 32, hidden), BF16)],
    )
    out_came = exchange(out_send, "seq", 1)
    f_half = add_low(f_keep, exchange(f_send, "head", 1))
    f_own = add_low(f_half, exchange(f_half, "head", 2))
    f_other = exchange(f_own, "head", 1)
    (send,) = in_vmem(
        functools.partial(attend_back_body, long_rows, seqs),
        [((8, chunk, LANES), BF16)],
        (place, long_lengths, short_lengths),
        far(mixed, q_all, kv_all, att_t, log_row) + (after(grad_came, out_send),),
    )
    mixed_came = lax.all_to_all(send, "seq", 0, 0, tiled=True)
    ffn_blocks = in_vmem(
        scatter_z_body,
        [((2 * shard + 32, hidden), BF16, "far")] * 4,
        (place,),
        far(ffn_keep, ffn_came, out_keep, out_came),
    )
    ffn_blocks = [ffn_blocks[0]] + [exchange(ffn_blocks[i], "seq", 2 * i) for i in (1, 2, 3)]
    proj_keep, proj_send, keep, send, taps_grad = in_vmem(
        project_back_body,
        [
            ((4, packed_rows, LANES), BF16, "far"),
            ((4, packed_rows, LANES), BF16, "far"),
            ((tokens // 2, width), BF16),
            ((tokens // 2, width), BF16),
            (conv_taps.shape, F32),
        ],
        (place,),
        (mixed_came,) + far(normed, proj_full),
        scratch=[
            ((tokens, width), BF16),
            ((3, tokens, local), BF16),
            ((8, packed_rows, LANES), BF16),
        ],
    )
    proj_came = exchange(proj_send, "seq", 1)
    half = add_low(keep, exchange(send, "head", 1))
    own = add_low(half, exchange(half, "head", 2))
    other = exchange(own, "head", 1)
    proj_blocks = in_vmem(
        scatter_z_body,
        [((packed_rows, LANES), BF16)] * 4,
        (place,),
        far(proj_keep) + (proj_came,),
    )
    proj_blocks = [proj_blocks[0]] + [exchange(proj_blocks[i], "seq", 2 * i) for i in (1, 2, 3)]
    long_input_grad, short_input_grad = in_vmem(
        input_grad_body,
        [(long_input.shape, F32), (short_input.shape, F32)],
        (place,),
        (own, other) + far(grad_mid, gain, long_input, short_input),
        scratch=[((tokens, width), F32)],
    )
    up_grad, down_grad, out_grad, feed_part = in_vmem(
        ffn_grad_body,
        [
            (up_weight.shape, F32),
            (down_t.shape, F32),
            (out_weight.shape, F32),
            ((1, shard), F32),
        ],
        (),
        far(*ffn_blocks, up_weight) + (feed_gain,),
    )
    proj_grad, attention_part = in_vmem(
        proj_grad_body,
        [(proj_weight.shape, F32), ((1, shard), F32)],
        (),
        (*proj_blocks, *far(proj_weight), attention_gain),
    )
    gains = jnp.concatenate([attention_part, feed_part], axis=0)
    gains = gains + exchange(gains, "head", 1)
    gains = gains + exchange(gains, "head", 2)

    f_own, f_other = f_own.astype(F32), f_other.astype(F32)
    core = lax.axis_index("head") % 2
    first = jnp.where(core == 0, f_own, f_other)
    second = jnp.where(core == 0, f_other, f_own)
    output = (mid + jnp.concatenate([first, second], axis=0)).astype(BF16)
    output = output.reshape(seqs, rows, width)
    return (
        output[:, long_rows:],
        output[:, :long_rows],
        short_input_grad,
        long_input_grad,
        proj_grad,
        out_grad,
        taps_grad,
        gains[0],
        up_grad,
        down_grad.T,
        gains[1],
    )


def fits_pairs(short_input, long_input, proj_weight):
    seqs, long_rows, _ = long_input.shape
    short_seqs, short_rows, _ = short_input.shape
    return (
        lax.axis_size("seq") == 8
        and lax.axis_size("head") == 4
        and seqs == 2
        and short_seqs == 2
        and proj_weight.shape[2] == 3 * HEAD_DIM
        and proj_weight.shape[1] % 32 == 0
        and long_rows % 32 == 0
        and short_rows % 32 == 0
        and 8 * long_rows <= 2048
    )


def shards(short_input, long_input, *rest):
    proj_weight = rest[4]
    if fits_pairs(short_input, long_input, proj_weight):
        return pair_shards(short_input, long_input, *rest)
    return ring_shards(short_input, long_input, *rest)


def solution(mesh):
    placed = (
        P(None, "seq", None),
        P(None, "seq", None),
        P(None, "seq", None),
        P(None, "seq", None),
        P(),
        P(),
        P(None, "seq", "head"),
        P("head", "seq"),
        P(None, ("head", "seq")),
        P("seq"),
        P("seq", "head"),
        P("head", "seq"),
        P("seq"),
    )
    return jax.shard_map(
        shards,
        mesh=mesh,
        in_specs=placed,
        out_specs=(
            P(None, "seq", None),
            P(None, "seq", None),
            P(None, "seq", None),
            P(None, "seq", None),
            P(None, "seq", "head"),
            P("head", "seq"),
            P(None, ("head", "seq")),
            P("seq"),
            P("seq", "head"),
            P("head", "seq"),
            P("seq"),
        ),
        check_vma=False,
    )
```

```python
import functools

import jax
import jax.numpy as jnp
import numpy as np
from jax import lax
from jax.experimental import pallas as pl
from jax.experimental.pallas import tpu as pltpu
from jax.sharding import PartitionSpec as P

HEAD_DIM = 64


norm_eps = 1e-06
mask_fill = -1e30
block_limit = 2048


def passed_along(block, axis, distance):
    devices = range(lax.axis_size(axis))
    route = [((i - distance) % len(devices), i) for i in devices]
    return lax.ppermute(block, axis, route)


def shifted(array, axis, by):
    peers = lax.axis_size(axis)
    pairs = [(i, i + by) for i in range(peers) if 0 <= i + by < peers]
    return lax.ppermute(array, axis, pairs)


def block_rows(row_count):
    size_rows = min(row_count, block_limit)
    while row_count % size_rows != 0:
        size_rows = size_rows - 1
    return size_rows


def norm_forward(values_in, gain_row):
    inv_root = lax.rsqrt(jnp.mean(values_in * values_in, axis=-1, keepdims=True) + norm_eps)
    return (values_in * inv_root * gain_row, inv_root)


def norm_backward(values_in, inv_root, gain_row, grad_in):
    weighted = grad_in * gain_row
    inner_mean = jnp.mean(weighted * values_in, axis=-1, keepdims=True)
    grad_values = inv_root * weighted - values_in * inv_root * inv_root * inv_root * inner_mean
    grad_gain = jnp.sum(grad_in * values_in * inv_root, axis=(0, 1))
    return (grad_values, grad_gain)


def allowed_mask(query_pos, key_pos, lengths):
    causal = key_pos[None, :] <= query_pos[:, None]
    inside = key_pos[None, :] < lengths[:, None]
    return jnp.logical_and(causal[None, None], inside[:, None, None, :])


def block_scores(query_rows, key_rows, query_pos, key_pos, lengths):
    allowed = allowed_mask(query_pos, key_pos, lengths)
    raw_scores = jnp.einsum(
        "bqhe,bkhe->bhqk", query_rows, key_rows, preferred_element_type=jnp.float32
    ) * HEAD_DIM ** (-0.5)
    return (jnp.where(allowed, raw_scores, mask_fill), allowed)


def block_grads(
    query_rows, grad_rows, log_rows, delta_rows, key_rows, value_rows, query_pos, key_pos, lengths
):
    scores, allowed = block_scores(query_rows, key_rows, query_pos, key_pos, lengths)
    prob_rows = jnp.where(
        allowed, jnp.exp(scores - jnp.transpose(log_rows, (0, 2, 1))[..., None]), 0.0
    )
    grad_probs = jnp.einsum(
        "bqhe,bkhe->bhqk", grad_rows, value_rows, preferred_element_type=jnp.float32
    )
    grad_scores = (
        prob_rows * (grad_probs - jnp.transpose(delta_rows, (0, 2, 1))[..., None])
    ).astype(jnp.bfloat16)
    grad_query = jnp.einsum(
        "bhqk,bkhe->bqhe", grad_scores, key_rows, preferred_element_type=jnp.float32
    ) * HEAD_DIM ** (-0.5)
    grad_key = jnp.einsum(
        "bhqk,bqhe->bkhe", grad_scores, query_rows, preferred_element_type=jnp.float32
    ) * HEAD_DIM ** (-0.5)
    grad_value = jnp.einsum(
        "bhqk,bqhe->bkhe",
        prob_rows.astype(jnp.bfloat16),
        grad_rows,
        preferred_element_type=jnp.float32,
    )
    return (grad_query, grad_key, grad_value)


def attend_forward(queries, keys_here, values_here, query_pos, lengths):
    seq_count, span_rows, head_count, head_width = queries.shape
    initial = (
        jnp.full((seq_count, head_count, span_rows), mask_fill, jnp.float32),
        jnp.zeros((seq_count, head_count, span_rows), jnp.float32),
        jnp.zeros((seq_count, span_rows, head_count, head_width), jnp.float32),
    )
    key_piece = lax.all_gather(keys_here, "seq", axis=1, tiled=True)
    value_piece = lax.all_gather(values_here, "seq", axis=1, tiled=True)
    row_count = key_piece.shape[1]
    size_rows = block_rows(row_count)

    def one_block(block_index, carried_state):
        running_top, running_sum, acc_rows = carried_state
        offset = block_index * size_rows
        key_rows = lax.dynamic_slice_in_dim(key_piece, offset, size_rows, 1)
        value_rows = lax.dynamic_slice_in_dim(value_piece, offset, size_rows, 1)
        key_pos = offset + jnp.arange(size_rows, dtype=jnp.int32)
        scores, allowed = block_scores(queries, key_rows, query_pos, key_pos, lengths)
        new_top = jnp.maximum(running_top, jnp.max(scores, axis=-1))
        exp_terms = jnp.where(allowed, jnp.exp(scores - new_top[..., None]), 0.0)
        shrink = jnp.exp(running_top - new_top)
        running_sum = running_sum * shrink + jnp.sum(exp_terms, axis=-1)
        acc_rows = acc_rows * jnp.transpose(shrink, (0, 2, 1))[..., None] + jnp.einsum(
            "bhqk,bkhe->bqhe",
            exp_terms.astype(jnp.bfloat16),
            value_rows,
            preferred_element_type=jnp.float32,
        )
        return (new_top, running_sum, acc_rows)

    running_top, running_sum, acc_rows = lax.fori_loop(
        0, row_count // size_rows, one_block, initial
    )
    attention = acc_rows / jnp.transpose(running_sum, (0, 2, 1))[..., None]
    log_totals = jnp.transpose(running_top + jnp.log(running_sum), (0, 2, 1))
    return (attention, log_totals)


def pass_sums(grad_keys, grad_values):
    return (
        passed_along(grad_keys.astype(jnp.bfloat16), "seq", 1).astype(grad_keys.dtype),
        passed_along(grad_values.astype(jnp.bfloat16), "seq", 1).astype(grad_values.dtype),
    )


def attend_backward(
    queries, keys_here, values_here, grad_attention, log_totals, delta_rows, query_pos, lengths
):
    seq_count, span_rows, head_count, head_width = queries.shape
    zeros_local = jnp.zeros(queries.shape, jnp.float32)
    seq_size = lax.axis_size("seq")
    my_index = lax.axis_index("seq")
    local_pos = jnp.arange(span_rows, dtype=jnp.int32)

    def step_grads(step, key_piece, value_piece):
        anchor = jnp.mod(my_index - step, seq_size)
        key_pos = anchor * span_rows + local_pos
        return block_grads(
            queries,
            grad_attention,
            log_totals,
            delta_rows,
            key_piece,
            value_piece,
            query_pos,
            key_pos,
            lengths,
        )

    def cycle_step(step, state):
        key_piece, value_piece, grad_keys, grad_values, grad_query = state
        query_part, key_part, value_part = step_grads(step, key_piece, value_piece)
        key_piece, value_piece = shifted((key_piece, value_piece), "seq", 1)
        grad_keys, grad_values = pass_sums(grad_keys + key_part, grad_values + value_part)
        return (key_piece, value_piece, grad_keys, grad_values, grad_query + query_part)

    final_state = lax.fori_loop(
        0, seq_size - 1, cycle_step, (keys_here, values_here, zeros_local, zeros_local, zeros_local)
    )
    key_piece, value_piece, grad_keys, grad_values, grad_query = final_state
    query_part, key_part, value_part = step_grads(seq_size - 1, key_piece, value_piece)
    grad_key, grad_value = pass_sums(grad_keys + key_part, grad_values + value_part)
    grad_query = grad_query + query_part
    return (grad_query, grad_key, grad_value)


def micro_batch(inputs, cotangent, lengths, weights):
    proj_full, out_full, taps_full, attend_gain, up_full, down_full, ffn_gain = weights
    seq_count, span_rows, model_width = inputs.shape
    local_width = proj_full.shape[2]
    heads_here = local_width // HEAD_DIM
    query_pos = lax.axis_index("seq") * span_rows + jnp.arange(span_rows, dtype=jnp.int32)
    valid_rows = (query_pos[None, :] < lengths[:, None])[..., None]
    residual_in = inputs.astype(jnp.float32)
    normed, inv_first = norm_forward(residual_in, attend_gain)
    normed_low = normed.astype(jnp.bfloat16)
    mixed_qkv = jnp.einsum(
        "btd,cde->cbte", normed_low, proj_full, preferred_element_type=jnp.float32
    ).astype(jnp.bfloat16)
    borrowed = shifted(mixed_qkv[:, :, span_rows - 2 :, :], "seq", 1)
    extended = jnp.concatenate([borrowed, mixed_qkv], axis=2).astype(jnp.float32)
    tap_table = taps_full.astype(jnp.float32).reshape(3, 3, local_width)
    tap_now = tap_table[:, 0][:, None, None, :]
    tap_one = tap_table[:, 1][:, None, None, :]
    tap_two = tap_table[:, 2][:, None, None, :]
    conved = (
        tap_now * extended[:, :, 2:]
        + tap_one * extended[:, :, 1:-1]
        + tap_two * extended[:, :, :-2]
    )
    conv_out = conved.astype(jnp.bfloat16).reshape(3, seq_count, span_rows, heads_here, HEAD_DIM)
    queries, keys_here, values_here = (conv_out[0], conv_out[1], conv_out[2])
    attention, log_totals = attend_forward(queries, keys_here, values_here, query_pos, lengths)
    attention_low = attention.astype(jnp.bfloat16).reshape(seq_count, span_rows, local_width)
    attend_part = jnp.einsum(
        "bte,ed->btd", attention_low, out_full, preferred_element_type=jnp.float32
    )
    mid_residual = residual_in + lax.psum(attend_part.astype(jnp.bfloat16), "head").astype(
        jnp.float32
    )
    normed_ffn, inv_second = norm_forward(mid_residual, ffn_gain)
    normed_ffn_low = normed_ffn.astype(jnp.bfloat16)
    up_proj = jnp.einsum("btd,df->btf", normed_ffn_low, up_full, preferred_element_type=jnp.float32)
    relu_up = jnp.maximum(up_proj, 0.0)
    squared = (relu_up * relu_up).astype(jnp.bfloat16)
    ffn_part = jnp.einsum("btf,fd->btd", squared, down_full, preferred_element_type=jnp.float32)
    output = (
        mid_residual + lax.psum(ffn_part.astype(jnp.bfloat16), "head").astype(jnp.float32)
    ).astype(jnp.bfloat16)
    grad_out = jnp.where(valid_rows, cotangent.astype(jnp.float32), 0.0)
    grad_out_low = grad_out.astype(jnp.bfloat16)
    down_term = jnp.einsum("btf,btd->fd", squared, grad_out_low, preferred_element_type=jnp.float32)
    grad_squared = jnp.einsum(
        "btd,fd->btf", grad_out_low, down_full, preferred_element_type=jnp.float32
    )
    grad_up = (grad_squared * 2.0 * relu_up).astype(jnp.bfloat16)
    up_term = jnp.einsum("btd,btf->df", normed_ffn_low, grad_up, preferred_element_type=jnp.float32)
    grad_normed_ffn = lax.psum(
        jnp.einsum("btf,df->btd", grad_up, up_full, preferred_element_type=jnp.float32).astype(
            jnp.bfloat16
        ),
        "head",
    ).astype(jnp.float32)
    grad_through, feed_term = norm_backward(mid_residual, inv_second, ffn_gain, grad_normed_ffn)
    grad_mid = grad_out + grad_through
    grad_mid_low = grad_mid.astype(jnp.bfloat16)
    out_term = jnp.einsum(
        "bte,btd->ed", attention_low, grad_mid_low, preferred_element_type=jnp.float32
    )
    grad_attention = jnp.einsum(
        "btd,ed->bte", grad_mid_low, out_full, preferred_element_type=jnp.float32
    )
    grad_attention = grad_attention.astype(jnp.bfloat16).reshape(
        seq_count, span_rows, heads_here, HEAD_DIM
    )
    delta_rows = jnp.einsum("bqhe,bqhe->bqh", grad_attention.astype(jnp.float32), attention)
    grad_query, grad_key, grad_value = attend_backward(
        queries, keys_here, values_here, grad_attention, log_totals, delta_rows, query_pos, lengths
    )
    grad_conv = jnp.stack([grad_query, grad_key, grad_value]).reshape(
        3, seq_count, span_rows, local_width
    )
    taps_term = jnp.stack(
        [
            jnp.sum(grad_conv * extended[:, :, 2:], axis=(1, 2)),
            jnp.sum(grad_conv * extended[:, :, 1:-1], axis=(1, 2)),
            jnp.sum(grad_conv * extended[:, :, :-2], axis=(1, 2)),
        ],
        axis=1,
    ).reshape(9, local_width)
    full_grad = jnp.pad(grad_conv, ((0, 0), (0, 0), (2, 2), (0, 0)))
    grad_extended = (
        tap_now * full_grad[:, :, 0 : span_rows + 2]
        + tap_one * full_grad[:, :, 1 : span_rows + 3]
        + tap_two * full_grad[:, :, 2 : span_rows + 4]
    )
    returned = shifted(grad_extended[:, :, :2], "seq", -1)
    grad_mixed = jnp.concatenate(
        [grad_extended[:, :, 2:span_rows], grad_extended[:, :, span_rows:] + returned], axis=2
    ).astype(jnp.bfloat16)
    proj_term = jnp.einsum(
        "btd,cbte->cde", normed_low, grad_mixed, preferred_element_type=jnp.float32
    )
    grad_normed = lax.psum(
        jnp.einsum(
            "cbte,cde->btd", grad_mixed, proj_full, preferred_element_type=jnp.float32
        ).astype(jnp.bfloat16),
        "head",
    ).astype(jnp.float32)
    grad_first, attention_term = norm_backward(residual_in, inv_first, attend_gain, grad_normed)
    grad_input = grad_mid + grad_first
    return (
        output,
        grad_input,
        (proj_term, out_term, taps_term, attention_term, up_term, down_term, feed_term),
    )


def ring_shards(
    short_input,
    long_input,
    short_cotangent,
    long_cotangent,
    short_lengths,
    long_lengths,
    proj_weight,
    out_weight,
    conv_taps,
    attention_gain,
    up_weight,
    down_weight,
    feed_gain,
):
    proj_full, out_full, taps_full, attend_gain = (
        lax.all_gather(proj_weight, "seq", axis=1, tiled=True),
        lax.all_gather(out_weight, "seq", axis=1, tiled=True),
        lax.all_gather(conv_taps, "seq", axis=1, tiled=True),
        lax.all_gather(attention_gain, "seq", axis=0, tiled=True),
    )
    up_full, down_full, ffn_gain = (
        lax.all_gather(up_weight, "seq", axis=0, tiled=True),
        lax.all_gather(down_weight, "seq", axis=1, tiled=True),
        lax.all_gather(feed_gain, "seq", axis=0, tiled=True),
    )
    weights = (
        proj_full,
        out_full,
        taps_full,
        attend_gain.astype(jnp.float32),
        up_full,
        down_full,
        ffn_gain.astype(jnp.float32),
    )
    short_output, short_input_grad, short_terms = micro_batch(
        short_input, short_cotangent, short_lengths, weights
    )
    long_output, long_input_grad, long_terms = micro_batch(
        long_input, long_cotangent, long_lengths, weights
    )
    summed = tuple(
        (first_term + second_term for first_term, second_term in zip(short_terms, long_terms))
    )
    reduced = (
        lax.psum_scatter(summed[0], "seq", scatter_dimension=1, tiled=True),
        lax.psum_scatter(summed[1], "seq", scatter_dimension=1, tiled=True),
        lax.psum_scatter(summed[2], "seq", scatter_dimension=1, tiled=True),
        lax.psum_scatter(summed[3], "seq", scatter_dimension=0, tiled=True),
        lax.psum_scatter(summed[4], "seq", scatter_dimension=0, tiled=True),
        lax.psum_scatter(summed[5], "seq", scatter_dimension=1, tiled=True),
        lax.psum_scatter(summed[6], "seq", scatter_dimension=0, tiled=True),
    )
    return (
        short_output,
        long_output,
        short_input_grad,
        long_input_grad,
        reduced[0],
        reduced[1],
        reduced[2],
        reduced[3],
        reduced[4],
        reduced[5],
        reduced[6],
    )


LANES = 128
FENCE = 10**11
NT = (((1,), (1,)), ((), ()))
TN = (((0,), (0,)), ((), ()))
F32 = jnp.float32
BF16 = jnp.bfloat16


def dot(a, b, dims=(((1,), (0,)), ((), ()))):
    return lax.dot_general(a, b, dims, preferred_element_type=F32)


def in_vmem(body, outs, scalars, arrays, scratch=(), limit_mib=16, fence=False):
    return pl.pallas_call(
        body,
        out_shape=[
            pltpu.HBM(*out[:2]) if len(out) == 3 else jax.ShapeDtypeStruct(*out) for out in outs
        ],
        in_specs=[pl.BlockSpec(memory_space=pltpu.SMEM)] * len(scalars)
        + [pl.BlockSpec(memory_space=pltpu.VMEM)] * len(arrays),
        out_specs=[pl.BlockSpec(memory_space=pltpu.VMEM)] * len(outs),
        scratch_shapes=[pltpu.VMEM(shape, kind) for shape, kind in scratch],
        compiler_params=pltpu.CompilerParams(vmem_limit_bytes=limit_mib * 1024 * 1024),
        cost_estimate=pl.CostEstimate(
            flops=FENCE if fence else 0, bytes_accessed=0, transcendentals=0
        ),
    )(*scalars, *arrays)


def far(*arrays):
    return tuple(pltpu.with_memory_space_constraint(array, pltpu.HBM) for array in arrays)


def after(array, *others):
    return lax.optimization_barrier((array, *others))[0]


def marker(*arrays):
    def body(*refs):
        refs[-1][...] = jnp.zeros_like(refs[-1])

    return pl.pallas_call(
        body,
        out_shape=jax.ShapeDtypeStruct((8, LANES), F32),
        in_specs=[pl.BlockSpec(memory_space=pl.ANY)] * len(arrays),
        out_specs=pl.BlockSpec(memory_space=pltpu.VMEM),
        cost_estimate=pl.CostEstimate(flops=FENCE, bytes_accessed=0, transcendentals=0),
    )(*arrays)


def exchange(array, axis, mask):
    size = lax.axis_size(axis)
    return lax.ppermute(array, axis, [(i, i ^ mask) for i in range(size)])


def add_low(a, b):
    return (a.astype(F32) + b.astype(F32)).astype(BF16)


def shift_back(rows, by):
    index = lax.broadcasted_iota(jnp.int32, rows.shape, 0)
    return jnp.where(index >= by, pltpu.roll(rows, by, axis=0), 0.0)


def shift_ahead(rows, by):
    count = rows.shape[0]
    index = lax.broadcasted_iota(jnp.int32, rows.shape, 0)
    return jnp.where(index < count - by, pltpu.roll(rows, count - by, axis=0), 0.0)


def fold(rows):
    half = rows.shape[0] // 2
    return jnp.concatenate([rows[:half], rows[half:]], axis=1)


def unfold(rows):
    return jnp.concatenate([rows[:, :HEAD_DIM], rows[:, HEAD_DIM:]], axis=0)


def pack_proj_body(proj, gain, packed):
    rows = proj.shape[1]
    for c in range(3):
        packed[c * rows : (c + 1) * rows, :] = proj[c, :, :LANES]
    narrow = jnp.concatenate([proj[c, :, LANES:] for c in range(3)], axis=0)
    packed[3 * rows : 9 * rows // 2, :] = fold(narrow)
    gain_row = gain[...].astype(F32).reshape(1, rows)
    gain_row = jnp.concatenate([gain_row, jnp.zeros((1, LANES - rows), F32)], axis=1)
    packed[9 * rows // 2 :, :] = jnp.broadcast_to(gain_row, (16, LANES)).astype(BF16)


def unpack_blocks(packed, rows, count):
    narrow = unfold(packed[count * rows : 3 * count * rows // 2, :])
    return [
        (packed[i * rows : (i + 1) * rows, :], narrow[i * rows : (i + 1) * rows, :])
        for i in range(count)
    ]


def narrow_pack(block, store):
    groups = block.shape[0] // 16
    for g in range(groups):
        rows = block[16 * g : 16 * g + 16, :]
        store(0, LANES * g, rows[:, :LANES])
        tail = rows[:, LANES:]
        store(16, LANES * g, jnp.concatenate([tail, jnp.zeros_like(tail)], axis=1))


def pack_ffn_body(up, down, out, gain, packed):
    rows = up.shape[0]
    gain_column = gain[...].astype(F32).reshape(1, rows).T
    packed[:rows, :] = (up[...].astype(F32) * gain_column).astype(BF16)
    packed[rows : 2 * rows, :] = down[...]

    def store(row, lane, value):
        packed[2 * rows + row : 2 * rows + row + 16, lane : lane + LANES] = value

    narrow_pack(out[...].astype(F32).T.astype(BF16), store)


def place_ffn_body(place, *refs):
    whole, out = refs[8:]
    rows = out.shape[0] // 8
    for i in range(8):
        owner = jnp.bitwise_xor(place[0], i)
        part = refs[i]
        whole[owner] = part[: 2 * rows, :]
        for g in range(rows // 16):
            at = pl.ds(pl.multiple_of(owner * rows + 16 * g, 16), 16)
            out[at, :LANES] = part[2 * rows : 2 * rows + 16, LANES * g : LANES * g + LANES]
            out[at, LANES:] = part[2 * rows + 16 :, LANES * g : LANES * g + HEAD_DIM]


def project_body(place, *refs):
    parts = refs[:8]
    long_in, short_in, taps, send, normed, weight, gain, gain_rows = refs[8:]
    seqs, long_rows, _ = long_in.shape
    rows = long_rows + short_in.shape[1]
    for i in range(8):
        packed = parts[i][...]
        shard = weight.shape[1] // 8
        owner = jnp.bitwise_xor(place[0], i)
        gain_rows[pl.ds(owner, 1), :] = packed[9 * shard // 2 :, :].astype(F32)[:1]
        at = pl.ds(pl.multiple_of(owner * shard, shard), shard)
        for c, (wide, narrow) in enumerate(unpack_blocks(packed, shard, 3)):
            weight[c, at, :LANES] = wide
            weight[c, at, LANES:] = narrow
    gain[...] = jnp.concatenate([gain_rows[j : j + 1, :shard] for j in range(8)], axis=1)
    for b in range(seqs):
        values = jnp.concatenate([long_in[b], short_in[b]], axis=0).astype(F32)
        root = lax.rsqrt(jnp.mean(values * values, axis=-1, keepdims=True) + norm_eps)
        normed[b * rows : (b + 1) * rows, :] = (values * root * gain[...]).astype(BF16)
    mixed = [dot(normed[...], weight[c]).astype(BF16) for c in range(3)]
    tap_rows = jnp.concatenate(
        [taps[...], jnp.zeros((16 - taps.shape[0], taps.shape[1]), BF16)], axis=0
    )
    tap_rows = jnp.concatenate(
        [tap_rows, jnp.zeros((16, LANES - taps.shape[1]), BF16)], axis=1
    )
    half = rows // 2
    for dest in range(8):
        if dest < 3 * seqs:
            e, b = dest // seqs, dest % seqs
            lanes = slice(e * HEAD_DIM, (e + 1) * HEAD_DIM)
            q, k, v = [m[b * rows : (b + 1) * rows, lanes] for m in mixed]
            send[dest, :rows, :] = jnp.concatenate([k, v], axis=1)
            send[dest, rows : rows + half, :] = fold(q)
        else:
            send[dest, : rows + half, :] = jnp.zeros((rows + half, LANES), BF16)
        send[dest, rows + half :, :] = tap_rows


def head_taps(place, came, rows, seqs):
    first = rows + rows // 2
    width = 3 * HEAD_DIM // 8
    whole = jnp.concatenate(
        [came[j, first:, :].astype(F32)[:, :width] for j in range(8)], axis=1
    )
    e = place[0] // seqs
    mine = whole[:, :HEAD_DIM]
    for other in (1, 2):
        mine = jnp.where(
            e == other, whole[:, other * HEAD_DIM : (other + 1) * HEAD_DIM], mine
        )
    taps_q = [mine[m : m + 1, :] for m in range(3)]
    taps_kv = [
        jnp.concatenate([mine[3 + m : 4 + m, :], mine[6 + m : 7 + m, :]], axis=1) for m in range(3)
    ]
    return taps_q, taps_kv


def own_pair(came, long_rows, rows):
    q_rows = [unfold(came[j, rows : rows + rows // 2, :]) for j in range(8)]
    result = []
    for part in (slice(0, long_rows), slice(long_rows, rows)):
        q = jnp.concatenate([piece[part] for piece in q_rows], axis=0).astype(F32)
        kv = jnp.concatenate([came[j, part, :] for j in range(8)], axis=0).astype(F32)
        result.append((q, kv))
    return result


def convolve(rows, taps):
    return taps[0] * rows + taps[1] * shift_back(rows, 1) + taps[2] * shift_back(rows, 2)


def attend_body(
    long_rows, seqs, place, long_lengths, short_lengths, came, send, q_all, kv_all, att_t, log_row, kept
):
    rows = (came.shape[1] - 16) * 2 // 3
    kept[...] = came[...]
    taps_q, taps_kv = head_taps(place, came, rows, seqs)
    b = place[0] % seqs
    first = 0
    results = []
    for lengths, (q_mixed, kv_mixed) in zip(
        (long_lengths, short_lengths), own_pair(came, long_rows, rows)
    ):
        count = q_mixed.shape[0]
        block = min(256, count)
        length = lengths[b]
        q = (convolve(q_mixed, taps_q).astype(BF16).astype(F32) * HEAD_DIM ** (-0.5)).astype(BF16)
        kv = convolve(kv_mixed, taps_kv).astype(BF16)
        kv_t = kv.astype(F32).T.astype(BF16)
        q_all[first : first + count, :] = q
        kv_all[first : first + count, :] = kv
        k = kv[:, :HEAD_DIM]
        v_t = kv_t[HEAD_DIM:, :]
        pieces = []
        for start in range(0, count, block):
            stop = start + block
            scores = dot(k[:stop], q[start:stop], NT)
            key_pos = lax.broadcasted_iota(jnp.int32, scores.shape, 0)
            query_pos = lax.broadcasted_iota(jnp.int32, scores.shape, 1) + start
            allowed = jnp.logical_and(key_pos <= query_pos, key_pos < length)
            scores = jnp.where(allowed, scores, mask_fill)
            top = jnp.max(scores, axis=0, keepdims=True)
            terms = jnp.exp(scores - top)
            total = jnp.sum(terms, axis=0, keepdims=True)
            out_t = dot(v_t[:, :stop], terms.astype(BF16)) / total
            att_t[:, first + start : first + stop] = out_t
            log_row[:, first + start : first + stop] = top + jnp.log(total)
            pieces.append(out_t.T.astype(BF16))
        results.append(jnp.concatenate(pieces, axis=0))
        first += count
    short_rows = rows - long_rows
    for j in range(8):
        mine = jnp.concatenate(
            [
                results[0][j * long_rows : (j + 1) * long_rows],
                results[1][j * short_rows : (j + 1) * short_rows],
            ],
            axis=0,
        )
        send[j, :, :] = fold(mine)


def pair_rows(came, seqs):
    columns = []
    for e in range(3):
        columns.append(
            jnp.concatenate([unfold(came[seqs * e + b]) for b in range(seqs)], axis=0)
        )
    return jnp.concatenate(columns, axis=1)


def out_proj_body(place, came, out, att, keep, send, scratch):
    att[...] = pair_rows(came, 2)
    scratch[...] = dot(att[...], out[...], NT).astype(BF16)
    split_halves(place, scratch, keep, send)


def feed_body(
    long_rows,
    place,
    long_lengths,
    short_lengths,
    own,
    other,
    long_in,
    short_in,
    long_cot,
    short_cot,
    gathered,
    mid_ref,
    normed_ref,
    squared_ref,
    grad_up_ref,
    grad_out_ref,
    keep,
    send,
    scratch,
    attended,
    up,
    down,
):
    seqs = long_in.shape[0]
    shard = gathered.shape[1] // 2
    for s in range(8):
        up[s * shard : (s + 1) * shard, :] = gathered[s, :shard, :]
        down[s * shard : (s + 1) * shard, :] = gathered[s, shard:, :]
    rows = long_rows + short_in.shape[1]
    join_halves(place, attended, own, other)
    for b in range(seqs):
        at = slice(b * rows, (b + 1) * rows)
        residual = jnp.concatenate([long_in[b], short_in[b]], axis=0).astype(F32)
        mid = residual + attended[at, :]
        mid_ref[at, :] = mid
        root = lax.rsqrt(jnp.mean(mid * mid, axis=-1, keepdims=True) + norm_eps)
        normed_ref[at, :] = (mid * root).astype(BF16)
        for cot, lengths, first, count in (
            (long_cot, long_lengths, b * rows, long_rows),
            (short_cot, short_lengths, b * rows + long_rows, rows - long_rows),
        ):
            value = cot[b]
            position = lax.broadcasted_iota(jnp.int32, value.shape, 0) + place[0] * count
            grad_out_ref[first : first + count, :] = jnp.where(
                position < lengths[b], value.astype(F32), 0.0
            ).astype(BF16)
    relu = jnp.maximum(dot(normed_ref[...], up[...]), 0.0)
    squared_ref[...] = (relu * relu).astype(BF16)
    grad_squared = dot(grad_out_ref[...], down[...])
    grad_up_ref[...] = (grad_squared * 2.0 * relu).astype(BF16)
    scratch[...] = dot(grad_up_ref[...], up[...], NT).astype(BF16)
    split_halves(place, scratch, keep, send)


def split_halves(place, whole, keep, send):
    half = whole.shape[0] // 2
    core = place[1] % 2
    keep[...] = whole[pl.ds(pl.multiple_of(core * half, half), half), :]
    send[...] = whole[pl.ds(pl.multiple_of((1 - core) * half, half), half), :]


def join_halves(place, whole, own, other):
    half = own.shape[0]
    core = place[1] % 2
    whole[pl.ds(pl.multiple_of(core * half, half), half), :] = own[...].astype(whole.dtype)
    whole[pl.ds(pl.multiple_of((1 - core) * half, half), half), :] = other[...].astype(whole.dtype)


def split_y(place, blocks, keep, send):
    y = place[0] % 2
    for z in range(4):
        keep[z] = blocks[2 * z + y]
        send[z] = blocks[2 * z + 1 - y]


def up_term_body(place, normed, grad_up, keep, send, blocks):
    rows = blocks.shape[1]
    term = dot(normed[...], grad_up[...], TN).astype(BF16)
    for s in range(8):
        blocks[s] = term[s * rows : (s + 1) * rows]
    split_y(place, blocks, keep, send)


def down_term_body(
    place, squared, grad_out, gathered, keep, send, f_keep, f_send, scratch, down, blocks
):
    rows = gathered.shape[1] // 2
    for s in range(8):
        down[s * rows : (s + 1) * rows, :] = gathered[s, rows:, :]
    term = dot(grad_out[...], squared[...], TN).astype(BF16)
    for s in range(8):
        blocks[s] = term[s * rows : (s + 1) * rows]
    split_y(place, blocks, keep, send)
    scratch[...] = dot(squared[...], down[...], NT).astype(BF16)
    split_halves(place, scratch, f_keep, f_send)


def middle_body(
    place, own, other, mid_ref, grad_out, out, att, grad_mid_ref, send, keep_out, send_out, scratch, low_ref, blocks
):
    join_halves(place, scratch, own, other)
    seqs = 2
    rows = mid_ref.shape[0] // seqs
    for b in range(seqs):
        at = slice(b * rows, (b + 1) * rows)
        mid = mid_ref[at, :]
        weighted = scratch[at, :]
        root = lax.rsqrt(jnp.mean(mid * mid, axis=-1, keepdims=True) + norm_eps)
        inner = jnp.mean(weighted * mid, axis=-1, keepdims=True)
        grad_mid = grad_out[at, :].astype(F32) + (
            root * weighted - mid * (root * root * root * inner)
        )
        grad_mid_ref[at, :] = grad_mid
        low_ref[at, :] = grad_mid.astype(BF16)
    grad_att = dot(low_ref[...], out[...]).astype(BF16)
    for dest in range(8):
        if dest < 3 * seqs:
            e, b = dest // seqs, dest % seqs
            send[dest] = fold(
                grad_att[b * rows : (b + 1) * rows, e * HEAD_DIM : (e + 1) * HEAD_DIM]
            )
        else:
            send[dest] = jnp.zeros_like(send[dest])
    term = dot(low_ref[...], att[...], TN).astype(BF16)
    shard = term.shape[0] // 8
    for s in range(8):

        def store(row, lane, value):
            blocks[s, row : row + 16, lane : lane + LANES] = value

        narrow_pack(term[s * shard : (s + 1) * shard], store)
    split_y(place, blocks, keep_out, send_out)


def attend_back_body(
    long_rows,
    seqs,
    place,
    long_lengths,
    short_lengths,
    came,
    q_all,
    kv_all,
    att_t,
    log_row,
    grad_came,
    send,
):
    rows = (came.shape[1] - 16) * 2 // 3
    short_rows = rows - long_rows
    taps_q, taps_kv = head_taps(place, came, rows, seqs)
    b = place[0] % seqs
    e = place[0] // seqs
    grads = [unfold(grad_came[j]) for j in range(8)]
    first = 0
    terms_q = [0.0, 0.0, 0.0]
    terms_kv = [0.0, 0.0, 0.0]
    results = []
    for lengths, part, (q_mixed, kv_mixed) in zip(
        (long_lengths, short_lengths),
        (slice(0, long_rows), slice(long_rows, rows)),
        own_pair(came, long_rows, rows),
    ):
        count = q_mixed.shape[0]
        block = min(256, count)
        length = lengths[b]
        at = slice(first, first + count)
        grad = jnp.concatenate([g[part] for g in grads], axis=0)
        q = q_all[at, :]
        kv = kv_all[at, :]
        kv_t = kv.astype(F32).T.astype(BF16)
        delta = jnp.sum(grad.astype(F32).T * att_t[:, at], axis=0, keepdims=True)
        log_total = log_row[:, at]
        k, v = kv[:, :HEAD_DIM], kv[:, HEAD_DIM:]
        k_t = kv_t[:HEAD_DIM, :]
        grad_q = None
        grad_kv = []
        for start in range(0, count, block):
            stop = start + block
            scores = dot(k[start:stop], q[start:], NT)
            key_pos = lax.broadcasted_iota(jnp.int32, scores.shape, 0)
            query_pos = lax.broadcasted_iota(jnp.int32, scores.shape, 1)
            allowed = jnp.logical_and(key_pos <= query_pos, key_pos + start < length)
            prob = jnp.where(allowed, jnp.exp(scores - log_total[:, start:]), 0.0)
            grad_prob = dot(v[start:stop], grad[start:], NT)
            grad_scores = (prob * (grad_prob - delta[:, start:])).astype(BF16)
            grad_k = dot(grad_scores, q[start:])
            grad_v = dot(prob.astype(BF16), grad[start:])
            grad_kv.append(jnp.concatenate([grad_k, grad_v], axis=1))
            part_q = dot(k_t[:, start:stop], grad_scores)
            if start == 0:
                grad_q = part_q
            else:
                grad_q = jnp.concatenate(
                    [grad_q[:, :start], grad_q[:, start:] + part_q], axis=1
                )
        grad_q = grad_q.T * HEAD_DIM ** (-0.5)
        grad_kv = jnp.concatenate(grad_kv, axis=0)
        pair = []
        for grad_conv, mixed, taps, terms in (
            (grad_q, q_mixed, taps_q, terms_q),
            (grad_kv, kv_mixed, taps_kv, terms_kv),
        ):
            for m in range(3):
                back = mixed if m == 0 else shift_back(mixed, m)
                terms[m] = terms[m] + jnp.sum(grad_conv * back, axis=0, keepdims=True)
            pair.append(
                (
                    taps[0] * grad_conv
                    + taps[1] * shift_ahead(grad_conv, 1)
                    + taps[2] * shift_ahead(grad_conv, 2)
                ).astype(BF16)
            )
        results.append(pair)
        first += count
    table = jnp.concatenate(
        terms_q
        + [t[:, :HEAD_DIM] for t in terms_kv]
        + [t[:, HEAD_DIM:] for t in terms_kv]
        + [jnp.zeros((7, HEAD_DIM), F32)],
        axis=0,
    )
    table = jnp.concatenate([jnp.where(e == i, table, 0.0) for i in range(3)], axis=1)
    width = 3 * HEAD_DIM // 8
    for j in range(8):
        mine = [
            jnp.concatenate(
                [
                    results[0][i][j * long_rows : (j + 1) * long_rows],
                    results[1][i][j * short_rows : (j + 1) * short_rows],
                ],
                axis=0,
            )
            for i in range(2)
        ]
        send[j, :rows, :] = mine[1]
        send[j, rows : rows + rows // 2, :] = fold(mine[0])
        send[j, rows + rows // 2 :, :] = jnp.concatenate(
            [table[:, j * width : (j + 1) * width], jnp.zeros((16, LANES - width), F32)], axis=1
        ).astype(BF16)


def place_grad_mixed(came, grad_mixed):
    seqs = 2
    rows = (came.shape[1] - 16) * 2 // 3
    for e in range(3):
        for b in range(seqs):
            j = seqs * e + b
            at = slice(b * rows, (b + 1) * rows)
            lanes = slice(e * HEAD_DIM, (e + 1) * HEAD_DIM)
            grad_mixed[0, at, lanes] = unfold(came[j, rows : rows + rows // 2, :])
            grad_mixed[1, at, lanes] = came[j, :rows, :HEAD_DIM]
            grad_mixed[2, at, lanes] = came[j, :rows, HEAD_DIM:]


def proj_term_body(place, came, normed, keep, send, grad_mixed, blocks):
    place_grad_mixed(came, grad_mixed)
    shard = normed.shape[1] // 8
    terms = [dot(normed[...], grad_mixed[c], TN).astype(BF16) for c in range(3)]
    for s in range(8):
        at = slice(s * shard, (s + 1) * shard)
        for c in range(3):
            blocks[s, c * shard : (c + 1) * shard, :] = terms[c][at, :LANES]
        blocks[s, 3 * shard :, :] = fold(
            jnp.concatenate([terms[c][at, LANES:] for c in range(3)], axis=0)
        )
    split_y(place, blocks, keep, send)


def project_back_body(place, came, weight, keep, send, taps, scratch, grad_mixed):
    place_grad_mixed(came, grad_mixed)
    rows = (came.shape[1] - 16) * 2 // 3
    total = came[0, rows + rows // 2 :, :].astype(F32)
    for j in range(1, 6):
        total = total + came[j, rows + rows // 2 :, :].astype(F32)
    taps[...] = total[: taps.shape[0], : taps.shape[1]]
    total = dot(grad_mixed[0], weight[0], NT)
    for c in (1, 2):
        total = total + dot(grad_mixed[c], weight[c], NT)
    scratch[...] = total.astype(BF16)
    split_halves(place, scratch, keep, send)


def input_grad_body(
    place, own, other, grad_mid, gain, long_in, short_in, long_out, short_out, scratch
):
    join_halves(place, scratch, own, other)
    seqs, long_rows, _ = long_in.shape
    rows = long_rows + short_in.shape[1]
    for b in range(seqs):
        at = slice(b * rows, (b + 1) * rows)
        values = jnp.concatenate([long_in[b], short_in[b]], axis=0).astype(F32)
        weighted = scratch[at, :] * gain[...]
        root = lax.rsqrt(jnp.mean(values * values, axis=-1, keepdims=True) + norm_eps)
        inner = jnp.mean(weighted * values, axis=-1, keepdims=True)
        grad = grad_mid[at, :] + (root * weighted - values * (root * root * root * inner))
        long_out[b] = grad[:long_rows]
        short_out[b] = grad[long_rows:]


def output_body(place, own, other, mid, long_out, short_out, scratch):
    join_halves(place, scratch, own, other)
    seqs, long_rows, _ = long_out.shape
    rows = long_rows + short_out.shape[1]
    for b in range(seqs):
        at = slice(b * rows, (b + 1) * rows)
        value = (mid[at, :] + scratch[at, :]).astype(BF16)
        long_out[b] = value[:long_rows]
        short_out[b] = value[long_rows:]


def scatter_z_body(place, *refs):
    count = (len(refs) - 4) // 2
    outs = refs[2 * count :]
    z = place[0] // 2
    for i in range(4):
        block = jnp.bitwise_xor(z, i)
        first = 0
        for a in range(count):
            keep, came = refs[2 * a], refs[2 * a + 1]
            rows = keep.shape[1]
            outs[i][first : first + rows, :] = (
                keep[block].astype(F32) + came[block].astype(F32)
            ).astype(BF16)
            first += rows


def near_body(place, *refs):
    pairs = len(refs[:-3]) // 2
    near, own, across = refs[-3:]
    z = place[0] // 2
    for i, target in ((0, own), (1, near.at[0]), (2, across), (3, near.at[1])):
        block = jnp.bitwise_xor(z, i)
        first = 0
        for p in range(pairs):
            keep, came = refs[2 * p], refs[2 * p + 1]
            rows = keep.shape[1]
            target[first : first + rows, :] = (
                keep[block].astype(F32) + came[block].astype(F32)
            ).astype(BF16)
            first += rows


def across_body(across, near, out):
    out[...] = (across[...].astype(F32) + near[1].astype(F32)).astype(BF16)


def sum_blocks(blocks):
    return (blocks[0][...].astype(F32) + blocks[1][...].astype(F32)) + (
        blocks[2][...].astype(F32) + blocks[3][...].astype(F32)
    )


def proj_grad_body(b0, b1, b2, b3, proj, gain, grad, gain_grad):
    total = sum_blocks((b0, b1, b2, b3))
    rows = proj.shape[1]
    column = 0.0
    for c, (wide, narrow) in enumerate(unpack_blocks(total, rows, 3)):
        term = jnp.concatenate([wide, narrow], axis=1)
        column = column + jnp.sum(term * proj[c].astype(F32), axis=1, keepdims=True)
        grad[c] = term
    gain_grad[...] = column.T / gain[...].astype(F32).reshape(1, rows)


def ffn_grad_body(
    up_own, up_near, up_across, own, near, across, up, gain, up_grad, down_grad, out_grad, gain_grad
):
    rows = up.shape[0]
    raw = up_own[...].astype(F32) + up_near[0].astype(F32) + up_across[...].astype(F32)
    total = own[...].astype(F32) + near[0].astype(F32) + across[...].astype(F32)
    gain_grad[...] = jnp.sum(raw * up[...].astype(F32), axis=1, keepdims=True).T
    up_grad[...] = raw * gain[...].astype(F32).reshape(1, rows).T
    down_grad[...] = total[:rows]
    wide = total[rows : rows + 16]
    narrow = total[rows + 16 :]
    out = jnp.concatenate(
        [
            jnp.concatenate(
                [
                    wide[:, LANES * g : LANES * (g + 1)],
                    narrow[:, LANES * g : LANES * g + HEAD_DIM],
                ],
                axis=1,
            )
            for g in range(rows // 16)
        ],
        axis=0,
    )
    out_grad[...] = out.T


def pair_shards(
    short_input,
    long_input,
    short_cotangent,
    long_cotangent,
    short_lengths,
    long_lengths,
    proj_weight,
    out_weight,
    conv_taps,
    attention_gain,
    up_weight,
    down_weight,
    feed_gain,
):
    seqs, long_rows, width = long_input.shape
    short_rows = short_input.shape[1]
    rows = long_rows + short_rows
    tokens = seqs * rows
    shard = proj_weight.shape[1]
    local = proj_weight.shape[2]
    hidden = up_weight.shape[1]
    long_len, short_len = 8 * long_rows, 8 * short_rows
    total_len = long_len + short_len
    place = jnp.stack([lax.axis_index("seq"), lax.axis_index("head")]).astype(jnp.int32)
    packed_rows = shard * 9 // 2
    chunk = rows + rows // 2 + 16
    down_t = down_weight.T

    (proj_packed,) = in_vmem(
        pack_proj_body,
        [((packed_rows + 16, LANES), BF16)],
        (),
        far(proj_weight) + (attention_gain,),
    )
    (ffn_packed,) = in_vmem(
        pack_ffn_body,
        [((2 * shard + 32, hidden), BF16)],
        (),
        far(up_weight, down_t, out_weight) + (feed_gain,),
    )
    proj_z = [proj_packed] + [exchange(proj_packed, "seq", mask) for mask in (2, 4, 6)]
    proj_parts = [proj_packed, exchange(proj_packed, "seq", 1)]
    for piece in proj_z[1:]:
        proj_parts += [piece, exchange(piece, "seq", 1)]
    ffn_0 = after(ffn_packed, *proj_z)
    ffn_1 = exchange(ffn_0, "seq", 1)
    ffn_2 = exchange(ffn_0, "seq", 2)
    ffn_4 = exchange(ffn_0, "seq", 4)
    send, normed, proj_full, gain = in_vmem(
        project_body,
        [
            ((8, chunk, LANES), BF16),
            ((tokens, width), BF16, "far"),
            ((3, width, local), BF16, "far"),
            ((1, width), F32, "far"),
        ],
        (place,),
        (*proj_parts, *far(long_input, short_input, conv_taps)),
        scratch=[((8, LANES), F32)],
        fence=True,
    )
    came = lax.all_to_all(send, "seq", 0, 0, tiled=True)
    across_z = marker(ffn_4, ffn_1, send)
    ffn_2, ffn_4 = after(ffn_2, across_z), after(ffn_4, across_z)
    ffn_6 = exchange(ffn_4, "seq", 2)
    ffn_3 = exchange(ffn_2, "seq", 1)
    ffn_5 = exchange(ffn_4, "seq", 1)
    ffn_7 = exchange(ffn_6, "seq", 1)
    att_send, q_all, kv_all, att_t, log_row, mixed = in_vmem(
        functools.partial(attend_body, long_rows, seqs),
        [
            ((8, rows // 2, LANES), BF16),
            ((total_len, HEAD_DIM), BF16, "far"),
            ((total_len, 2 * HEAD_DIM), BF16, "far"),
            ((HEAD_DIM, total_len), F32, "far"),
            ((1, total_len), F32, "far"),
            ((8, chunk, LANES), BF16, "far"),
        ],
        (place, long_lengths, short_lengths),
        (came,),
        fence=True,
    )
    att_0 = lax.all_to_all(att_send, "seq", 0, 0, tiled=True)
    ffn_full, out_full = in_vmem(
        place_ffn_body,
        [((8, 2 * shard, hidden), BF16, "far"), ((width, local), BF16, "far")],
        (place,),
        far(after(ffn_packed, att_send), ffn_1, ffn_2, ffn_3, ffn_4, ffn_5, ffn_6, ffn_7),
    )
    att_0 = after(att_0, out_full)
    att, keep, send = in_vmem(
        out_proj_body,
        [
            ((tokens, local), BF16, "far"),
            ((tokens // 2, width), BF16),
            ((tokens // 2, width), BF16),
        ],
        (place,),
        (att_0,) + far(out_full),
        scratch=[((tokens, width), BF16)],
    )
    half = add_low(keep, exchange(send, "head", 1))
    own = add_low(half, exchange(half, "head", 2))
    other = exchange(own, "head", 1)
    mid, normed_ffn, squared, grad_up, grad_out, keep, send = in_vmem(
        functools.partial(feed_body, long_rows),
        [
            ((tokens, width), F32, "far"),
            ((tokens, width), BF16, "far"),
            ((tokens, hidden), BF16, "far"),
            ((tokens, hidden), BF16, "far"),
            ((tokens, width), BF16, "far"),
            ((tokens // 2, width), BF16),
            ((tokens // 2, width), BF16),
        ],
        (place, long_lengths, short_lengths),
        (own, other)
        + far(long_input, short_input, long_cotangent, short_cotangent, ffn_full),
        scratch=[
            ((tokens, width), BF16),
            ((tokens, width), F32),
            ((width, hidden), BF16),
            ((width, hidden), BF16),
        ],
        limit_mib=32,
    )
    half = add_low(keep, exchange(send, "head", 1))
    up_keep, up_send = in_vmem(
        up_term_body,
        [((4, shard, hidden), BF16, "far")] * 2,
        (place,),
        far(after(normed_ffn, half), grad_up),
        scratch=[((8, shard, hidden), BF16)],
    )
    up_came = exchange(up_send, "seq", 1)
    down_keep, down_send, f_keep, f_send = in_vmem(
        down_term_body,
        [((4, shard, hidden), BF16, "far")] * 2 + [((tokens // 2, width), BF16, "far")] * 2,
        (place,),
        far(after(squared, up_send), grad_out, ffn_full),
        scratch=[
            ((tokens, width), BF16),
            ((width, hidden), BF16),
            ((8, shard, hidden), BF16),
        ],
        fence=True,
    )
    own = add_low(half, after(exchange(half, "head", 2), down_send))
    other = exchange(own, "head", 1)
    grad_mid, send, out_keep, out_send = in_vmem(
        middle_body,
        [
            ((tokens, width), F32, "far"),
            ((8, rows // 2, LANES), BF16),
            ((4, 32, hidden), BF16, "far"),
            ((4, 32, hidden), BF16, "far"),
        ],
        (place,),
        (own, other) + far(mid, grad_out, out_full, att),
        scratch=[((tokens, width), F32), ((tokens, width), BF16), ((8, 32, hidden), BF16)],
        fence=True,
    )
    grad_came = lax.all_to_all(send, "seq", 0, 0, tiled=True)
    down_came = exchange(after(down_send, send), "seq", 1)
    out_came = exchange(out_send, "seq", 1)
    up_near, up_own, up_across = in_vmem(
        near_body,
        [((2, shard, hidden), BF16, "far")] + [((shard, hidden), BF16, "far")] * 2,
        (place,),
        far(up_keep, after(up_came, grad_mid)),
        fence=True,
    )
    up_near = exchange(up_near, "seq", 2)
    grad_came = after(grad_came, up_own)
    f_half = add_low(f_keep, exchange(f_send, "head", 1))
    f_own = add_low(f_half, exchange(f_half, "head", 2))
    f_other = exchange(f_own, "head", 1)
    long_output, short_output = in_vmem(
        output_body,
        [(long_input.shape, BF16), (short_input.shape, BF16)],
        (place,),
        (f_own, f_other) + far(mid),
        scratch=[((tokens, width), F32)],
    )
    (send,) = in_vmem(
        functools.partial(attend_back_body, long_rows, seqs),
        [((8, chunk, LANES), BF16)],
        (place, long_lengths, short_lengths),
        far(mixed, q_all, kv_all, att_t, log_row) + (grad_came,),
    )
    mixed_came = lax.all_to_all(after(send, up_near), "seq", 0, 0, tiled=True)
    near, ffn_own, across = in_vmem(
        near_body,
        [((2, shard + 32, hidden), BF16, "far")] + [((shard + 32, hidden), BF16, "far")] * 2,
        (place,),
        far(down_keep, after(down_came, send), out_keep, out_came),
        fence=True,
    )
    near = exchange(near, "seq", 2)
    (up_across,) = in_vmem(
        across_body, [((shard, hidden), BF16, "far")], (), far(after(up_across, across), up_near)
    )
    up_across = exchange(up_across, "seq", 4)
    mixed_came = after(mixed_came, long_output, ffn_own)
    proj_keep, proj_send = in_vmem(
        proj_term_body,
        [((4, packed_rows, LANES), BF16, "far"), ((4, packed_rows, LANES), BF16, "far")],
        (place,),
        (mixed_came,) + far(normed),
        scratch=[((3, tokens, local), BF16), ((8, packed_rows, LANES), BF16)],
    )
    proj_came = exchange(proj_send, "seq", 1)
    keep, send, taps_grad = in_vmem(
        project_back_body,
        [
            ((tokens // 2, width), BF16),
            ((tokens // 2, width), BF16),
            (conv_taps.shape, F32),
        ],
        (place,),
        (after(mixed_came, proj_send, up_across, near),) + far(proj_full),
        scratch=[((tokens, width), BF16), ((3, tokens, local), BF16)],
        fence=True,
    )
    half = add_low(keep, exchange(send, "head", 1))
    (across,) = in_vmem(
        across_body, [((shard + 32, hidden), BF16, "far")], (), far(after(across, send), near)
    )
    across = exchange(across, "seq", 4)
    own = add_low(half, exchange(half, "head", 2))
    other = exchange(own, "head", 1)
    proj_blocks = in_vmem(
        scatter_z_body,
        [((packed_rows, LANES), BF16)] * 4,
        (place,),
        far(proj_keep) + (proj_came,),
    )
    proj_blocks = [proj_blocks[0]] + [exchange(proj_blocks[i], "seq", 2 * i) for i in (1, 2, 3)]
    up_grad, down_grad, out_grad, feed_part = in_vmem(
        ffn_grad_body,
        [
            (up_weight.shape, F32),
            (down_t.shape, F32),
            (out_weight.shape, F32),
            ((1, shard), F32),
        ],
        (),
        far(after(up_own, proj_blocks[0]), up_near, up_across, ffn_own, near, across, up_weight)
        + (feed_gain,),
    )
    proj_blocks[3] = after(proj_blocks[3], up_grad)
    proj_grad, attention_part = in_vmem(
        proj_grad_body,
        [(proj_weight.shape, F32), ((1, shard), F32)],
        (),
        (*proj_blocks, *far(proj_weight), attention_gain),
    )
    long_input_grad, short_input_grad = in_vmem(
        input_grad_body,
        [(long_input.shape, F32), (short_input.shape, F32)],
        (place,),
        (own, other) + far(after(grad_mid, attention_part), gain, long_input, short_input),
        scratch=[((tokens, width), F32)],
    )
    gains = jnp.concatenate([attention_part, feed_part], axis=0)
    gains = gains + exchange(gains, "head", 1)
    gains = gains + after(exchange(gains, "head", 2), long_input_grad)

    return (
        short_output,
        long_output,
        short_input_grad,
        long_input_grad,
        proj_grad,
        out_grad,
        taps_grad,
        gains[0],
        up_grad,
        down_grad.T,
        gains[1],
    )


def fits_pairs(short_input, long_input, proj_weight):
    seqs, long_rows, _ = long_input.shape
    short_seqs, short_rows, _ = short_input.shape
    return (
        lax.axis_size("seq") == 8
        and lax.axis_size("head") == 4
        and seqs == 2
        and short_seqs == 2
        and proj_weight.shape[2] == 3 * HEAD_DIM
        and proj_weight.shape[1] % 32 == 0
        and long_rows % 32 == 0
        and short_rows % 32 == 0
        and 8 * long_rows <= 2048
    )


def shards(short_input, long_input, *rest):
    proj_weight = rest[4]
    if fits_pairs(short_input, long_input, proj_weight):
        return pair_shards(short_input, long_input, *rest)
    return ring_shards(short_input, long_input, *rest)


def solution(mesh):
    placed = (
        P(None, "seq", None),
        P(None, "seq", None),
        P(None, "seq", None),
        P(None, "seq", None),
        P(),
        P(),
        P(None, "seq", "head"),
        P("head", "seq"),
        P(None, ("head", "seq")),
        P("seq"),
        P("seq", "head"),
        P("head", "seq"),
        P("seq"),
    )
    return jax.shard_map(
        shards,
        mesh=mesh,
        in_specs=placed,
        out_specs=(
            P(None, "seq", None),
            P(None, "seq", None),
            P(None, "seq", None),
            P(None, "seq", None),
            P(None, "seq", "head"),
            P("head", "seq"),
            P(None, ("head", "seq")),
            P("seq"),
            P("seq", "head"),
            P("head", "seq"),
            P("seq"),
        ),
        check_vma=False,
    )
```

```python
import functools

import jax
import jax.numpy as jnp
import numpy as np
from jax import lax
from jax.experimental import pallas as pl
from jax.experimental.pallas import tpu as pltpu
from jax.sharding import PartitionSpec as P

HEAD_DIM = 64


norm_eps = 1e-06
mask_fill = -1e30
block_limit = 2048


def passed_along(block, axis, distance):
    devices = range(lax.axis_size(axis))
    route = [((i - distance) % len(devices), i) for i in devices]
    return lax.ppermute(block, axis, route)


def shifted(array, axis, by):
    peers = lax.axis_size(axis)
    pairs = [(i, i + by) for i in range(peers) if 0 <= i + by < peers]
    return lax.ppermute(array, axis, pairs)


def block_rows(row_count):
    size_rows = min(row_count, block_limit)
    while row_count % size_rows != 0:
        size_rows = size_rows - 1
    return size_rows


def norm_forward(values_in, gain_row):
    inv_root = lax.rsqrt(jnp.mean(values_in * values_in, axis=-1, keepdims=True) + norm_eps)
    return (values_in * inv_root * gain_row, inv_root)


def norm_backward(values_in, inv_root, gain_row, grad_in):
    weighted = grad_in * gain_row
    inner_mean = jnp.mean(weighted * values_in, axis=-1, keepdims=True)
    grad_values = inv_root * weighted - values_in * inv_root * inv_root * inv_root * inner_mean
    grad_gain = jnp.sum(grad_in * values_in * inv_root, axis=(0, 1))
    return (grad_values, grad_gain)


def allowed_mask(query_pos, key_pos, lengths):
    causal = key_pos[None, :] <= query_pos[:, None]
    inside = key_pos[None, :] < lengths[:, None]
    return jnp.logical_and(causal[None, None], inside[:, None, None, :])


def block_scores(query_rows, key_rows, query_pos, key_pos, lengths):
    allowed = allowed_mask(query_pos, key_pos, lengths)
    raw_scores = jnp.einsum(
        "bqhe,bkhe->bhqk", query_rows, key_rows, preferred_element_type=jnp.float32
    ) * HEAD_DIM ** (-0.5)
    return (jnp.where(allowed, raw_scores, mask_fill), allowed)


def block_grads(
    query_rows, grad_rows, log_rows, delta_rows, key_rows, value_rows, query_pos, key_pos, lengths
):
    scores, allowed = block_scores(query_rows, key_rows, query_pos, key_pos, lengths)
    prob_rows = jnp.where(
        allowed, jnp.exp(scores - jnp.transpose(log_rows, (0, 2, 1))[..., None]), 0.0
    )
    grad_probs = jnp.einsum(
        "bqhe,bkhe->bhqk", grad_rows, value_rows, preferred_element_type=jnp.float32
    )
    grad_scores = (
        prob_rows * (grad_probs - jnp.transpose(delta_rows, (0, 2, 1))[..., None])
    ).astype(jnp.bfloat16)
    grad_query = jnp.einsum(
        "bhqk,bkhe->bqhe", grad_scores, key_rows, preferred_element_type=jnp.float32
    ) * HEAD_DIM ** (-0.5)
    grad_key = jnp.einsum(
        "bhqk,bqhe->bkhe", grad_scores, query_rows, preferred_element_type=jnp.float32
    ) * HEAD_DIM ** (-0.5)
    grad_value = jnp.einsum(
        "bhqk,bqhe->bkhe",
        prob_rows.astype(jnp.bfloat16),
        grad_rows,
        preferred_element_type=jnp.float32,
    )
    return (grad_query, grad_key, grad_value)


def attend_forward(queries, keys_here, values_here, query_pos, lengths):
    seq_count, span_rows, head_count, head_width = queries.shape
    initial = (
        jnp.full((seq_count, head_count, span_rows), mask_fill, jnp.float32),
        jnp.zeros((seq_count, head_count, span_rows), jnp.float32),
        jnp.zeros((seq_count, span_rows, head_count, head_width), jnp.float32),
    )
    key_piece = lax.all_gather(keys_here, "seq", axis=1, tiled=True)
    value_piece = lax.all_gather(values_here, "seq", axis=1, tiled=True)
    row_count = key_piece.shape[1]
    size_rows = block_rows(row_count)

    def one_block(block_index, carried_state):
        running_top, running_sum, acc_rows = carried_state
        offset = block_index * size_rows
        key_rows = lax.dynamic_slice_in_dim(key_piece, offset, size_rows, 1)
        value_rows = lax.dynamic_slice_in_dim(value_piece, offset, size_rows, 1)
        key_pos = offset + jnp.arange(size_rows, dtype=jnp.int32)
        scores, allowed = block_scores(queries, key_rows, query_pos, key_pos, lengths)
        new_top = jnp.maximum(running_top, jnp.max(scores, axis=-1))
        exp_terms = jnp.where(allowed, jnp.exp(scores - new_top[..., None]), 0.0)
        shrink = jnp.exp(running_top - new_top)
        running_sum = running_sum * shrink + jnp.sum(exp_terms, axis=-1)
        acc_rows = acc_rows * jnp.transpose(shrink, (0, 2, 1))[..., None] + jnp.einsum(
            "bhqk,bkhe->bqhe",
            exp_terms.astype(jnp.bfloat16),
            value_rows,
            preferred_element_type=jnp.float32,
        )
        return (new_top, running_sum, acc_rows)

    running_top, running_sum, acc_rows = lax.fori_loop(
        0, row_count // size_rows, one_block, initial
    )
    attention = acc_rows / jnp.transpose(running_sum, (0, 2, 1))[..., None]
    log_totals = jnp.transpose(running_top + jnp.log(running_sum), (0, 2, 1))
    return (attention, log_totals)


def pass_sums(grad_keys, grad_values):
    return (
        passed_along(grad_keys.astype(jnp.bfloat16), "seq", 1).astype(grad_keys.dtype),
        passed_along(grad_values.astype(jnp.bfloat16), "seq", 1).astype(grad_values.dtype),
    )


def attend_backward(
    queries, keys_here, values_here, grad_attention, log_totals, delta_rows, query_pos, lengths
):
    seq_count, span_rows, head_count, head_width = queries.shape
    zeros_local = jnp.zeros(queries.shape, jnp.float32)
    seq_size = lax.axis_size("seq")
    my_index = lax.axis_index("seq")
    local_pos = jnp.arange(span_rows, dtype=jnp.int32)

    def step_grads(step, key_piece, value_piece):
        anchor = jnp.mod(my_index - step, seq_size)
        key_pos = anchor * span_rows + local_pos
        return block_grads(
            queries,
            grad_attention,
            log_totals,
            delta_rows,
            key_piece,
            value_piece,
            query_pos,
            key_pos,
            lengths,
        )

    def cycle_step(step, state):
        key_piece, value_piece, grad_keys, grad_values, grad_query = state
        query_part, key_part, value_part = step_grads(step, key_piece, value_piece)
        key_piece, value_piece = shifted((key_piece, value_piece), "seq", 1)
        grad_keys, grad_values = pass_sums(grad_keys + key_part, grad_values + value_part)
        return (key_piece, value_piece, grad_keys, grad_values, grad_query + query_part)

    final_state = lax.fori_loop(
        0, seq_size - 1, cycle_step, (keys_here, values_here, zeros_local, zeros_local, zeros_local)
    )
    key_piece, value_piece, grad_keys, grad_values, grad_query = final_state
    query_part, key_part, value_part = step_grads(seq_size - 1, key_piece, value_piece)
    grad_key, grad_value = pass_sums(grad_keys + key_part, grad_values + value_part)
    grad_query = grad_query + query_part
    return (grad_query, grad_key, grad_value)


def micro_batch(inputs, cotangent, lengths, weights):
    proj_full, out_full, taps_full, attend_gain, up_full, down_full, ffn_gain = weights
    seq_count, span_rows, model_width = inputs.shape
    local_width = proj_full.shape[2]
    heads_here = local_width // HEAD_DIM
    query_pos = lax.axis_index("seq") * span_rows + jnp.arange(span_rows, dtype=jnp.int32)
    valid_rows = (query_pos[None, :] < lengths[:, None])[..., None]
    residual_in = inputs.astype(jnp.float32)
    normed, inv_first = norm_forward(residual_in, attend_gain)
    normed_low = normed.astype(jnp.bfloat16)
    mixed_qkv = jnp.einsum(
        "btd,cde->cbte", normed_low, proj_full, preferred_element_type=jnp.float32
    ).astype(jnp.bfloat16)
    borrowed = shifted(mixed_qkv[:, :, span_rows - 2 :, :], "seq", 1)
    extended = jnp.concatenate([borrowed, mixed_qkv], axis=2).astype(jnp.float32)
    tap_table = taps_full.astype(jnp.float32).reshape(3, 3, local_width)
    tap_now = tap_table[:, 0][:, None, None, :]
    tap_one = tap_table[:, 1][:, None, None, :]
    tap_two = tap_table[:, 2][:, None, None, :]
    conved = (
        tap_now * extended[:, :, 2:]
        + tap_one * extended[:, :, 1:-1]
        + tap_two * extended[:, :, :-2]
    )
    conv_out = conved.astype(jnp.bfloat16).reshape(3, seq_count, span_rows, heads_here, HEAD_DIM)
    queries, keys_here, values_here = (conv_out[0], conv_out[1], conv_out[2])
    attention, log_totals = attend_forward(queries, keys_here, values_here, query_pos, lengths)
    attention_low = attention.astype(jnp.bfloat16).reshape(seq_count, span_rows, local_width)
    attend_part = jnp.einsum(
        "bte,ed->btd", attention_low, out_full, preferred_element_type=jnp.float32
    )
    mid_residual = residual_in + lax.psum(attend_part.astype(jnp.bfloat16), "head").astype(
        jnp.float32
    )
    normed_ffn, inv_second = norm_forward(mid_residual, ffn_gain)
    normed_ffn_low = normed_ffn.astype(jnp.bfloat16)
    up_proj = jnp.einsum("btd,df->btf", normed_ffn_low, up_full, preferred_element_type=jnp.float32)
    relu_up = jnp.maximum(up_proj, 0.0)
    squared = (relu_up * relu_up).astype(jnp.bfloat16)
    ffn_part = jnp.einsum("btf,fd->btd", squared, down_full, preferred_element_type=jnp.float32)
    output = (
        mid_residual + lax.psum(ffn_part.astype(jnp.bfloat16), "head").astype(jnp.float32)
    ).astype(jnp.bfloat16)
    grad_out = jnp.where(valid_rows, cotangent.astype(jnp.float32), 0.0)
    grad_out_low = grad_out.astype(jnp.bfloat16)
    down_term = jnp.einsum("btf,btd->fd", squared, grad_out_low, preferred_element_type=jnp.float32)
    grad_squared = jnp.einsum(
        "btd,fd->btf", grad_out_low, down_full, preferred_element_type=jnp.float32
    )
    grad_up = (grad_squared * 2.0 * relu_up).astype(jnp.bfloat16)
    up_term = jnp.einsum("btd,btf->df", normed_ffn_low, grad_up, preferred_element_type=jnp.float32)
    grad_normed_ffn = lax.psum(
        jnp.einsum("btf,df->btd", grad_up, up_full, preferred_element_type=jnp.float32).astype(
            jnp.bfloat16
        ),
        "head",
    ).astype(jnp.float32)
    grad_through, feed_term = norm_backward(mid_residual, inv_second, ffn_gain, grad_normed_ffn)
    grad_mid = grad_out + grad_through
    grad_mid_low = grad_mid.astype(jnp.bfloat16)
    out_term = jnp.einsum(
        "bte,btd->ed", attention_low, grad_mid_low, preferred_element_type=jnp.float32
    )
    grad_attention = jnp.einsum(
        "btd,ed->bte", grad_mid_low, out_full, preferred_element_type=jnp.float32
    )
    grad_attention = grad_attention.astype(jnp.bfloat16).reshape(
        seq_count, span_rows, heads_here, HEAD_DIM
    )
    delta_rows = jnp.einsum("bqhe,bqhe->bqh", grad_attention.astype(jnp.float32), attention)
    grad_query, grad_key, grad_value = attend_backward(
        queries, keys_here, values_here, grad_attention, log_totals, delta_rows, query_pos, lengths
    )
    grad_conv = jnp.stack([grad_query, grad_key, grad_value]).reshape(
        3, seq_count, span_rows, local_width
    )
    taps_term = jnp.stack(
        [
            jnp.sum(grad_conv * extended[:, :, 2:], axis=(1, 2)),
            jnp.sum(grad_conv * extended[:, :, 1:-1], axis=(1, 2)),
            jnp.sum(grad_conv * extended[:, :, :-2], axis=(1, 2)),
        ],
        axis=1,
    ).reshape(9, local_width)
    full_grad = jnp.pad(grad_conv, ((0, 0), (0, 0), (2, 2), (0, 0)))
    grad_extended = (
        tap_now * full_grad[:, :, 0 : span_rows + 2]
        + tap_one * full_grad[:, :, 1 : span_rows + 3]
        + tap_two * full_grad[:, :, 2 : span_rows + 4]
    )
    returned = shifted(grad_extended[:, :, :2], "seq", -1)
    grad_mixed = jnp.concatenate(
        [grad_extended[:, :, 2:span_rows], grad_extended[:, :, span_rows:] + returned], axis=2
    ).astype(jnp.bfloat16)
    proj_term = jnp.einsum(
        "btd,cbte->cde", normed_low, grad_mixed, preferred_element_type=jnp.float32
    )
    grad_normed = lax.psum(
        jnp.einsum(
            "cbte,cde->btd", grad_mixed, proj_full, preferred_element_type=jnp.float32
        ).astype(jnp.bfloat16),
        "head",
    ).astype(jnp.float32)
    grad_first, attention_term = norm_backward(residual_in, inv_first, attend_gain, grad_normed)
    grad_input = grad_mid + grad_first
    return (
        output,
        grad_input,
        (proj_term, out_term, taps_term, attention_term, up_term, down_term, feed_term),
    )


def ring_shards(
    short_input,
    long_input,
    short_cotangent,
    long_cotangent,
    short_lengths,
    long_lengths,
    proj_weight,
    out_weight,
    conv_taps,
    attention_gain,
    up_weight,
    down_weight,
    feed_gain,
):
    proj_full, out_full, taps_full, attend_gain = (
        lax.all_gather(proj_weight, "seq", axis=1, tiled=True),
        lax.all_gather(out_weight, "seq", axis=1, tiled=True),
        lax.all_gather(conv_taps, "seq", axis=1, tiled=True),
        lax.all_gather(attention_gain, "seq", axis=0, tiled=True),
    )
    up_full, down_full, ffn_gain = (
        lax.all_gather(up_weight, "seq", axis=0, tiled=True),
        lax.all_gather(down_weight, "seq", axis=1, tiled=True),
        lax.all_gather(feed_gain, "seq", axis=0, tiled=True),
    )
    weights = (
        proj_full,
        out_full,
        taps_full,
        attend_gain.astype(jnp.float32),
        up_full,
        down_full,
        ffn_gain.astype(jnp.float32),
    )
    short_output, short_input_grad, short_terms = micro_batch(
        short_input, short_cotangent, short_lengths, weights
    )
    long_output, long_input_grad, long_terms = micro_batch(
        long_input, long_cotangent, long_lengths, weights
    )
    summed = tuple(
        (first_term + second_term for first_term, second_term in zip(short_terms, long_terms))
    )
    reduced = (
        lax.psum_scatter(summed[0], "seq", scatter_dimension=1, tiled=True),
        lax.psum_scatter(summed[1], "seq", scatter_dimension=1, tiled=True),
        lax.psum_scatter(summed[2], "seq", scatter_dimension=1, tiled=True),
        lax.psum_scatter(summed[3], "seq", scatter_dimension=0, tiled=True),
        lax.psum_scatter(summed[4], "seq", scatter_dimension=0, tiled=True),
        lax.psum_scatter(summed[5], "seq", scatter_dimension=1, tiled=True),
        lax.psum_scatter(summed[6], "seq", scatter_dimension=0, tiled=True),
    )
    return (
        short_output,
        long_output,
        short_input_grad,
        long_input_grad,
        reduced[0],
        reduced[1],
        reduced[2],
        reduced[3],
        reduced[4],
        reduced[5],
        reduced[6],
    )


LANES = 128
FENCE = 10**11
NT = (((1,), (1,)), ((), ()))
TN = (((0,), (0,)), ((), ()))
F32 = jnp.float32
BF16 = jnp.bfloat16


def dot(a, b, dims=(((1,), (0,)), ((), ()))):
    return lax.dot_general(a, b, dims, preferred_element_type=F32)


def in_vmem(body, outs, scalars, arrays, scratch=(), limit_mib=16, fence=False):
    return pl.pallas_call(
        body,
        out_shape=[
            pltpu.HBM(*out[:2]) if len(out) == 3 else jax.ShapeDtypeStruct(*out) for out in outs
        ],
        in_specs=[pl.BlockSpec(memory_space=pltpu.SMEM)] * len(scalars)
        + [pl.BlockSpec(memory_space=pltpu.VMEM)] * len(arrays),
        out_specs=[pl.BlockSpec(memory_space=pltpu.VMEM)] * len(outs),
        scratch_shapes=[pltpu.VMEM(shape, kind) for shape, kind in scratch],
        compiler_params=pltpu.CompilerParams(vmem_limit_bytes=limit_mib * 1024 * 1024),
        cost_estimate=pl.CostEstimate(
            flops=FENCE if fence else 0, bytes_accessed=0, transcendentals=0
        ),
    )(*scalars, *arrays)


def far(*arrays):
    return tuple(pltpu.with_memory_space_constraint(array, pltpu.HBM) for array in arrays)


def after(array, *others):
    return lax.optimization_barrier((array, *others))[0]


def marker(*arrays):
    def body(*refs):
        refs[-1][...] = jnp.zeros_like(refs[-1])

    return pl.pallas_call(
        body,
        out_shape=jax.ShapeDtypeStruct((8, LANES), F32),
        in_specs=[pl.BlockSpec(memory_space=pl.ANY)] * len(arrays),
        out_specs=pl.BlockSpec(memory_space=pltpu.VMEM),
        cost_estimate=pl.CostEstimate(flops=FENCE, bytes_accessed=0, transcendentals=0),
    )(*arrays)


def exchange(array, axis, mask):
    size = lax.axis_size(axis)
    return lax.ppermute(array, axis, [(i, i ^ mask) for i in range(size)])


def add_low(a, b):
    return (a.astype(F32) + b.astype(F32)).astype(BF16)


def shift_back(rows, by):
    index = lax.broadcasted_iota(jnp.int32, rows.shape, 0)
    return jnp.where(index >= by, pltpu.roll(rows, by, axis=0), 0.0)


def shift_ahead(rows, by):
    count = rows.shape[0]
    index = lax.broadcasted_iota(jnp.int32, rows.shape, 0)
    return jnp.where(index < count - by, pltpu.roll(rows, count - by, axis=0), 0.0)


def fold(rows):
    half = rows.shape[0] // 2
    return jnp.concatenate([rows[:half], rows[half:]], axis=1)


def unfold(rows):
    return jnp.concatenate([rows[:, :HEAD_DIM], rows[:, HEAD_DIM:]], axis=0)


def pack_proj_body(proj, gain, packed):
    rows = proj.shape[1]
    for c in range(3):
        packed[c * rows : (c + 1) * rows, :] = proj[c, :, :LANES]
    narrow = jnp.concatenate([proj[c, :, LANES:] for c in range(3)], axis=0)
    packed[3 * rows : 9 * rows // 2, :] = fold(narrow)
    gain_row = gain[...].astype(F32).reshape(1, rows)
    gain_row = jnp.concatenate([gain_row, jnp.zeros((1, LANES - rows), F32)], axis=1)
    packed[9 * rows // 2 :, :] = jnp.broadcast_to(gain_row, (16, LANES)).astype(BF16)


def unpack_blocks(packed, rows, count):
    narrow = unfold(packed[count * rows : 3 * count * rows // 2, :])
    return [
        (packed[i * rows : (i + 1) * rows, :], narrow[i * rows : (i + 1) * rows, :])
        for i in range(count)
    ]


def narrow_pack(block, store):
    groups = block.shape[0] // 16
    for g in range(groups):
        rows = block[16 * g : 16 * g + 16, :]
        store(0, LANES * g, rows[:, :LANES])
        tail = rows[:, LANES:]
        store(16, LANES * g, jnp.concatenate([tail, jnp.zeros_like(tail)], axis=1))


def pack_ffn_body(up, down, out, gain, packed):
    rows = up.shape[0]
    gain_column = gain[...].astype(F32).reshape(1, rows).T
    packed[:rows, :] = (up[...].astype(F32) * gain_column).astype(BF16)
    packed[rows : 2 * rows, :] = down[...]

    def store(row, lane, value):
        packed[2 * rows + row : 2 * rows + row + 16, lane : lane + LANES] = value

    narrow_pack(out[...].astype(F32).T.astype(BF16), store)


def place_ffn_body(place, *refs):
    whole, out = refs[8:]
    rows = out.shape[0] // 8
    for i in range(8):
        owner = jnp.bitwise_xor(place[0], i)
        part = refs[i]
        whole[owner] = part[: 2 * rows, :]
        for g in range(rows // 16):
            at = pl.ds(pl.multiple_of(owner * rows + 16 * g, 16), 16)
            out[at, :LANES] = part[2 * rows : 2 * rows + 16, LANES * g : LANES * g + LANES]
            out[at, LANES:] = part[2 * rows + 16 :, LANES * g : LANES * g + HEAD_DIM]


def project_body(place, *refs):
    parts = refs[:8]
    long_in, short_in, taps, send, normed, weight, gain, gain_rows = refs[8:]
    seqs, long_rows, _ = long_in.shape
    rows = long_rows + short_in.shape[1]
    for i in range(8):
        packed = parts[i][...]
        shard = weight.shape[1] // 8
        owner = jnp.bitwise_xor(place[0], i)
        gain_rows[pl.ds(owner, 1), :] = packed[9 * shard // 2 :, :].astype(F32)[:1]
        at = pl.ds(pl.multiple_of(owner * shard, shard), shard)
        for c, (wide, narrow) in enumerate(unpack_blocks(packed, shard, 3)):
            weight[c, at, :LANES] = wide
            weight[c, at, LANES:] = narrow
    gain[...] = jnp.concatenate([gain_rows[j : j + 1, :shard] for j in range(8)], axis=1)
    for b in range(seqs):
        values = jnp.concatenate([long_in[b], short_in[b]], axis=0).astype(F32)
        root = lax.rsqrt(jnp.mean(values * values, axis=-1, keepdims=True) + norm_eps)
        normed[b * rows : (b + 1) * rows, :] = (values * root * gain[...]).astype(BF16)
    mixed = [dot(normed[...], weight[c]).astype(BF16) for c in range(3)]
    tap_rows = jnp.concatenate(
        [taps[...], jnp.zeros((16 - taps.shape[0], taps.shape[1]), BF16)], axis=0
    )
    tap_rows = jnp.concatenate(
        [tap_rows, jnp.zeros((16, LANES - taps.shape[1]), BF16)], axis=1
    )
    half = rows // 2
    for dest in range(8):
        if dest < 3 * seqs:
            e, b = dest // seqs, dest % seqs
            lanes = slice(e * HEAD_DIM, (e + 1) * HEAD_DIM)
            q, k, v = [m[b * rows : (b + 1) * rows, lanes] for m in mixed]
            send[dest, :rows, :] = jnp.concatenate([k, v], axis=1)
            send[dest, rows : rows + half, :] = fold(q)
        else:
            send[dest, : rows + half, :] = jnp.zeros((rows + half, LANES), BF16)
        send[dest, rows + half :, :] = tap_rows


def head_taps(place, came, rows, seqs):
    first = rows + rows // 2
    width = 3 * HEAD_DIM // 8
    whole = jnp.concatenate(
        [came[j, first:, :].astype(F32)[:, :width] for j in range(8)], axis=1
    )
    e = place[0] // seqs
    mine = whole[:, :HEAD_DIM]
    for other in (1, 2):
        mine = jnp.where(
            e == other, whole[:, other * HEAD_DIM : (other + 1) * HEAD_DIM], mine
        )
    taps_q = [mine[m : m + 1, :] for m in range(3)]
    taps_kv = [
        jnp.concatenate([mine[3 + m : 4 + m, :], mine[6 + m : 7 + m, :]], axis=1) for m in range(3)
    ]
    return taps_q, taps_kv


def own_pair(came, long_rows, rows):
    q_rows = [unfold(came[j, rows : rows + rows // 2, :]) for j in range(8)]
    result = []
    for part in (slice(0, long_rows), slice(long_rows, rows)):
        q = jnp.concatenate([piece[part] for piece in q_rows], axis=0).astype(F32)
        kv = jnp.concatenate([came[j, part, :] for j in range(8)], axis=0).astype(F32)
        result.append((q, kv))
    return result


def convolve(rows, taps):
    return taps[0] * rows + taps[1] * shift_back(rows, 1) + taps[2] * shift_back(rows, 2)


def attend_body(
    long_rows, seqs, place, long_lengths, short_lengths, came, send, q_all, kv_all, att_t, log_row, kept
):
    rows = (came.shape[1] - 16) * 2 // 3
    kept[...] = came[...]
    taps_q, taps_kv = head_taps(place, came, rows, seqs)
    b = place[0] % seqs
    first = 0
    results = []
    for lengths, (q_mixed, kv_mixed) in zip(
        (long_lengths, short_lengths), own_pair(came, long_rows, rows)
    ):
        count = q_mixed.shape[0]
        block = min(256, count)
        length = lengths[b]
        q = (convolve(q_mixed, taps_q).astype(BF16).astype(F32) * HEAD_DIM ** (-0.5)).astype(BF16)
        kv = convolve(kv_mixed, taps_kv).astype(BF16)
        kv_t = kv.astype(F32).T.astype(BF16)
        q_all[first : first + count, :] = q
        kv_all[first : first + count, :] = kv
        k = kv[:, :HEAD_DIM]
        v_t = kv_t[HEAD_DIM:, :]
        pieces = []
        for start in range(0, count, block):
            stop = start + block
            scores = dot(k[:stop], q[start:stop], NT)
            key_pos = lax.broadcasted_iota(jnp.int32, scores.shape, 0)
            query_pos = lax.broadcasted_iota(jnp.int32, scores.shape, 1) + start
            allowed = jnp.logical_and(key_pos <= query_pos, key_pos < length)
            scores = jnp.where(allowed, scores, mask_fill)
            top = jnp.max(scores, axis=0, keepdims=True)
            terms = jnp.exp(scores - top)
            total = jnp.sum(terms, axis=0, keepdims=True)
            out_t = dot(v_t[:, :stop], terms.astype(BF16)) / total
            att_t[:, first + start : first + stop] = out_t
            log_row[:, first + start : first + stop] = top + jnp.log(total)
            pieces.append(out_t.T.astype(BF16))
        results.append(jnp.concatenate(pieces, axis=0))
        first += count
    short_rows = rows - long_rows
    for j in range(8):
        mine = jnp.concatenate(
            [
                results[0][j * long_rows : (j + 1) * long_rows],
                results[1][j * short_rows : (j + 1) * short_rows],
            ],
            axis=0,
        )
        send[j, :, :] = fold(mine)


def pair_rows(came, seqs):
    columns = []
    for e in range(3):
        columns.append(
            jnp.concatenate([unfold(came[seqs * e + b]) for b in range(seqs)], axis=0)
        )
    return jnp.concatenate(columns, axis=1)


def out_proj_body(place, came, out, att, keep, send, scratch):
    att[...] = pair_rows(came, 2)
    scratch[...] = dot(att[...], out[...], NT).astype(BF16)
    split_halves(place, scratch, keep, send)


def feed_body(
    long_rows,
    place,
    long_lengths,
    short_lengths,
    own,
    other,
    long_in,
    short_in,
    long_cot,
    short_cot,
    gathered,
    mid_ref,
    squared_ref,
    grad_out_ref,
    keep,
    send,
    up_keep,
    up_send,
    scratch,
    attended,
    up,
    down,
    blocks,
    normed_ref,
    grad_up_ref,
):
    seqs = long_in.shape[0]
    shard = gathered.shape[1] // 2
    for s in range(8):
        up[s * shard : (s + 1) * shard, :] = gathered[s, :shard, :]
        down[s * shard : (s + 1) * shard, :] = gathered[s, shard:, :]
    rows = long_rows + short_in.shape[1]
    join_halves(place, attended, own, other)
    for b in range(seqs):
        at = slice(b * rows, (b + 1) * rows)
        residual = jnp.concatenate([long_in[b], short_in[b]], axis=0).astype(F32)
        mid = residual + attended[at, :]
        mid_ref[at, :] = mid
        root = lax.rsqrt(jnp.mean(mid * mid, axis=-1, keepdims=True) + norm_eps)
        normed_ref[at, :] = (mid * root).astype(BF16)
        for cot, lengths, first, count in (
            (long_cot, long_lengths, b * rows, long_rows),
            (short_cot, short_lengths, b * rows + long_rows, rows - long_rows),
        ):
            value = cot[b]
            position = lax.broadcasted_iota(jnp.int32, value.shape, 0) + place[0] * count
            grad_out_ref[first : first + count, :] = jnp.where(
                position < lengths[b], value.astype(F32), 0.0
            ).astype(BF16)
    relu = jnp.maximum(dot(normed_ref[...], up[...]), 0.0)
    squared_ref[...] = (relu * relu).astype(BF16)
    grad_squared = dot(grad_out_ref[...], down[...])
    grad_up_ref[...] = (grad_squared * 2.0 * relu).astype(BF16)
    scratch[...] = dot(grad_up_ref[...], up[...], NT).astype(BF16)
    split_halves(place, scratch, keep, send)
    term = dot(normed_ref[...], grad_up_ref[...], TN).astype(BF16)
    for s in range(8):
        blocks[s] = term[s * shard : (s + 1) * shard]
    split_y(place, blocks, up_keep, up_send)


def split_halves(place, whole, keep, send):
    half = whole.shape[0] // 2
    core = place[1] % 2
    keep[...] = whole[pl.ds(pl.multiple_of(core * half, half), half), :]
    send[...] = whole[pl.ds(pl.multiple_of((1 - core) * half, half), half), :]


def join_halves(place, whole, own, other):
    half = own.shape[0]
    core = place[1] % 2
    whole[pl.ds(pl.multiple_of(core * half, half), half), :] = own[...].astype(whole.dtype)
    whole[pl.ds(pl.multiple_of((1 - core) * half, half), half), :] = other[...].astype(whole.dtype)


def split_y(place, blocks, keep, send):
    y = place[0] % 2
    for z in range(4):
        keep[z] = blocks[2 * z + y]
        send[z] = blocks[2 * z + 1 - y]


def down_term_body(
    place, squared, grad_out, gathered, near, own, across, f_keep, f_send, scratch, down, blocks
):
    rows = gathered.shape[1] // 2
    for s in range(8):
        down[s * rows : (s + 1) * rows, :] = gathered[s, rows:, :]
    term = dot(grad_out[...], squared[...], TN).astype(BF16)
    for s in range(8):
        blocks[s] = term[s * rows : (s + 1) * rows]
    z = place[0] // 2
    for i, target in ((0, own), (1, near.at[0]), (2, across), (3, near.at[1])):
        for y in range(2):
            target[y] = blocks[2 * jnp.bitwise_xor(z, i) + y]
    scratch[...] = dot(squared[...], down[...], NT).astype(BF16)
    split_halves(place, scratch, f_keep, f_send)


def down_across_body(across, near, out):
    out[...] = (across[...].astype(F32) + near[1].astype(F32)).astype(BF16)


def down_y_body(place, own, near, across, keep, send):
    y = place[0] % 2
    for target, block in ((keep, y), (send, 1 - y)):
        target[...] = (
            own[block].astype(F32) + near[0, block].astype(F32) + across[block].astype(F32)
        ).astype(BF16)


def middle_body(
    place, own, other, mid_ref, grad_out, out, att, grad_mid_ref, send, keep_out, send_out, scratch, low_ref, blocks
):
    join_halves(place, scratch, own, other)
    seqs = 2
    rows = mid_ref.shape[0] // seqs
    for b in range(seqs):
        at = slice(b * rows, (b + 1) * rows)
        mid = mid_ref[at, :]
        weighted = scratch[at, :]
        root = lax.rsqrt(jnp.mean(mid * mid, axis=-1, keepdims=True) + norm_eps)
        inner = jnp.mean(weighted * mid, axis=-1, keepdims=True)
        grad_mid = grad_out[at, :].astype(F32) + (
            root * weighted - mid * (root * root * root * inner)
        )
        grad_mid_ref[at, :] = grad_mid
        low_ref[at, :] = grad_mid.astype(BF16)
    grad_att = dot(low_ref[...], out[...]).astype(BF16)
    for dest in range(8):
        if dest < 3 * seqs:
            e, b = dest // seqs, dest % seqs
            send[dest] = fold(
                grad_att[b * rows : (b + 1) * rows, e * HEAD_DIM : (e + 1) * HEAD_DIM]
            )
        else:
            send[dest] = jnp.zeros_like(send[dest])
    term = dot(low_ref[...], att[...], TN).astype(BF16)
    shard = term.shape[0] // 8
    for s in range(8):

        def store(row, lane, value):
            blocks[s, row : row + 16, lane : lane + LANES] = value

        narrow_pack(term[s * shard : (s + 1) * shard], store)
    split_y(place, blocks, keep_out, send_out)


def attend_back_body(
    long_rows,
    seqs,
    place,
    long_lengths,
    short_lengths,
    came,
    q_all,
    kv_all,
    att_t,
    log_row,
    grad_came,
    send,
):
    rows = (came.shape[1] - 16) * 2 // 3
    short_rows = rows - long_rows
    taps_q, taps_kv = head_taps(place, came, rows, seqs)
    b = place[0] % seqs
    e = place[0] // seqs
    grads = [unfold(grad_came[j]) for j in range(8)]
    first = 0
    terms_q = [0.0, 0.0, 0.0]
    terms_kv = [0.0, 0.0, 0.0]
    results = []
    for lengths, part, (q_mixed, kv_mixed) in zip(
        (long_lengths, short_lengths),
        (slice(0, long_rows), slice(long_rows, rows)),
        own_pair(came, long_rows, rows),
    ):
        count = q_mixed.shape[0]
        block = min(256, count)
        length = lengths[b]
        at = slice(first, first + count)
        grad = jnp.concatenate([g[part] for g in grads], axis=0)
        q = q_all[at, :]
        kv = kv_all[at, :]
        kv_t = kv.astype(F32).T.astype(BF16)
        delta = jnp.sum(grad.astype(F32).T * att_t[:, at], axis=0, keepdims=True)
        log_total = log_row[:, at]
        k, v = kv[:, :HEAD_DIM], kv[:, HEAD_DIM:]
        k_t = kv_t[:HEAD_DIM, :]
        grad_q = None
        grad_kv = []
        for start in range(0, count, block):
            stop = start + block
            scores = dot(k[start:stop], q[start:], NT)
            key_pos = lax.broadcasted_iota(jnp.int32, scores.shape, 0)
            query_pos = lax.broadcasted_iota(jnp.int32, scores.shape, 1)
            allowed = jnp.logical_and(key_pos <= query_pos, key_pos + start < length)
            prob = jnp.where(allowed, jnp.exp(scores - log_total[:, start:]), 0.0)
            grad_prob = dot(v[start:stop], grad[start:], NT)
            grad_scores = (prob * (grad_prob - delta[:, start:])).astype(BF16)
            grad_k = dot(grad_scores, q[start:])
            grad_v = dot(prob.astype(BF16), grad[start:])
            grad_kv.append(jnp.concatenate([grad_k, grad_v], axis=1))
            part_q = dot(k_t[:, start:stop], grad_scores)
            if start == 0:
                grad_q = part_q
            else:
                grad_q = jnp.concatenate(
                    [grad_q[:, :start], grad_q[:, start:] + part_q], axis=1
                )
        grad_q = grad_q.T * HEAD_DIM ** (-0.5)
        grad_kv = jnp.concatenate(grad_kv, axis=0)
        pair = []
        for grad_conv, mixed, taps, terms in (
            (grad_q, q_mixed, taps_q, terms_q),
            (grad_kv, kv_mixed, taps_kv, terms_kv),
        ):
            for m in range(3):
                back = mixed if m == 0 else shift_back(mixed, m)
                terms[m] = terms[m] + jnp.sum(grad_conv * back, axis=0, keepdims=True)
            pair.append(
                (
                    taps[0] * grad_conv
                    + taps[1] * shift_ahead(grad_conv, 1)
                    + taps[2] * shift_ahead(grad_conv, 2)
                ).astype(BF16)
            )
        results.append(pair)
        first += count
    table = jnp.concatenate(
        terms_q
        + [t[:, :HEAD_DIM] for t in terms_kv]
        + [t[:, HEAD_DIM:] for t in terms_kv]
        + [jnp.zeros((7, HEAD_DIM), F32)],
        axis=0,
    )
    table = jnp.concatenate([jnp.where(e == i, table, 0.0) for i in range(3)], axis=1)
    width = 3 * HEAD_DIM // 8
    for j in range(8):
        mine = [
            jnp.concatenate(
                [
                    results[0][i][j * long_rows : (j + 1) * long_rows],
                    results[1][i][j * short_rows : (j + 1) * short_rows],
                ],
                axis=0,
            )
            for i in range(2)
        ]
        send[j, :rows, :] = mine[1]
        send[j, rows : rows + rows // 2, :] = fold(mine[0])
        send[j, rows + rows // 2 :, :] = jnp.concatenate(
            [table[:, j * width : (j + 1) * width], jnp.zeros((16, LANES - width), F32)], axis=1
        ).astype(BF16)


def place_grad_mixed(came, grad_mixed):
    seqs = 2
    rows = (came.shape[1] - 16) * 2 // 3
    for e in range(3):
        for b in range(seqs):
            j = seqs * e + b
            at = slice(b * rows, (b + 1) * rows)
            lanes = slice(e * HEAD_DIM, (e + 1) * HEAD_DIM)
            grad_mixed[0, at, lanes] = unfold(came[j, rows : rows + rows // 2, :])
            grad_mixed[1, at, lanes] = came[j, :rows, :HEAD_DIM]
            grad_mixed[2, at, lanes] = came[j, :rows, HEAD_DIM:]


def project_back_body(
    place, came, normed, weight, keep_p, send_p, keep, send, taps, scratch, grad_mixed, blocks
):
    place_grad_mixed(came, grad_mixed)
    shard = normed.shape[1] // 8
    terms = [dot(normed[...], grad_mixed[c], TN).astype(BF16) for c in range(3)]
    for s in range(8):
        at = slice(s * shard, (s + 1) * shard)
        for c in range(3):
            blocks[s, c * shard : (c + 1) * shard, :] = terms[c][at, :LANES]
        blocks[s, 3 * shard :, :] = fold(
            jnp.concatenate([terms[c][at, LANES:] for c in range(3)], axis=0)
        )
    split_y(place, blocks, keep_p, send_p)
    rows = (came.shape[1] - 16) * 2 // 3
    total = came[0, rows + rows // 2 :, :].astype(F32)
    for j in range(1, 6):
        total = total + came[j, rows + rows // 2 :, :].astype(F32)
    taps[...] = total[: taps.shape[0], : taps.shape[1]]
    total = dot(grad_mixed[0], weight[0], NT)
    for c in (1, 2):
        total = total + dot(grad_mixed[c], weight[c], NT)
    scratch[...] = total.astype(BF16)
    split_halves(place, scratch, keep, send)


def input_grad_body(
    place, own, other, grad_mid, gain, long_in, short_in, long_out, short_out, scratch
):
    join_halves(place, scratch, own, other)
    seqs, long_rows, _ = long_in.shape
    rows = long_rows + short_in.shape[1]
    for b in range(seqs):
        at = slice(b * rows, (b + 1) * rows)
        values = jnp.concatenate([long_in[b], short_in[b]], axis=0).astype(F32)
        weighted = scratch[at, :] * gain[...]
        root = lax.rsqrt(jnp.mean(values * values, axis=-1, keepdims=True) + norm_eps)
        inner = jnp.mean(weighted * values, axis=-1, keepdims=True)
        grad = grad_mid[at, :] + (root * weighted - values * (root * root * root * inner))
        long_out[b] = grad[:long_rows]
        short_out[b] = grad[long_rows:]


def output_body(place, own, other, mid, long_out, short_out, scratch):
    join_halves(place, scratch, own, other)
    seqs, long_rows, _ = long_out.shape
    rows = long_rows + short_out.shape[1]
    for b in range(seqs):
        at = slice(b * rows, (b + 1) * rows)
        value = (mid[at, :] + scratch[at, :]).astype(BF16)
        long_out[b] = value[:long_rows]
        short_out[b] = value[long_rows:]


def scatter_z_body(place, *refs):
    count = (len(refs) - 4) // 2
    outs = refs[2 * count :]
    z = place[0] // 2
    for i in range(4):
        block = jnp.bitwise_xor(z, i)
        first = 0
        for a in range(count):
            keep, came = refs[2 * a], refs[2 * a + 1]
            rows = keep.shape[1]
            outs[i][first : first + rows, :] = (
                keep[block].astype(F32) + came[block].astype(F32)
            ).astype(BF16)
            first += rows


def near_body(place, *refs):
    pairs = len(refs[:-3]) // 2
    near, own, across = refs[-3:]
    z = place[0] // 2
    for i, target in ((0, own), (1, near.at[0]), (2, across), (3, near.at[1])):
        block = jnp.bitwise_xor(z, i)
        first = 0
        for p in range(pairs):
            keep, came = refs[2 * p], refs[2 * p + 1]
            rows = keep.shape[1]
            target[first : first + rows, :] = (
                keep[block].astype(F32) + came[block].astype(F32)
            ).astype(BF16)
            first += rows


def across_body(across, near, out):
    out[...] = (across[...].astype(F32) + near[1].astype(F32)).astype(BF16)


def sum_blocks(blocks):
    return (blocks[0][...].astype(F32) + blocks[1][...].astype(F32)) + (
        blocks[2][...].astype(F32) + blocks[3][...].astype(F32)
    )


def proj_grad_body(b0, b1, b2, b3, proj, gain, grad, gain_grad):
    total = sum_blocks((b0, b1, b2, b3))
    rows = proj.shape[1]
    column = 0.0
    for c, (wide, narrow) in enumerate(unpack_blocks(total, rows, 3)):
        term = jnp.concatenate([wide, narrow], axis=1)
        column = column + jnp.sum(term * proj[c].astype(F32), axis=1, keepdims=True)
        grad[c] = term
    gain_grad[...] = column.T / gain[...].astype(F32).reshape(1, rows)


def ffn_grad_body(
    own, near, across, down_keep, down_came, up, gain, up_grad, down_grad, out_grad, gain_grad
):
    rows = up.shape[0]
    total = own[...].astype(F32) + near[0].astype(F32) + across[...].astype(F32)
    raw = total[:rows]
    gain_grad[...] = jnp.sum(raw * up[...].astype(F32), axis=1, keepdims=True).T
    up_grad[...] = raw * gain[...].astype(F32).reshape(1, rows).T
    down_grad[...] = down_keep[...].astype(F32) + down_came[...].astype(F32)
    wide = total[rows : rows + 16]
    narrow = total[rows + 16 :]
    out = jnp.concatenate(
        [
            jnp.concatenate(
                [
                    wide[:, LANES * g : LANES * (g + 1)],
                    narrow[:, LANES * g : LANES * g + HEAD_DIM],
                ],
                axis=1,
            )
            for g in range(rows // 16)
        ],
        axis=0,
    )
    out_grad[...] = out.T


def pair_shards(
    short_input,
    long_input,
    short_cotangent,
    long_cotangent,
    short_lengths,
    long_lengths,
    proj_weight,
    out_weight,
    conv_taps,
    attention_gain,
    up_weight,
    down_weight,
    feed_gain,
):
    seqs, long_rows, width = long_input.shape
    short_rows = short_input.shape[1]
    rows = long_rows + short_rows
    tokens = seqs * rows
    shard = proj_weight.shape[1]
    local = proj_weight.shape[2]
    hidden = up_weight.shape[1]
    long_len, short_len = 8 * long_rows, 8 * short_rows
    total_len = long_len + short_len
    place = jnp.stack([lax.axis_index("seq"), lax.axis_index("head")]).astype(jnp.int32)
    packed_rows = shard * 9 // 2
    chunk = rows + rows // 2 + 16
    down_t = down_weight.T

    (proj_packed,) = in_vmem(
        pack_proj_body,
        [((packed_rows + 16, LANES), BF16)],
        (),
        far(proj_weight) + (attention_gain,),
    )
    (ffn_packed,) = in_vmem(
        pack_ffn_body,
        [((2 * shard + 32, hidden), BF16)],
        (),
        far(up_weight, down_t, out_weight) + (feed_gain,),
    )
    proj_z = [proj_packed] + [exchange(proj_packed, "seq", mask) for mask in (2, 4, 6)]
    proj_parts = [proj_packed, exchange(proj_packed, "seq", 1)]
    for piece in proj_z[1:]:
        proj_parts += [piece, exchange(piece, "seq", 1)]
    ffn_0 = after(ffn_packed, *proj_z)
    ffn_1 = exchange(ffn_0, "seq", 1)
    ffn_2 = exchange(ffn_0, "seq", 2)
    ffn_4 = exchange(ffn_0, "seq", 4)
    send, normed, proj_full, gain = in_vmem(
        project_body,
        [
            ((8, chunk, LANES), BF16),
            ((tokens, width), BF16, "far"),
            ((3, width, local), BF16, "far"),
            ((1, width), F32, "far"),
        ],
        (place,),
        (*proj_parts, *far(long_input, short_input, conv_taps)),
        scratch=[((8, LANES), F32)],
        fence=True,
    )
    came = lax.all_to_all(send, "seq", 0, 0, tiled=True)
    across_z = marker(ffn_4, ffn_1, send)
    ffn_2, ffn_4 = after(ffn_2, across_z), after(ffn_4, across_z)
    ffn_6 = exchange(ffn_4, "seq", 2)
    ffn_3 = exchange(ffn_2, "seq", 1)
    ffn_5 = exchange(ffn_4, "seq", 1)
    ffn_7 = exchange(ffn_6, "seq", 1)
    att_send, q_all, kv_all, att_t, log_row, mixed = in_vmem(
        functools.partial(attend_body, long_rows, seqs),
        [
            ((8, rows // 2, LANES), BF16),
            ((total_len, HEAD_DIM), BF16, "far"),
            ((total_len, 2 * HEAD_DIM), BF16, "far"),
            ((HEAD_DIM, total_len), F32, "far"),
            ((1, total_len), F32, "far"),
            ((8, chunk, LANES), BF16, "far"),
        ],
        (place, long_lengths, short_lengths),
        (came,),
        fence=True,
    )
    att_0 = lax.all_to_all(att_send, "seq", 0, 0, tiled=True)
    ffn_full, out_full = in_vmem(
        place_ffn_body,
        [((8, 2 * shard, hidden), BF16, "far"), ((width, local), BF16, "far")],
        (place,),
        far(after(ffn_packed, att_send), ffn_1, ffn_2, ffn_3, ffn_4, ffn_5, ffn_6, ffn_7),
    )
    att_0 = after(att_0, out_full)
    att, keep, send = in_vmem(
        out_proj_body,
        [
            ((tokens, local), BF16, "far"),
            ((tokens // 2, width), BF16),
            ((tokens // 2, width), BF16),
        ],
        (place,),
        (att_0,) + far(out_full),
        scratch=[((tokens, width), BF16)],
    )
    half = add_low(keep, exchange(send, "head", 1))
    own = add_low(half, exchange(half, "head", 2))
    other = exchange(own, "head", 1)
    mid, squared, grad_out, keep, send, up_keep, up_send = in_vmem(
        functools.partial(feed_body, long_rows),
        [
            ((tokens, width), F32, "far"),
            ((tokens, hidden), BF16, "far"),
            ((tokens, width), BF16, "far"),
            ((tokens // 2, width), BF16),
            ((tokens // 2, width), BF16),
            ((4, shard, hidden), BF16, "far"),
            ((4, shard, hidden), BF16, "far"),
        ],
        (place, long_lengths, short_lengths),
        (own, other)
        + far(long_input, short_input, long_cotangent, short_cotangent, ffn_full),
        scratch=[
            ((tokens, width), BF16),
            ((tokens, width), F32),
            ((width, hidden), BF16),
            ((width, hidden), BF16),
            ((8, shard, hidden), BF16),
            ((tokens, width), BF16),
            ((tokens, hidden), BF16),
        ],
        limit_mib=32,
    )
    half = add_low(keep, exchange(send, "head", 1))
    up_came = exchange(up_send, "seq", 1)
    down_near, down_own, down_across, f_keep, f_send = in_vmem(
        down_term_body,
        [((2, 2, shard, hidden), BF16, "far")]
        + [((2, shard, hidden), BF16, "far")] * 2
        + [((tokens // 2, width), BF16, "far")] * 2,
        (place,),
        far(after(squared, half), grad_out, ffn_full),
        scratch=[
            ((tokens, width), BF16),
            ((width, hidden), BF16),
            ((8, shard, hidden), BF16),
        ],
        fence=True,
    )
    down_near = exchange(down_near, "seq", 2)
    own = add_low(half, after(exchange(half, "head", 2), f_send))
    other = exchange(own, "head", 1)
    grad_mid, send, out_keep, out_send = in_vmem(
        middle_body,
        [
            ((tokens, width), F32, "far"),
            ((8, rows // 2, LANES), BF16),
            ((4, 32, hidden), BF16, "far"),
            ((4, 32, hidden), BF16, "far"),
        ],
        (place,),
        (own, other) + far(mid, grad_out, out_full, att),
        scratch=[((tokens, width), F32), ((tokens, width), BF16), ((8, 32, hidden), BF16)],
    )
    grad_came = lax.all_to_all(send, "seq", 0, 0, tiled=True)
    out_came = exchange(out_send, "seq", 1)
    (down_across,) = in_vmem(
        down_across_body,
        [((2, shard, hidden), BF16, "far")],
        (),
        far(after(down_across, send, up_came), down_near),
        fence=True,
    )
    grad_came = after(grad_came, down_across)
    down_across = exchange(down_across, "seq", 4)
    f_half = add_low(f_keep, exchange(after(f_send, send), "head", 1))
    f_own = add_low(f_half, exchange(f_half, "head", 2))
    f_other = exchange(f_own, "head", 1)
    long_output, short_output = in_vmem(
        output_body,
        [(long_input.shape, BF16), (short_input.shape, BF16)],
        (place,),
        (f_own, f_other) + far(mid),
        scratch=[((tokens, width), F32)],
    )
    (send,) = in_vmem(
        functools.partial(attend_back_body, long_rows, seqs),
        [((8, chunk, LANES), BF16)],
        (place, long_lengths, short_lengths),
        far(mixed, q_all, kv_all, att_t, log_row) + (grad_came,),
        fence=True,
    )
    mixed_came = lax.all_to_all(send, "seq", 0, 0, tiled=True)
    down_keep, down_send = in_vmem(
        down_y_body,
        [((shard, hidden), BF16, "far")] * 2,
        (place,),
        far(after(down_own, send), down_near, down_across),
    )
    down_came = exchange(down_send, "seq", 1)
    near, ffn_own, across = in_vmem(
        near_body,
        [((2, shard + 32, hidden), BF16, "far")] + [((shard + 32, hidden), BF16, "far")] * 2,
        (place,),
        far(up_keep, after(up_came, send), out_keep, out_came),
        fence=True,
    )
    near = exchange(near, "seq", 2)
    mixed_came = after(mixed_came, long_output, ffn_own, down_send)
    proj_keep, proj_send, keep, send, taps_grad = in_vmem(
        project_back_body,
        [
            ((4, packed_rows, LANES), BF16, "far"),
            ((4, packed_rows, LANES), BF16),
            ((tokens // 2, width), BF16),
            ((tokens // 2, width), BF16),
            (conv_taps.shape, F32),
        ],
        (place,),
        (mixed_came,) + far(normed, proj_full),
        scratch=[
            ((tokens, width), BF16),
            ((3, tokens, local), BF16),
            ((8, packed_rows, LANES), BF16),
        ],
        fence=True,
    )
    proj_came = exchange(proj_send, "seq", 1)
    send = after(send, near)
    half = add_low(keep, exchange(send, "head", 1))
    (across,) = in_vmem(
        across_body, [((shard + 32, hidden), BF16, "far")], (), far(after(across, send), near)
    )
    across = exchange(across, "seq", 4)
    own = add_low(half, after(exchange(half, "head", 2), proj_came))
    other = exchange(own, "head", 1)
    proj_blocks = in_vmem(
        scatter_z_body,
        [((packed_rows, LANES), BF16)] * 4,
        (place,),
        far(proj_keep) + (proj_came,),
    )
    proj_blocks = [proj_blocks[0]] + [exchange(proj_blocks[i], "seq", 2 * i) for i in (1, 2, 3)]
    up_grad, down_grad, out_grad, feed_part = in_vmem(
        ffn_grad_body,
        [
            (up_weight.shape, F32),
            (down_t.shape, F32),
            (out_weight.shape, F32),
            ((1, shard), F32),
        ],
        (),
        far(after(ffn_own, proj_blocks[0]), near, across, down_keep, down_came, up_weight)
        + (feed_gain,),
    )
    proj_blocks[3] = after(proj_blocks[3], up_grad)
    proj_grad, attention_part = in_vmem(
        proj_grad_body,
        [(proj_weight.shape, F32), ((1, shard), F32)],
        (),
        (*proj_blocks, *far(proj_weight), attention_gain),
    )
    long_input_grad, short_input_grad = in_vmem(
        input_grad_body,
        [(long_input.shape, F32), (short_input.shape, F32)],
        (place,),
        (own, other) + far(after(grad_mid, attention_part), gain, long_input, short_input),
        scratch=[((tokens, width), F32)],
    )
    gains = jnp.concatenate([attention_part, feed_part], axis=0)
    across_x = exchange(gains, "head", 2) + exchange(gains, "head", 3)
    gains = (gains + exchange(gains, "head", 1)) + after(across_x, long_input_grad)

    return (
        short_output,
        long_output,
        short_input_grad,
        long_input_grad,
        proj_grad,
        out_grad,
        taps_grad,
        gains[0],
        up_grad,
        down_grad.T,
        gains[1],
    )


def fits_pairs(short_input, long_input, proj_weight):
    seqs, long_rows, _ = long_input.shape
    short_seqs, short_rows, _ = short_input.shape
    return (
        lax.axis_size("seq") == 8
        and lax.axis_size("head") == 4
        and seqs == 2
        and short_seqs == 2
        and proj_weight.shape[2] == 3 * HEAD_DIM
        and proj_weight.shape[1] % 32 == 0
        and long_rows % 32 == 0
        and short_rows % 32 == 0
        and 8 * long_rows <= 2048
    )


def shards(short_input, long_input, *rest):
    proj_weight = rest[4]
    if fits_pairs(short_input, long_input, proj_weight):
        return pair_shards(short_input, long_input, *rest)
    return ring_shards(short_input, long_input, *rest)


def solution(mesh):
    placed = (
        P(None, "seq", None),
        P(None, "seq", None),
        P(None, "seq", None),
        P(None, "seq", None),
        P(),
        P(),
        P(None, "seq", "head"),
        P("head", "seq"),
        P(None, ("head", "seq")),
        P("seq"),
        P("seq", "head"),
        P("head", "seq"),
        P("seq"),
    )
    return jax.shard_map(
        shards,
        mesh=mesh,
        in_specs=placed,
        out_specs=(
            P(None, "seq", None),
            P(None, "seq", None),
            P(None, "seq", None),
            P(None, "seq", None),
            P(None, "seq", "head"),
            P("head", "seq"),
            P(None, ("head", "seq")),
            P("seq"),
            P("seq", "head"),
            P("head", "seq"),
            P("seq"),
        ),
        check_vma=False,
    )
```

```python
import functools

import jax
import jax.numpy as jnp
import numpy as np
from jax import lax
from jax.experimental import pallas as pl
from jax.experimental.pallas import tpu as pltpu
from jax.sharding import PartitionSpec as P

HEAD_DIM = 64


norm_eps = 1e-06
mask_fill = -1e30
block_limit = 2048


def passed_along(block, axis, distance):
    devices = range(lax.axis_size(axis))
    route = [((i - distance) % len(devices), i) for i in devices]
    return lax.ppermute(block, axis, route)


def shifted(array, axis, by):
    peers = lax.axis_size(axis)
    pairs = [(i, i + by) for i in range(peers) if 0 <= i + by < peers]
    return lax.ppermute(array, axis, pairs)


def block_rows(row_count):
    size_rows = min(row_count, block_limit)
    while row_count % size_rows != 0:
        size_rows = size_rows - 1
    return size_rows


def norm_forward(values_in, gain_row):
    inv_root = lax.rsqrt(jnp.mean(values_in * values_in, axis=-1, keepdims=True) + norm_eps)
    return (values_in * inv_root * gain_row, inv_root)


def norm_backward(values_in, inv_root, gain_row, grad_in):
    weighted = grad_in * gain_row
    inner_mean = jnp.mean(weighted * values_in, axis=-1, keepdims=True)
    grad_values = inv_root * weighted - values_in * inv_root * inv_root * inv_root * inner_mean
    grad_gain = jnp.sum(grad_in * values_in * inv_root, axis=(0, 1))
    return (grad_values, grad_gain)


def allowed_mask(query_pos, key_pos, lengths):
    causal = key_pos[None, :] <= query_pos[:, None]
    inside = key_pos[None, :] < lengths[:, None]
    return jnp.logical_and(causal[None, None], inside[:, None, None, :])


def block_scores(query_rows, key_rows, query_pos, key_pos, lengths):
    allowed = allowed_mask(query_pos, key_pos, lengths)
    raw_scores = jnp.einsum(
        "bqhe,bkhe->bhqk", query_rows, key_rows, preferred_element_type=jnp.float32
    ) * HEAD_DIM ** (-0.5)
    return (jnp.where(allowed, raw_scores, mask_fill), allowed)


def block_grads(
    query_rows, grad_rows, log_rows, delta_rows, key_rows, value_rows, query_pos, key_pos, lengths
):
    scores, allowed = block_scores(query_rows, key_rows, query_pos, key_pos, lengths)
    prob_rows = jnp.where(
        allowed, jnp.exp(scores - jnp.transpose(log_rows, (0, 2, 1))[..., None]), 0.0
    )
    grad_probs = jnp.einsum(
        "bqhe,bkhe->bhqk", grad_rows, value_rows, preferred_element_type=jnp.float32
    )
    grad_scores = (
        prob_rows * (grad_probs - jnp.transpose(delta_rows, (0, 2, 1))[..., None])
    ).astype(jnp.bfloat16)
    grad_query = jnp.einsum(
        "bhqk,bkhe->bqhe", grad_scores, key_rows, preferred_element_type=jnp.float32
    ) * HEAD_DIM ** (-0.5)
    grad_key = jnp.einsum(
        "bhqk,bqhe->bkhe", grad_scores, query_rows, preferred_element_type=jnp.float32
    ) * HEAD_DIM ** (-0.5)
    grad_value = jnp.einsum(
        "bhqk,bqhe->bkhe",
        prob_rows.astype(jnp.bfloat16),
        grad_rows,
        preferred_element_type=jnp.float32,
    )
    return (grad_query, grad_key, grad_value)


def attend_forward(queries, keys_here, values_here, query_pos, lengths):
    seq_count, span_rows, head_count, head_width = queries.shape
    initial = (
        jnp.full((seq_count, head_count, span_rows), mask_fill, jnp.float32),
        jnp.zeros((seq_count, head_count, span_rows), jnp.float32),
        jnp.zeros((seq_count, span_rows, head_count, head_width), jnp.float32),
    )
    key_piece = lax.all_gather(keys_here, "seq", axis=1, tiled=True)
    value_piece = lax.all_gather(values_here, "seq", axis=1, tiled=True)
    row_count = key_piece.shape[1]
    size_rows = block_rows(row_count)

    def one_block(block_index, carried_state):
        running_top, running_sum, acc_rows = carried_state
        offset = block_index * size_rows
        key_rows = lax.dynamic_slice_in_dim(key_piece, offset, size_rows, 1)
        value_rows = lax.dynamic_slice_in_dim(value_piece, offset, size_rows, 1)
        key_pos = offset + jnp.arange(size_rows, dtype=jnp.int32)
        scores, allowed = block_scores(queries, key_rows, query_pos, key_pos, lengths)
        new_top = jnp.maximum(running_top, jnp.max(scores, axis=-1))
        exp_terms = jnp.where(allowed, jnp.exp(scores - new_top[..., None]), 0.0)
        shrink = jnp.exp(running_top - new_top)
        running_sum = running_sum * shrink + jnp.sum(exp_terms, axis=-1)
        acc_rows = acc_rows * jnp.transpose(shrink, (0, 2, 1))[..., None] + jnp.einsum(
            "bhqk,bkhe->bqhe",
            exp_terms.astype(jnp.bfloat16),
            value_rows,
            preferred_element_type=jnp.float32,
        )
        return (new_top, running_sum, acc_rows)

    running_top, running_sum, acc_rows = lax.fori_loop(
        0, row_count // size_rows, one_block, initial
    )
    attention = acc_rows / jnp.transpose(running_sum, (0, 2, 1))[..., None]
    log_totals = jnp.transpose(running_top + jnp.log(running_sum), (0, 2, 1))
    return (attention, log_totals)


def pass_sums(grad_keys, grad_values):
    return (
        passed_along(grad_keys.astype(jnp.bfloat16), "seq", 1).astype(grad_keys.dtype),
        passed_along(grad_values.astype(jnp.bfloat16), "seq", 1).astype(grad_values.dtype),
    )


def attend_backward(
    queries, keys_here, values_here, grad_attention, log_totals, delta_rows, query_pos, lengths
):
    seq_count, span_rows, head_count, head_width = queries.shape
    zeros_local = jnp.zeros(queries.shape, jnp.float32)
    seq_size = lax.axis_size("seq")
    my_index = lax.axis_index("seq")
    local_pos = jnp.arange(span_rows, dtype=jnp.int32)

    def step_grads(step, key_piece, value_piece):
        anchor = jnp.mod(my_index - step, seq_size)
        key_pos = anchor * span_rows + local_pos
        return block_grads(
            queries,
            grad_attention,
            log_totals,
            delta_rows,
            key_piece,
            value_piece,
            query_pos,
            key_pos,
            lengths,
        )

    def cycle_step(step, state):
        key_piece, value_piece, grad_keys, grad_values, grad_query = state
        query_part, key_part, value_part = step_grads(step, key_piece, value_piece)
        key_piece, value_piece = shifted((key_piece, value_piece), "seq", 1)
        grad_keys, grad_values = pass_sums(grad_keys + key_part, grad_values + value_part)
        return (key_piece, value_piece, grad_keys, grad_values, grad_query + query_part)

    final_state = lax.fori_loop(
        0, seq_size - 1, cycle_step, (keys_here, values_here, zeros_local, zeros_local, zeros_local)
    )
    key_piece, value_piece, grad_keys, grad_values, grad_query = final_state
    query_part, key_part, value_part = step_grads(seq_size - 1, key_piece, value_piece)
    grad_key, grad_value = pass_sums(grad_keys + key_part, grad_values + value_part)
    grad_query = grad_query + query_part
    return (grad_query, grad_key, grad_value)


def micro_batch(inputs, cotangent, lengths, weights):
    proj_full, out_full, taps_full, attend_gain, up_full, down_full, ffn_gain = weights
    seq_count, span_rows, model_width = inputs.shape
    local_width = proj_full.shape[2]
    heads_here = local_width // HEAD_DIM
    query_pos = lax.axis_index("seq") * span_rows + jnp.arange(span_rows, dtype=jnp.int32)
    valid_rows = (query_pos[None, :] < lengths[:, None])[..., None]
    residual_in = inputs.astype(jnp.float32)
    normed, inv_first = norm_forward(residual_in, attend_gain)
    normed_low = normed.astype(jnp.bfloat16)
    mixed_qkv = jnp.einsum(
        "btd,cde->cbte", normed_low, proj_full, preferred_element_type=jnp.float32
    ).astype(jnp.bfloat16)
    borrowed = shifted(mixed_qkv[:, :, span_rows - 2 :, :], "seq", 1)
    extended = jnp.concatenate([borrowed, mixed_qkv], axis=2).astype(jnp.float32)
    tap_table = taps_full.astype(jnp.float32).reshape(3, 3, local_width)
    tap_now = tap_table[:, 0][:, None, None, :]
    tap_one = tap_table[:, 1][:, None, None, :]
    tap_two = tap_table[:, 2][:, None, None, :]
    conved = (
        tap_now * extended[:, :, 2:]
        + tap_one * extended[:, :, 1:-1]
        + tap_two * extended[:, :, :-2]
    )
    conv_out = conved.astype(jnp.bfloat16).reshape(3, seq_count, span_rows, heads_here, HEAD_DIM)
    queries, keys_here, values_here = (conv_out[0], conv_out[1], conv_out[2])
    attention, log_totals = attend_forward(queries, keys_here, values_here, query_pos, lengths)
    attention_low = attention.astype(jnp.bfloat16).reshape(seq_count, span_rows, local_width)
    attend_part = jnp.einsum(
        "bte,ed->btd", attention_low, out_full, preferred_element_type=jnp.float32
    )
    mid_residual = residual_in + lax.psum(attend_part.astype(jnp.bfloat16), "head").astype(
        jnp.float32
    )
    normed_ffn, inv_second = norm_forward(mid_residual, ffn_gain)
    normed_ffn_low = normed_ffn.astype(jnp.bfloat16)
    up_proj = jnp.einsum("btd,df->btf", normed_ffn_low, up_full, preferred_element_type=jnp.float32)
    relu_up = jnp.maximum(up_proj, 0.0)
    squared = (relu_up * relu_up).astype(jnp.bfloat16)
    ffn_part = jnp.einsum("btf,fd->btd", squared, down_full, preferred_element_type=jnp.float32)
    output = (
        mid_residual + lax.psum(ffn_part.astype(jnp.bfloat16), "head").astype(jnp.float32)
    ).astype(jnp.bfloat16)
    grad_out = jnp.where(valid_rows, cotangent.astype(jnp.float32), 0.0)
    grad_out_low = grad_out.astype(jnp.bfloat16)
    down_term = jnp.einsum("btf,btd->fd", squared, grad_out_low, preferred_element_type=jnp.float32)
    grad_squared = jnp.einsum(
        "btd,fd->btf", grad_out_low, down_full, preferred_element_type=jnp.float32
    )
    grad_up = (grad_squared * 2.0 * relu_up).astype(jnp.bfloat16)
    up_term = jnp.einsum("btd,btf->df", normed_ffn_low, grad_up, preferred_element_type=jnp.float32)
    grad_normed_ffn = lax.psum(
        jnp.einsum("btf,df->btd", grad_up, up_full, preferred_element_type=jnp.float32).astype(
            jnp.bfloat16
        ),
        "head",
    ).astype(jnp.float32)
    grad_through, feed_term = norm_backward(mid_residual, inv_second, ffn_gain, grad_normed_ffn)
    grad_mid = grad_out + grad_through
    grad_mid_low = grad_mid.astype(jnp.bfloat16)
    out_term = jnp.einsum(
        "bte,btd->ed", attention_low, grad_mid_low, preferred_element_type=jnp.float32
    )
    grad_attention = jnp.einsum(
        "btd,ed->bte", grad_mid_low, out_full, preferred_element_type=jnp.float32
    )
    grad_attention = grad_attention.astype(jnp.bfloat16).reshape(
        seq_count, span_rows, heads_here, HEAD_DIM
    )
    delta_rows = jnp.einsum("bqhe,bqhe->bqh", grad_attention.astype(jnp.float32), attention)
    grad_query, grad_key, grad_value = attend_backward(
        queries, keys_here, values_here, grad_attention, log_totals, delta_rows, query_pos, lengths
    )
    grad_conv = jnp.stack([grad_query, grad_key, grad_value]).reshape(
        3, seq_count, span_rows, local_width
    )
    taps_term = jnp.stack(
        [
            jnp.sum(grad_conv * extended[:, :, 2:], axis=(1, 2)),
            jnp.sum(grad_conv * extended[:, :, 1:-1], axis=(1, 2)),
            jnp.sum(grad_conv * extended[:, :, :-2], axis=(1, 2)),
        ],
        axis=1,
    ).reshape(9, local_width)
    full_grad = jnp.pad(grad_conv, ((0, 0), (0, 0), (2, 2), (0, 0)))
    grad_extended = (
        tap_now * full_grad[:, :, 0 : span_rows + 2]
        + tap_one * full_grad[:, :, 1 : span_rows + 3]
        + tap_two * full_grad[:, :, 2 : span_rows + 4]
    )
    returned = shifted(grad_extended[:, :, :2], "seq", -1)
    grad_mixed = jnp.concatenate(
        [grad_extended[:, :, 2:span_rows], grad_extended[:, :, span_rows:] + returned], axis=2
    ).astype(jnp.bfloat16)
    proj_term = jnp.einsum(
        "btd,cbte->cde", normed_low, grad_mixed, preferred_element_type=jnp.float32
    )
    grad_normed = lax.psum(
        jnp.einsum(
            "cbte,cde->btd", grad_mixed, proj_full, preferred_element_type=jnp.float32
        ).astype(jnp.bfloat16),
        "head",
    ).astype(jnp.float32)
    grad_first, attention_term = norm_backward(residual_in, inv_first, attend_gain, grad_normed)
    grad_input = grad_mid + grad_first
    return (
        output,
        grad_input,
        (proj_term, out_term, taps_term, attention_term, up_term, down_term, feed_term),
    )


def ring_shards(
    short_input,
    long_input,
    short_cotangent,
    long_cotangent,
    short_lengths,
    long_lengths,
    proj_weight,
    out_weight,
    conv_taps,
    attention_gain,
    up_weight,
    down_weight,
    feed_gain,
):
    proj_full, out_full, taps_full, attend_gain = (
        lax.all_gather(proj_weight, "seq", axis=1, tiled=True),
        lax.all_gather(out_weight, "seq", axis=1, tiled=True),
        lax.all_gather(conv_taps, "seq", axis=1, tiled=True),
        lax.all_gather(attention_gain, "seq", axis=0, tiled=True),
    )
    up_full, down_full, ffn_gain = (
        lax.all_gather(up_weight, "seq", axis=0, tiled=True),
        lax.all_gather(down_weight, "seq", axis=1, tiled=True),
        lax.all_gather(feed_gain, "seq", axis=0, tiled=True),
    )
    weights = (
        proj_full,
        out_full,
        taps_full,
        attend_gain.astype(jnp.float32),
        up_full,
        down_full,
        ffn_gain.astype(jnp.float32),
    )
    short_output, short_input_grad, short_terms = micro_batch(
        short_input, short_cotangent, short_lengths, weights
    )
    long_output, long_input_grad, long_terms = micro_batch(
        long_input, long_cotangent, long_lengths, weights
    )
    summed = tuple(
        (first_term + second_term for first_term, second_term in zip(short_terms, long_terms))
    )
    reduced = (
        lax.psum_scatter(summed[0], "seq", scatter_dimension=1, tiled=True),
        lax.psum_scatter(summed[1], "seq", scatter_dimension=1, tiled=True),
        lax.psum_scatter(summed[2], "seq", scatter_dimension=1, tiled=True),
        lax.psum_scatter(summed[3], "seq", scatter_dimension=0, tiled=True),
        lax.psum_scatter(summed[4], "seq", scatter_dimension=0, tiled=True),
        lax.psum_scatter(summed[5], "seq", scatter_dimension=1, tiled=True),
        lax.psum_scatter(summed[6], "seq", scatter_dimension=0, tiled=True),
    )
    return (
        short_output,
        long_output,
        short_input_grad,
        long_input_grad,
        reduced[0],
        reduced[1],
        reduced[2],
        reduced[3],
        reduced[4],
        reduced[5],
        reduced[6],
    )


LANES = 128
FENCE = 10**11
NT = (((1,), (1,)), ((), ()))
TN = (((0,), (0,)), ((), ()))
F32 = jnp.float32
BF16 = jnp.bfloat16


def dot(a, b, dims=(((1,), (0,)), ((), ()))):
    return lax.dot_general(a, b, dims, preferred_element_type=F32)


def in_vmem(body, outs, scalars, arrays, scratch=(), limit_mib=16, fence=False):
    return pl.pallas_call(
        body,
        out_shape=[
            pltpu.HBM(*out[:2]) if len(out) == 3 else jax.ShapeDtypeStruct(*out) for out in outs
        ],
        in_specs=[pl.BlockSpec(memory_space=pltpu.SMEM)] * len(scalars)
        + [pl.BlockSpec(memory_space=pltpu.VMEM)] * len(arrays),
        out_specs=[pl.BlockSpec(memory_space=pltpu.VMEM)] * len(outs),
        scratch_shapes=[pltpu.VMEM(shape, kind) for shape, kind in scratch],
        compiler_params=pltpu.CompilerParams(vmem_limit_bytes=limit_mib * 1024 * 1024),
        cost_estimate=pl.CostEstimate(
            flops=FENCE if fence else 0, bytes_accessed=0, transcendentals=0
        ),
    )(*scalars, *arrays)


def far(*arrays):
    return tuple(pltpu.with_memory_space_constraint(array, pltpu.HBM) for array in arrays)


def after(array, *others):
    return lax.optimization_barrier((array, *others))[0]


def marker(*arrays):
    def body(*refs):
        refs[-1][...] = jnp.zeros_like(refs[-1])

    return pl.pallas_call(
        body,
        out_shape=jax.ShapeDtypeStruct((8, LANES), F32),
        in_specs=[pl.BlockSpec(memory_space=pl.ANY)] * len(arrays),
        out_specs=pl.BlockSpec(memory_space=pltpu.VMEM),
        cost_estimate=pl.CostEstimate(flops=FENCE, bytes_accessed=0, transcendentals=0),
    )(*arrays)


def exchange(array, axis, mask):
    size = lax.axis_size(axis)
    return lax.ppermute(array, axis, [(i, i ^ mask) for i in range(size)])


def add_low(a, b):
    return (a.astype(F32) + b.astype(F32)).astype(BF16)


def shift_back(rows, by):
    index = lax.broadcasted_iota(jnp.int32, rows.shape, 0)
    return jnp.where(index >= by, pltpu.roll(rows, by, axis=0), 0.0)


def shift_ahead(rows, by):
    count = rows.shape[0]
    index = lax.broadcasted_iota(jnp.int32, rows.shape, 0)
    return jnp.where(index < count - by, pltpu.roll(rows, count - by, axis=0), 0.0)


def fold(rows):
    half = rows.shape[0] // 2
    return jnp.concatenate([rows[:half], rows[half:]], axis=1)


def unfold(rows):
    return jnp.concatenate([rows[:, :HEAD_DIM], rows[:, HEAD_DIM:]], axis=0)


def pack_proj_body(proj, gain, packed):
    rows = proj.shape[1]
    for c in range(3):
        packed[c * rows : (c + 1) * rows, :] = proj[c, :, :LANES]
    narrow = jnp.concatenate([proj[c, :, LANES:] for c in range(3)], axis=0)
    packed[3 * rows : 9 * rows // 2, :] = fold(narrow)
    gain_row = gain[...].astype(F32).reshape(1, rows)
    gain_row = jnp.concatenate([gain_row, jnp.zeros((1, LANES - rows), F32)], axis=1)
    packed[9 * rows // 2 :, :] = jnp.broadcast_to(gain_row, (16, LANES)).astype(BF16)


def unpack_blocks(packed, rows, count):
    narrow = unfold(packed[count * rows : 3 * count * rows // 2, :])
    return [
        (packed[i * rows : (i + 1) * rows, :], narrow[i * rows : (i + 1) * rows, :])
        for i in range(count)
    ]


def narrow_pack(block, store):
    groups = block.shape[0] // 16
    for g in range(groups):
        rows = block[16 * g : 16 * g + 16, :]
        store(0, LANES * g, rows[:, :LANES])
        tail = rows[:, LANES:]
        store(16, LANES * g, jnp.concatenate([tail, jnp.zeros_like(tail)], axis=1))


def pack_ffn_body(up, down, out, gain, packed):
    rows = up.shape[0]
    gain_column = gain[...].astype(F32).reshape(1, rows).T
    packed[:rows, :] = (up[...].astype(F32) * gain_column).astype(BF16)
    packed[rows : 2 * rows, :] = down[...]

    def store(row, lane, value):
        packed[2 * rows + row : 2 * rows + row + 16, lane : lane + LANES] = value

    narrow_pack(out[...].astype(F32).T.astype(BF16), store)


def place_ffn_body(place, *refs):
    up, down, out, out_now = refs[8:]
    rows = out.shape[0] // 8
    for i in range(8):
        owner = jnp.bitwise_xor(place[0], i)
        part = refs[i]
        first = pl.ds(pl.multiple_of(owner * rows, rows), rows)
        up[first, :] = part[:rows, :]
        down[first, :] = part[rows : 2 * rows, :]
        for g in range(rows // 16):
            at = pl.ds(pl.multiple_of(owner * rows + 16 * g, 16), 16)
            out[at, :LANES] = part[2 * rows : 2 * rows + 16, LANES * g : LANES * g + LANES]
            out[at, LANES:] = part[2 * rows + 16 :, LANES * g : LANES * g + HEAD_DIM]
    out_now[...] = out[...]


def project_body(place, *refs):
    parts = refs[:8]
    long_in, short_in, taps, send, normed, weight, gain, gain_rows = refs[8:]
    seqs, long_rows, _ = long_in.shape
    rows = long_rows + short_in.shape[1]
    for i in range(8):
        packed = parts[i][...]
        shard = weight.shape[1] // 8
        owner = jnp.bitwise_xor(place[0], i)
        gain_rows[pl.ds(owner, 1), :] = packed[9 * shard // 2 :, :].astype(F32)[:1]
        at = pl.ds(pl.multiple_of(owner * shard, shard), shard)
        for c, (wide, narrow) in enumerate(unpack_blocks(packed, shard, 3)):
            weight[c, at, :LANES] = wide
            weight[c, at, LANES:] = narrow
    gain[...] = jnp.concatenate([gain_rows[j : j + 1, :shard] for j in range(8)], axis=1)
    for b in range(seqs):
        values = jnp.concatenate([long_in[b], short_in[b]], axis=0).astype(F32)
        root = lax.rsqrt(jnp.mean(values * values, axis=-1, keepdims=True) + norm_eps)
        normed[b * rows : (b + 1) * rows, :] = (values * root * gain[...]).astype(BF16)
    mixed = [dot(normed[...], weight[c]).astype(BF16) for c in range(3)]
    tap_rows = jnp.concatenate(
        [taps[...], jnp.zeros((16 - taps.shape[0], taps.shape[1]), BF16)], axis=0
    )
    tap_rows = jnp.concatenate(
        [tap_rows, jnp.zeros((16, LANES - taps.shape[1]), BF16)], axis=1
    )
    half = rows // 2
    for dest in range(8):
        if dest < 3 * seqs:
            e, b = dest // seqs, dest % seqs
            lanes = slice(e * HEAD_DIM, (e + 1) * HEAD_DIM)
            q, k, v = [m[b * rows : (b + 1) * rows, lanes] for m in mixed]
            send[dest, :rows, :] = jnp.concatenate([k, v], axis=1)
            send[dest, rows : rows + half, :] = fold(q)
        else:
            send[dest, : rows + half, :] = jnp.zeros((rows + half, LANES), BF16)
        send[dest, rows + half :, :] = tap_rows


def head_taps(place, came, rows, seqs):
    first = rows + rows // 2
    width = 3 * HEAD_DIM // 8
    whole = jnp.concatenate(
        [came[j, first:, :].astype(F32)[:, :width] for j in range(8)], axis=1
    )
    e = place[0] // seqs
    mine = whole[:, :HEAD_DIM]
    for other in (1, 2):
        mine = jnp.where(
            e == other, whole[:, other * HEAD_DIM : (other + 1) * HEAD_DIM], mine
        )
    taps_q = [mine[m : m + 1, :] for m in range(3)]
    taps_kv = [
        jnp.concatenate([mine[3 + m : 4 + m, :], mine[6 + m : 7 + m, :]], axis=1) for m in range(3)
    ]
    return taps_q, taps_kv


def own_pair(came, long_rows, rows):
    q_rows = [unfold(came[j, rows : rows + rows // 2, :]) for j in range(8)]
    result = []
    for part in (slice(0, long_rows), slice(long_rows, rows)):
        q = jnp.concatenate([piece[part] for piece in q_rows], axis=0).astype(F32)
        kv = jnp.concatenate([came[j, part, :] for j in range(8)], axis=0).astype(F32)
        result.append((q, kv))
    return result


def convolve(rows, taps):
    return taps[0] * rows + taps[1] * shift_back(rows, 1) + taps[2] * shift_back(rows, 2)


def attend_body(
    long_rows, seqs, place, long_lengths, short_lengths, came, send, q_all, kv_all, att_t, log_row, kept
):
    rows = (came.shape[1] - 16) * 2 // 3
    kept[...] = came[...]
    taps_q, taps_kv = head_taps(place, came, rows, seqs)
    b = place[0] % seqs
    first = 0
    results = []
    for lengths, (q_mixed, kv_mixed) in zip(
        (long_lengths, short_lengths), own_pair(came, long_rows, rows)
    ):
        count = q_mixed.shape[0]
        block = min(256, count)
        length = lengths[b]
        q = (convolve(q_mixed, taps_q).astype(BF16).astype(F32) * HEAD_DIM ** (-0.5)).astype(BF16)
        kv = convolve(kv_mixed, taps_kv).astype(BF16)
        kv_t = kv.astype(F32).T.astype(BF16)
        q_all[first : first + count, :] = q
        kv_all[first : first + count, :] = kv
        k = kv[:, :HEAD_DIM]
        v_t = kv_t[HEAD_DIM:, :]
        pieces = []
        for start in range(0, count, block):
            stop = start + block
            scores = dot(k[:stop], q[start:stop], NT)
            key_pos = lax.broadcasted_iota(jnp.int32, scores.shape, 0)
            query_pos = lax.broadcasted_iota(jnp.int32, scores.shape, 1) + start
            allowed = jnp.logical_and(key_pos <= query_pos, key_pos < length)
            scores = jnp.where(allowed, scores, mask_fill)
            top = jnp.max(scores, axis=0, keepdims=True)
            terms = jnp.exp(scores - top)
            total = jnp.sum(terms, axis=0, keepdims=True)
            out_t = dot(v_t[:, :stop], terms.astype(BF16)) / total
            att_t[:, first + start : first + stop] = out_t
            log_row[:, first + start : first + stop] = top + jnp.log(total)
            pieces.append(out_t.T.astype(BF16))
        results.append(jnp.concatenate(pieces, axis=0))
        first += count
    short_rows = rows - long_rows
    for j in range(8):
        mine = jnp.concatenate(
            [
                results[0][j * long_rows : (j + 1) * long_rows],
                results[1][j * short_rows : (j + 1) * short_rows],
            ],
            axis=0,
        )
        send[j, :, :] = fold(mine)


def pair_rows(came, seqs):
    columns = []
    for e in range(3):
        columns.append(
            jnp.concatenate([unfold(came[seqs * e + b]) for b in range(seqs)], axis=0)
        )
    return jnp.concatenate(columns, axis=1)


def out_proj_body(place, came, out, att, keep, send, scratch):
    att[...] = pair_rows(came, 2)
    scratch[...] = dot(att[...], out[...], NT).astype(BF16)
    split_halves(place, scratch, keep, send)


def feed_body(
    long_rows,
    place,
    long_lengths,
    short_lengths,
    own,
    other,
    long_in,
    short_in,
    long_cot,
    short_cot,
    up,
    down,
    mid_ref,
    squared_ref,
    grad_out_ref,
    keep,
    send,
    up_keep,
    up_send,
    scratch,
    attended,
    blocks,
    normed_ref,
    grad_up_ref,
):
    seqs = long_in.shape[0]
    shard = up.shape[0] // 8
    rows = long_rows + short_in.shape[1]
    join_halves(place, attended, own, other)
    for b in range(seqs):
        at = slice(b * rows, (b + 1) * rows)
        residual = jnp.concatenate([long_in[b], short_in[b]], axis=0).astype(F32)
        mid = residual + attended[at, :]
        mid_ref[at, :] = mid
        root = lax.rsqrt(jnp.mean(mid * mid, axis=-1, keepdims=True) + norm_eps)
        normed_ref[at, :] = (mid * root).astype(BF16)
        for cot, lengths, first, count in (
            (long_cot, long_lengths, b * rows, long_rows),
            (short_cot, short_lengths, b * rows + long_rows, rows - long_rows),
        ):
            value = cot[b]
            position = lax.broadcasted_iota(jnp.int32, value.shape, 0) + place[0] * count
            grad_out_ref[first : first + count, :] = jnp.where(
                position < lengths[b], value.astype(F32), 0.0
            ).astype(BF16)
    relu = jnp.maximum(dot(normed_ref[...], up[...]), 0.0)
    squared_ref[...] = (relu * relu).astype(BF16)
    grad_squared = dot(grad_out_ref[...], down[...])
    grad_up_ref[...] = (grad_squared * 2.0 * relu).astype(BF16)
    scratch[...] = dot(grad_up_ref[...], up[...], NT).astype(BF16)
    split_halves(place, scratch, keep, send)
    term = dot(normed_ref[...], grad_up_ref[...], TN).astype(BF16)
    for s in range(8):
        blocks[s] = term[s * shard : (s + 1) * shard]
    split_y(place, blocks, up_keep, up_send)


def split_halves(place, whole, keep, send):
    half = whole.shape[0] // 2
    core = place[1] % 2
    keep[...] = whole[pl.ds(pl.multiple_of(core * half, half), half), :]
    send[...] = whole[pl.ds(pl.multiple_of((1 - core) * half, half), half), :]


def join_halves(place, whole, own, other):
    half = own.shape[0]
    core = place[1] % 2
    whole[pl.ds(pl.multiple_of(core * half, half), half), :] = own[...].astype(whole.dtype)
    whole[pl.ds(pl.multiple_of((1 - core) * half, half), half), :] = other[...].astype(whole.dtype)


def split_y(place, blocks, keep, send):
    y = place[0] % 2
    for z in range(4):
        keep[z] = blocks[2 * z + y]
        send[z] = blocks[2 * z + 1 - y]


def down_term_body(
    place, squared, grad_out, down, near, own, across, f_keep, f_send, scratch, blocks
):
    rows = blocks.shape[1]
    term = dot(grad_out[...], squared[...], TN).astype(BF16)
    for s in range(8):
        blocks[s] = term[s * rows : (s + 1) * rows]
    z = place[0] // 2
    for i, target in ((0, own), (1, near.at[0]), (2, across), (3, near.at[1])):
        for y in range(2):
            target[y] = blocks[2 * jnp.bitwise_xor(z, i) + y]
    scratch[...] = dot(squared[...], down[...], NT).astype(BF16)
    split_halves(place, scratch, f_keep, f_send)


def down_across_body(across, near, out):
    out[...] = (across[...].astype(F32) + near[1].astype(F32)).astype(BF16)


def down_y_body(place, own, near, across, keep, send):
    y = place[0] % 2
    for target, block in ((keep, y), (send, 1 - y)):
        target[...] = (
            own[block].astype(F32) + near[0, block].astype(F32) + across[block].astype(F32)
        ).astype(BF16)


def middle_body(
    place, own, other, mid_ref, grad_out, out, att, grad_mid_ref, send, keep_out, send_out, scratch, low_ref, blocks
):
    join_halves(place, scratch, own, other)
    seqs = 2
    rows = mid_ref.shape[0] // seqs
    for b in range(seqs):
        at = slice(b * rows, (b + 1) * rows)
        mid = mid_ref[at, :]
        weighted = scratch[at, :]
        root = lax.rsqrt(jnp.mean(mid * mid, axis=-1, keepdims=True) + norm_eps)
        inner = jnp.mean(weighted * mid, axis=-1, keepdims=True)
        grad_mid = grad_out[at, :].astype(F32) + (
            root * weighted - mid * (root * root * root * inner)
        )
        grad_mid_ref[at, :] = grad_mid
        low_ref[at, :] = grad_mid.astype(BF16)
    grad_att = dot(low_ref[...], out[...]).astype(BF16)
    for dest in range(8):
        if dest < 3 * seqs:
            e, b = dest // seqs, dest % seqs
            send[dest] = fold(
                grad_att[b * rows : (b + 1) * rows, e * HEAD_DIM : (e + 1) * HEAD_DIM]
            )
        else:
            send[dest] = jnp.zeros_like(send[dest])
    term = dot(low_ref[...], att[...], TN).astype(BF16)
    shard = term.shape[0] // 8
    for s in range(8):

        def store(row, lane, value):
            blocks[s, row : row + 16, lane : lane + LANES] = value

        narrow_pack(term[s * shard : (s + 1) * shard], store)
    split_y(place, blocks, keep_out, send_out)


def attend_back_body(
    long_rows,
    seqs,
    place,
    long_lengths,
    short_lengths,
    came,
    q_all,
    kv_all,
    att_t,
    log_row,
    grad_came,
    send,
):
    rows = (came.shape[1] - 16) * 2 // 3
    short_rows = rows - long_rows
    taps_q, taps_kv = head_taps(place, came, rows, seqs)
    b = place[0] % seqs
    e = place[0] // seqs
    grads = [unfold(grad_came[j]) for j in range(8)]
    first = 0
    terms_q = [0.0, 0.0, 0.0]
    terms_kv = [0.0, 0.0, 0.0]
    results = []
    for lengths, part, (q_mixed, kv_mixed) in zip(
        (long_lengths, short_lengths),
        (slice(0, long_rows), slice(long_rows, rows)),
        own_pair(came, long_rows, rows),
    ):
        count = q_mixed.shape[0]
        block = min(256, count)
        length = lengths[b]
        at = slice(first, first + count)
        grad = jnp.concatenate([g[part] for g in grads], axis=0)
        q = q_all[at, :]
        kv = kv_all[at, :]
        kv_t = kv.astype(F32).T.astype(BF16)
        delta = jnp.sum(grad.astype(F32).T * att_t[:, at], axis=0, keepdims=True)
        log_total = log_row[:, at]
        k, v = kv[:, :HEAD_DIM], kv[:, HEAD_DIM:]
        k_t = kv_t[:HEAD_DIM, :]
        grad_q = None
        grad_kv = []
        for start in range(0, count, block):
            stop = start + block
            scores = dot(k[start:stop], q[start:], NT)
            key_pos = lax.broadcasted_iota(jnp.int32, scores.shape, 0)
            query_pos = lax.broadcasted_iota(jnp.int32, scores.shape, 1)
            allowed = jnp.logical_and(key_pos <= query_pos, key_pos + start < length)
            prob = jnp.where(allowed, jnp.exp(scores - log_total[:, start:]), 0.0)
            grad_prob = dot(v[start:stop], grad[start:], NT)
            grad_scores = (prob * (grad_prob - delta[:, start:])).astype(BF16)
            grad_k = dot(grad_scores, q[start:])
            grad_v = dot(prob.astype(BF16), grad[start:])
            grad_kv.append(jnp.concatenate([grad_k, grad_v], axis=1))
            part_q = dot(k_t[:, start:stop], grad_scores)
            if start == 0:
                grad_q = part_q
            else:
                grad_q = jnp.concatenate(
                    [grad_q[:, :start], grad_q[:, start:] + part_q], axis=1
                )
        grad_q = grad_q.T * HEAD_DIM ** (-0.5)
        grad_kv = jnp.concatenate(grad_kv, axis=0)
        pair = []
        for grad_conv, mixed, taps, terms in (
            (grad_q, q_mixed, taps_q, terms_q),
            (grad_kv, kv_mixed, taps_kv, terms_kv),
        ):
            for m in range(3):
                back = mixed if m == 0 else shift_back(mixed, m)
                terms[m] = terms[m] + jnp.sum(grad_conv * back, axis=0, keepdims=True)
            pair.append(
                (
                    taps[0] * grad_conv
                    + taps[1] * shift_ahead(grad_conv, 1)
                    + taps[2] * shift_ahead(grad_conv, 2)
                ).astype(BF16)
            )
        results.append(pair)
        first += count
    table = jnp.concatenate(
        terms_q
        + [t[:, :HEAD_DIM] for t in terms_kv]
        + [t[:, HEAD_DIM:] for t in terms_kv]
        + [jnp.zeros((7, HEAD_DIM), F32)],
        axis=0,
    )
    table = jnp.concatenate([jnp.where(e == i, table, 0.0) for i in range(3)], axis=1)
    width = 3 * HEAD_DIM // 8
    for j in range(8):
        mine = [
            jnp.concatenate(
                [
                    results[0][i][j * long_rows : (j + 1) * long_rows],
                    results[1][i][j * short_rows : (j + 1) * short_rows],
                ],
                axis=0,
            )
            for i in range(2)
        ]
        send[j, :rows, :] = mine[1]
        send[j, rows : rows + rows // 2, :] = fold(mine[0])
        send[j, rows + rows // 2 :, :] = jnp.concatenate(
            [table[:, j * width : (j + 1) * width], jnp.zeros((16, LANES - width), F32)], axis=1
        ).astype(BF16)


def place_grad_mixed(came, grad_mixed):
    seqs = 2
    rows = (came.shape[1] - 16) * 2 // 3
    for e in range(3):
        for b in range(seqs):
            j = seqs * e + b
            at = slice(b * rows, (b + 1) * rows)
            lanes = slice(e * HEAD_DIM, (e + 1) * HEAD_DIM)
            grad_mixed[0, at, lanes] = unfold(came[j, rows : rows + rows // 2, :])
            grad_mixed[1, at, lanes] = came[j, :rows, :HEAD_DIM]
            grad_mixed[2, at, lanes] = came[j, :rows, HEAD_DIM:]


def project_back_body(
    place, came, normed, weight, keep_p, send_p, keep, send, taps, scratch, grad_mixed, blocks
):
    place_grad_mixed(came, grad_mixed)
    shard = normed.shape[1] // 8
    terms = [dot(normed[...], grad_mixed[c], TN).astype(BF16) for c in range(3)]
    for s in range(8):
        at = slice(s * shard, (s + 1) * shard)
        for c in range(3):
            blocks[s, c * shard : (c + 1) * shard, :] = terms[c][at, :LANES]
        blocks[s, 3 * shard :, :] = fold(
            jnp.concatenate([terms[c][at, LANES:] for c in range(3)], axis=0)
        )
    split_y(place, blocks, keep_p, send_p)
    rows = (came.shape[1] - 16) * 2 // 3
    total = came[0, rows + rows // 2 :, :].astype(F32)
    for j in range(1, 6):
        total = total + came[j, rows + rows // 2 :, :].astype(F32)
    taps[...] = total[: taps.shape[0], : taps.shape[1]]
    total = dot(grad_mixed[0], weight[0], NT)
    for c in (1, 2):
        total = total + dot(grad_mixed[c], weight[c], NT)
    scratch[...] = total.astype(BF16)
    split_halves(place, scratch, keep, send)


def input_grad_body(
    place, own, other, grad_mid, gain, long_in, short_in, long_out, short_out, scratch
):
    join_halves(place, scratch, own, other)
    seqs, long_rows, _ = long_in.shape
    rows = long_rows + short_in.shape[1]
    for b in range(seqs):
        at = slice(b * rows, (b + 1) * rows)
        values = jnp.concatenate([long_in[b], short_in[b]], axis=0).astype(F32)
        weighted = scratch[at, :] * gain[...]
        root = lax.rsqrt(jnp.mean(values * values, axis=-1, keepdims=True) + norm_eps)
        inner = jnp.mean(weighted * values, axis=-1, keepdims=True)
        grad = grad_mid[at, :] + (root * weighted - values * (root * root * root * inner))
        long_out[b] = grad[:long_rows]
        short_out[b] = grad[long_rows:]


def output_body(place, own, other, mid, long_out, short_out, scratch):
    join_halves(place, scratch, own, other)
    seqs, long_rows, _ = long_out.shape
    rows = long_rows + short_out.shape[1]
    for b in range(seqs):
        at = slice(b * rows, (b + 1) * rows)
        value = (mid[at, :] + scratch[at, :]).astype(BF16)
        long_out[b] = value[:long_rows]
        short_out[b] = value[long_rows:]


def scatter_z_body(place, *refs):
    count = (len(refs) - 4) // 2
    outs = refs[2 * count :]
    z = place[0] // 2
    for i in range(4):
        block = jnp.bitwise_xor(z, i)
        first = 0
        for a in range(count):
            keep, came = refs[2 * a], refs[2 * a + 1]
            rows = keep.shape[1]
            outs[i][first : first + rows, :] = (
                keep[block].astype(F32) + came[block].astype(F32)
            ).astype(BF16)
            first += rows


def near_body(place, *refs):
    pairs = len(refs[:-3]) // 2
    near, own, across = refs[-3:]
    z = place[0] // 2
    for i, target in ((0, own), (1, near.at[0]), (2, across), (3, near.at[1])):
        block = jnp.bitwise_xor(z, i)
        first = 0
        for p in range(pairs):
            keep, came = refs[2 * p], refs[2 * p + 1]
            rows = keep.shape[1]
            target[first : first + rows, :] = (
                keep[block].astype(F32) + came[block].astype(F32)
            ).astype(BF16)
            first += rows


def across_body(across, near, out):
    out[...] = (across[...].astype(F32) + near[1].astype(F32)).astype(BF16)


def sum_blocks(blocks):
    return (blocks[0][...].astype(F32) + blocks[1][...].astype(F32)) + (
        blocks[2][...].astype(F32) + blocks[3][...].astype(F32)
    )


def proj_grad_body(b0, b1, b2, b3, proj, gain, grad, gain_grad):
    total = sum_blocks((b0, b1, b2, b3))
    rows = proj.shape[1]
    column = 0.0
    for c, (wide, narrow) in enumerate(unpack_blocks(total, rows, 3)):
        term = jnp.concatenate([wide, narrow], axis=1)
        column = column + jnp.sum(term * proj[c].astype(F32), axis=1, keepdims=True)
        grad[c] = term
    gain_grad[...] = column.T / gain[...].astype(F32).reshape(1, rows)


def ffn_grad_body(
    own, near, across, down_keep, down_came, up, gain, up_grad, down_grad, out_grad, gain_grad
):
    rows = up.shape[0]
    total = own[...].astype(F32) + near[0].astype(F32) + across[...].astype(F32)
    raw = total[:rows]
    gain_grad[...] = jnp.sum(raw * up[...].astype(F32), axis=1, keepdims=True).T
    up_grad[...] = raw * gain[...].astype(F32).reshape(1, rows).T
    down_grad[...] = down_keep[...].astype(F32) + down_came[...].astype(F32)
    wide = total[rows : rows + 16]
    narrow = total[rows + 16 :]
    out = jnp.concatenate(
        [
            jnp.concatenate(
                [
                    wide[:, LANES * g : LANES * (g + 1)],
                    narrow[:, LANES * g : LANES * g + HEAD_DIM],
                ],
                axis=1,
            )
            for g in range(rows // 16)
        ],
        axis=0,
    )
    out_grad[...] = out.T


def pair_shards(
    short_input,
    long_input,
    short_cotangent,
    long_cotangent,
    short_lengths,
    long_lengths,
    proj_weight,
    out_weight,
    conv_taps,
    attention_gain,
    up_weight,
    down_weight,
    feed_gain,
):
    seqs, long_rows, width = long_input.shape
    short_rows = short_input.shape[1]
    rows = long_rows + short_rows
    tokens = seqs * rows
    shard = proj_weight.shape[1]
    local = proj_weight.shape[2]
    hidden = up_weight.shape[1]
    long_len, short_len = 8 * long_rows, 8 * short_rows
    total_len = long_len + short_len
    place = jnp.stack([lax.axis_index("seq"), lax.axis_index("head")]).astype(jnp.int32)
    packed_rows = shard * 9 // 2
    chunk = rows + rows // 2 + 16
    down_t = down_weight.T

    (proj_packed,) = in_vmem(
        pack_proj_body,
        [((packed_rows + 16, LANES), BF16)],
        (),
        far(proj_weight, attention_gain),
    )
    (ffn_packed,) = in_vmem(
        pack_ffn_body,
        [((2 * shard + 32, hidden), BF16)],
        (),
        far(up_weight, down_t, out_weight, feed_gain),
    )
    proj_z = [proj_packed] + [exchange(proj_packed, "seq", mask) for mask in (2, 4, 6)]
    proj_parts = [proj_packed, exchange(after(proj_packed, ffn_packed), "seq", 1)]
    proj_parts += [proj_z[1], exchange(proj_z[1], "seq", 1)]
    proj_parts += [proj_z[2], exchange(proj_z[2], "seq", 1)]
    proj_parts += [proj_z[3], exchange(proj_z[3], "seq", 1)]
    ffn_0 = after(ffn_packed, *proj_z)
    ffn_1 = exchange(ffn_0, "seq", 1)
    ffn_2 = exchange(ffn_0, "seq", 2)
    ffn_4 = exchange(ffn_0, "seq", 4)
    send, normed, proj_full, gain = in_vmem(
        project_body,
        [
            ((8, chunk, LANES), BF16),
            ((tokens, width), BF16, "far"),
            ((3, width, local), BF16, "far"),
            ((1, width), F32, "far"),
        ],
        (place,),
        (*proj_parts, *far(long_input, short_input, conv_taps)),
        scratch=[((8, LANES), F32)],
        fence=True,
    )
    came = lax.all_to_all(send, "seq", 0, 0, tiled=True)
    across_z = marker(ffn_4, ffn_1, send)
    ffn_2 = after(ffn_2, across_z)
    ffn_4 = after(ffn_4, across_z)
    ffn_6 = exchange(ffn_4, "seq", 2)
    ffn_3 = exchange(ffn_2, "seq", 1)
    ffn_5 = exchange(ffn_4, "seq", 1)
    att_send, q_all, kv_all, att_t, log_row, mixed = in_vmem(
        functools.partial(attend_body, long_rows, seqs),
        [
            ((8, rows // 2, LANES), BF16),
            ((total_len, HEAD_DIM), BF16, "far"),
            ((total_len, 2 * HEAD_DIM), BF16, "far"),
            ((HEAD_DIM, total_len), F32, "far"),
            ((1, total_len), F32, "far"),
            ((8, chunk, LANES), BF16, "far"),
        ],
        (place, long_lengths, short_lengths),
        (came,),
        fence=True,
    )
    att_0 = lax.all_to_all(att_send, "seq", 0, 0, tiled=True)
    ffn_7 = exchange(ffn_6, "seq", 1)
    up_full, down_full, out_full, out_now = in_vmem(
        place_ffn_body,
        [((width, hidden), BF16, "far")] * 2
        + [((width, local), BF16, "far"), ((width, local), BF16)],
        (place,),
        far(after(ffn_packed, att_send), ffn_1, ffn_2, ffn_3, ffn_4, ffn_5, ffn_6, ffn_7),
    )
    att_0 = after(att_0, out_full)
    att, keep, send = in_vmem(
        out_proj_body,
        [
            ((tokens, local), BF16, "far"),
            ((tokens // 2, width), BF16),
            ((tokens // 2, width), BF16),
        ],
        (place,),
        (att_0, out_now),
        scratch=[((tokens, width), BF16)],
        fence=True,
    )
    half = add_low(keep, exchange(send, "head", 1))
    own = add_low(half, exchange(half, "head", 2))
    other = exchange(own, "head", 1)
    mid, squared, grad_out, keep, send, up_keep, up_send = in_vmem(
        functools.partial(feed_body, long_rows),
        [
            ((tokens, width), F32, "far"),
            ((tokens, hidden), BF16, "far"),
            ((tokens, width), BF16, "far"),
            ((tokens // 2, width), BF16),
            ((tokens // 2, width), BF16),
            ((4, shard, hidden), BF16, "far"),
            ((4, shard, hidden), BF16, "far"),
        ],
        (place, long_lengths, short_lengths),
        (own, other)
        + far(long_input, short_input, long_cotangent, short_cotangent, up_full, down_full),
        scratch=[
            ((tokens, width), BF16),
            ((tokens, width), F32),
            ((8, shard, hidden), BF16),
            ((tokens, width), BF16),
            ((tokens, hidden), BF16),
        ],
        limit_mib=32,
    )
    half = add_low(keep, exchange(send, "head", 1))
    up_came = exchange(up_send, "seq", 1)
    down_near, down_own, down_across, f_keep, f_send = in_vmem(
        down_term_body,
        [((2, 2, shard, hidden), BF16, "far")]
        + [((2, shard, hidden), BF16, "far")] * 2
        + [((tokens // 2, width), BF16, "far")] * 2,
        (place,),
        far(after(squared, half), grad_out, down_full),
        scratch=[
            ((tokens, width), BF16),
            ((8, shard, hidden), BF16),
        ],
        fence=True,
    )
    down_near = exchange(down_near, "seq", 2)
    own = add_low(half, after(exchange(half, "head", 2), f_send))
    other = exchange(own, "head", 1)
    grad_mid, send, out_keep, out_send = in_vmem(
        middle_body,
        [
            ((tokens, width), F32, "far"),
            ((8, rows // 2, LANES), BF16),
            ((4, 32, hidden), BF16, "far"),
            ((4, 32, hidden), BF16, "far"),
        ],
        (place,),
        (own, other) + far(mid, grad_out, out_full, att),
        scratch=[((tokens, width), F32), ((tokens, width), BF16), ((8, 32, hidden), BF16)],
    )
    grad_came = lax.all_to_all(send, "seq", 0, 0, tiled=True)
    out_came = exchange(out_send, "seq", 1)
    (down_across,) = in_vmem(
        down_across_body,
        [((2, shard, hidden), BF16, "far")],
        (),
        far(after(down_across, send, up_came), down_near),
        fence=True,
    )
    grad_came = after(grad_came, down_across)
    down_across = exchange(down_across, "seq", 4)
    f_half = add_low(f_keep, exchange(after(f_send, send), "head", 1))
    f_own = add_low(f_half, exchange(f_half, "head", 2))
    f_other = exchange(f_own, "head", 1)
    long_output, short_output = in_vmem(
        output_body,
        [(long_input.shape, BF16), (short_input.shape, BF16)],
        (place,),
        (f_own, f_other) + far(mid),
        scratch=[((tokens, width), F32)],
    )
    (send,) = in_vmem(
        functools.partial(attend_back_body, long_rows, seqs),
        [((8, chunk, LANES), BF16)],
        (place, long_lengths, short_lengths),
        far(mixed, q_all, kv_all, att_t, log_row) + (grad_came,),
        fence=True,
    )
    mixed_came = lax.all_to_all(send, "seq", 0, 0, tiled=True)
    near, ffn_own, across = in_vmem(
        near_body,
        [((2, shard + 32, hidden), BF16, "far")] + [((shard + 32, hidden), BF16, "far")] * 2,
        (place,),
        far(up_keep, after(up_came, send), out_keep, out_came),
        fence=True,
    )
    near = exchange(near, "seq", 2)
    down_keep, down_send = in_vmem(
        down_y_body,
        [((shard, hidden), BF16, "far")] * 2,
        (place,),
        far(after(down_own, ffn_own), down_near, down_across),
    )
    down_came = exchange(down_send, "seq", 1)
    mixed_came = after(mixed_came, long_output, down_send)
    proj_keep, proj_send, keep, send, taps_grad = in_vmem(
        project_back_body,
        [
            ((4, packed_rows, LANES), BF16, "far"),
            ((4, packed_rows, LANES), BF16),
            ((tokens // 2, width), BF16),
            ((tokens // 2, width), BF16),
            (conv_taps.shape, F32),
        ],
        (place,),
        (mixed_came,) + far(normed, proj_full),
        scratch=[
            ((tokens, width), BF16),
            ((3, tokens, local), BF16),
            ((8, packed_rows, LANES), BF16),
        ],
        fence=True,
    )
    proj_came = exchange(proj_send, "seq", 1)
    half = add_low(keep, exchange(send, "head", 1))
    (across,) = in_vmem(
        across_body, [((shard + 32, hidden), BF16, "far")], (), far(after(across, send), near)
    )
    across = exchange(across, "seq", 4)
    own = add_low(half, after(exchange(half, "head", 2), proj_came))
    other = exchange(own, "head", 1)
    proj_blocks = in_vmem(
        scatter_z_body,
        [((packed_rows, LANES), BF16)] * 4,
        (place,),
        far(proj_keep) + (proj_came,),
        fence=True,
    )
    proj_blocks = [proj_blocks[0]] + [exchange(proj_blocks[i], "seq", 2 * i) for i in (1, 2, 3)]
    up_grad, down_grad, out_grad, feed_part = in_vmem(
        ffn_grad_body,
        [
            (up_weight.shape, F32),
            (down_t.shape, F32),
            (out_weight.shape, F32),
            ((1, shard), F32),
        ],
        (),
        far(after(ffn_own, proj_blocks[0]), near, across, down_keep, down_came, up_weight)
        + (feed_gain,),
    )
    proj_blocks[3] = after(proj_blocks[3], up_grad)
    proj_grad, attention_part = in_vmem(
        proj_grad_body,
        [(proj_weight.shape, F32), ((1, shard), F32)],
        (),
        (*proj_blocks, *far(proj_weight), attention_gain),
    )
    long_input_grad, short_input_grad = in_vmem(
        input_grad_body,
        [(long_input.shape, F32), (short_input.shape, F32)],
        (place,),
        (own, other) + far(after(grad_mid, attention_part), gain, long_input, short_input),
        scratch=[((tokens, width), F32)],
    )
    gains = jnp.concatenate([attention_part, feed_part], axis=0)
    gains = gains + exchange(gains, "head", 1)
    gains = gains + after(exchange(gains, "head", 2), long_input_grad)

    return (
        short_output,
        long_output,
        short_input_grad,
        long_input_grad,
        proj_grad,
        out_grad,
        taps_grad,
        gains[0],
        up_grad,
        down_grad.T,
        gains[1],
    )


def fits_pairs(short_input, long_input, proj_weight):
    seqs, long_rows, _ = long_input.shape
    short_seqs, short_rows, _ = short_input.shape
    return (
        lax.axis_size("seq") == 8
        and lax.axis_size("head") == 4
        and seqs == 2
        and short_seqs == 2
        and proj_weight.shape[2] == 3 * HEAD_DIM
        and proj_weight.shape[1] % 32 == 0
        and long_rows % 32 == 0
        and short_rows % 32 == 0
        and 8 * long_rows <= 2048
    )


def shards(short_input, long_input, *rest):
    proj_weight = rest[4]
    if fits_pairs(short_input, long_input, proj_weight):
        return pair_shards(short_input, long_input, *rest)
    return ring_shards(short_input, long_input, *rest)


def solution(mesh):
    placed = (
        P(None, "seq", None),
        P(None, "seq", None),
        P(None, "seq", None),
        P(None, "seq", None),
        P(),
        P(),
        P(None, "seq", "head"),
        P("head", "seq"),
        P(None, ("head", "seq")),
        P("seq"),
        P("seq", "head"),
        P("head", "seq"),
        P("seq"),
    )
    return jax.shard_map(
        shards,
        mesh=mesh,
        in_specs=placed,
        out_specs=(
            P(None, "seq", None),
            P(None, "seq", None),
            P(None, "seq", None),
            P(None, "seq", None),
            P(None, "seq", "head"),
            P("head", "seq"),
            P(None, ("head", "seq")),
            P("seq"),
            P("seq", "head"),
            P("head", "seq"),
            P("seq"),
        ),
        check_vma=False,
    )
```

```python
import functools

import jax
import jax.numpy as jnp
import numpy as np
from jax import lax
from jax.experimental import pallas as pl
from jax.experimental.pallas import tpu as pltpu
from jax.sharding import PartitionSpec as P

HEAD_DIM = 64


norm_eps = 1e-06
mask_fill = -1e30
block_limit = 2048


def passed_along(block, axis, distance):
    devices = range(lax.axis_size(axis))
    route = [((i - distance) % len(devices), i) for i in devices]
    return lax.ppermute(block, axis, route)


def shifted(array, axis, by):
    peers = lax.axis_size(axis)
    pairs = [(i, i + by) for i in range(peers) if 0 <= i + by < peers]
    return lax.ppermute(array, axis, pairs)


def block_rows(row_count):
    size_rows = min(row_count, block_limit)
    while row_count % size_rows != 0:
        size_rows = size_rows - 1
    return size_rows


def norm_forward(values_in, gain_row):
    inv_root = lax.rsqrt(jnp.mean(values_in * values_in, axis=-1, keepdims=True) + norm_eps)
    return (values_in * inv_root * gain_row, inv_root)


def norm_backward(values_in, inv_root, gain_row, grad_in):
    weighted = grad_in * gain_row
    inner_mean = jnp.mean(weighted * values_in, axis=-1, keepdims=True)
    grad_values = inv_root * weighted - values_in * inv_root * inv_root * inv_root * inner_mean
    grad_gain = jnp.sum(grad_in * values_in * inv_root, axis=(0, 1))
    return (grad_values, grad_gain)


def allowed_mask(query_pos, key_pos, lengths):
    causal = key_pos[None, :] <= query_pos[:, None]
    inside = key_pos[None, :] < lengths[:, None]
    return jnp.logical_and(causal[None, None], inside[:, None, None, :])


def block_scores(query_rows, key_rows, query_pos, key_pos, lengths):
    allowed = allowed_mask(query_pos, key_pos, lengths)
    raw_scores = jnp.einsum(
        "bqhe,bkhe->bhqk", query_rows, key_rows, preferred_element_type=jnp.float32
    ) * HEAD_DIM ** (-0.5)
    return (jnp.where(allowed, raw_scores, mask_fill), allowed)


def block_grads(
    query_rows, grad_rows, log_rows, delta_rows, key_rows, value_rows, query_pos, key_pos, lengths
):
    scores, allowed = block_scores(query_rows, key_rows, query_pos, key_pos, lengths)
    prob_rows = jnp.where(
        allowed, jnp.exp(scores - jnp.transpose(log_rows, (0, 2, 1))[..., None]), 0.0
    )
    grad_probs = jnp.einsum(
        "bqhe,bkhe->bhqk", grad_rows, value_rows, preferred_element_type=jnp.float32
    )
    grad_scores = (
        prob_rows * (grad_probs - jnp.transpose(delta_rows, (0, 2, 1))[..., None])
    ).astype(jnp.bfloat16)
    grad_query = jnp.einsum(
        "bhqk,bkhe->bqhe", grad_scores, key_rows, preferred_element_type=jnp.float32
    ) * HEAD_DIM ** (-0.5)
    grad_key = jnp.einsum(
        "bhqk,bqhe->bkhe", grad_scores, query_rows, preferred_element_type=jnp.float32
    ) * HEAD_DIM ** (-0.5)
    grad_value = jnp.einsum(
        "bhqk,bqhe->bkhe",
        prob_rows.astype(jnp.bfloat16),
        grad_rows,
        preferred_element_type=jnp.float32,
    )
    return (grad_query, grad_key, grad_value)


def attend_forward(queries, keys_here, values_here, query_pos, lengths):
    seq_count, span_rows, head_count, head_width = queries.shape
    initial = (
        jnp.full((seq_count, head_count, span_rows), mask_fill, jnp.float32),
        jnp.zeros((seq_count, head_count, span_rows), jnp.float32),
        jnp.zeros((seq_count, span_rows, head_count, head_width), jnp.float32),
    )
    key_piece = lax.all_gather(keys_here, "seq", axis=1, tiled=True)
    value_piece = lax.all_gather(values_here, "seq", axis=1, tiled=True)
    row_count = key_piece.shape[1]
    size_rows = block_rows(row_count)

    def one_block(block_index, carried_state):
        running_top, running_sum, acc_rows = carried_state
        offset = block_index * size_rows
        key_rows = lax.dynamic_slice_in_dim(key_piece, offset, size_rows, 1)
        value_rows = lax.dynamic_slice_in_dim(value_piece, offset, size_rows, 1)
        key_pos = offset + jnp.arange(size_rows, dtype=jnp.int32)
        scores, allowed = block_scores(queries, key_rows, query_pos, key_pos, lengths)
        new_top = jnp.maximum(running_top, jnp.max(scores, axis=-1))
        exp_terms = jnp.where(allowed, jnp.exp(scores - new_top[..., None]), 0.0)
        shrink = jnp.exp(running_top - new_top)
        running_sum = running_sum * shrink + jnp.sum(exp_terms, axis=-1)
        acc_rows = acc_rows * jnp.transpose(shrink, (0, 2, 1))[..., None] + jnp.einsum(
            "bhqk,bkhe->bqhe",
            exp_terms.astype(jnp.bfloat16),
            value_rows,
            preferred_element_type=jnp.float32,
        )
        return (new_top, running_sum, acc_rows)

    running_top, running_sum, acc_rows = lax.fori_loop(
        0, row_count // size_rows, one_block, initial
    )
    attention = acc_rows / jnp.transpose(running_sum, (0, 2, 1))[..., None]
    log_totals = jnp.transpose(running_top + jnp.log(running_sum), (0, 2, 1))
    return (attention, log_totals)


def pass_sums(grad_keys, grad_values):
    return (
        passed_along(grad_keys.astype(jnp.bfloat16), "seq", 1).astype(grad_keys.dtype),
        passed_along(grad_values.astype(jnp.bfloat16), "seq", 1).astype(grad_values.dtype),
    )


def attend_backward(
    queries, keys_here, values_here, grad_attention, log_totals, delta_rows, query_pos, lengths
):
    seq_count, span_rows, head_count, head_width = queries.shape
    zeros_local = jnp.zeros(queries.shape, jnp.float32)
    seq_size = lax.axis_size("seq")
    my_index = lax.axis_index("seq")
    local_pos = jnp.arange(span_rows, dtype=jnp.int32)

    def step_grads(step, key_piece, value_piece):
        anchor = jnp.mod(my_index - step, seq_size)
        key_pos = anchor * span_rows + local_pos
        return block_grads(
            queries,
            grad_attention,
            log_totals,
            delta_rows,
            key_piece,
            value_piece,
            query_pos,
            key_pos,
            lengths,
        )

    def cycle_step(step, state):
        key_piece, value_piece, grad_keys, grad_values, grad_query = state
        query_part, key_part, value_part = step_grads(step, key_piece, value_piece)
        key_piece, value_piece = shifted((key_piece, value_piece), "seq", 1)
        grad_keys, grad_values = pass_sums(grad_keys + key_part, grad_values + value_part)
        return (key_piece, value_piece, grad_keys, grad_values, grad_query + query_part)

    final_state = lax.fori_loop(
        0, seq_size - 1, cycle_step, (keys_here, values_here, zeros_local, zeros_local, zeros_local)
    )
    key_piece, value_piece, grad_keys, grad_values, grad_query = final_state
    query_part, key_part, value_part = step_grads(seq_size - 1, key_piece, value_piece)
    grad_key, grad_value = pass_sums(grad_keys + key_part, grad_values + value_part)
    grad_query = grad_query + query_part
    return (grad_query, grad_key, grad_value)


def micro_batch(inputs, cotangent, lengths, weights):
    proj_full, out_full, taps_full, attend_gain, up_full, down_full, ffn_gain = weights
    seq_count, span_rows, model_width = inputs.shape
    local_width = proj_full.shape[2]
    heads_here = local_width // HEAD_DIM
    query_pos = lax.axis_index("seq") * span_rows + jnp.arange(span_rows, dtype=jnp.int32)
    valid_rows = (query_pos[None, :] < lengths[:, None])[..., None]
    residual_in = inputs.astype(jnp.float32)
    normed, inv_first = norm_forward(residual_in, attend_gain)
    normed_low = normed.astype(jnp.bfloat16)
    mixed_qkv = jnp.einsum(
        "btd,cde->cbte", normed_low, proj_full, preferred_element_type=jnp.float32
    ).astype(jnp.bfloat16)
    borrowed = shifted(mixed_qkv[:, :, span_rows - 2 :, :], "seq", 1)
    extended = jnp.concatenate([borrowed, mixed_qkv], axis=2).astype(jnp.float32)
    tap_table = taps_full.astype(jnp.float32).reshape(3, 3, local_width)
    tap_now = tap_table[:, 0][:, None, None, :]
    tap_one = tap_table[:, 1][:, None, None, :]
    tap_two = tap_table[:, 2][:, None, None, :]
    conved = (
        tap_now * extended[:, :, 2:]
        + tap_one * extended[:, :, 1:-1]
        + tap_two * extended[:, :, :-2]
    )
    conv_out = conved.astype(jnp.bfloat16).reshape(3, seq_count, span_rows, heads_here, HEAD_DIM)
    queries, keys_here, values_here = (conv_out[0], conv_out[1], conv_out[2])
    attention, log_totals = attend_forward(queries, keys_here, values_here, query_pos, lengths)
    attention_low = attention.astype(jnp.bfloat16).reshape(seq_count, span_rows, local_width)
    attend_part = jnp.einsum(
        "bte,ed->btd", attention_low, out_full, preferred_element_type=jnp.float32
    )
    mid_residual = residual_in + lax.psum(attend_part.astype(jnp.bfloat16), "head").astype(
        jnp.float32
    )
    normed_ffn, inv_second = norm_forward(mid_residual, ffn_gain)
    normed_ffn_low = normed_ffn.astype(jnp.bfloat16)
    up_proj = jnp.einsum("btd,df->btf", normed_ffn_low, up_full, preferred_element_type=jnp.float32)
    relu_up = jnp.maximum(up_proj, 0.0)
    squared = (relu_up * relu_up).astype(jnp.bfloat16)
    ffn_part = jnp.einsum("btf,fd->btd", squared, down_full, preferred_element_type=jnp.float32)
    output = (
        mid_residual + lax.psum(ffn_part.astype(jnp.bfloat16), "head").astype(jnp.float32)
    ).astype(jnp.bfloat16)
    grad_out = jnp.where(valid_rows, cotangent.astype(jnp.float32), 0.0)
    grad_out_low = grad_out.astype(jnp.bfloat16)
    down_term = jnp.einsum("btf,btd->fd", squared, grad_out_low, preferred_element_type=jnp.float32)
    grad_squared = jnp.einsum(
        "btd,fd->btf", grad_out_low, down_full, preferred_element_type=jnp.float32
    )
    grad_up = (grad_squared * 2.0 * relu_up).astype(jnp.bfloat16)
    up_term = jnp.einsum("btd,btf->df", normed_ffn_low, grad_up, preferred_element_type=jnp.float32)
    grad_normed_ffn = lax.psum(
        jnp.einsum("btf,df->btd", grad_up, up_full, preferred_element_type=jnp.float32).astype(
            jnp.bfloat16
        ),
        "head",
    ).astype(jnp.float32)
    grad_through, feed_term = norm_backward(mid_residual, inv_second, ffn_gain, grad_normed_ffn)
    grad_mid = grad_out + grad_through
    grad_mid_low = grad_mid.astype(jnp.bfloat16)
    out_term = jnp.einsum(
        "bte,btd->ed", attention_low, grad_mid_low, preferred_element_type=jnp.float32
    )
    grad_attention = jnp.einsum(
        "btd,ed->bte", grad_mid_low, out_full, preferred_element_type=jnp.float32
    )
    grad_attention = grad_attention.astype(jnp.bfloat16).reshape(
        seq_count, span_rows, heads_here, HEAD_DIM
    )
    delta_rows = jnp.einsum("bqhe,bqhe->bqh", grad_attention.astype(jnp.float32), attention)
    grad_query, grad_key, grad_value = attend_backward(
        queries, keys_here, values_here, grad_attention, log_totals, delta_rows, query_pos, lengths
    )
    grad_conv = jnp.stack([grad_query, grad_key, grad_value]).reshape(
        3, seq_count, span_rows, local_width
    )
    taps_term = jnp.stack(
        [
            jnp.sum(grad_conv * extended[:, :, 2:], axis=(1, 2)),
            jnp.sum(grad_conv * extended[:, :, 1:-1], axis=(1, 2)),
            jnp.sum(grad_conv * extended[:, :, :-2], axis=(1, 2)),
        ],
        axis=1,
    ).reshape(9, local_width)
    full_grad = jnp.pad(grad_conv, ((0, 0), (0, 0), (2, 2), (0, 0)))
    grad_extended = (
        tap_now * full_grad[:, :, 0 : span_rows + 2]
        + tap_one * full_grad[:, :, 1 : span_rows + 3]
        + tap_two * full_grad[:, :, 2 : span_rows + 4]
    )
    returned = shifted(grad_extended[:, :, :2], "seq", -1)
    grad_mixed = jnp.concatenate(
        [grad_extended[:, :, 2:span_rows], grad_extended[:, :, span_rows:] + returned], axis=2
    ).astype(jnp.bfloat16)
    proj_term = jnp.einsum(
        "btd,cbte->cde", normed_low, grad_mixed, preferred_element_type=jnp.float32
    )
    grad_normed = lax.psum(
        jnp.einsum(
            "cbte,cde->btd", grad_mixed, proj_full, preferred_element_type=jnp.float32
        ).astype(jnp.bfloat16),
        "head",
    ).astype(jnp.float32)
    grad_first, attention_term = norm_backward(residual_in, inv_first, attend_gain, grad_normed)
    grad_input = grad_mid + grad_first
    return (
        output,
        grad_input,
        (proj_term, out_term, taps_term, attention_term, up_term, down_term, feed_term),
    )


def ring_shards(
    short_input,
    long_input,
    short_cotangent,
    long_cotangent,
    short_lengths,
    long_lengths,
    proj_weight,
    out_weight,
    conv_taps,
    attention_gain,
    up_weight,
    down_weight,
    feed_gain,
):
    proj_full, out_full, taps_full, attend_gain = (
        lax.all_gather(proj_weight, "seq", axis=1, tiled=True),
        lax.all_gather(out_weight, "seq", axis=1, tiled=True),
        lax.all_gather(conv_taps, "seq", axis=1, tiled=True),
        lax.all_gather(attention_gain, "seq", axis=0, tiled=True),
    )
    up_full, down_full, ffn_gain = (
        lax.all_gather(up_weight, "seq", axis=0, tiled=True),
        lax.all_gather(down_weight, "seq", axis=1, tiled=True),
        lax.all_gather(feed_gain, "seq", axis=0, tiled=True),
    )
    weights = (
        proj_full,
        out_full,
        taps_full,
        attend_gain.astype(jnp.float32),
        up_full,
        down_full,
        ffn_gain.astype(jnp.float32),
    )
    short_output, short_input_grad, short_terms = micro_batch(
        short_input, short_cotangent, short_lengths, weights
    )
    long_output, long_input_grad, long_terms = micro_batch(
        long_input, long_cotangent, long_lengths, weights
    )
    summed = tuple(
        (first_term + second_term for first_term, second_term in zip(short_terms, long_terms))
    )
    reduced = (
        lax.psum_scatter(summed[0], "seq", scatter_dimension=1, tiled=True),
        lax.psum_scatter(summed[1], "seq", scatter_dimension=1, tiled=True),
        lax.psum_scatter(summed[2], "seq", scatter_dimension=1, tiled=True),
        lax.psum_scatter(summed[3], "seq", scatter_dimension=0, tiled=True),
        lax.psum_scatter(summed[4], "seq", scatter_dimension=0, tiled=True),
        lax.psum_scatter(summed[5], "seq", scatter_dimension=1, tiled=True),
        lax.psum_scatter(summed[6], "seq", scatter_dimension=0, tiled=True),
    )
    return (
        short_output,
        long_output,
        short_input_grad,
        long_input_grad,
        reduced[0],
        reduced[1],
        reduced[2],
        reduced[3],
        reduced[4],
        reduced[5],
        reduced[6],
    )


LANES = 128
FENCE = 10**11
NT = (((1,), (1,)), ((), ()))
TN = (((0,), (0,)), ((), ()))
F32 = jnp.float32
BF16 = jnp.bfloat16


def dot(a, b, dims=(((1,), (0,)), ((), ()))):
    return lax.dot_general(a, b, dims, preferred_element_type=F32)


def in_vmem(body, outs, scalars, arrays, scratch=(), limit_mib=16, fence=False):
    return pl.pallas_call(
        body,
        out_shape=[
            pltpu.HBM(*out[:2]) if len(out) == 3 else jax.ShapeDtypeStruct(*out) for out in outs
        ],
        in_specs=[pl.BlockSpec(memory_space=pltpu.SMEM)] * len(scalars)
        + [pl.BlockSpec(memory_space=pltpu.VMEM)] * len(arrays),
        out_specs=[pl.BlockSpec(memory_space=pltpu.VMEM)] * len(outs),
        scratch_shapes=[pltpu.VMEM(shape, kind) for shape, kind in scratch],
        compiler_params=pltpu.CompilerParams(vmem_limit_bytes=limit_mib * 1024 * 1024),
        cost_estimate=pl.CostEstimate(
            flops=FENCE if fence else 0, bytes_accessed=0, transcendentals=0
        ),
    )(*scalars, *arrays)


def far(*arrays):
    return tuple(pltpu.with_memory_space_constraint(array, pltpu.HBM) for array in arrays)


def after(array, *others):
    return lax.optimization_barrier((array, *others))[0]


def marker(*arrays):
    def body(*refs):
        refs[-1][...] = jnp.zeros_like(refs[-1])

    return pl.pallas_call(
        body,
        out_shape=jax.ShapeDtypeStruct((8, LANES), F32),
        in_specs=[pl.BlockSpec(memory_space=pl.ANY)] * len(arrays),
        out_specs=pl.BlockSpec(memory_space=pltpu.VMEM),
        cost_estimate=pl.CostEstimate(flops=FENCE, bytes_accessed=0, transcendentals=0),
    )(*arrays)


def exchange(array, axis, mask):
    size = lax.axis_size(axis)
    return lax.ppermute(array, axis, [(i, i ^ mask) for i in range(size)])


def add_low(a, b):
    return (a.astype(F32) + b.astype(F32)).astype(BF16)


def shift_back(rows, by):
    index = lax.broadcasted_iota(jnp.int32, rows.shape, 0)
    return jnp.where(index >= by, pltpu.roll(rows, by, axis=0), 0.0)


def shift_ahead(rows, by):
    count = rows.shape[0]
    index = lax.broadcasted_iota(jnp.int32, rows.shape, 0)
    return jnp.where(index < count - by, pltpu.roll(rows, count - by, axis=0), 0.0)


def fold(rows):
    half = rows.shape[0] // 2
    return jnp.concatenate([rows[:half], rows[half:]], axis=1)


def unfold(rows):
    return jnp.concatenate([rows[:, :HEAD_DIM], rows[:, HEAD_DIM:]], axis=0)


def pack_proj_body(proj, gain, packed):
    rows = proj.shape[1]
    for c in range(3):
        packed[c * rows : (c + 1) * rows, :] = proj[c, :, :LANES]
    narrow = jnp.concatenate([proj[c, :, LANES:] for c in range(3)], axis=0)
    packed[3 * rows : 9 * rows // 2, :] = fold(narrow)
    gain_row = gain[...].astype(F32).reshape(1, rows)
    gain_row = jnp.concatenate([gain_row, jnp.zeros((1, LANES - rows), F32)], axis=1)
    packed[9 * rows // 2 :, :] = jnp.broadcast_to(gain_row, (16, LANES)).astype(BF16)


def unpack_blocks(packed, rows, count):
    narrow = unfold(packed[count * rows : 3 * count * rows // 2, :])
    return [
        (packed[i * rows : (i + 1) * rows, :], narrow[i * rows : (i + 1) * rows, :])
        for i in range(count)
    ]


def narrow_pack(block, store):
    groups = block.shape[0] // 16
    for g in range(groups):
        rows = block[16 * g : 16 * g + 16, :]
        store(0, LANES * g, rows[:, :LANES])
        tail = rows[:, LANES:]
        store(16, LANES * g, jnp.concatenate([tail, jnp.zeros_like(tail)], axis=1))


def pack_ffn_body(up, down, out, gain, packed):
    rows = up.shape[0]
    gain_column = gain[...].astype(F32).reshape(1, rows).T
    packed[:rows, :] = (up[...].astype(F32) * gain_column).astype(BF16)
    packed[rows : 2 * rows, :] = down[...]

    def store(row, lane, value):
        packed[2 * rows + row : 2 * rows + row + 16, lane : lane + LANES] = value

    narrow_pack(out[...].astype(F32).T.astype(BF16), store)


def place_ffn_body(place, *refs):
    up, down, out, out_now = refs[8:]
    rows = out.shape[0] // 8
    for i in range(8):
        owner = jnp.bitwise_xor(place[0], i)
        part = refs[i]
        first = pl.ds(pl.multiple_of(owner * rows, rows), rows)
        up[first, :] = part[:rows, :]
        down[first, :] = part[rows : 2 * rows, :]
        for g in range(rows // 16):
            at = pl.ds(pl.multiple_of(owner * rows + 16 * g, 16), 16)
            out[at, :LANES] = part[2 * rows : 2 * rows + 16, LANES * g : LANES * g + LANES]
            out[at, LANES:] = part[2 * rows + 16 :, LANES * g : LANES * g + HEAD_DIM]
    out_now[...] = out[...]


def project_body(place, *refs):
    parts = refs[:8]
    long_in, short_in, taps, send, normed, weight, gain, gain_rows = refs[8:]
    seqs, long_rows, _ = long_in.shape
    rows = long_rows + short_in.shape[1]
    for i in range(8):
        packed = parts[i][...]
        shard = weight.shape[1] // 8
        owner = jnp.bitwise_xor(place[0], i)
        gain_rows[pl.ds(owner, 1), :] = packed[9 * shard // 2 :, :].astype(F32)[:1]
        at = pl.ds(pl.multiple_of(owner * shard, shard), shard)
        for c, (wide, narrow) in enumerate(unpack_blocks(packed, shard, 3)):
            weight[c, at, :LANES] = wide
            weight[c, at, LANES:] = narrow
    gain[...] = jnp.concatenate([gain_rows[j : j + 1, :shard] for j in range(8)], axis=1)
    for b in range(seqs):
        values = jnp.concatenate([long_in[b], short_in[b]], axis=0).astype(F32)
        root = lax.rsqrt(jnp.mean(values * values, axis=-1, keepdims=True) + norm_eps)
        normed[b * rows : (b + 1) * rows, :] = (values * root * gain[...]).astype(BF16)
    mixed = [dot(normed[...], weight[c]).astype(BF16) for c in range(3)]
    tap_rows = jnp.concatenate(
        [taps[...], jnp.zeros((16 - taps.shape[0], taps.shape[1]), BF16)], axis=0
    )
    tap_rows = jnp.concatenate(
        [tap_rows, jnp.zeros((16, LANES - taps.shape[1]), BF16)], axis=1
    )
    half = rows // 2
    for dest in range(8):
        if dest < 3 * seqs:
            e, b = dest // seqs, dest % seqs
            lanes = slice(e * HEAD_DIM, (e + 1) * HEAD_DIM)
            q, k, v = [m[b * rows : (b + 1) * rows, lanes] for m in mixed]
            send[dest, :rows, :] = jnp.concatenate([k, v], axis=1)
            send[dest, rows : rows + half, :] = fold(q)
        else:
            send[dest, : rows + half, :] = jnp.zeros((rows + half, LANES), BF16)
        send[dest, rows + half :, :] = tap_rows


def head_taps(place, came, rows, seqs):
    first = rows + rows // 2
    width = 3 * HEAD_DIM // 8
    whole = jnp.concatenate(
        [came[j, first:, :].astype(F32)[:, :width] for j in range(8)], axis=1
    )
    e = place[0] // seqs
    mine = whole[:, :HEAD_DIM]
    for other in (1, 2):
        mine = jnp.where(
            e == other, whole[:, other * HEAD_DIM : (other + 1) * HEAD_DIM], mine
        )
    taps_q = [mine[m : m + 1, :] for m in range(3)]
    taps_kv = [
        jnp.concatenate([mine[3 + m : 4 + m, :], mine[6 + m : 7 + m, :]], axis=1) for m in range(3)
    ]
    return taps_q, taps_kv


def own_pair(came, long_rows, rows):
    q_rows = [unfold(came[j, rows : rows + rows // 2, :]) for j in range(8)]
    result = []
    for part in (slice(0, long_rows), slice(long_rows, rows)):
        q = jnp.concatenate([piece[part] for piece in q_rows], axis=0).astype(F32)
        kv = jnp.concatenate([came[j, part, :] for j in range(8)], axis=0).astype(F32)
        result.append((q, kv))
    return result


def convolve(rows, taps):
    return taps[0] * rows + taps[1] * shift_back(rows, 1) + taps[2] * shift_back(rows, 2)


def attend_body(
    long_rows, seqs, place, long_lengths, short_lengths, came, send, q_all, kv_all, att_t, log_row, kept
):
    rows = (came.shape[1] - 16) * 2 // 3
    kept[...] = came[...]
    taps_q, taps_kv = head_taps(place, came, rows, seqs)
    b = place[0] % seqs
    first = 0
    results = []
    for lengths, (q_mixed, kv_mixed) in zip(
        (long_lengths, short_lengths), own_pair(came, long_rows, rows)
    ):
        count = q_mixed.shape[0]
        block = min(256, count)
        length = lengths[b]
        q = (convolve(q_mixed, taps_q).astype(BF16).astype(F32) * HEAD_DIM ** (-0.5)).astype(BF16)
        kv = convolve(kv_mixed, taps_kv).astype(BF16)
        kv_t = kv.astype(F32).T.astype(BF16)
        q_all[first : first + count, :] = q
        kv_all[first : first + count, :] = kv
        k = kv[:, :HEAD_DIM]
        v_t = kv_t[HEAD_DIM:, :]
        pieces = []
        for start in range(0, count, block):
            stop = start + block
            scores = dot(k[:stop], q[start:stop], NT)
            key_pos = lax.broadcasted_iota(jnp.int32, scores.shape, 0)
            query_pos = lax.broadcasted_iota(jnp.int32, scores.shape, 1) + start
            allowed = jnp.logical_and(key_pos <= query_pos, key_pos < length)
            scores = jnp.where(allowed, scores, mask_fill)
            top = jnp.max(scores, axis=0, keepdims=True)
            terms = jnp.exp(scores - top)
            total = jnp.sum(terms, axis=0, keepdims=True)
            out_t = dot(v_t[:, :stop], terms.astype(BF16)) / total
            att_t[:, first + start : first + stop] = out_t
            log_row[:, first + start : first + stop] = top + jnp.log(total)
            pieces.append(out_t.T.astype(BF16))
        results.append(jnp.concatenate(pieces, axis=0))
        first += count
    short_rows = rows - long_rows
    for j in range(8):
        mine = jnp.concatenate(
            [
                results[0][j * long_rows : (j + 1) * long_rows],
                results[1][j * short_rows : (j + 1) * short_rows],
            ],
            axis=0,
        )
        send[j, :, :] = fold(mine)


def pair_rows(came, seqs):
    columns = []
    for e in range(3):
        columns.append(
            jnp.concatenate([unfold(came[seqs * e + b]) for b in range(seqs)], axis=0)
        )
    return jnp.concatenate(columns, axis=1)


def out_proj_body(place, came, out, att, keep, send, scratch):
    att[...] = pair_rows(came, 2)
    scratch[...] = dot(att[...], out[...], NT).astype(BF16)
    split_halves(place, scratch, keep, send)


def feed_body(
    long_rows,
    place,
    long_lengths,
    short_lengths,
    own,
    other,
    long_in,
    short_in,
    long_cot,
    short_cot,
    up,
    down,
    mid_ref,
    squared_ref,
    grad_out_ref,
    keep,
    send,
    normed_ref,
    grad_up_ref,
    scratch,
    attended,
):
    seqs = long_in.shape[0]
    rows = long_rows + short_in.shape[1]
    join_halves(place, attended, own, other)
    for b in range(seqs):
        at = slice(b * rows, (b + 1) * rows)
        residual = jnp.concatenate([long_in[b], short_in[b]], axis=0).astype(F32)
        mid = residual + attended[at, :]
        mid_ref[at, :] = mid
        root = lax.rsqrt(jnp.mean(mid * mid, axis=-1, keepdims=True) + norm_eps)
        normed_ref[at, :] = (mid * root).astype(BF16)
        for cot, lengths, first, count in (
            (long_cot, long_lengths, b * rows, long_rows),
            (short_cot, short_lengths, b * rows + long_rows, rows - long_rows),
        ):
            value = cot[b]
            position = lax.broadcasted_iota(jnp.int32, value.shape, 0) + place[0] * count
            grad_out_ref[first : first + count, :] = jnp.where(
                position < lengths[b], value.astype(F32), 0.0
            ).astype(BF16)
    relu = jnp.maximum(dot(normed_ref[...], up[...]), 0.0)
    squared_ref[...] = (relu * relu).astype(BF16)
    grad_squared = dot(grad_out_ref[...], down[...])
    grad_up_ref[...] = (grad_squared * 2.0 * relu).astype(BF16)
    scratch[...] = dot(grad_up_ref[...], up[...], NT).astype(BF16)
    split_halves(place, scratch, keep, send)


def split_halves(place, whole, keep, send):
    half = whole.shape[0] // 2
    core = place[1] % 2
    keep[...] = whole[pl.ds(pl.multiple_of(core * half, half), half), :]
    send[...] = whole[pl.ds(pl.multiple_of((1 - core) * half, half), half), :]


def join_halves(place, whole, own, other):
    half = own.shape[0]
    core = place[1] % 2
    whole[pl.ds(pl.multiple_of(core * half, half), half), :] = own[...].astype(whole.dtype)
    whole[pl.ds(pl.multiple_of((1 - core) * half, half), half), :] = other[...].astype(whole.dtype)


def split_y(place, blocks, keep, send):
    y = place[0] % 2
    for z in range(4):
        keep[z] = blocks[2 * z + y]
        send[z] = blocks[2 * z + 1 - y]


def down_term_body(
    place,
    squared,
    grad_out,
    down,
    normed,
    grad_up,
    near,
    own,
    across,
    f_keep,
    f_send,
    up_keep,
    up_send,
    scratch,
    blocks,
):
    rows = blocks.shape[1]
    term = dot(normed[...], grad_up[...], TN).astype(BF16)
    for s in range(8):
        blocks[s] = term[s * rows : (s + 1) * rows]
    split_y(place, blocks, up_keep, up_send)
    term = dot(grad_out[...], squared[...], TN).astype(BF16)
    for s in range(8):
        blocks[s] = term[s * rows : (s + 1) * rows]
    z = place[0] // 2
    for i, target in ((0, own), (1, near.at[0]), (2, across), (3, near.at[1])):
        for y in range(2):
            target[y] = blocks[2 * jnp.bitwise_xor(z, i) + y]
    scratch[...] = dot(squared[...], down[...], NT).astype(BF16)
    split_halves(place, scratch, f_keep, f_send)


def down_across_body(across, near, out):
    out[...] = (across[...].astype(F32) + near[1].astype(F32)).astype(BF16)


def down_y_body(place, own, near, across, keep, send):
    y = place[0] % 2
    for target, block in ((keep, y), (send, 1 - y)):
        target[...] = (
            own[block].astype(F32) + near[0, block].astype(F32) + across[block].astype(F32)
        ).astype(BF16)


def middle_body(
    place, own, other, mid_ref, grad_out, out, att, grad_mid_ref, send, keep_out, send_out, scratch, low_ref, blocks
):
    join_halves(place, scratch, own, other)
    seqs = 2
    rows = mid_ref.shape[0] // seqs
    for b in range(seqs):
        at = slice(b * rows, (b + 1) * rows)
        mid = mid_ref[at, :]
        weighted = scratch[at, :]
        root = lax.rsqrt(jnp.mean(mid * mid, axis=-1, keepdims=True) + norm_eps)
        inner = jnp.mean(weighted * mid, axis=-1, keepdims=True)
        grad_mid = grad_out[at, :].astype(F32) + (
            root * weighted - mid * (root * root * root * inner)
        )
        grad_mid_ref[at, :] = grad_mid
        low_ref[at, :] = grad_mid.astype(BF16)
    grad_att = dot(low_ref[...], out[...]).astype(BF16)
    for dest in range(8):
        if dest < 3 * seqs:
            e, b = dest // seqs, dest % seqs
            send[dest] = fold(
                grad_att[b * rows : (b + 1) * rows, e * HEAD_DIM : (e + 1) * HEAD_DIM]
            )
        else:
            send[dest] = jnp.zeros_like(send[dest])
    term = dot(low_ref[...], att[...], TN).astype(BF16)
    shard = term.shape[0] // 8
    for s in range(8):

        def store(row, lane, value):
            blocks[s, row : row + 16, lane : lane + LANES] = value

        narrow_pack(term[s * shard : (s + 1) * shard], store)
    split_y(place, blocks, keep_out, send_out)


def attend_back_body(
    long_rows,
    seqs,
    place,
    long_lengths,
    short_lengths,
    came,
    q_all,
    kv_all,
    att_t,
    log_row,
    grad_came,
    send,
):
    rows = (came.shape[1] - 16) * 2 // 3
    short_rows = rows - long_rows
    taps_q, taps_kv = head_taps(place, came, rows, seqs)
    b = place[0] % seqs
    e = place[0] // seqs
    grads = [unfold(grad_came[j]) for j in range(8)]
    first = 0
    terms_q = [0.0, 0.0, 0.0]
    terms_kv = [0.0, 0.0, 0.0]
    results = []
    for lengths, part, (q_mixed, kv_mixed) in zip(
        (long_lengths, short_lengths),
        (slice(0, long_rows), slice(long_rows, rows)),
        own_pair(came, long_rows, rows),
    ):
        count = q_mixed.shape[0]
        block = min(256, count)
        length = lengths[b]
        at = slice(first, first + count)
        grad = jnp.concatenate([g[part] for g in grads], axis=0)
        q = q_all[at, :]
        kv = kv_all[at, :]
        kv_t = kv.astype(F32).T.astype(BF16)
        delta = jnp.sum(grad.astype(F32).T * att_t[:, at], axis=0, keepdims=True)
        log_total = log_row[:, at]
        k, v = kv[:, :HEAD_DIM], kv[:, HEAD_DIM:]
        k_t = kv_t[:HEAD_DIM, :]
        grad_q = None
        grad_kv = []
        for start in range(0, count, block):
            stop = start + block
            scores = dot(k[start:stop], q[start:], NT)
            key_pos = lax.broadcasted_iota(jnp.int32, scores.shape, 0)
            query_pos = lax.broadcasted_iota(jnp.int32, scores.shape, 1)
            allowed = jnp.logical_and(key_pos <= query_pos, key_pos + start < length)
            prob = jnp.where(allowed, jnp.exp(scores - log_total[:, start:]), 0.0)
            grad_prob = dot(v[start:stop], grad[start:], NT)
            grad_scores = (prob * (grad_prob - delta[:, start:])).astype(BF16)
            grad_k = dot(grad_scores, q[start:])
            grad_v = dot(prob.astype(BF16), grad[start:])
            grad_kv.append(jnp.concatenate([grad_k, grad_v], axis=1))
            part_q = dot(k_t[:, start:stop], grad_scores)
            if start == 0:
                grad_q = part_q
            else:
                grad_q = jnp.concatenate(
                    [grad_q[:, :start], grad_q[:, start:] + part_q], axis=1
                )
        grad_q = grad_q.T * HEAD_DIM ** (-0.5)
        grad_kv = jnp.concatenate(grad_kv, axis=0)
        pair = []
        for grad_conv, mixed, taps, terms in (
            (grad_q, q_mixed, taps_q, terms_q),
            (grad_kv, kv_mixed, taps_kv, terms_kv),
        ):
            grad_mixed = 0.0
            for m in range(3):
                ahead = grad_conv if m == 0 else shift_ahead(grad_conv, m)
                terms[m] = terms[m] + jnp.sum(ahead * mixed, axis=0, keepdims=True)
                grad_mixed = grad_mixed + taps[m] * ahead
            pair.append(grad_mixed.astype(BF16))
        results.append(pair)
        first += count
    table = jnp.concatenate(
        terms_q
        + [t[:, :HEAD_DIM] for t in terms_kv]
        + [t[:, HEAD_DIM:] for t in terms_kv]
        + [jnp.zeros((7, HEAD_DIM), F32)],
        axis=0,
    )
    table = jnp.concatenate([jnp.where(e == i, table, 0.0) for i in range(3)], axis=1)
    width = 3 * HEAD_DIM // 8
    for j in range(8):
        mine = [
            jnp.concatenate(
                [
                    results[0][i][j * long_rows : (j + 1) * long_rows],
                    results[1][i][j * short_rows : (j + 1) * short_rows],
                ],
                axis=0,
            )
            for i in range(2)
        ]
        send[j, :rows, :] = mine[1]
        send[j, rows : rows + rows // 2, :] = fold(mine[0])
        send[j, rows + rows // 2 :, :] = jnp.concatenate(
            [table[:, j * width : (j + 1) * width], jnp.zeros((16, LANES - width), F32)], axis=1
        ).astype(BF16)


def place_grad_mixed(came, grad_mixed):
    seqs = 2
    rows = (came.shape[1] - 16) * 2 // 3
    for e in range(3):
        for b in range(seqs):
            j = seqs * e + b
            at = slice(b * rows, (b + 1) * rows)
            lanes = slice(e * HEAD_DIM, (e + 1) * HEAD_DIM)
            grad_mixed[0, at, lanes] = unfold(came[j, rows : rows + rows // 2, :])
            grad_mixed[1, at, lanes] = came[j, :rows, :HEAD_DIM]
            grad_mixed[2, at, lanes] = came[j, :rows, HEAD_DIM:]


def project_back_body(
    place, came, normed, weight, keep_p, send_p, keep, send, taps, scratch, grad_mixed, blocks
):
    place_grad_mixed(came, grad_mixed)
    shard = normed.shape[1] // 8
    terms = [dot(normed[...], grad_mixed[c], TN).astype(BF16) for c in range(3)]
    for s in range(8):
        at = slice(s * shard, (s + 1) * shard)
        for c in range(3):
            blocks[s, c * shard : (c + 1) * shard, :] = terms[c][at, :LANES]
        blocks[s, 3 * shard :, :] = fold(
            jnp.concatenate([terms[c][at, LANES:] for c in range(3)], axis=0)
        )
    split_y(place, blocks, keep_p, send_p)
    rows = (came.shape[1] - 16) * 2 // 3
    total = came[0, rows + rows // 2 :, :].astype(F32)
    for j in range(1, 6):
        total = total + came[j, rows + rows // 2 :, :].astype(F32)
    taps[...] = total[: taps.shape[0], : taps.shape[1]]
    total = dot(grad_mixed[0], weight[0], NT)
    for c in (1, 2):
        total = total + dot(grad_mixed[c], weight[c], NT)
    scratch[...] = total.astype(BF16)
    split_halves(place, scratch, keep, send)


def input_grad_body(
    place, own, other, grad_mid, gain, long_in, short_in, long_out, short_out, scratch
):
    join_halves(place, scratch, own, other)
    seqs, long_rows, _ = long_in.shape
    rows = long_rows + short_in.shape[1]
    for b in range(seqs):
        at = slice(b * rows, (b + 1) * rows)
        values = jnp.concatenate([long_in[b], short_in[b]], axis=0).astype(F32)
        weighted = scratch[at, :] * gain[...]
        root = lax.rsqrt(jnp.mean(values * values, axis=-1, keepdims=True) + norm_eps)
        inner = jnp.mean(weighted * values, axis=-1, keepdims=True)
        grad = grad_mid[at, :] + (root * weighted - values * (root * root * root * inner))
        long_out[b] = grad[:long_rows]
        short_out[b] = grad[long_rows:]


def output_body(place, own, other, mid, long_out, short_out, scratch):
    join_halves(place, scratch, own, other)
    seqs, long_rows, _ = long_out.shape
    rows = long_rows + short_out.shape[1]
    for b in range(seqs):
        at = slice(b * rows, (b + 1) * rows)
        value = (mid[at, :] + scratch[at, :]).astype(BF16)
        long_out[b] = value[:long_rows]
        short_out[b] = value[long_rows:]


def scatter_z_body(place, *refs):
    count = (len(refs) - 4) // 2
    outs = refs[2 * count :]
    z = place[0] // 2
    for i in range(4):
        block = jnp.bitwise_xor(z, i)
        first = 0
        for a in range(count):
            keep, came = refs[2 * a], refs[2 * a + 1]
            rows = keep.shape[1]
            outs[i][first : first + rows, :] = (
                keep[block].astype(F32) + came[block].astype(F32)
            ).astype(BF16)
            first += rows


def near_body(place, *refs):
    pairs = len(refs[:-3]) // 2
    near, own, across = refs[-3:]
    z = place[0] // 2
    for i, target in ((0, own), (1, near.at[0]), (2, across), (3, near.at[1])):
        block = jnp.bitwise_xor(z, i)
        first = 0
        for p in range(pairs):
            keep, came = refs[2 * p], refs[2 * p + 1]
            rows = keep.shape[1]
            target[first : first + rows, :] = (
                keep[block].astype(F32) + came[block].astype(F32)
            ).astype(BF16)
            first += rows


def across_body(across, near, out):
    out[...] = (across[...].astype(F32) + near[1].astype(F32)).astype(BF16)


def sum_blocks(blocks):
    return (blocks[0][...].astype(F32) + blocks[1][...].astype(F32)) + (
        blocks[2][...].astype(F32) + blocks[3][...].astype(F32)
    )


def proj_grad_body(b0, b1, b2, b3, proj, gain, grad, gain_grad):
    total = sum_blocks((b0, b1, b2, b3))
    rows = proj.shape[1]
    column = 0.0
    for c, (wide, narrow) in enumerate(unpack_blocks(total, rows, 3)):
        term = jnp.concatenate([wide, narrow], axis=1)
        column = column + jnp.sum(term * proj[c].astype(F32), axis=1, keepdims=True)
        grad[c] = term
    gain_grad[...] = column.T / gain[...].astype(F32).reshape(1, rows)


def ffn_grad_body(
    own, near, across, down_keep, down_came, up, gain, up_grad, down_grad, out_grad, gain_grad
):
    rows = up.shape[0]
    total = own[...].astype(F32) + near[0].astype(F32) + across[...].astype(F32)
    raw = total[:rows]
    gain_grad[...] = jnp.sum(raw * up[...].astype(F32), axis=1, keepdims=True).T
    up_grad[...] = raw * gain[...].astype(F32).reshape(1, rows).T
    down_grad[...] = down_keep[...].astype(F32) + down_came[...].astype(F32)
    wide = total[rows : rows + 16]
    narrow = total[rows + 16 :]
    out = jnp.concatenate(
        [
            jnp.concatenate(
                [
                    wide[:, LANES * g : LANES * (g + 1)],
                    narrow[:, LANES * g : LANES * g + HEAD_DIM],
                ],
                axis=1,
            )
            for g in range(rows // 16)
        ],
        axis=0,
    )
    out_grad[...] = out.T


def pair_shards(
    short_input,
    long_input,
    short_cotangent,
    long_cotangent,
    short_lengths,
    long_lengths,
    proj_weight,
    out_weight,
    conv_taps,
    attention_gain,
    up_weight,
    down_weight,
    feed_gain,
):
    seqs, long_rows, width = long_input.shape
    short_rows = short_input.shape[1]
    rows = long_rows + short_rows
    tokens = seqs * rows
    shard = proj_weight.shape[1]
    local = proj_weight.shape[2]
    hidden = up_weight.shape[1]
    long_len, short_len = 8 * long_rows, 8 * short_rows
    total_len = long_len + short_len
    place = jnp.stack([lax.axis_index("seq"), lax.axis_index("head")]).astype(jnp.int32)
    packed_rows = shard * 9 // 2
    chunk = rows + rows // 2 + 16
    down_t = down_weight.T

    (proj_packed,) = in_vmem(
        pack_proj_body,
        [((packed_rows + 16, LANES), BF16)],
        (),
        far(proj_weight, attention_gain),
    )
    (ffn_packed,) = in_vmem(
        pack_ffn_body,
        [((2 * shard + 32, hidden), BF16)],
        (),
        far(up_weight, down_t, out_weight, feed_gain),
    )
    proj_z = [proj_packed] + [exchange(proj_packed, "seq", mask) for mask in (2, 4, 6)]
    proj_parts = [proj_packed, exchange(after(proj_packed, ffn_packed), "seq", 1)]
    proj_parts += [proj_z[1], exchange(proj_z[1], "seq", 1)]
    proj_parts += [proj_z[2], exchange(proj_z[2], "seq", 1)]
    proj_parts += [proj_z[3], exchange(proj_z[3], "seq", 1)]
    ffn_0 = after(ffn_packed, *proj_z)
    ffn_1 = exchange(ffn_0, "seq", 1)
    ffn_2 = exchange(ffn_0, "seq", 2)
    ffn_4 = exchange(ffn_0, "seq", 4)
    send, normed, proj_full, gain = in_vmem(
        project_body,
        [
            ((8, chunk, LANES), BF16),
            ((tokens, width), BF16, "far"),
            ((3, width, local), BF16, "far"),
            ((1, width), F32, "far"),
        ],
        (place,),
        (*proj_parts, *far(long_input, short_input, conv_taps)),
        scratch=[((8, LANES), F32)],
        fence=True,
    )
    came = lax.all_to_all(send, "seq", 0, 0, tiled=True)
    across_z = marker(ffn_4, ffn_1, send)
    ffn_2 = after(ffn_2, across_z)
    ffn_4 = after(ffn_4, across_z)
    ffn_6 = exchange(ffn_4, "seq", 2)
    ffn_3 = exchange(ffn_2, "seq", 1)
    ffn_5 = exchange(ffn_4, "seq", 1)
    att_send, q_all, kv_all, att_t, log_row, mixed = in_vmem(
        functools.partial(attend_body, long_rows, seqs),
        [
            ((8, rows // 2, LANES), BF16),
            ((total_len, HEAD_DIM), BF16, "far"),
            ((total_len, 2 * HEAD_DIM), BF16, "far"),
            ((HEAD_DIM, total_len), F32, "far"),
            ((1, total_len), F32, "far"),
            ((8, chunk, LANES), BF16, "far"),
        ],
        (place, long_lengths, short_lengths),
        (came,),
        fence=True,
    )
    att_0 = lax.all_to_all(att_send, "seq", 0, 0, tiled=True)
    ffn_7 = exchange(ffn_6, "seq", 1)
    up_full, down_full, out_full, out_now = in_vmem(
        place_ffn_body,
        [((width, hidden), BF16, "far")] * 2
        + [((width, local), BF16, "far"), ((width, local), BF16)],
        (place,),
        far(after(ffn_packed, att_send), ffn_1, ffn_2, ffn_3, ffn_4, ffn_5, ffn_6, ffn_7),
    )
    att_0 = after(att_0, out_full)
    att, keep, send = in_vmem(
        out_proj_body,
        [
            ((tokens, local), BF16, "far"),
            ((tokens // 2, width), BF16),
            ((tokens // 2, width), BF16),
        ],
        (place,),
        (att_0, out_now),
        scratch=[((tokens, width), BF16)],
        fence=True,
    )
    half = add_low(keep, exchange(send, "head", 1))
    own = add_low(half, exchange(half, "head", 2))
    other = exchange(own, "head", 1)
    mid, squared, grad_out, keep, send, normed_ffn, grad_up = in_vmem(
        functools.partial(feed_body, long_rows),
        [
            ((tokens, width), F32, "far"),
            ((tokens, hidden), BF16, "far"),
            ((tokens, width), BF16, "far"),
            ((tokens // 2, width), BF16),
            ((tokens // 2, width), BF16),
            ((tokens, width), BF16, "far"),
            ((tokens, hidden), BF16, "far"),
        ],
        (place, long_lengths, short_lengths),
        (own, other)
        + far(long_input, short_input, long_cotangent, short_cotangent, up_full, down_full),
        scratch=[
            ((tokens, width), BF16),
            ((tokens, width), F32),
        ],
        limit_mib=32,
    )
    half = add_low(keep, exchange(send, "head", 1))
    down_near, down_own, down_across, f_keep, f_send, up_keep, up_send = in_vmem(
        down_term_body,
        [((2, 2, shard, hidden), BF16, "far")]
        + [((2, shard, hidden), BF16, "far")] * 2
        + [((tokens // 2, width), BF16, "far")] * 2
        + [((4, shard, hidden), BF16, "far")] * 2,
        (place,),
        far(after(squared, half), grad_out, down_full, normed_ffn, grad_up),
        scratch=[
            ((tokens, width), BF16),
            ((8, shard, hidden), BF16),
        ],
        limit_mib=32,
        fence=True,
    )
    down_near = exchange(down_near, "seq", 2)
    up_came = exchange(up_send, "seq", 1)
    own = add_low(half, after(exchange(half, "head", 2), f_send))
    other = exchange(own, "head", 1)
    grad_mid, send, out_keep, out_send = in_vmem(
        middle_body,
        [
            ((tokens, width), F32, "far"),
            ((8, rows // 2, LANES), BF16),
            ((4, 32, hidden), BF16, "far"),
            ((4, 32, hidden), BF16, "far"),
        ],
        (place,),
        (own, other) + far(mid, grad_out, out_full, att),
        scratch=[((tokens, width), F32), ((tokens, width), BF16), ((8, 32, hidden), BF16)],
    )
    grad_came = lax.all_to_all(send, "seq", 0, 0, tiled=True)
    out_came = exchange(out_send, "seq", 1)
    (down_across,) = in_vmem(
        down_across_body,
        [((2, shard, hidden), BF16, "far")],
        (),
        far(after(down_across, send, up_came), down_near),
        fence=True,
    )
    grad_came = after(grad_came, down_across)
    down_across = exchange(down_across, "seq", 4)
    f_half = add_low(f_keep, exchange(after(f_send, send), "head", 1))
    f_own = add_low(f_half, exchange(f_half, "head", 2))
    f_other = exchange(f_own, "head", 1)
    long_output, short_output = in_vmem(
        output_body,
        [(long_input.shape, BF16), (short_input.shape, BF16)],
        (place,),
        (f_own, f_other) + far(mid),
        scratch=[((tokens, width), F32)],
    )
    (send,) = in_vmem(
        functools.partial(attend_back_body, long_rows, seqs),
        [((8, chunk, LANES), BF16)],
        (place, long_lengths, short_lengths),
        far(mixed, q_all, kv_all, att_t, log_row) + (grad_came,),
        fence=True,
    )
    mixed_came = lax.all_to_all(send, "seq", 0, 0, tiled=True)
    near, ffn_own, across = in_vmem(
        near_body,
        [((2, shard + 32, hidden), BF16, "far")] + [((shard + 32, hidden), BF16, "far")] * 2,
        (place,),
        far(up_keep, after(up_came, send), out_keep, out_came),
        fence=True,
    )
    near = exchange(near, "seq", 2)
    down_keep, down_send = in_vmem(
        down_y_body,
        [((shard, hidden), BF16, "far")] * 2,
        (place,),
        far(after(down_own, ffn_own), down_near, down_across),
    )
    down_came = exchange(down_send, "seq", 1)
    mixed_came = after(mixed_came, long_output, down_send)
    proj_keep, proj_send, keep, send, taps_grad = in_vmem(
        project_back_body,
        [
            ((4, packed_rows, LANES), BF16, "far"),
            ((4, packed_rows, LANES), BF16),
            ((tokens // 2, width), BF16),
            ((tokens // 2, width), BF16),
            (conv_taps.shape, F32),
        ],
        (place,),
        (mixed_came,) + far(normed, proj_full),
        scratch=[
            ((tokens, width), BF16),
            ((3, tokens, local), BF16),
            ((8, packed_rows, LANES), BF16),
        ],
        fence=True,
    )
    proj_came = exchange(proj_send, "seq", 1)
    half = add_low(keep, exchange(send, "head", 1))
    (across,) = in_vmem(
        across_body, [((shard + 32, hidden), BF16, "far")], (), far(across, near)
    )
    across = exchange(across, "seq", 4)
    own = add_low(half, after(exchange(half, "head", 2), proj_came))
    other = exchange(own, "head", 1)
    proj_blocks = in_vmem(
        scatter_z_body,
        [((packed_rows, LANES), BF16)] * 4,
        (place,),
        far(proj_keep) + (proj_came,),
        fence=True,
    )
    proj_blocks = [proj_blocks[0]] + [exchange(proj_blocks[i], "seq", 2 * i) for i in (1, 2, 3)]
    up_grad, down_grad, out_grad, feed_part = in_vmem(
        ffn_grad_body,
        [
            (up_weight.shape, F32),
            (down_t.shape, F32),
            (out_weight.shape, F32),
            ((1, shard), F32),
        ],
        (),
        far(after(ffn_own, proj_blocks[0]), near, across, down_keep, down_came, up_weight)
        + (feed_gain,),
    )
    proj_blocks[3] = after(proj_blocks[3], up_grad)
    proj_grad, attention_part = in_vmem(
        proj_grad_body,
        [(proj_weight.shape, F32), ((1, shard), F32)],
        (),
        (*proj_blocks, *far(proj_weight), attention_gain),
    )
    long_input_grad, short_input_grad = in_vmem(
        input_grad_body,
        [(long_input.shape, F32), (short_input.shape, F32)],
        (place,),
        (own, other) + far(after(grad_mid, attention_part), gain, long_input, short_input),
        scratch=[((tokens, width), F32)],
    )
    gains = jnp.concatenate([attention_part, feed_part], axis=0)
    gains = gains + exchange(gains, "head", 1)
    gains = gains + after(exchange(gains, "head", 2), long_input_grad)

    return (
        short_output,
        long_output,
        short_input_grad,
        long_input_grad,
        proj_grad,
        out_grad,
        taps_grad,
        gains[0],
        up_grad,
        down_grad.T,
        gains[1],
    )


def fits_pairs(short_input, long_input, proj_weight):
    seqs, long_rows, _ = long_input.shape
    short_seqs, short_rows, _ = short_input.shape
    return (
        lax.axis_size("seq") == 8
        and lax.axis_size("head") == 4
        and seqs == 2
        and short_seqs == 2
        and proj_weight.shape[2] == 3 * HEAD_DIM
        and proj_weight.shape[1] % 32 == 0
        and long_rows % 32 == 0
        and short_rows % 32 == 0
        and 8 * long_rows <= 2048
    )


def shards(short_input, long_input, *rest):
    proj_weight = rest[4]
    if fits_pairs(short_input, long_input, proj_weight):
        return pair_shards(short_input, long_input, *rest)
    return ring_shards(short_input, long_input, *rest)


def solution(mesh):
    placed = (
        P(None, "seq", None),
        P(None, "seq", None),
        P(None, "seq", None),
        P(None, "seq", None),
        P(),
        P(),
        P(None, "seq", "head"),
        P("head", "seq"),
        P(None, ("head", "seq")),
        P("seq"),
        P("seq", "head"),
        P("head", "seq"),
        P("seq"),
    )
    return jax.shard_map(
        shards,
        mesh=mesh,
        in_specs=placed,
        out_specs=(
            P(None, "seq", None),
            P(None, "seq", None),
            P(None, "seq", None),
            P(None, "seq", None),
            P(None, "seq", "head"),
            P("head", "seq"),
            P(None, ("head", "seq")),
            P("seq"),
            P("seq", "head"),
            P("head", "seq"),
            P("seq"),
        ),
        check_vma=False,
    )
```

```python
import functools

import jax
import jax.numpy as jnp
import numpy as np
from jax import lax
from jax.experimental import pallas as pl
from jax.experimental.pallas import tpu as pltpu
from jax.sharding import PartitionSpec as P

HEAD_DIM = 64


norm_eps = 1e-06
mask_fill = -1e30
block_limit = 2048


def passed_along(block, axis, distance):
    devices = range(lax.axis_size(axis))
    route = [((i - distance) % len(devices), i) for i in devices]
    return lax.ppermute(block, axis, route)


def shifted(array, axis, by):
    peers = lax.axis_size(axis)
    pairs = [(i, i + by) for i in range(peers) if 0 <= i + by < peers]
    return lax.ppermute(array, axis, pairs)


def block_rows(row_count):
    size_rows = min(row_count, block_limit)
    while row_count % size_rows != 0:
        size_rows = size_rows - 1
    return size_rows


def norm_forward(values_in, gain_row):
    inv_root = lax.rsqrt(jnp.mean(values_in * values_in, axis=-1, keepdims=True) + norm_eps)
    return (values_in * inv_root * gain_row, inv_root)


def norm_backward(values_in, inv_root, gain_row, grad_in):
    weighted = grad_in * gain_row
    inner_mean = jnp.mean(weighted * values_in, axis=-1, keepdims=True)
    grad_values = inv_root * weighted - values_in * inv_root * inv_root * inv_root * inner_mean
    grad_gain = jnp.sum(grad_in * values_in * inv_root, axis=(0, 1))
    return (grad_values, grad_gain)


def allowed_mask(query_pos, key_pos, lengths):
    causal = key_pos[None, :] <= query_pos[:, None]
    inside = key_pos[None, :] < lengths[:, None]
    return jnp.logical_and(causal[None, None], inside[:, None, None, :])


def block_scores(query_rows, key_rows, query_pos, key_pos, lengths):
    allowed = allowed_mask(query_pos, key_pos, lengths)
    raw_scores = jnp.einsum(
        "bqhe,bkhe->bhqk", query_rows, key_rows, preferred_element_type=jnp.float32
    ) * HEAD_DIM ** (-0.5)
    return (jnp.where(allowed, raw_scores, mask_fill), allowed)


def block_grads(
    query_rows, grad_rows, log_rows, delta_rows, key_rows, value_rows, query_pos, key_pos, lengths
):
    scores, allowed = block_scores(query_rows, key_rows, query_pos, key_pos, lengths)
    prob_rows = jnp.where(
        allowed, jnp.exp(scores - jnp.transpose(log_rows, (0, 2, 1))[..., None]), 0.0
    )
    grad_probs = jnp.einsum(
        "bqhe,bkhe->bhqk", grad_rows, value_rows, preferred_element_type=jnp.float32
    )
    grad_scores = (
        prob_rows * (grad_probs - jnp.transpose(delta_rows, (0, 2, 1))[..., None])
    ).astype(jnp.bfloat16)
    grad_query = jnp.einsum(
        "bhqk,bkhe->bqhe", grad_scores, key_rows, preferred_element_type=jnp.float32
    ) * HEAD_DIM ** (-0.5)
    grad_key = jnp.einsum(
        "bhqk,bqhe->bkhe", grad_scores, query_rows, preferred_element_type=jnp.float32
    ) * HEAD_DIM ** (-0.5)
    grad_value = jnp.einsum(
        "bhqk,bqhe->bkhe",
        prob_rows.astype(jnp.bfloat16),
        grad_rows,
        preferred_element_type=jnp.float32,
    )
    return (grad_query, grad_key, grad_value)


def attend_forward(queries, keys_here, values_here, query_pos, lengths):
    seq_count, span_rows, head_count, head_width = queries.shape
    initial = (
        jnp.full((seq_count, head_count, span_rows), mask_fill, jnp.float32),
        jnp.zeros((seq_count, head_count, span_rows), jnp.float32),
        jnp.zeros((seq_count, span_rows, head_count, head_width), jnp.float32),
    )
    key_piece = lax.all_gather(keys_here, "seq", axis=1, tiled=True)
    value_piece = lax.all_gather(values_here, "seq", axis=1, tiled=True)
    row_count = key_piece.shape[1]
    size_rows = block_rows(row_count)

    def one_block(block_index, carried_state):
        running_top, running_sum, acc_rows = carried_state
        offset = block_index * size_rows
        key_rows = lax.dynamic_slice_in_dim(key_piece, offset, size_rows, 1)
        value_rows = lax.dynamic_slice_in_dim(value_piece, offset, size_rows, 1)
        key_pos = offset + jnp.arange(size_rows, dtype=jnp.int32)
        scores, allowed = block_scores(queries, key_rows, query_pos, key_pos, lengths)
        new_top = jnp.maximum(running_top, jnp.max(scores, axis=-1))
        exp_terms = jnp.where(allowed, jnp.exp(scores - new_top[..., None]), 0.0)
        shrink = jnp.exp(running_top - new_top)
        running_sum = running_sum * shrink + jnp.sum(exp_terms, axis=-1)
        acc_rows = acc_rows * jnp.transpose(shrink, (0, 2, 1))[..., None] + jnp.einsum(
            "bhqk,bkhe->bqhe",
            exp_terms.astype(jnp.bfloat16),
            value_rows,
            preferred_element_type=jnp.float32,
        )
        return (new_top, running_sum, acc_rows)

    running_top, running_sum, acc_rows = lax.fori_loop(
        0, row_count // size_rows, one_block, initial
    )
    attention = acc_rows / jnp.transpose(running_sum, (0, 2, 1))[..., None]
    log_totals = jnp.transpose(running_top + jnp.log(running_sum), (0, 2, 1))
    return (attention, log_totals)


def pass_sums(grad_keys, grad_values):
    return (
        passed_along(grad_keys.astype(jnp.bfloat16), "seq", 1).astype(grad_keys.dtype),
        passed_along(grad_values.astype(jnp.bfloat16), "seq", 1).astype(grad_values.dtype),
    )


def attend_backward(
    queries, keys_here, values_here, grad_attention, log_totals, delta_rows, query_pos, lengths
):
    seq_count, span_rows, head_count, head_width = queries.shape
    zeros_local = jnp.zeros(queries.shape, jnp.float32)
    seq_size = lax.axis_size("seq")
    my_index = lax.axis_index("seq")
    local_pos = jnp.arange(span_rows, dtype=jnp.int32)

    def step_grads(step, key_piece, value_piece):
        anchor = jnp.mod(my_index - step, seq_size)
        key_pos = anchor * span_rows + local_pos
        return block_grads(
            queries,
            grad_attention,
            log_totals,
            delta_rows,
            key_piece,
            value_piece,
            query_pos,
            key_pos,
            lengths,
        )

    def cycle_step(step, state):
        key_piece, value_piece, grad_keys, grad_values, grad_query = state
        query_part, key_part, value_part = step_grads(step, key_piece, value_piece)
        key_piece, value_piece = shifted((key_piece, value_piece), "seq", 1)
        grad_keys, grad_values = pass_sums(grad_keys + key_part, grad_values + value_part)
        return (key_piece, value_piece, grad_keys, grad_values, grad_query + query_part)

    final_state = lax.fori_loop(
        0, seq_size - 1, cycle_step, (keys_here, values_here, zeros_local, zeros_local, zeros_local)
    )
    key_piece, value_piece, grad_keys, grad_values, grad_query = final_state
    query_part, key_part, value_part = step_grads(seq_size - 1, key_piece, value_piece)
    grad_key, grad_value = pass_sums(grad_keys + key_part, grad_values + value_part)
    grad_query = grad_query + query_part
    return (grad_query, grad_key, grad_value)


def micro_batch(inputs, cotangent, lengths, weights):
    proj_full, out_full, taps_full, attend_gain, up_full, down_full, ffn_gain = weights
    seq_count, span_rows, model_width = inputs.shape
    local_width = proj_full.shape[2]
    heads_here = local_width // HEAD_DIM
    query_pos = lax.axis_index("seq") * span_rows + jnp.arange(span_rows, dtype=jnp.int32)
    valid_rows = (query_pos[None, :] < lengths[:, None])[..., None]
    residual_in = inputs.astype(jnp.float32)
    normed, inv_first = norm_forward(residual_in, attend_gain)
    normed_low = normed.astype(jnp.bfloat16)
    mixed_qkv = jnp.einsum(
        "btd,cde->cbte", normed_low, proj_full, preferred_element_type=jnp.float32
    ).astype(jnp.bfloat16)
    borrowed = shifted(mixed_qkv[:, :, span_rows - 2 :, :], "seq", 1)
    extended = jnp.concatenate([borrowed, mixed_qkv], axis=2).astype(jnp.float32)
    tap_table = taps_full.astype(jnp.float32).reshape(3, 3, local_width)
    tap_now = tap_table[:, 0][:, None, None, :]
    tap_one = tap_table[:, 1][:, None, None, :]
    tap_two = tap_table[:, 2][:, None, None, :]
    conved = (
        tap_now * extended[:, :, 2:]
        + tap_one * extended[:, :, 1:-1]
        + tap_two * extended[:, :, :-2]
    )
    conv_out = conved.astype(jnp.bfloat16).reshape(3, seq_count, span_rows, heads_here, HEAD_DIM)
    queries, keys_here, values_here = (conv_out[0], conv_out[1], conv_out[2])
    attention, log_totals = attend_forward(queries, keys_here, values_here, query_pos, lengths)
    attention_low = attention.astype(jnp.bfloat16).reshape(seq_count, span_rows, local_width)
    attend_part = jnp.einsum(
        "bte,ed->btd", attention_low, out_full, preferred_element_type=jnp.float32
    )
    mid_residual = residual_in + lax.psum(attend_part.astype(jnp.bfloat16), "head").astype(
        jnp.float32
    )
    normed_ffn, inv_second = norm_forward(mid_residual, ffn_gain)
    normed_ffn_low = normed_ffn.astype(jnp.bfloat16)
    up_proj = jnp.einsum("btd,df->btf", normed_ffn_low, up_full, preferred_element_type=jnp.float32)
    relu_up = jnp.maximum(up_proj, 0.0)
    squared = (relu_up * relu_up).astype(jnp.bfloat16)
    ffn_part = jnp.einsum("btf,fd->btd", squared, down_full, preferred_element_type=jnp.float32)
    output = (
        mid_residual + lax.psum(ffn_part.astype(jnp.bfloat16), "head").astype(jnp.float32)
    ).astype(jnp.bfloat16)
    grad_out = jnp.where(valid_rows, cotangent.astype(jnp.float32), 0.0)
    grad_out_low = grad_out.astype(jnp.bfloat16)
    down_term = jnp.einsum("btf,btd->fd", squared, grad_out_low, preferred_element_type=jnp.float32)
    grad_squared = jnp.einsum(
        "btd,fd->btf", grad_out_low, down_full, preferred_element_type=jnp.float32
    )
    grad_up = (grad_squared * 2.0 * relu_up).astype(jnp.bfloat16)
    up_term = jnp.einsum("btd,btf->df", normed_ffn_low, grad_up, preferred_element_type=jnp.float32)
    grad_normed_ffn = lax.psum(
        jnp.einsum("btf,df->btd", grad_up, up_full, preferred_element_type=jnp.float32).astype(
            jnp.bfloat16
        ),
        "head",
    ).astype(jnp.float32)
    grad_through, feed_term = norm_backward(mid_residual, inv_second, ffn_gain, grad_normed_ffn)
    grad_mid = grad_out + grad_through
    grad_mid_low = grad_mid.astype(jnp.bfloat16)
    out_term = jnp.einsum(
        "bte,btd->ed", attention_low, grad_mid_low, preferred_element_type=jnp.float32
    )
    grad_attention = jnp.einsum(
        "btd,ed->bte", grad_mid_low, out_full, preferred_element_type=jnp.float32
    )
    grad_attention = grad_attention.astype(jnp.bfloat16).reshape(
        seq_count, span_rows, heads_here, HEAD_DIM
    )
    delta_rows = jnp.einsum("bqhe,bqhe->bqh", grad_attention.astype(jnp.float32), attention)
    grad_query, grad_key, grad_value = attend_backward(
        queries, keys_here, values_here, grad_attention, log_totals, delta_rows, query_pos, lengths
    )
    grad_conv = jnp.stack([grad_query, grad_key, grad_value]).reshape(
        3, seq_count, span_rows, local_width
    )
    taps_term = jnp.stack(
        [
            jnp.sum(grad_conv * extended[:, :, 2:], axis=(1, 2)),
            jnp.sum(grad_conv * extended[:, :, 1:-1], axis=(1, 2)),
            jnp.sum(grad_conv * extended[:, :, :-2], axis=(1, 2)),
        ],
        axis=1,
    ).reshape(9, local_width)
    full_grad = jnp.pad(grad_conv, ((0, 0), (0, 0), (2, 2), (0, 0)))
    grad_extended = (
        tap_now * full_grad[:, :, 0 : span_rows + 2]
        + tap_one * full_grad[:, :, 1 : span_rows + 3]
        + tap_two * full_grad[:, :, 2 : span_rows + 4]
    )
    returned = shifted(grad_extended[:, :, :2], "seq", -1)
    grad_mixed = jnp.concatenate(
        [grad_extended[:, :, 2:span_rows], grad_extended[:, :, span_rows:] + returned], axis=2
    ).astype(jnp.bfloat16)
    proj_term = jnp.einsum(
        "btd,cbte->cde", normed_low, grad_mixed, preferred_element_type=jnp.float32
    )
    grad_normed = lax.psum(
        jnp.einsum(
            "cbte,cde->btd", grad_mixed, proj_full, preferred_element_type=jnp.float32
        ).astype(jnp.bfloat16),
        "head",
    ).astype(jnp.float32)
    grad_first, attention_term = norm_backward(residual_in, inv_first, attend_gain, grad_normed)
    grad_input = grad_mid + grad_first
    return (
        output,
        grad_input,
        (proj_term, out_term, taps_term, attention_term, up_term, down_term, feed_term),
    )


def ring_shards(
    short_input,
    long_input,
    short_cotangent,
    long_cotangent,
    short_lengths,
    long_lengths,
    proj_weight,
    out_weight,
    conv_taps,
    attention_gain,
    up_weight,
    down_weight,
    feed_gain,
):
    proj_full, out_full, taps_full, attend_gain = (
        lax.all_gather(proj_weight, "seq", axis=1, tiled=True),
        lax.all_gather(out_weight, "seq", axis=1, tiled=True),
        lax.all_gather(conv_taps, "seq", axis=1, tiled=True),
        lax.all_gather(attention_gain, "seq", axis=0, tiled=True),
    )
    up_full, down_full, ffn_gain = (
        lax.all_gather(up_weight, "seq", axis=0, tiled=True),
        lax.all_gather(down_weight, "seq", axis=1, tiled=True),
        lax.all_gather(feed_gain, "seq", axis=0, tiled=True),
    )
    weights = (
        proj_full,
        out_full,
        taps_full,
        attend_gain.astype(jnp.float32),
        up_full,
        down_full,
        ffn_gain.astype(jnp.float32),
    )
    short_output, short_input_grad, short_terms = micro_batch(
        short_input, short_cotangent, short_lengths, weights
    )
    long_output, long_input_grad, long_terms = micro_batch(
        long_input, long_cotangent, long_lengths, weights
    )
    summed = tuple(
        (first_term + second_term for first_term, second_term in zip(short_terms, long_terms))
    )
    reduced = (
        lax.psum_scatter(summed[0], "seq", scatter_dimension=1, tiled=True),
        lax.psum_scatter(summed[1], "seq", scatter_dimension=1, tiled=True),
        lax.psum_scatter(summed[2], "seq", scatter_dimension=1, tiled=True),
        lax.psum_scatter(summed[3], "seq", scatter_dimension=0, tiled=True),
        lax.psum_scatter(summed[4], "seq", scatter_dimension=0, tiled=True),
        lax.psum_scatter(summed[5], "seq", scatter_dimension=1, tiled=True),
        lax.psum_scatter(summed[6], "seq", scatter_dimension=0, tiled=True),
    )
    return (
        short_output,
        long_output,
        short_input_grad,
        long_input_grad,
        reduced[0],
        reduced[1],
        reduced[2],
        reduced[3],
        reduced[4],
        reduced[5],
        reduced[6],
    )


LANES = 128
FENCE = 10**11
NT = (((1,), (1,)), ((), ()))
TN = (((0,), (0,)), ((), ()))
F32 = jnp.float32
BF16 = jnp.bfloat16


def dot(a, b, dims=(((1,), (0,)), ((), ()))):
    return lax.dot_general(a, b, dims, preferred_element_type=F32)


def in_vmem(body, outs, scalars, arrays, scratch=(), limit_mib=16, fence=False):
    return pl.pallas_call(
        body,
        out_shape=[
            pltpu.HBM(*out[:2]) if len(out) == 3 else jax.ShapeDtypeStruct(*out) for out in outs
        ],
        in_specs=[pl.BlockSpec(memory_space=pltpu.SMEM)] * len(scalars)
        + [pl.BlockSpec(memory_space=pltpu.VMEM)] * len(arrays),
        out_specs=[pl.BlockSpec(memory_space=pltpu.VMEM)] * len(outs),
        scratch_shapes=[pltpu.VMEM(shape, kind) for shape, kind in scratch],
        compiler_params=pltpu.CompilerParams(vmem_limit_bytes=limit_mib * 1024 * 1024),
        cost_estimate=pl.CostEstimate(
            flops=FENCE if fence else 0, bytes_accessed=0, transcendentals=0
        ),
    )(*scalars, *arrays)


def far(*arrays):
    return tuple(pltpu.with_memory_space_constraint(array, pltpu.HBM) for array in arrays)


def after(array, *others):
    return lax.optimization_barrier((array, *others))[0]


def marker(*arrays):
    def body(*refs):
        refs[-1][...] = jnp.zeros_like(refs[-1])

    return pl.pallas_call(
        body,
        out_shape=jax.ShapeDtypeStruct((8, LANES), F32),
        in_specs=[pl.BlockSpec(memory_space=pl.ANY)] * len(arrays),
        out_specs=pl.BlockSpec(memory_space=pltpu.VMEM),
        cost_estimate=pl.CostEstimate(flops=FENCE, bytes_accessed=0, transcendentals=0),
    )(*arrays)


def exchange(array, axis, mask):
    size = lax.axis_size(axis)
    return lax.ppermute(array, axis, [(i, i ^ mask) for i in range(size)])


def add_low(a, b):
    return (a.astype(F32) + b.astype(F32)).astype(BF16)


def shift_back(rows, by):
    index = lax.broadcasted_iota(jnp.int32, rows.shape, 0)
    return jnp.where(index >= by, pltpu.roll(rows, by, axis=0), 0.0)


def shift_ahead(rows, by):
    count = rows.shape[0]
    index = lax.broadcasted_iota(jnp.int32, rows.shape, 0)
    return jnp.where(index < count - by, pltpu.roll(rows, count - by, axis=0), 0.0)


def fold(rows):
    half = rows.shape[0] // 2
    return jnp.concatenate([rows[:half], rows[half:]], axis=1)


def unfold(rows):
    return jnp.concatenate([rows[:, :HEAD_DIM], rows[:, HEAD_DIM:]], axis=0)


def pack_proj_body(proj, gain, packed):
    rows = proj.shape[1]
    for c in range(3):
        packed[c * rows : (c + 1) * rows, :] = proj[c, :, :LANES]
    narrow = jnp.concatenate([proj[c, :, LANES:] for c in range(3)], axis=0)
    packed[3 * rows : 9 * rows // 2, :] = fold(narrow)
    gain_row = gain[...].astype(F32).reshape(1, rows)
    gain_row = jnp.concatenate([gain_row, jnp.zeros((1, LANES - rows), F32)], axis=1)
    packed[9 * rows // 2 :, :] = jnp.broadcast_to(gain_row, (16, LANES)).astype(BF16)


def unpack_blocks(packed, rows, count):
    narrow = unfold(packed[count * rows : 3 * count * rows // 2, :])
    return [
        (packed[i * rows : (i + 1) * rows, :], narrow[i * rows : (i + 1) * rows, :])
        for i in range(count)
    ]


def narrow_pack(block, store):
    groups = block.shape[0] // 16
    for g in range(groups):
        rows = block[16 * g : 16 * g + 16, :]
        store(0, LANES * g, rows[:, :LANES])
        tail = rows[:, LANES:]
        store(16, LANES * g, jnp.concatenate([tail, jnp.zeros_like(tail)], axis=1))


def pack_out_body(out, packed):
    def store(row, lane, value):
        packed[row : row + 16, lane : lane + LANES] = value

    narrow_pack(out[...].astype(F32).T.astype(BF16), store)


def pack_ffn_body(up, down, out, out_x, gain, packed):
    rows = up.shape[0]
    gain_column = gain[...].astype(F32).reshape(1, rows).T
    packed[:rows, :] = (up[...].astype(F32) * gain_column).astype(BF16)
    packed[rows : 2 * rows, :] = down[...]
    packed[2 * rows : 2 * rows + 16, :] = out[:16, :]
    packed[2 * rows + 16 : 2 * rows + 32, :] = out_x[:16, :]
    for g in range(rows // 16):
        lanes = slice(LANES * g, LANES * g + HEAD_DIM)
        packed[2 * rows + 32 :, LANES * g : LANES * (g + 1)] = jnp.concatenate(
            [out[16:, lanes], out_x[16:, lanes]], axis=1
        )


def place_ffn_body(place, *refs):
    up, down, out, out_now, out_x = refs[8:]
    rows = out.shape[0] // 8
    for i in range(8):
        owner = jnp.bitwise_xor(place[0], i)
        part = refs[i]
        first = pl.ds(pl.multiple_of(owner * rows, rows), rows)
        up[first, :] = part[:rows, :]
        down[first, :] = part[rows : 2 * rows, :]
        for g in range(rows // 16):
            at = pl.ds(pl.multiple_of(owner * rows + 16 * g, 16), 16)
            lanes = slice(LANES * g, LANES * (g + 1))
            narrow = part[2 * rows + 32 :, lanes]
            out[at, :LANES] = part[2 * rows : 2 * rows + 16, lanes]
            out[at, LANES:] = narrow[:, :HEAD_DIM]
            out_x[at, :LANES] = part[2 * rows + 16 : 2 * rows + 32, lanes]
            out_x[at, LANES:] = narrow[:, HEAD_DIM:]
    out_now[...] = out[...]


def project_body(place, *refs):
    parts = refs[:8]
    long_in, short_in, taps, send, normed, weight, gain, gain_rows = refs[8:]
    seqs, long_rows, _ = long_in.shape
    rows = long_rows + short_in.shape[1]
    for i in range(8):
        packed = parts[i][...]
        shard = weight.shape[1] // 8
        owner = jnp.bitwise_xor(place[0], i)
        gain_rows[pl.ds(owner, 1), :] = packed[9 * shard // 2 :, :].astype(F32)[:1]
        at = pl.ds(pl.multiple_of(owner * shard, shard), shard)
        for c, (wide, narrow) in enumerate(unpack_blocks(packed, shard, 3)):
            weight[c, at, :LANES] = wide
            weight[c, at, LANES:] = narrow
    gain[...] = jnp.concatenate([gain_rows[j : j + 1, :shard] for j in range(8)], axis=1)
    for b in range(seqs):
        values = jnp.concatenate([long_in[b], short_in[b]], axis=0).astype(F32)
        root = lax.rsqrt(jnp.mean(values * values, axis=-1, keepdims=True) + norm_eps)
        normed[b * rows : (b + 1) * rows, :] = (values * root * gain[...]).astype(BF16)
    mixed = [dot(normed[...], weight[c]).astype(BF16) for c in range(3)]
    tap_rows = jnp.concatenate(
        [taps[...], jnp.zeros((16 - taps.shape[0], taps.shape[1]), BF16)], axis=0
    )
    tap_rows = jnp.concatenate(
        [tap_rows, jnp.zeros((16, LANES - taps.shape[1]), BF16)], axis=1
    )
    half = rows // 2
    for dest in range(8):
        if dest < 3 * seqs:
            e, b = dest // seqs, dest % seqs
            lanes = slice(e * HEAD_DIM, (e + 1) * HEAD_DIM)
            q, k, v = [m[b * rows : (b + 1) * rows, lanes] for m in mixed]
            send[dest, :rows, :] = jnp.concatenate([k, v], axis=1)
            send[dest, rows : rows + half, :] = fold(q)
        else:
            send[dest, : rows + half, :] = jnp.zeros((rows + half, LANES), BF16)
        send[dest, rows + half :, :] = tap_rows


def head_taps(place, came, rows, seqs):
    first = rows + rows // 2
    width = 3 * HEAD_DIM // 8
    whole = jnp.concatenate(
        [came[j, first:, :].astype(F32)[:, :width] for j in range(8)], axis=1
    )
    e = place[0] // seqs
    mine = whole[:, :HEAD_DIM]
    for other in (1, 2):
        mine = jnp.where(
            e == other, whole[:, other * HEAD_DIM : (other + 1) * HEAD_DIM], mine
        )
    taps_q = [mine[m : m + 1, :] for m in range(3)]
    taps_kv = [
        jnp.concatenate([mine[3 + m : 4 + m, :], mine[6 + m : 7 + m, :]], axis=1) for m in range(3)
    ]
    return taps_q, taps_kv


def own_pair(came, long_rows, rows):
    q_rows = [unfold(came[j, rows : rows + rows // 2, :]) for j in range(8)]
    result = []
    for part in (slice(0, long_rows), slice(long_rows, rows)):
        q = jnp.concatenate([piece[part] for piece in q_rows], axis=0).astype(F32)
        kv = jnp.concatenate([came[j, part, :] for j in range(8)], axis=0).astype(F32)
        result.append((q, kv))
    return result


def convolve(rows, taps):
    return taps[0] * rows + taps[1] * shift_back(rows, 1) + taps[2] * shift_back(rows, 2)


def attend_body(
    long_rows, seqs, place, long_lengths, short_lengths, came, send, q_all, kv_all, att_t, log_row, kept
):
    rows = (came.shape[1] - 16) * 2 // 3
    kept[...] = came[...]
    taps_q, taps_kv = head_taps(place, came, rows, seqs)
    b = place[0] % seqs
    first = 0
    results = []
    for lengths, (q_mixed, kv_mixed) in zip(
        (long_lengths, short_lengths), own_pair(came, long_rows, rows)
    ):
        count = q_mixed.shape[0]
        block = min(256, count)
        length = lengths[b]
        q = (convolve(q_mixed, taps_q).astype(BF16).astype(F32) * HEAD_DIM ** (-0.5)).astype(BF16)
        kv = convolve(kv_mixed, taps_kv).astype(BF16)
        kv_t = kv.astype(F32).T.astype(BF16)
        q_all[first : first + count, :] = q
        kv_all[first : first + count, :] = kv
        k = kv[:, :HEAD_DIM]
        v_t = kv_t[HEAD_DIM:, :]
        pieces = []
        for start in range(0, count, block):
            stop = start + block
            scores = dot(k[:stop], q[start:stop], NT)
            key_pos = lax.broadcasted_iota(jnp.int32, scores.shape, 0)
            query_pos = lax.broadcasted_iota(jnp.int32, scores.shape, 1) + start
            allowed = jnp.logical_and(key_pos <= query_pos, key_pos < length)
            scores = jnp.where(allowed, scores, mask_fill)
            top = jnp.max(scores, axis=0, keepdims=True)
            terms = jnp.exp(scores - top)
            total = jnp.sum(terms, axis=0, keepdims=True)
            out_t = dot(v_t[:, :stop], terms.astype(BF16)) / total
            att_t[:, first + start : first + stop] = out_t
            log_row[:, first + start : first + stop] = top + jnp.log(total)
            pieces.append(out_t.T.astype(BF16))
        results.append(jnp.concatenate(pieces, axis=0))
        first += count
    short_rows = rows - long_rows
    for j in range(8):
        mine = jnp.concatenate(
            [
                results[0][j * long_rows : (j + 1) * long_rows],
                results[1][j * short_rows : (j + 1) * short_rows],
            ],
            axis=0,
        )
        send[j, :, :] = fold(mine)


def pair_rows(came, seqs):
    columns = []
    for e in range(3):
        columns.append(
            jnp.concatenate([unfold(came[seqs * e + b]) for b in range(seqs)], axis=0)
        )
    return jnp.concatenate(columns, axis=1)


def out_proj_body(came, came_x, out, out_x, att, part):
    att[...] = pair_rows(came, 2)
    total = dot(att[...], out[...], NT)
    part[...] = (total + dot(pair_rows(came_x, 2), out_x[...], NT)).astype(BF16)


def feed_body(
    long_rows,
    place,
    long_lengths,
    short_lengths,
    own,
    other,
    long_in,
    short_in,
    long_cot,
    short_cot,
    up,
    down,
    mid_ref,
    squared_ref,
    grad_out_ref,
    keep,
    send,
    normed_ref,
    grad_up_ref,
    scratch,
    attended,
):
    seqs = long_in.shape[0]
    rows = long_rows + short_in.shape[1]
    attended[...] = own[...].astype(F32) + other[...].astype(F32)
    for b in range(seqs):
        at = slice(b * rows, (b + 1) * rows)
        residual = jnp.concatenate([long_in[b], short_in[b]], axis=0).astype(F32)
        mid = residual + attended[at, :]
        mid_ref[at, :] = mid
        root = lax.rsqrt(jnp.mean(mid * mid, axis=-1, keepdims=True) + norm_eps)
        normed_ref[at, :] = (mid * root).astype(BF16)
        for cot, lengths, first, count in (
            (long_cot, long_lengths, b * rows, long_rows),
            (short_cot, short_lengths, b * rows + long_rows, rows - long_rows),
        ):
            value = cot[b]
            position = lax.broadcasted_iota(jnp.int32, value.shape, 0) + place[0] * count
            grad_out_ref[first : first + count, :] = jnp.where(
                position < lengths[b], value.astype(F32), 0.0
            ).astype(BF16)
    relu = jnp.maximum(dot(normed_ref[...], up[...]), 0.0)
    squared_ref[...] = (relu * relu).astype(BF16)
    grad_squared = dot(grad_out_ref[...], down[...])
    grad_up_ref[...] = (grad_squared * 2.0 * relu).astype(BF16)
    scratch[...] = dot(grad_up_ref[...], up[...], NT).astype(BF16)
    split_halves(place, scratch, keep, send)


def split_halves(place, whole, keep, send):
    half = whole.shape[0] // 2
    core = place[1] % 2
    keep[...] = whole[pl.ds(pl.multiple_of(core * half, half), half), :]
    send[...] = whole[pl.ds(pl.multiple_of((1 - core) * half, half), half), :]


def join_halves(place, whole, own, other):
    half = own.shape[0]
    core = place[1] % 2
    whole[pl.ds(pl.multiple_of(core * half, half), half), :] = own[...].astype(whole.dtype)
    whole[pl.ds(pl.multiple_of((1 - core) * half, half), half), :] = other[...].astype(whole.dtype)


def split_y(place, blocks, keep, send):
    y = place[0] % 2
    for z in range(4):
        keep[z] = blocks[2 * z + y]
        send[z] = blocks[2 * z + 1 - y]


def down_term_body(
    place,
    squared,
    grad_out,
    down,
    normed,
    grad_up,
    near,
    own,
    across,
    f_keep,
    f_send,
    up_keep,
    up_send,
    scratch,
    blocks,
):
    rows = blocks.shape[1]
    term = dot(normed[...], grad_up[...], TN).astype(BF16)
    for s in range(8):
        blocks[s] = term[s * rows : (s + 1) * rows]
    split_y(place, blocks, up_keep, up_send)
    term = dot(grad_out[...], squared[...], TN).astype(BF16)
    for s in range(8):
        blocks[s] = term[s * rows : (s + 1) * rows]
    z = place[0] // 2
    for i, target in ((0, own), (1, near.at[0]), (2, across), (3, near.at[1])):
        for y in range(2):
            target[y] = blocks[2 * jnp.bitwise_xor(z, i) + y]
    scratch[...] = dot(squared[...], down[...], NT).astype(BF16)
    split_halves(place, scratch, f_keep, f_send)


def down_across_body(across, near, out):
    out[...] = (across[...].astype(F32) + near[1].astype(F32)).astype(BF16)


def down_y_body(place, own, near, across, keep, send):
    y = place[0] % 2
    for target, block in ((keep, y), (send, 1 - y)):
        target[...] = (
            own[block].astype(F32) + near[0, block].astype(F32) + across[block].astype(F32)
        ).astype(BF16)


def middle_body(
    place, own, other, mid_ref, grad_out, out, att, grad_mid_ref, send, keep_out, send_out, scratch, low_ref, blocks
):
    join_halves(place, scratch, own, other)
    seqs = 2
    rows = mid_ref.shape[0] // seqs
    for b in range(seqs):
        at = slice(b * rows, (b + 1) * rows)
        mid = mid_ref[at, :]
        weighted = scratch[at, :]
        root = lax.rsqrt(jnp.mean(mid * mid, axis=-1, keepdims=True) + norm_eps)
        inner = jnp.mean(weighted * mid, axis=-1, keepdims=True)
        grad_mid = grad_out[at, :].astype(F32) + (
            root * weighted - mid * (root * root * root * inner)
        )
        grad_mid_ref[at, :] = grad_mid
        low_ref[at, :] = grad_mid.astype(BF16)
    grad_att = dot(low_ref[...], out[...]).astype(BF16)
    for dest in range(8):
        if dest < 3 * seqs:
            e, b = dest // seqs, dest % seqs
            send[dest] = fold(
                grad_att[b * rows : (b + 1) * rows, e * HEAD_DIM : (e + 1) * HEAD_DIM]
            )
        else:
            send[dest] = jnp.zeros_like(send[dest])
    term = dot(low_ref[...], att[...], TN).astype(BF16)
    shard = term.shape[0] // 8
    for s in range(8):

        def store(row, lane, value):
            blocks[s, row : row + 16, lane : lane + LANES] = value

        narrow_pack(term[s * shard : (s + 1) * shard], store)
    split_y(place, blocks, keep_out, send_out)


def attend_back_body(
    long_rows,
    seqs,
    place,
    long_lengths,
    short_lengths,
    came,
    q_all,
    kv_all,
    att_t,
    log_row,
    grad_came,
    send,
):
    rows = (came.shape[1] - 16) * 2 // 3
    short_rows = rows - long_rows
    taps_q, taps_kv = head_taps(place, came, rows, seqs)
    b = place[0] % seqs
    e = place[0] // seqs
    grads = [unfold(grad_came[j]) for j in range(8)]
    first = 0
    terms_q = [0.0, 0.0, 0.0]
    terms_kv = [0.0, 0.0, 0.0]
    results = []
    for lengths, part, (q_mixed, kv_mixed) in zip(
        (long_lengths, short_lengths),
        (slice(0, long_rows), slice(long_rows, rows)),
        own_pair(came, long_rows, rows),
    ):
        count = q_mixed.shape[0]
        block = min(256, count)
        length = lengths[b]
        at = slice(first, first + count)
        grad = jnp.concatenate([g[part] for g in grads], axis=0)
        q = q_all[at, :]
        kv = kv_all[at, :]
        kv_t = kv.astype(F32).T.astype(BF16)
        delta = jnp.sum(grad.astype(F32).T * att_t[:, at], axis=0, keepdims=True)
        log_total = log_row[:, at]
        k, v = kv[:, :HEAD_DIM], kv[:, HEAD_DIM:]
        k_t = kv_t[:HEAD_DIM, :]
        grad_q = None
        grad_kv = []
        for start in range(0, count, block):
            stop = start + block
            scores = dot(k[start:stop], q[start:], NT)
            key_pos = lax.broadcasted_iota(jnp.int32, scores.shape, 0)
            query_pos = lax.broadcasted_iota(jnp.int32, scores.shape, 1)
            allowed = jnp.logical_and(key_pos <= query_pos, key_pos + start < length)
            prob = jnp.where(allowed, jnp.exp(scores - log_total[:, start:]), 0.0)
            grad_prob = dot(v[start:stop], grad[start:], NT)
            grad_scores = (prob * (grad_prob - delta[:, start:])).astype(BF16)
            grad_k = dot(grad_scores, q[start:])
            grad_v = dot(prob.astype(BF16), grad[start:])
            grad_kv.append(jnp.concatenate([grad_k, grad_v], axis=1))
            part_q = dot(k_t[:, start:stop], grad_scores)
            if start == 0:
                grad_q = part_q
            else:
                grad_q = jnp.concatenate(
                    [grad_q[:, :start], grad_q[:, start:] + part_q], axis=1
                )
        grad_q = grad_q.T * HEAD_DIM ** (-0.5)
        grad_kv = jnp.concatenate(grad_kv, axis=0)
        pair = []
        for grad_conv, mixed, taps, terms in (
            (grad_q, q_mixed, taps_q, terms_q),
            (grad_kv, kv_mixed, taps_kv, terms_kv),
        ):
            grad_mixed = 0.0
            for m in range(3):
                ahead = grad_conv if m == 0 else shift_ahead(grad_conv, m)
                terms[m] = terms[m] + jnp.sum(ahead * mixed, axis=0, keepdims=True)
                grad_mixed = grad_mixed + taps[m] * ahead
            pair.append(grad_mixed.astype(BF16))
        results.append(pair)
        first += count
    table = jnp.concatenate(
        terms_q
        + [t[:, :HEAD_DIM] for t in terms_kv]
        + [t[:, HEAD_DIM:] for t in terms_kv]
        + [jnp.zeros((7, HEAD_DIM), F32)],
        axis=0,
    )
    table = jnp.concatenate([jnp.where(e == i, table, 0.0) for i in range(3)], axis=1)
    width = 3 * HEAD_DIM // 8
    for j in range(8):
        mine = [
            jnp.concatenate(
                [
                    results[0][i][j * long_rows : (j + 1) * long_rows],
                    results[1][i][j * short_rows : (j + 1) * short_rows],
                ],
                axis=0,
            )
            for i in range(2)
        ]
        send[j, :rows, :] = mine[1]
        send[j, rows : rows + rows // 2, :] = fold(mine[0])
        send[j, rows + rows // 2 :, :] = jnp.concatenate(
            [table[:, j * width : (j + 1) * width], jnp.zeros((16, LANES - width), F32)], axis=1
        ).astype(BF16)


def place_grad_mixed(came, grad_mixed):
    seqs = 2
    rows = (came.shape[1] - 16) * 2 // 3
    for e in range(3):
        for b in range(seqs):
            j = seqs * e + b
            at = slice(b * rows, (b + 1) * rows)
            lanes = slice(e * HEAD_DIM, (e + 1) * HEAD_DIM)
            grad_mixed[0, at, lanes] = unfold(came[j, rows : rows + rows // 2, :])
            grad_mixed[1, at, lanes] = came[j, :rows, :HEAD_DIM]
            grad_mixed[2, at, lanes] = came[j, :rows, HEAD_DIM:]


def project_back_body(
    place, came, normed, weight, keep_p, send_p, keep, send, taps, scratch, grad_mixed, blocks
):
    place_grad_mixed(came, grad_mixed)
    shard = normed.shape[1] // 8
    terms = [dot(normed[...], grad_mixed[c], TN).astype(BF16) for c in range(3)]
    for s in range(8):
        at = slice(s * shard, (s + 1) * shard)
        for c in range(3):
            blocks[s, c * shard : (c + 1) * shard, :] = terms[c][at, :LANES]
        blocks[s, 3 * shard :, :] = fold(
            jnp.concatenate([terms[c][at, LANES:] for c in range(3)], axis=0)
        )
    split_y(place, blocks, keep_p, send_p)
    rows = (came.shape[1] - 16) * 2 // 3
    total = came[0, rows + rows // 2 :, :].astype(F32)
    for j in range(1, 6):
        total = total + came[j, rows + rows // 2 :, :].astype(F32)
    taps[...] = total[: taps.shape[0], : taps.shape[1]]
    total = dot(grad_mixed[0], weight[0], NT)
    for c in (1, 2):
        total = total + dot(grad_mixed[c], weight[c], NT)
    scratch[...] = total.astype(BF16)
    split_halves(place, scratch, keep, send)


def input_grad_body(
    place, own, other, grad_mid, gain, long_in, short_in, long_out, short_out, scratch
):
    join_halves(place, scratch, own, other)
    seqs, long_rows, _ = long_in.shape
    rows = long_rows + short_in.shape[1]
    for b in range(seqs):
        at = slice(b * rows, (b + 1) * rows)
        values = jnp.concatenate([long_in[b], short_in[b]], axis=0).astype(F32)
        weighted = scratch[at, :] * gain[...]
        root = lax.rsqrt(jnp.mean(values * values, axis=-1, keepdims=True) + norm_eps)
        inner = jnp.mean(weighted * values, axis=-1, keepdims=True)
        grad = grad_mid[at, :] + (root * weighted - values * (root * root * root * inner))
        long_out[b] = grad[:long_rows]
        short_out[b] = grad[long_rows:]


def output_body(place, own, other, mid, long_out, short_out, scratch):
    join_halves(place, scratch, own, other)
    seqs, long_rows, _ = long_out.shape
    rows = long_rows + short_out.shape[1]
    for b in range(seqs):
        at = slice(b * rows, (b + 1) * rows)
        value = (mid[at, :] + scratch[at, :]).astype(BF16)
        long_out[b] = value[:long_rows]
        short_out[b] = value[long_rows:]


def scatter_z_body(place, *refs):
    count = (len(refs) - 4) // 2
    outs = refs[2 * count :]
    z = place[0] // 2
    for i in range(4):
        block = jnp.bitwise_xor(z, i)
        first = 0
        for a in range(count):
            keep, came = refs[2 * a], refs[2 * a + 1]
            rows = keep.shape[1]
            outs[i][first : first + rows, :] = (
                keep[block].astype(F32) + came[block].astype(F32)
            ).astype(BF16)
            first += rows


def near_body(place, *refs):
    pairs = len(refs[:-3]) // 2
    near, own, across = refs[-3:]
    z = place[0] // 2
    for i, target in ((0, own), (1, near.at[0]), (2, across), (3, near.at[1])):
        block = jnp.bitwise_xor(z, i)
        first = 0
        for p in range(pairs):
            keep, came = refs[2 * p], refs[2 * p + 1]
            rows = keep.shape[1]
            target[first : first + rows, :] = (
                keep[block].astype(F32) + came[block].astype(F32)
            ).astype(BF16)
            first += rows


def across_body(across, near, out):
    out[...] = (across[...].astype(F32) + near[1].astype(F32)).astype(BF16)


def sum_blocks(blocks):
    return (blocks[0][...].astype(F32) + blocks[1][...].astype(F32)) + (
        blocks[2][...].astype(F32) + blocks[3][...].astype(F32)
    )


def proj_grad_body(b0, b1, b2, b3, proj, gain, grad, gain_grad):
    total = sum_blocks((b0, b1, b2, b3))
    rows = proj.shape[1]
    column = 0.0
    for c, (wide, narrow) in enumerate(unpack_blocks(total, rows, 3)):
        term = jnp.concatenate([wide, narrow], axis=1)
        column = column + jnp.sum(term * proj[c].astype(F32), axis=1, keepdims=True)
        grad[c] = term
    gain_grad[...] = column.T / gain[...].astype(F32).reshape(1, rows)


def ffn_grad_body(
    own, near, across, down_keep, down_came, up, gain, up_grad, down_grad, out_grad, gain_grad
):
    rows = up.shape[0]
    total = own[...].astype(F32) + near[0].astype(F32) + across[...].astype(F32)
    raw = total[:rows]
    gain_grad[...] = jnp.sum(raw * up[...].astype(F32), axis=1, keepdims=True).T
    up_grad[...] = raw * gain[...].astype(F32).reshape(1, rows).T
    down_grad[...] = down_keep[...].astype(F32) + down_came[...].astype(F32)
    wide = total[rows : rows + 16]
    narrow = total[rows + 16 :]
    out = jnp.concatenate(
        [
            jnp.concatenate(
                [
                    wide[:, LANES * g : LANES * (g + 1)],
                    narrow[:, LANES * g : LANES * g + HEAD_DIM],
                ],
                axis=1,
            )
            for g in range(rows // 16)
        ],
        axis=0,
    )
    out_grad[...] = out.T


def pair_shards(
    short_input,
    long_input,
    short_cotangent,
    long_cotangent,
    short_lengths,
    long_lengths,
    proj_weight,
    out_weight,
    conv_taps,
    attention_gain,
    up_weight,
    down_weight,
    feed_gain,
):
    seqs, long_rows, width = long_input.shape
    short_rows = short_input.shape[1]
    rows = long_rows + short_rows
    tokens = seqs * rows
    shard = proj_weight.shape[1]
    local = proj_weight.shape[2]
    hidden = up_weight.shape[1]
    long_len, short_len = 8 * long_rows, 8 * short_rows
    total_len = long_len + short_len
    place = jnp.stack([lax.axis_index("seq"), lax.axis_index("head")]).astype(jnp.int32)
    packed_rows = shard * 9 // 2
    chunk = rows + rows // 2 + 16
    down_t = down_weight.T

    (proj_packed,) = in_vmem(
        pack_proj_body,
        [((packed_rows + 16, LANES), BF16)],
        (),
        far(proj_weight, attention_gain),
    )
    (out_packed,) = in_vmem(pack_out_body, [((32, hidden), BF16)], (), far(out_weight))
    out_packed_x = exchange(out_packed, "head", 2)
    (ffn_packed,) = in_vmem(
        pack_ffn_body,
        [((2 * shard + 48, hidden), BF16)],
        (),
        far(up_weight, down_t) + (out_packed, out_packed_x) + far(feed_gain),
    )
    proj_z = [proj_packed] + [exchange(proj_packed, "seq", mask) for mask in (2, 4, 6)]
    proj_parts = [proj_packed, exchange(after(proj_packed, ffn_packed), "seq", 1)]
    proj_parts += [proj_z[1], exchange(proj_z[1], "seq", 1)]
    proj_parts += [proj_z[2], exchange(proj_z[2], "seq", 1)]
    proj_parts += [proj_z[3], exchange(proj_z[3], "seq", 1)]
    ffn_0 = after(ffn_packed, *proj_z)
    ffn_1 = exchange(ffn_0, "seq", 1)
    ffn_2 = exchange(ffn_0, "seq", 2)
    ffn_4 = exchange(ffn_0, "seq", 4)
    send, normed, proj_full, gain = in_vmem(
        project_body,
        [
            ((8, chunk, LANES), BF16),
            ((tokens, width), BF16, "far"),
            ((3, width, local), BF16, "far"),
            ((1, width), F32, "far"),
        ],
        (place,),
        (*proj_parts, *far(long_input, short_input, conv_taps)),
        scratch=[((8, LANES), F32)],
        fence=True,
    )
    came = lax.all_to_all(send, "seq", 0, 0, tiled=True)
    across_z = marker(ffn_4, ffn_1, send)
    ffn_2 = after(ffn_2, across_z)
    ffn_4 = after(ffn_4, across_z)
    ffn_6 = exchange(ffn_4, "seq", 2)
    ffn_3 = exchange(ffn_2, "seq", 1)
    ffn_5 = exchange(ffn_4, "seq", 1)
    att_send, q_all, kv_all, att_t, log_row, mixed = in_vmem(
        functools.partial(attend_body, long_rows, seqs),
        [
            ((8, rows // 2, LANES), BF16),
            ((total_len, HEAD_DIM), BF16, "far"),
            ((total_len, 2 * HEAD_DIM), BF16, "far"),
            ((HEAD_DIM, total_len), F32, "far"),
            ((1, total_len), F32, "far"),
            ((8, chunk, LANES), BF16, "far"),
        ],
        (place, long_lengths, short_lengths),
        (came,),
        fence=True,
    )
    att_0 = lax.all_to_all(att_send, "seq", 0, 0, tiled=True)
    ffn_7 = exchange(ffn_6, "seq", 1)
    up_full, down_full, out_full, out_now, out_x = in_vmem(
        place_ffn_body,
        [((width, hidden), BF16, "far")] * 2
        + [((width, local), BF16, "far"), ((width, local), BF16), ((width, local), BF16)],
        (place,),
        far(after(ffn_packed, att_send), ffn_1, ffn_2, ffn_3, ffn_4, ffn_5, ffn_6, ffn_7),
    )
    att_0 = after(att_0, out_full)
    att_x = exchange(att_0, "head", 2)
    att, own = in_vmem(
        out_proj_body,
        [((tokens, local), BF16, "far"), ((tokens, width), BF16)],
        (),
        (att_0, att_x, out_now, out_x),
        fence=True,
    )
    other = exchange(own, "head", 1)
    mid, squared, grad_out, keep, send, normed_ffn, grad_up = in_vmem(
        functools.partial(feed_body, long_rows),
        [
            ((tokens, width), F32, "far"),
            ((tokens, hidden), BF16, "far"),
            ((tokens, width), BF16, "far"),
            ((tokens // 2, width), BF16),
            ((tokens // 2, width), BF16),
            ((tokens, width), BF16, "far"),
            ((tokens, hidden), BF16, "far"),
        ],
        (place, long_lengths, short_lengths),
        (own, other)
        + far(long_input, short_input, long_cotangent, short_cotangent, up_full, down_full),
        scratch=[
            ((tokens, width), BF16),
            ((tokens, width), F32),
        ],
        limit_mib=32,
    )
    half = add_low(keep, exchange(send, "head", 1))
    down_near, down_own, down_across, f_keep, f_send, up_keep, up_send = in_vmem(
        down_term_body,
        [((2, 2, shard, hidden), BF16, "far")]
        + [((2, shard, hidden), BF16, "far")] * 2
        + [((tokens // 2, width), BF16, "far")] * 2
        + [((4, shard, hidden), BF16, "far")] * 2,
        (place,),
        far(after(squared, half), grad_out, down_full, normed_ffn, grad_up),
        scratch=[
            ((tokens, width), BF16),
            ((8, shard, hidden), BF16),
        ],
        limit_mib=32,
        fence=True,
    )
    down_near = exchange(down_near, "seq", 2)
    up_came = exchange(up_send, "seq", 1)
    own = add_low(half, after(exchange(half, "head", 2), f_send))
    other = exchange(own, "head", 1)
    grad_mid, send, out_keep, out_send = in_vmem(
        middle_body,
        [
            ((tokens, width), F32, "far"),
            ((8, rows // 2, LANES), BF16),
            ((4, 32, hidden), BF16, "far"),
            ((4, 32, hidden), BF16, "far"),
        ],
        (place,),
        (own, other) + far(mid, grad_out, out_full, att),
        scratch=[((tokens, width), F32), ((tokens, width), BF16), ((8, 32, hidden), BF16)],
    )
    grad_came = lax.all_to_all(send, "seq", 0, 0, tiled=True)
    out_came = exchange(out_send, "seq", 1)
    (down_across,) = in_vmem(
        down_across_body,
        [((2, shard, hidden), BF16, "far")],
        (),
        far(after(down_across, send, up_came), down_near),
        fence=True,
    )
    grad_came = after(grad_came, down_across)
    down_across = exchange(down_across, "seq", 4)
    f_half = add_low(f_keep, exchange(after(f_send, send), "head", 1))
    f_own = add_low(f_half, exchange(f_half, "head", 2))
    f_other = exchange(f_own, "head", 1)
    long_output, short_output = in_vmem(
        output_body,
        [(long_input.shape, BF16), (short_input.shape, BF16)],
        (place,),
        (f_own, f_other) + far(mid),
        scratch=[((tokens, width), F32)],
    )
    (send,) = in_vmem(
        functools.partial(attend_back_body, long_rows, seqs),
        [((8, chunk, LANES), BF16)],
        (place, long_lengths, short_lengths),
        far(mixed, q_all, kv_all, att_t, log_row) + (grad_came,),
        fence=True,
    )
    mixed_came = lax.all_to_all(send, "seq", 0, 0, tiled=True)
    near, ffn_own, across = in_vmem(
        near_body,
        [((2, shard + 32, hidden), BF16, "far")] + [((shard + 32, hidden), BF16, "far")] * 2,
        (place,),
        far(up_keep, after(up_came, send), out_keep, out_came),
        fence=True,
    )
    near = exchange(near, "seq", 2)
    down_keep, down_send = in_vmem(
        down_y_body,
        [((shard, hidden), BF16, "far")] * 2,
        (place,),
        far(after(down_own, ffn_own), down_near, down_across),
    )
    down_came = exchange(down_send, "seq", 1)
    mixed_came = after(mixed_came, long_output, down_send)
    proj_keep, proj_send, keep, send, taps_grad = in_vmem(
        project_back_body,
        [
            ((4, packed_rows, LANES), BF16, "far"),
            ((4, packed_rows, LANES), BF16),
            ((tokens // 2, width), BF16),
            ((tokens // 2, width), BF16),
            (conv_taps.shape, F32),
        ],
        (place,),
        (mixed_came,) + far(normed, proj_full),
        scratch=[
            ((tokens, width), BF16),
            ((3, tokens, local), BF16),
            ((8, packed_rows, LANES), BF16),
        ],
        fence=True,
    )
    proj_came = exchange(proj_send, "seq", 1)
    half = add_low(keep, exchange(send, "head", 1))
    (across,) = in_vmem(
        across_body, [((shard + 32, hidden), BF16, "far")], (), far(across, near)
    )
    across = exchange(across, "seq", 4)
    own = add_low(half, after(exchange(half, "head", 2), proj_came))
    other = exchange(own, "head", 1)
    proj_blocks = in_vmem(
        scatter_z_body,
        [((packed_rows, LANES), BF16)] * 4,
        (place,),
        far(proj_keep) + (proj_came,),
        fence=True,
    )
    proj_blocks = [proj_blocks[0]] + [exchange(proj_blocks[i], "seq", 2 * i) for i in (1, 2, 3)]
    up_grad, down_grad, out_grad, feed_part = in_vmem(
        ffn_grad_body,
        [
            (up_weight.shape, F32),
            (down_t.shape, F32),
            (out_weight.shape, F32),
            ((1, shard), F32),
        ],
        (),
        far(after(ffn_own, proj_blocks[0]), near, across, down_keep, down_came, up_weight)
        + (feed_gain,),
    )
    proj_blocks[3] = after(proj_blocks[3], up_grad)
    proj_grad, attention_part = in_vmem(
        proj_grad_body,
        [(proj_weight.shape, F32), ((1, shard), F32)],
        (),
        (*proj_blocks, *far(proj_weight), attention_gain),
    )
    long_input_grad, short_input_grad = in_vmem(
        input_grad_body,
        [(long_input.shape, F32), (short_input.shape, F32)],
        (place,),
        (own, other) + far(after(grad_mid, attention_part), gain, long_input, short_input),
        scratch=[((tokens, width), F32)],
    )
    gains = jnp.concatenate([attention_part, feed_part], axis=0)
    gains = gains + exchange(gains, "head", 1)
    gains = gains + after(exchange(gains, "head", 2), long_input_grad)

    return (
        short_output,
        long_output,
        short_input_grad,
        long_input_grad,
        proj_grad,
        out_grad,
        taps_grad,
        gains[0],
        up_grad,
        down_grad.T,
        gains[1],
    )


def fits_pairs(short_input, long_input, proj_weight):
    seqs, long_rows, _ = long_input.shape
    short_seqs, short_rows, _ = short_input.shape
    return (
        lax.axis_size("seq") == 8
        and lax.axis_size("head") == 4
        and seqs == 2
        and short_seqs == 2
        and proj_weight.shape[2] == 3 * HEAD_DIM
        and proj_weight.shape[1] % 32 == 0
        and long_rows % 32 == 0
        and short_rows % 32 == 0
        and 8 * long_rows <= 2048
    )


def shards(short_input, long_input, *rest):
    proj_weight = rest[4]
    if fits_pairs(short_input, long_input, proj_weight):
        return pair_shards(short_input, long_input, *rest)
    return ring_shards(short_input, long_input, *rest)


def solution(mesh):
    placed = (
        P(None, "seq", None),
        P(None, "seq", None),
        P(None, "seq", None),
        P(None, "seq", None),
        P(),
        P(),
        P(None, "seq", "head"),
        P("head", "seq"),
        P(None, ("head", "seq")),
        P("seq"),
        P("seq", "head"),
        P("head", "seq"),
        P("seq"),
    )
    return jax.shard_map(
        shards,
        mesh=mesh,
        in_specs=placed,
        out_specs=(
            P(None, "seq", None),
            P(None, "seq", None),
            P(None, "seq", None),
            P(None, "seq", None),
            P(None, "seq", "head"),
            P("head", "seq"),
            P(None, ("head", "seq")),
            P("seq"),
            P("seq", "head"),
            P("head", "seq"),
            P("seq"),
        ),
        check_vma=False,
    )
```

```python
import functools

import jax
import jax.numpy as jnp
import numpy as np
from jax import lax
from jax.experimental import pallas as pl
from jax.experimental.pallas import tpu as pltpu
from jax.sharding import PartitionSpec as P

HEAD_DIM = 64


norm_eps = 1e-06
mask_fill = -1e30
block_limit = 2048


def passed_along(block, axis, distance):
    devices = range(lax.axis_size(axis))
    route = [((i - distance) % len(devices), i) for i in devices]
    return lax.ppermute(block, axis, route)


def shifted(array, axis, by):
    peers = lax.axis_size(axis)
    pairs = [(i, i + by) for i in range(peers) if 0 <= i + by < peers]
    return lax.ppermute(array, axis, pairs)


def block_rows(row_count):
    size_rows = min(row_count, block_limit)
    while row_count % size_rows != 0:
        size_rows = size_rows - 1
    return size_rows


def norm_forward(values_in, gain_row):
    inv_root = lax.rsqrt(jnp.mean(values_in * values_in, axis=-1, keepdims=True) + norm_eps)
    return (values_in * inv_root * gain_row, inv_root)


def norm_backward(values_in, inv_root, gain_row, grad_in):
    weighted = grad_in * gain_row
    inner_mean = jnp.mean(weighted * values_in, axis=-1, keepdims=True)
    grad_values = inv_root * weighted - values_in * inv_root * inv_root * inv_root * inner_mean
    grad_gain = jnp.sum(grad_in * values_in * inv_root, axis=(0, 1))
    return (grad_values, grad_gain)


def allowed_mask(query_pos, key_pos, lengths):
    causal = key_pos[None, :] <= query_pos[:, None]
    inside = key_pos[None, :] < lengths[:, None]
    return jnp.logical_and(causal[None, None], inside[:, None, None, :])


def block_scores(query_rows, key_rows, query_pos, key_pos, lengths):
    allowed = allowed_mask(query_pos, key_pos, lengths)
    raw_scores = jnp.einsum(
        "bqhe,bkhe->bhqk", query_rows, key_rows, preferred_element_type=jnp.float32
    ) * HEAD_DIM ** (-0.5)
    return (jnp.where(allowed, raw_scores, mask_fill), allowed)


def block_grads(
    query_rows, grad_rows, log_rows, delta_rows, key_rows, value_rows, query_pos, key_pos, lengths
):
    scores, allowed = block_scores(query_rows, key_rows, query_pos, key_pos, lengths)
    prob_rows = jnp.where(
        allowed, jnp.exp(scores - jnp.transpose(log_rows, (0, 2, 1))[..., None]), 0.0
    )
    grad_probs = jnp.einsum(
        "bqhe,bkhe->bhqk", grad_rows, value_rows, preferred_element_type=jnp.float32
    )
    grad_scores = (
        prob_rows * (grad_probs - jnp.transpose(delta_rows, (0, 2, 1))[..., None])
    ).astype(jnp.bfloat16)
    grad_query = jnp.einsum(
        "bhqk,bkhe->bqhe", grad_scores, key_rows, preferred_element_type=jnp.float32
    ) * HEAD_DIM ** (-0.5)
    grad_key = jnp.einsum(
        "bhqk,bqhe->bkhe", grad_scores, query_rows, preferred_element_type=jnp.float32
    ) * HEAD_DIM ** (-0.5)
    grad_value = jnp.einsum(
        "bhqk,bqhe->bkhe",
        prob_rows.astype(jnp.bfloat16),
        grad_rows,
        preferred_element_type=jnp.float32,
    )
    return (grad_query, grad_key, grad_value)


def attend_forward(queries, keys_here, values_here, query_pos, lengths):
    seq_count, span_rows, head_count, head_width = queries.shape
    initial = (
        jnp.full((seq_count, head_count, span_rows), mask_fill, jnp.float32),
        jnp.zeros((seq_count, head_count, span_rows), jnp.float32),
        jnp.zeros((seq_count, span_rows, head_count, head_width), jnp.float32),
    )
    key_piece = lax.all_gather(keys_here, "seq", axis=1, tiled=True)
    value_piece = lax.all_gather(values_here, "seq", axis=1, tiled=True)
    row_count = key_piece.shape[1]
    size_rows = block_rows(row_count)

    def one_block(block_index, carried_state):
        running_top, running_sum, acc_rows = carried_state
        offset = block_index * size_rows
        key_rows = lax.dynamic_slice_in_dim(key_piece, offset, size_rows, 1)
        value_rows = lax.dynamic_slice_in_dim(value_piece, offset, size_rows, 1)
        key_pos = offset + jnp.arange(size_rows, dtype=jnp.int32)
        scores, allowed = block_scores(queries, key_rows, query_pos, key_pos, lengths)
        new_top = jnp.maximum(running_top, jnp.max(scores, axis=-1))
        exp_terms = jnp.where(allowed, jnp.exp(scores - new_top[..., None]), 0.0)
        shrink = jnp.exp(running_top - new_top)
        running_sum = running_sum * shrink + jnp.sum(exp_terms, axis=-1)
        acc_rows = acc_rows * jnp.transpose(shrink, (0, 2, 1))[..., None] + jnp.einsum(
            "bhqk,bkhe->bqhe",
            exp_terms.astype(jnp.bfloat16),
            value_rows,
            preferred_element_type=jnp.float32,
        )
        return (new_top, running_sum, acc_rows)

    running_top, running_sum, acc_rows = lax.fori_loop(
        0, row_count // size_rows, one_block, initial
    )
    attention = acc_rows / jnp.transpose(running_sum, (0, 2, 1))[..., None]
    log_totals = jnp.transpose(running_top + jnp.log(running_sum), (0, 2, 1))
    return (attention, log_totals)


def pass_sums(grad_keys, grad_values):
    return (
        passed_along(grad_keys.astype(jnp.bfloat16), "seq", 1).astype(grad_keys.dtype),
        passed_along(grad_values.astype(jnp.bfloat16), "seq", 1).astype(grad_values.dtype),
    )


def attend_backward(
    queries, keys_here, values_here, grad_attention, log_totals, delta_rows, query_pos, lengths
):
    seq_count, span_rows, head_count, head_width = queries.shape
    zeros_local = jnp.zeros(queries.shape, jnp.float32)
    seq_size = lax.axis_size("seq")
    my_index = lax.axis_index("seq")
    local_pos = jnp.arange(span_rows, dtype=jnp.int32)

    def step_grads(step, key_piece, value_piece):
        anchor = jnp.mod(my_index - step, seq_size)
        key_pos = anchor * span_rows + local_pos
        return block_grads(
            queries,
            grad_attention,
            log_totals,
            delta_rows,
            key_piece,
            value_piece,
            query_pos,
            key_pos,
            lengths,
        )

    def cycle_step(step, state):
        key_piece, value_piece, grad_keys, grad_values, grad_query = state
        query_part, key_part, value_part = step_grads(step, key_piece, value_piece)
        key_piece, value_piece = shifted((key_piece, value_piece), "seq", 1)
        grad_keys, grad_values = pass_sums(grad_keys + key_part, grad_values + value_part)
        return (key_piece, value_piece, grad_keys, grad_values, grad_query + query_part)

    final_state = lax.fori_loop(
        0, seq_size - 1, cycle_step, (keys_here, values_here, zeros_local, zeros_local, zeros_local)
    )
    key_piece, value_piece, grad_keys, grad_values, grad_query = final_state
    query_part, key_part, value_part = step_grads(seq_size - 1, key_piece, value_piece)
    grad_key, grad_value = pass_sums(grad_keys + key_part, grad_values + value_part)
    grad_query = grad_query + query_part
    return (grad_query, grad_key, grad_value)


def micro_batch(inputs, cotangent, lengths, weights):
    proj_full, out_full, taps_full, attend_gain, up_full, down_full, ffn_gain = weights
    seq_count, span_rows, model_width = inputs.shape
    local_width = proj_full.shape[2]
    heads_here = local_width // HEAD_DIM
    query_pos = lax.axis_index("seq") * span_rows + jnp.arange(span_rows, dtype=jnp.int32)
    valid_rows = (query_pos[None, :] < lengths[:, None])[..., None]
    residual_in = inputs.astype(jnp.float32)
    normed, inv_first = norm_forward(residual_in, attend_gain)
    normed_low = normed.astype(jnp.bfloat16)
    mixed_qkv = jnp.einsum(
        "btd,cde->cbte", normed_low, proj_full, preferred_element_type=jnp.float32
    ).astype(jnp.bfloat16)
    borrowed = shifted(mixed_qkv[:, :, span_rows - 2 :, :], "seq", 1)
    extended = jnp.concatenate([borrowed, mixed_qkv], axis=2).astype(jnp.float32)
    tap_table = taps_full.astype(jnp.float32).reshape(3, 3, local_width)
    tap_now = tap_table[:, 0][:, None, None, :]
    tap_one = tap_table[:, 1][:, None, None, :]
    tap_two = tap_table[:, 2][:, None, None, :]
    conved = (
        tap_now * extended[:, :, 2:]
        + tap_one * extended[:, :, 1:-1]
        + tap_two * extended[:, :, :-2]
    )
    conv_out = conved.astype(jnp.bfloat16).reshape(3, seq_count, span_rows, heads_here, HEAD_DIM)
    queries, keys_here, values_here = (conv_out[0], conv_out[1], conv_out[2])
    attention, log_totals = attend_forward(queries, keys_here, values_here, query_pos, lengths)
    attention_low = attention.astype(jnp.bfloat16).reshape(seq_count, span_rows, local_width)
    attend_part = jnp.einsum(
        "bte,ed->btd", attention_low, out_full, preferred_element_type=jnp.float32
    )
    mid_residual = residual_in + lax.psum(attend_part.astype(jnp.bfloat16), "head").astype(
        jnp.float32
    )
    normed_ffn, inv_second = norm_forward(mid_residual, ffn_gain)
    normed_ffn_low = normed_ffn.astype(jnp.bfloat16)
    up_proj = jnp.einsum("btd,df->btf", normed_ffn_low, up_full, preferred_element_type=jnp.float32)
    relu_up = jnp.maximum(up_proj, 0.0)
    squared = (relu_up * relu_up).astype(jnp.bfloat16)
    ffn_part = jnp.einsum("btf,fd->btd", squared, down_full, preferred_element_type=jnp.float32)
    output = (
        mid_residual + lax.psum(ffn_part.astype(jnp.bfloat16), "head").astype(jnp.float32)
    ).astype(jnp.bfloat16)
    grad_out = jnp.where(valid_rows, cotangent.astype(jnp.float32), 0.0)
    grad_out_low = grad_out.astype(jnp.bfloat16)
    down_term = jnp.einsum("btf,btd->fd", squared, grad_out_low, preferred_element_type=jnp.float32)
    grad_squared = jnp.einsum(
        "btd,fd->btf", grad_out_low, down_full, preferred_element_type=jnp.float32
    )
    grad_up = (grad_squared * 2.0 * relu_up).astype(jnp.bfloat16)
    up_term = jnp.einsum("btd,btf->df", normed_ffn_low, grad_up, preferred_element_type=jnp.float32)
    grad_normed_ffn = lax.psum(
        jnp.einsum("btf,df->btd", grad_up, up_full, preferred_element_type=jnp.float32).astype(
            jnp.bfloat16
        ),
        "head",
    ).astype(jnp.float32)
    grad_through, feed_term = norm_backward(mid_residual, inv_second, ffn_gain, grad_normed_ffn)
    grad_mid = grad_out + grad_through
    grad_mid_low = grad_mid.astype(jnp.bfloat16)
    out_term = jnp.einsum(
        "bte,btd->ed", attention_low, grad_mid_low, preferred_element_type=jnp.float32
    )
    grad_attention = jnp.einsum(
        "btd,ed->bte", grad_mid_low, out_full, preferred_element_type=jnp.float32
    )
    grad_attention = grad_attention.astype(jnp.bfloat16).reshape(
        seq_count, span_rows, heads_here, HEAD_DIM
    )
    delta_rows = jnp.einsum("bqhe,bqhe->bqh", grad_attention.astype(jnp.float32), attention)
    grad_query, grad_key, grad_value = attend_backward(
        queries, keys_here, values_here, grad_attention, log_totals, delta_rows, query_pos, lengths
    )
    grad_conv = jnp.stack([grad_query, grad_key, grad_value]).reshape(
        3, seq_count, span_rows, local_width
    )
    taps_term = jnp.stack(
        [
            jnp.sum(grad_conv * extended[:, :, 2:], axis=(1, 2)),
            jnp.sum(grad_conv * extended[:, :, 1:-1], axis=(1, 2)),
            jnp.sum(grad_conv * extended[:, :, :-2], axis=(1, 2)),
        ],
        axis=1,
    ).reshape(9, local_width)
    full_grad = jnp.pad(grad_conv, ((0, 0), (0, 0), (2, 2), (0, 0)))
    grad_extended = (
        tap_now * full_grad[:, :, 0 : span_rows + 2]
        + tap_one * full_grad[:, :, 1 : span_rows + 3]
        + tap_two * full_grad[:, :, 2 : span_rows + 4]
    )
    returned = shifted(grad_extended[:, :, :2], "seq", -1)
    grad_mixed = jnp.concatenate(
        [grad_extended[:, :, 2:span_rows], grad_extended[:, :, span_rows:] + returned], axis=2
    ).astype(jnp.bfloat16)
    proj_term = jnp.einsum(
        "btd,cbte->cde", normed_low, grad_mixed, preferred_element_type=jnp.float32
    )
    grad_normed = lax.psum(
        jnp.einsum(
            "cbte,cde->btd", grad_mixed, proj_full, preferred_element_type=jnp.float32
        ).astype(jnp.bfloat16),
        "head",
    ).astype(jnp.float32)
    grad_first, attention_term = norm_backward(residual_in, inv_first, attend_gain, grad_normed)
    grad_input = grad_mid + grad_first
    return (
        output,
        grad_input,
        (proj_term, out_term, taps_term, attention_term, up_term, down_term, feed_term),
    )


def ring_shards(
    short_input,
    long_input,
    short_cotangent,
    long_cotangent,
    short_lengths,
    long_lengths,
    proj_weight,
    out_weight,
    conv_taps,
    attention_gain,
    up_weight,
    down_weight,
    feed_gain,
):
    proj_full, out_full, taps_full, attend_gain = (
        lax.all_gather(proj_weight, "seq", axis=1, tiled=True),
        lax.all_gather(out_weight, "seq", axis=1, tiled=True),
        lax.all_gather(conv_taps, "seq", axis=1, tiled=True),
        lax.all_gather(attention_gain, "seq", axis=0, tiled=True),
    )
    up_full, down_full, ffn_gain = (
        lax.all_gather(up_weight, "seq", axis=0, tiled=True),
        lax.all_gather(down_weight, "seq", axis=1, tiled=True),
        lax.all_gather(feed_gain, "seq", axis=0, tiled=True),
    )
    weights = (
        proj_full,
        out_full,
        taps_full,
        attend_gain.astype(jnp.float32),
        up_full,
        down_full,
        ffn_gain.astype(jnp.float32),
    )
    short_output, short_input_grad, short_terms = micro_batch(
        short_input, short_cotangent, short_lengths, weights
    )
    long_output, long_input_grad, long_terms = micro_batch(
        long_input, long_cotangent, long_lengths, weights
    )
    summed = tuple(
        (first_term + second_term for first_term, second_term in zip(short_terms, long_terms))
    )
    reduced = (
        lax.psum_scatter(summed[0], "seq", scatter_dimension=1, tiled=True),
        lax.psum_scatter(summed[1], "seq", scatter_dimension=1, tiled=True),
        lax.psum_scatter(summed[2], "seq", scatter_dimension=1, tiled=True),
        lax.psum_scatter(summed[3], "seq", scatter_dimension=0, tiled=True),
        lax.psum_scatter(summed[4], "seq", scatter_dimension=0, tiled=True),
        lax.psum_scatter(summed[5], "seq", scatter_dimension=1, tiled=True),
        lax.psum_scatter(summed[6], "seq", scatter_dimension=0, tiled=True),
    )
    return (
        short_output,
        long_output,
        short_input_grad,
        long_input_grad,
        reduced[0],
        reduced[1],
        reduced[2],
        reduced[3],
        reduced[4],
        reduced[5],
        reduced[6],
    )


LANES = 128
FENCE = 10**11
NT = (((1,), (1,)), ((), ()))
TN = (((0,), (0,)), ((), ()))
F32 = jnp.float32
BF16 = jnp.bfloat16


def dot(a, b, dims=(((1,), (0,)), ((), ()))):
    return lax.dot_general(a, b, dims, preferred_element_type=F32)


def in_vmem(body, outs, scalars, arrays, scratch=(), limit_mib=16, fence=False):
    return pl.pallas_call(
        body,
        out_shape=[
            pltpu.HBM(*out[:2]) if len(out) == 3 else jax.ShapeDtypeStruct(*out) for out in outs
        ],
        in_specs=[pl.BlockSpec(memory_space=pltpu.SMEM)] * len(scalars)
        + [pl.BlockSpec(memory_space=pltpu.VMEM)] * len(arrays),
        out_specs=[pl.BlockSpec(memory_space=pltpu.VMEM)] * len(outs),
        scratch_shapes=[pltpu.VMEM(shape, kind) for shape, kind in scratch],
        compiler_params=pltpu.CompilerParams(vmem_limit_bytes=limit_mib * 1024 * 1024),
        cost_estimate=pl.CostEstimate(
            flops=FENCE if fence else 0, bytes_accessed=0, transcendentals=0
        ),
    )(*scalars, *arrays)


def far(*arrays):
    return tuple(pltpu.with_memory_space_constraint(array, pltpu.HBM) for array in arrays)


def after(array, *others):
    return lax.optimization_barrier((array, *others))[0]


def marker(*arrays):
    def body(*refs):
        refs[-1][...] = jnp.zeros_like(refs[-1])

    return pl.pallas_call(
        body,
        out_shape=jax.ShapeDtypeStruct((8, LANES), F32),
        in_specs=[pl.BlockSpec(memory_space=pl.ANY)] * len(arrays),
        out_specs=pl.BlockSpec(memory_space=pltpu.VMEM),
        cost_estimate=pl.CostEstimate(flops=FENCE, bytes_accessed=0, transcendentals=0),
    )(*arrays)


def exchange(array, axis, mask):
    size = lax.axis_size(axis)
    return lax.ppermute(array, axis, [(i, i ^ mask) for i in range(size)])


def add_low(a, b):
    return (a.astype(F32) + b.astype(F32)).astype(BF16)


def shift_back(rows, by):
    index = lax.broadcasted_iota(jnp.int32, rows.shape, 0)
    return jnp.where(index >= by, pltpu.roll(rows, by, axis=0), 0.0)


def shift_ahead(rows, by):
    count = rows.shape[0]
    index = lax.broadcasted_iota(jnp.int32, rows.shape, 0)
    return jnp.where(index < count - by, pltpu.roll(rows, count - by, axis=0), 0.0)


def fold(rows):
    half = rows.shape[0] // 2
    return jnp.concatenate([rows[:half], rows[half:]], axis=1)


def unfold(rows):
    return jnp.concatenate([rows[:, :HEAD_DIM], rows[:, HEAD_DIM:]], axis=0)


def pack_proj_body(proj, gain, packed):
    rows = proj.shape[1]
    for c in range(3):
        packed[c * rows : (c + 1) * rows, :] = proj[c, :, :LANES]
    narrow = jnp.concatenate([proj[c, :, LANES:] for c in range(3)], axis=0)
    packed[3 * rows : 9 * rows // 2, :] = fold(narrow)
    gain_row = gain[...].astype(F32).reshape(1, rows)
    gain_row = jnp.concatenate([gain_row, jnp.zeros((1, LANES - rows), F32)], axis=1)
    packed[9 * rows // 2 :, :] = jnp.broadcast_to(gain_row, (16, LANES)).astype(BF16)


def unpack_blocks(packed, rows, count):
    narrow = unfold(packed[count * rows : 3 * count * rows // 2, :])
    return [
        (packed[i * rows : (i + 1) * rows, :], narrow[i * rows : (i + 1) * rows, :])
        for i in range(count)
    ]


def narrow_pack(block, store):
    groups = block.shape[0] // 16
    for g in range(groups):
        rows = block[16 * g : 16 * g + 16, :]
        store(0, LANES * g, rows[:, :LANES])
        tail = rows[:, LANES:]
        store(16, LANES * g, jnp.concatenate([tail, jnp.zeros_like(tail)], axis=1))


def pack_out_body(out, packed):
    def store(row, lane, value):
        packed[row : row + 16, lane : lane + LANES] = value

    narrow_pack(out[...].astype(F32).T.astype(BF16), store)


def pack_ffn_body(up, down, out, out_x, gain, packed):
    rows = up.shape[0]
    gain_column = gain[...].astype(F32).reshape(1, rows).T
    packed[:rows, :] = (up[...].astype(F32) * gain_column).astype(BF16)
    packed[rows : 2 * rows, :] = down[...]
    packed[2 * rows : 2 * rows + 16, :] = out[:16, :]
    packed[2 * rows + 16 : 2 * rows + 32, :] = out_x[:16, :]
    for g in range(rows // 16):
        lanes = slice(LANES * g, LANES * g + HEAD_DIM)
        packed[2 * rows + 32 :, LANES * g : LANES * (g + 1)] = jnp.concatenate(
            [out[16:, lanes], out_x[16:, lanes]], axis=1
        )


def place_ffn_body(place, *refs):
    up, down, out, out_now, out_x = refs[8:]
    rows = out.shape[0] // 8
    for i in range(8):
        owner = jnp.bitwise_xor(place[0], i)
        part = refs[i]
        first = pl.ds(pl.multiple_of(owner * rows, rows), rows)
        up[first, :] = part[:rows, :]
        down[first, :] = part[rows : 2 * rows, :]
        for g in range(rows // 16):
            at = pl.ds(pl.multiple_of(owner * rows + 16 * g, 16), 16)
            lanes = slice(LANES * g, LANES * (g + 1))
            narrow = part[2 * rows + 32 :, lanes]
            out[at, :LANES] = part[2 * rows : 2 * rows + 16, lanes]
            out[at, LANES:] = narrow[:, :HEAD_DIM]
            out_x[at, :LANES] = part[2 * rows + 16 : 2 * rows + 32, lanes]
            out_x[at, LANES:] = narrow[:, HEAD_DIM:]
    out_now[...] = out[...]


def project_body(place, *refs):
    parts = refs[:8]
    long_in, short_in, taps, send, normed, weight, gain, gain_rows = refs[8:]
    seqs, long_rows, _ = long_in.shape
    rows = long_rows + short_in.shape[1]
    for i in range(8):
        packed = parts[i][...]
        shard = weight.shape[1] // 8
        owner = jnp.bitwise_xor(place[0], i)
        gain_rows[pl.ds(owner, 1), :] = packed[9 * shard // 2 :, :].astype(F32)[:1]
        at = pl.ds(pl.multiple_of(owner * shard, shard), shard)
        for c, (wide, narrow) in enumerate(unpack_blocks(packed, shard, 3)):
            weight[c, at, :LANES] = wide
            weight[c, at, LANES:] = narrow
    gain[...] = jnp.concatenate([gain_rows[j : j + 1, :shard] for j in range(8)], axis=1)
    for b in range(seqs):
        values = jnp.concatenate([long_in[b], short_in[b]], axis=0).astype(F32)
        root = lax.rsqrt(jnp.mean(values * values, axis=-1, keepdims=True) + norm_eps)
        normed[b * rows : (b + 1) * rows, :] = (values * root * gain[...]).astype(BF16)
    mixed = [dot(normed[...], weight[c]).astype(BF16) for c in range(3)]
    tap_rows = jnp.concatenate(
        [taps[...], jnp.zeros((16 - taps.shape[0], taps.shape[1]), BF16)], axis=0
    )
    tap_rows = jnp.concatenate(
        [tap_rows, jnp.zeros((16, LANES - taps.shape[1]), BF16)], axis=1
    )
    half = rows // 2
    for dest in range(8):
        if dest < 3 * seqs:
            e, b = dest // seqs, dest % seqs
            lanes = slice(e * HEAD_DIM, (e + 1) * HEAD_DIM)
            q, k, v = [m[b * rows : (b + 1) * rows, lanes] for m in mixed]
            send[dest, :rows, :] = jnp.concatenate([k, v], axis=1)
            send[dest, rows : rows + half, :] = fold(q)
        else:
            send[dest, : rows + half, :] = jnp.zeros((rows + half, LANES), BF16)
        send[dest, rows + half :, :] = tap_rows


def head_taps(place, came, rows, seqs):
    first = rows + rows // 2
    width = 3 * HEAD_DIM // 8
    whole = jnp.concatenate(
        [came[j, first:, :].astype(F32)[:, :width] for j in range(8)], axis=1
    )
    e = place[0] // seqs
    mine = whole[:, :HEAD_DIM]
    for other in (1, 2):
        mine = jnp.where(
            e == other, whole[:, other * HEAD_DIM : (other + 1) * HEAD_DIM], mine
        )
    taps_q = [mine[m : m + 1, :] for m in range(3)]
    taps_kv = [
        jnp.concatenate([mine[3 + m : 4 + m, :], mine[6 + m : 7 + m, :]], axis=1) for m in range(3)
    ]
    return taps_q, taps_kv


def own_pair(came, long_rows, rows):
    q_rows = [unfold(came[j, rows : rows + rows // 2, :]) for j in range(8)]
    result = []
    for part in (slice(0, long_rows), slice(long_rows, rows)):
        q = jnp.concatenate([piece[part] for piece in q_rows], axis=0).astype(F32)
        kv = jnp.concatenate([came[j, part, :] for j in range(8)], axis=0).astype(F32)
        result.append((q, kv))
    return result


def convolve(rows, taps):
    return taps[0] * rows + taps[1] * shift_back(rows, 1) + taps[2] * shift_back(rows, 2)


def attend_body(
    long_rows, seqs, place, long_lengths, short_lengths, came, send, q_all, kv_all, att_t, log_row, kept
):
    rows = (came.shape[1] - 16) * 2 // 3
    kept[...] = came[...]
    taps_q, taps_kv = head_taps(place, came, rows, seqs)
    b = place[0] % seqs
    first = 0
    results = []
    for lengths, (q_mixed, kv_mixed) in zip(
        (long_lengths, short_lengths), own_pair(came, long_rows, rows)
    ):
        count = q_mixed.shape[0]
        block = min(256, count)
        length = lengths[b]
        q = (convolve(q_mixed, taps_q).astype(BF16).astype(F32) * HEAD_DIM ** (-0.5)).astype(BF16)
        kv = convolve(kv_mixed, taps_kv).astype(BF16)
        kv_t = kv.astype(F32).T.astype(BF16)
        q_all[first : first + count, :] = q
        kv_all[first : first + count, :] = kv
        k = kv[:, :HEAD_DIM]
        v_t = kv_t[HEAD_DIM:, :]
        pieces = []
        for start in range(0, count, block):
            stop = start + block
            scores = dot(k[:stop], q[start:stop], NT)
            key_pos = lax.broadcasted_iota(jnp.int32, scores.shape, 0)
            query_pos = lax.broadcasted_iota(jnp.int32, scores.shape, 1) + start
            allowed = jnp.logical_and(key_pos <= query_pos, key_pos < length)
            scores = jnp.where(allowed, scores, mask_fill)
            top = jnp.max(scores, axis=0, keepdims=True)
            terms = jnp.exp(scores - top)
            total = jnp.sum(terms, axis=0, keepdims=True)
            out_t = dot(v_t[:, :stop], terms.astype(BF16)) / total
            att_t[:, first + start : first + stop] = out_t
            log_row[:, first + start : first + stop] = top + jnp.log(total)
            pieces.append(out_t.T.astype(BF16))
        results.append(jnp.concatenate(pieces, axis=0))
        first += count
    short_rows = rows - long_rows
    for j in range(8):
        mine = jnp.concatenate(
            [
                results[0][j * long_rows : (j + 1) * long_rows],
                results[1][j * short_rows : (j + 1) * short_rows],
            ],
            axis=0,
        )
        send[j, :, :] = fold(mine)


def pair_rows(came, seqs):
    columns = []
    for e in range(3):
        columns.append(
            jnp.concatenate([unfold(came[seqs * e + b]) for b in range(seqs)], axis=0)
        )
    return jnp.concatenate(columns, axis=1)


def out_proj_body(came, came_x, out, out_x, att, part):
    att[...] = pair_rows(came, 2)
    total = dot(att[...], out[...], NT)
    part[...] = (total + dot(pair_rows(came_x, 2), out_x[...], NT)).astype(BF16)


def feed_body(
    long_rows,
    place,
    long_lengths,
    short_lengths,
    own,
    other,
    long_in,
    short_in,
    long_cot,
    short_cot,
    up,
    down,
    mid_ref,
    squared_ref,
    grad_out_ref,
    keep,
    send,
    normed_ref,
    grad_up_ref,
    scratch,
    attended,
):
    seqs = long_in.shape[0]
    rows = long_rows + short_in.shape[1]
    attended[...] = own[...].astype(F32) + other[...].astype(F32)
    for b in range(seqs):
        at = slice(b * rows, (b + 1) * rows)
        residual = jnp.concatenate([long_in[b], short_in[b]], axis=0).astype(F32)
        mid = residual + attended[at, :]
        mid_ref[at, :] = mid
        root = lax.rsqrt(jnp.mean(mid * mid, axis=-1, keepdims=True) + norm_eps)
        normed_ref[at, :] = (mid * root).astype(BF16)
        for cot, lengths, first, count in (
            (long_cot, long_lengths, b * rows, long_rows),
            (short_cot, short_lengths, b * rows + long_rows, rows - long_rows),
        ):
            value = cot[b]
            position = lax.broadcasted_iota(jnp.int32, value.shape, 0) + place[0] * count
            grad_out_ref[first : first + count, :] = jnp.where(
                position < lengths[b], value.astype(F32), 0.0
            ).astype(BF16)
    relu = jnp.maximum(dot(normed_ref[...], up[...]), 0.0)
    squared_ref[...] = (relu * relu).astype(BF16)
    grad_squared = dot(grad_out_ref[...], down[...])
    grad_up_ref[...] = (grad_squared * 2.0 * relu).astype(BF16)
    scratch[...] = dot(grad_up_ref[...], up[...], NT).astype(BF16)
    split_halves(place, scratch, keep, send)


def split_halves(place, whole, keep, send):
    half = whole.shape[0] // 2
    core = place[1] % 2
    keep[...] = whole[pl.ds(pl.multiple_of(core * half, half), half), :]
    send[...] = whole[pl.ds(pl.multiple_of((1 - core) * half, half), half), :]


def join_halves(place, whole, own, other):
    half = own.shape[0]
    core = place[1] % 2
    whole[pl.ds(pl.multiple_of(core * half, half), half), :] = own[...].astype(whole.dtype)
    whole[pl.ds(pl.multiple_of((1 - core) * half, half), half), :] = other[...].astype(whole.dtype)


def split_y(place, blocks, keep, send):
    y = place[0] % 2
    for z in range(4):
        keep[z] = blocks[2 * z + y]
        send[z] = blocks[2 * z + 1 - y]


def down_term_body(
    place,
    squared,
    grad_out,
    down,
    normed,
    grad_up,
    near,
    own,
    across,
    f_keep,
    f_send,
    up_keep,
    up_send,
    scratch,
    blocks,
):
    rows = blocks.shape[1]
    term = dot(normed[...], grad_up[...], TN).astype(BF16)
    for s in range(8):
        blocks[s] = term[s * rows : (s + 1) * rows]
    split_y(place, blocks, up_keep, up_send)
    term = dot(grad_out[...], squared[...], TN).astype(BF16)
    for s in range(8):
        blocks[s] = term[s * rows : (s + 1) * rows]
    z = place[0] // 2
    for i, target in ((0, own), (1, near.at[0]), (2, across), (3, near.at[1])):
        for y in range(2):
            target[y] = blocks[2 * jnp.bitwise_xor(z, i) + y]
    scratch[...] = dot(squared[...], down[...], NT).astype(BF16)
    split_halves(place, scratch, f_keep, f_send)


def down_across_body(across, near, out):
    out[...] = (across[...].astype(F32) + near[1].astype(F32)).astype(BF16)


def down_y_body(place, own, near, across, keep, send):
    y = place[0] % 2
    for target, block in ((keep, y), (send, 1 - y)):
        target[...] = (
            own[block].astype(F32) + near[0, block].astype(F32) + across[block].astype(F32)
        ).astype(BF16)


def middle_body(
    place, own, other, mid_ref, grad_out, out, att, grad_mid_ref, send, keep_out, send_out, scratch, low_ref, blocks
):
    join_halves(place, scratch, own, other)
    seqs = 2
    rows = mid_ref.shape[0] // seqs
    for b in range(seqs):
        at = slice(b * rows, (b + 1) * rows)
        mid = mid_ref[at, :]
        weighted = scratch[at, :]
        root = lax.rsqrt(jnp.mean(mid * mid, axis=-1, keepdims=True) + norm_eps)
        inner = jnp.mean(weighted * mid, axis=-1, keepdims=True)
        grad_mid = grad_out[at, :].astype(F32) + (
            root * weighted - mid * (root * root * root * inner)
        )
        grad_mid_ref[at, :] = grad_mid
        low_ref[at, :] = grad_mid.astype(BF16)
    grad_att = dot(low_ref[...], out[...]).astype(BF16)
    for dest in range(8):
        if dest < 3 * seqs:
            e, b = dest // seqs, dest % seqs
            send[dest] = fold(
                grad_att[b * rows : (b + 1) * rows, e * HEAD_DIM : (e + 1) * HEAD_DIM]
            )
        else:
            send[dest] = jnp.zeros_like(send[dest])
    term = dot(low_ref[...], att[...], TN).astype(BF16)
    shard = term.shape[0] // 8
    for s in range(8):

        def store(row, lane, value):
            blocks[s, row : row + 16, lane : lane + LANES] = value

        narrow_pack(term[s * shard : (s + 1) * shard], store)
    split_y(place, blocks, keep_out, send_out)


def attend_back_body(
    long_rows,
    seqs,
    place,
    long_lengths,
    short_lengths,
    came,
    q_all,
    kv_all,
    att_t,
    log_row,
    grad_came,
    send,
):
    rows = (came.shape[1] - 16) * 2 // 3
    short_rows = rows - long_rows
    taps_q, taps_kv = head_taps(place, came, rows, seqs)
    b = place[0] % seqs
    e = place[0] // seqs
    grads = [unfold(grad_came[j]) for j in range(8)]
    first = 0
    terms_q = [0.0, 0.0, 0.0]
    terms_kv = [0.0, 0.0, 0.0]
    results = []
    for lengths, part, (q_mixed, kv_mixed) in zip(
        (long_lengths, short_lengths),
        (slice(0, long_rows), slice(long_rows, rows)),
        own_pair(came, long_rows, rows),
    ):
        count = q_mixed.shape[0]
        block = min(256, count)
        length = lengths[b]
        at = slice(first, first + count)
        grad = jnp.concatenate([g[part] for g in grads], axis=0)
        q = q_all[at, :]
        kv = kv_all[at, :]
        kv_t = kv.astype(F32).T.astype(BF16)
        delta = jnp.sum(grad.astype(F32).T * att_t[:, at], axis=0, keepdims=True)
        log_total = log_row[:, at]
        k, v = kv[:, :HEAD_DIM], kv[:, HEAD_DIM:]
        k_t = kv_t[:HEAD_DIM, :]
        grad_q = None
        grad_kv = []
        for start in range(0, count, block):
            stop = start + block
            scores = dot(k[start:stop], q[start:], NT)
            key_pos = lax.broadcasted_iota(jnp.int32, scores.shape, 0)
            query_pos = lax.broadcasted_iota(jnp.int32, scores.shape, 1)
            allowed = jnp.logical_and(key_pos <= query_pos, key_pos + start < length)
            prob = jnp.where(allowed, jnp.exp(scores - log_total[:, start:]), 0.0)
            grad_prob = dot(v[start:stop], grad[start:], NT)
            grad_scores = (prob * (grad_prob - delta[:, start:])).astype(BF16)
            grad_k = dot(grad_scores, q[start:])
            grad_v = dot(prob.astype(BF16), grad[start:])
            grad_kv.append(jnp.concatenate([grad_k, grad_v], axis=1))
            part_q = dot(k_t[:, start:stop], grad_scores)
            if start == 0:
                grad_q = part_q
            else:
                grad_q = jnp.concatenate(
                    [grad_q[:, :start], grad_q[:, start:] + part_q], axis=1
                )
        grad_q = grad_q.T * HEAD_DIM ** (-0.5)
        grad_kv = jnp.concatenate(grad_kv, axis=0)
        pair = []
        for grad_conv, mixed, taps, terms in (
            (grad_q, q_mixed, taps_q, terms_q),
            (grad_kv, kv_mixed, taps_kv, terms_kv),
        ):
            grad_mixed = 0.0
            for m in range(3):
                ahead = grad_conv if m == 0 else shift_ahead(grad_conv, m)
                terms[m] = terms[m] + jnp.sum(ahead * mixed, axis=0, keepdims=True)
                grad_mixed = grad_mixed + taps[m] * ahead
            pair.append(grad_mixed.astype(BF16))
        results.append(pair)
        first += count
    table = jnp.concatenate(
        terms_q
        + [t[:, :HEAD_DIM] for t in terms_kv]
        + [t[:, HEAD_DIM:] for t in terms_kv]
        + [jnp.zeros((7, HEAD_DIM), F32)],
        axis=0,
    )
    table = jnp.concatenate([jnp.where(e == i, table, 0.0) for i in range(3)], axis=1)
    width = 3 * HEAD_DIM // 8
    for j in range(8):
        mine = [
            jnp.concatenate(
                [
                    results[0][i][j * long_rows : (j + 1) * long_rows],
                    results[1][i][j * short_rows : (j + 1) * short_rows],
                ],
                axis=0,
            )
            for i in range(2)
        ]
        send[j, :rows, :] = mine[1]
        send[j, rows : rows + rows // 2, :] = fold(mine[0])
        send[j, rows + rows // 2 :, :] = jnp.concatenate(
            [table[:, j * width : (j + 1) * width], jnp.zeros((16, LANES - width), F32)], axis=1
        ).astype(BF16)


def place_grad_mixed(came, grad_mixed):
    seqs = 2
    rows = (came.shape[1] - 16) * 2 // 3
    for e in range(3):
        for b in range(seqs):
            j = seqs * e + b
            at = slice(b * rows, (b + 1) * rows)
            lanes = slice(e * HEAD_DIM, (e + 1) * HEAD_DIM)
            grad_mixed[0, at, lanes] = unfold(came[j, rows : rows + rows // 2, :])
            grad_mixed[1, at, lanes] = came[j, :rows, :HEAD_DIM]
            grad_mixed[2, at, lanes] = came[j, :rows, HEAD_DIM:]


def project_back_body(
    place, came, normed, weight, keep_p, send_p, keep, send, taps, scratch, grad_mixed, blocks
):
    place_grad_mixed(came, grad_mixed)
    shard = normed.shape[1] // 8
    terms = [dot(normed[...], grad_mixed[c], TN).astype(BF16) for c in range(3)]
    for s in range(8):
        at = slice(s * shard, (s + 1) * shard)
        for c in range(3):
            blocks[s, c * shard : (c + 1) * shard, :] = terms[c][at, :LANES]
        blocks[s, 3 * shard :, :] = fold(
            jnp.concatenate([terms[c][at, LANES:] for c in range(3)], axis=0)
        )
    split_y(place, blocks, keep_p, send_p)
    rows = (came.shape[1] - 16) * 2 // 3
    total = came[0, rows + rows // 2 :, :].astype(F32)
    for j in range(1, 6):
        total = total + came[j, rows + rows // 2 :, :].astype(F32)
    taps[...] = total[: taps.shape[0], : taps.shape[1]]
    total = dot(grad_mixed[0], weight[0], NT)
    for c in (1, 2):
        total = total + dot(grad_mixed[c], weight[c], NT)
    scratch[...] = total.astype(BF16)
    split_halves(place, scratch, keep, send)


def input_grad_body(
    place, own, other, grad_mid, gain, long_in, short_in, long_out, short_out, scratch
):
    join_halves(place, scratch, own, other)
    seqs, long_rows, _ = long_in.shape
    rows = long_rows + short_in.shape[1]
    for b in range(seqs):
        at = slice(b * rows, (b + 1) * rows)
        values = jnp.concatenate([long_in[b], short_in[b]], axis=0).astype(F32)
        weighted = scratch[at, :] * gain[...]
        root = lax.rsqrt(jnp.mean(values * values, axis=-1, keepdims=True) + norm_eps)
        inner = jnp.mean(weighted * values, axis=-1, keepdims=True)
        grad = grad_mid[at, :] + (root * weighted - values * (root * root * root * inner))
        long_out[b] = grad[:long_rows]
        short_out[b] = grad[long_rows:]


def output_body(place, own, other, mid, long_out, short_out, scratch):
    join_halves(place, scratch, own, other)
    seqs, long_rows, _ = long_out.shape
    rows = long_rows + short_out.shape[1]
    for b in range(seqs):
        at = slice(b * rows, (b + 1) * rows)
        value = (mid[at, :] + scratch[at, :]).astype(BF16)
        long_out[b] = value[:long_rows]
        short_out[b] = value[long_rows:]


def scatter_z_body(place, *refs):
    count = (len(refs) - 4) // 2
    outs = refs[2 * count :]
    z = place[0] // 2
    for i in range(4):
        block = jnp.bitwise_xor(z, i)
        first = 0
        for a in range(count):
            keep, came = refs[2 * a], refs[2 * a + 1]
            rows = keep.shape[1]
            outs[i][first : first + rows, :] = (
                keep[block].astype(F32) + came[block].astype(F32)
            ).astype(BF16)
            first += rows


def near_body(place, *refs):
    pairs = len(refs[:-3]) // 2
    near, own, across = refs[-3:]
    z = place[0] // 2
    for i, target in ((0, own), (1, near.at[0]), (2, across), (3, near.at[1])):
        block = jnp.bitwise_xor(z, i)
        first = 0
        for p in range(pairs):
            keep, came = refs[2 * p], refs[2 * p + 1]
            rows = keep.shape[1]
            target[first : first + rows, :] = (
                keep[block].astype(F32) + came[block].astype(F32)
            ).astype(BF16)
            first += rows


def across_body(across, near, out):
    out[...] = (across[...].astype(F32) + near[1].astype(F32)).astype(BF16)


def sum_blocks(blocks):
    return (blocks[0][...].astype(F32) + blocks[1][...].astype(F32)) + (
        blocks[2][...].astype(F32) + blocks[3][...].astype(F32)
    )


def proj_grad_body(b0, b1, b2, b3, proj, gain, grad, gain_grad):
    total = sum_blocks((b0, b1, b2, b3))
    rows = proj.shape[1]
    column = 0.0
    for c, (wide, narrow) in enumerate(unpack_blocks(total, rows, 3)):
        term = jnp.concatenate([wide, narrow], axis=1)
        column = column + jnp.sum(term * proj[c].astype(F32), axis=1, keepdims=True)
        grad[c] = term
    gain_grad[...] = column.T / gain[...].astype(F32).reshape(1, rows)


def ffn_grad_body(
    own, near, across, down_keep, down_came, up, gain, up_grad, down_grad, out_grad, gain_grad
):
    rows = up.shape[0]
    total = own[...].astype(F32) + near[0].astype(F32) + across[...].astype(F32)
    raw = total[:rows]
    gain_grad[...] = jnp.sum(raw * up[...].astype(F32), axis=1, keepdims=True).T
    up_grad[...] = raw * gain[...].astype(F32).reshape(1, rows).T
    down_grad[...] = down_keep[...].astype(F32) + down_came[...].astype(F32)
    wide = total[rows : rows + 16]
    narrow = total[rows + 16 :]
    out = jnp.concatenate(
        [
            jnp.concatenate(
                [
                    wide[:, LANES * g : LANES * (g + 1)],
                    narrow[:, LANES * g : LANES * g + HEAD_DIM],
                ],
                axis=1,
            )
            for g in range(rows // 16)
        ],
        axis=0,
    )
    out_grad[...] = out.T


def pair_shards(
    short_input,
    long_input,
    short_cotangent,
    long_cotangent,
    short_lengths,
    long_lengths,
    proj_weight,
    out_weight,
    conv_taps,
    attention_gain,
    up_weight,
    down_weight,
    feed_gain,
):
    seqs, long_rows, width = long_input.shape
    short_rows = short_input.shape[1]
    rows = long_rows + short_rows
    tokens = seqs * rows
    shard = proj_weight.shape[1]
    local = proj_weight.shape[2]
    hidden = up_weight.shape[1]
    long_len, short_len = 8 * long_rows, 8 * short_rows
    total_len = long_len + short_len
    place = jnp.stack([lax.axis_index("seq"), lax.axis_index("head")]).astype(jnp.int32)
    packed_rows = shard * 9 // 2
    chunk = rows + rows // 2 + 16
    down_t = down_weight.T

    (proj_packed,) = in_vmem(
        pack_proj_body,
        [((packed_rows + 16, LANES), BF16)],
        (),
        far(proj_weight, attention_gain),
    )
    (out_packed,) = in_vmem(pack_out_body, [((32, hidden), BF16)], (), far(out_weight))
    out_packed_x = exchange(out_packed, "head", 2)
    (ffn_packed,) = in_vmem(
        pack_ffn_body,
        [((2 * shard + 48, hidden), BF16)],
        (),
        far(up_weight, down_t) + (out_packed, out_packed_x) + far(feed_gain),
    )
    proj_z = [proj_packed] + [exchange(proj_packed, "seq", mask) for mask in (2, 4, 6)]
    proj_parts = [proj_packed, exchange(after(proj_packed, ffn_packed), "seq", 1)]
    proj_parts += [proj_z[1], exchange(proj_z[1], "seq", 1)]
    proj_parts += [proj_z[2], exchange(proj_z[2], "seq", 1)]
    proj_parts += [proj_z[3], exchange(proj_z[3], "seq", 1)]
    ffn_0 = after(ffn_packed, *proj_z)
    ffn_1 = exchange(ffn_packed, "seq", 1)
    ffn_2 = exchange(ffn_0, "seq", 2)
    ffn_4 = exchange(ffn_0, "seq", 4)
    send, normed, proj_full, gain = in_vmem(
        project_body,
        [
            ((8, chunk, LANES), BF16),
            ((tokens, width), BF16, "far"),
            ((3, width, local), BF16, "far"),
            ((1, width), F32, "far"),
        ],
        (place,),
        (*proj_parts, *far(long_input, short_input, conv_taps)),
        scratch=[((8, LANES), F32)],
        fence=True,
    )
    came = lax.all_to_all(send, "seq", 0, 0, tiled=True)
    across_z = marker(ffn_4, ffn_1, send)
    ffn_2 = after(ffn_2, across_z)
    ffn_4 = after(ffn_4, across_z)
    ffn_6 = exchange(ffn_4, "seq", 2)
    ffn_3 = exchange(ffn_2, "seq", 1)
    ffn_5 = exchange(ffn_4, "seq", 1)
    att_send, q_all, kv_all, att_t, log_row, mixed = in_vmem(
        functools.partial(attend_body, long_rows, seqs),
        [
            ((8, rows // 2, LANES), BF16),
            ((total_len, HEAD_DIM), BF16, "far"),
            ((total_len, 2 * HEAD_DIM), BF16, "far"),
            ((HEAD_DIM, total_len), F32, "far"),
            ((1, total_len), F32, "far"),
            ((8, chunk, LANES), BF16, "far"),
        ],
        (place, long_lengths, short_lengths),
        (came,),
        fence=True,
    )
    att_0 = lax.all_to_all(att_send, "seq", 0, 0, tiled=True)
    ffn_7 = exchange(ffn_6, "seq", 1)
    up_full, down_full, out_full, out_now, out_x = in_vmem(
        place_ffn_body,
        [((width, hidden), BF16, "far")] * 2
        + [((width, local), BF16, "far"), ((width, local), BF16), ((width, local), BF16)],
        (place,),
        far(after(ffn_packed, att_send), ffn_1, ffn_2, ffn_3, ffn_4, ffn_5, ffn_6, ffn_7),
    )
    att_0 = after(att_0, out_full)
    att_x = exchange(att_0, "head", 2)
    att, own = in_vmem(
        out_proj_body,
        [((tokens, local), BF16, "far"), ((tokens, width), BF16)],
        (),
        (att_0, att_x, out_now, out_x),
        fence=True,
    )
    other = exchange(own, "head", 1)
    mid, squared, grad_out, keep, send, normed_ffn, grad_up = in_vmem(
        functools.partial(feed_body, long_rows),
        [
            ((tokens, width), F32, "far"),
            ((tokens, hidden), BF16, "far"),
            ((tokens, width), BF16, "far"),
            ((tokens // 2, width), BF16),
            ((tokens // 2, width), BF16),
            ((tokens, width), BF16, "far"),
            ((tokens, hidden), BF16, "far"),
        ],
        (place, long_lengths, short_lengths),
        (own, other)
        + far(long_input, short_input, long_cotangent, short_cotangent, up_full, down_full),
        scratch=[
            ((tokens, width), BF16),
            ((tokens, width), F32),
        ],
        limit_mib=32,
    )
    half = add_low(keep, exchange(send, "head", 1))
    down_near, down_own, down_across, f_keep, f_send, up_keep, up_send = in_vmem(
        down_term_body,
        [((2, 2, shard, hidden), BF16, "far")]
        + [((2, shard, hidden), BF16, "far")] * 2
        + [((tokens // 2, width), BF16, "far")] * 2
        + [((4, shard, hidden), BF16, "far")] * 2,
        (place,),
        far(after(squared, half), grad_out, down_full, normed_ffn, grad_up),
        scratch=[
            ((tokens, width), BF16),
            ((8, shard, hidden), BF16),
        ],
        limit_mib=32,
        fence=True,
    )
    down_near = exchange(down_near, "seq", 2)
    up_came = exchange(up_send, "seq", 1)
    own = add_low(half, after(exchange(half, "head", 2), f_send))
    other = exchange(own, "head", 1)
    grad_mid, send, out_keep, out_send = in_vmem(
        middle_body,
        [
            ((tokens, width), F32, "far"),
            ((8, rows // 2, LANES), BF16),
            ((4, 32, hidden), BF16, "far"),
            ((4, 32, hidden), BF16, "far"),
        ],
        (place,),
        (own, other) + far(mid, grad_out, out_full, att),
        scratch=[((tokens, width), F32), ((tokens, width), BF16), ((8, 32, hidden), BF16)],
    )
    grad_came = lax.all_to_all(send, "seq", 0, 0, tiled=True)
    out_came = exchange(out_send, "seq", 1)
    (down_across,) = in_vmem(
        down_across_body,
        [((2, shard, hidden), BF16, "far")],
        (),
        far(after(down_across, send, up_came), down_near),
        fence=True,
    )
    grad_came = after(grad_came, down_across)
    down_across = exchange(down_across, "seq", 4)
    f_half = add_low(f_keep, exchange(after(f_send, send), "head", 1))
    f_own = add_low(f_half, exchange(f_half, "head", 2))
    f_other = exchange(f_own, "head", 1)
    long_output, short_output = in_vmem(
        output_body,
        [(long_input.shape, BF16), (short_input.shape, BF16)],
        (place,),
        (f_own, f_other) + far(mid),
        scratch=[((tokens, width), F32)],
    )
    (send,) = in_vmem(
        functools.partial(attend_back_body, long_rows, seqs),
        [((8, chunk, LANES), BF16)],
        (place, long_lengths, short_lengths),
        far(mixed, q_all, kv_all, att_t, log_row) + (grad_came,),
        fence=True,
    )
    mixed_came = lax.all_to_all(send, "seq", 0, 0, tiled=True)
    near, ffn_own, across = in_vmem(
        near_body,
        [((2, shard + 32, hidden), BF16, "far")] + [((shard + 32, hidden), BF16, "far")] * 2,
        (place,),
        far(up_keep, after(up_came, send), out_keep, out_came),
        fence=True,
    )
    near = exchange(near, "seq", 2)
    down_keep, down_send = in_vmem(
        down_y_body,
        [((shard, hidden), BF16, "far")] * 2,
        (place,),
        far(after(down_own, ffn_own), down_near, down_across),
    )
    down_came = exchange(down_send, "seq", 1)
    mixed_came = after(mixed_came, long_output, down_send)
    proj_keep, proj_send, keep, send, taps_grad = in_vmem(
        project_back_body,
        [
            ((4, packed_rows, LANES), BF16, "far"),
            ((4, packed_rows, LANES), BF16),
            ((tokens // 2, width), BF16),
            ((tokens // 2, width), BF16),
            (conv_taps.shape, F32),
        ],
        (place,),
        (mixed_came,) + far(normed, proj_full),
        scratch=[
            ((tokens, width), BF16),
            ((3, tokens, local), BF16),
            ((8, packed_rows, LANES), BF16),
        ],
        fence=True,
    )
    proj_came = exchange(proj_send, "seq", 1)
    half = add_low(keep, exchange(send, "head", 1))
    (across,) = in_vmem(
        across_body, [((shard + 32, hidden), BF16, "far")], (), far(across, near)
    )
    across = exchange(across, "seq", 4)
    own = add_low(half, after(exchange(half, "head", 2), proj_came))
    other = exchange(own, "head", 1)
    proj_blocks = in_vmem(
        scatter_z_body,
        [((packed_rows, LANES), BF16)] * 4,
        (place,),
        far(proj_keep) + (proj_came,),
        fence=True,
    )
    proj_blocks = [proj_blocks[0]] + [exchange(proj_blocks[i], "seq", 2 * i) for i in (1, 2, 3)]
    up_grad, down_grad, out_grad, feed_part = in_vmem(
        ffn_grad_body,
        [
            (up_weight.shape, F32),
            (down_t.shape, F32),
            (out_weight.shape, F32),
            ((1, shard), F32),
        ],
        (),
        far(after(ffn_own, proj_blocks[0]), near, across, down_keep, down_came, up_weight)
        + (feed_gain,),
    )
    proj_blocks[3] = after(proj_blocks[3], up_grad)
    proj_grad, attention_part = in_vmem(
        proj_grad_body,
        [(proj_weight.shape, F32), ((1, shard), F32)],
        (),
        (*proj_blocks, *far(proj_weight), attention_gain),
    )
    long_input_grad, short_input_grad = in_vmem(
        input_grad_body,
        [(long_input.shape, F32), (short_input.shape, F32)],
        (place,),
        (own, other) + far(after(grad_mid, attention_part), gain, long_input, short_input),
        scratch=[((tokens, width), F32)],
    )
    gains = jnp.concatenate([attention_part, feed_part], axis=0)
    gains = gains + exchange(gains, "head", 1)
    gains = gains + after(exchange(gains, "head", 2), long_input_grad)

    return (
        short_output,
        long_output,
        short_input_grad,
        long_input_grad,
        proj_grad,
        out_grad,
        taps_grad,
        gains[0],
        up_grad,
        down_grad.T,
        gains[1],
    )


def fits_pairs(short_input, long_input, proj_weight):
    seqs, long_rows, _ = long_input.shape
    short_seqs, short_rows, _ = short_input.shape
    return (
        lax.axis_size("seq") == 8
        and lax.axis_size("head") == 4
        and seqs == 2
        and short_seqs == 2
        and proj_weight.shape[2] == 3 * HEAD_DIM
        and proj_weight.shape[1] % 32 == 0
        and long_rows % 32 == 0
        and short_rows % 32 == 0
        and 8 * long_rows <= 2048
    )


def shards(short_input, long_input, *rest):
    proj_weight = rest[4]
    if fits_pairs(short_input, long_input, proj_weight):
        return pair_shards(short_input, long_input, *rest)
    return ring_shards(short_input, long_input, *rest)


def solution(mesh):
    placed = (
        P(None, "seq", None),
        P(None, "seq", None),
        P(None, "seq", None),
        P(None, "seq", None),
        P(),
        P(),
        P(None, "seq", "head"),
        P("head", "seq"),
        P(None, ("head", "seq")),
        P("seq"),
        P("seq", "head"),
        P("head", "seq"),
        P("seq"),
    )
    return jax.shard_map(
        shards,
        mesh=mesh,
        in_specs=placed,
        out_specs=(
            P(None, "seq", None),
            P(None, "seq", None),
            P(None, "seq", None),
            P(None, "seq", None),
            P(None, "seq", "head"),
            P("head", "seq"),
            P(None, ("head", "seq")),
            P("seq"),
            P("seq", "head"),
            P("head", "seq"),
            P("seq"),
        ),
        check_vma=False,
    )
```

```python
import functools

import jax
import jax.numpy as jnp
import numpy as np
from jax import lax
from jax.experimental import pallas as pl
from jax.experimental.pallas import tpu as pltpu
from jax.sharding import PartitionSpec as P

HEAD_DIM = 64


norm_eps = 1e-06
mask_fill = -1e30
block_limit = 2048


def passed_along(block, axis, distance):
    devices = range(lax.axis_size(axis))
    route = [((i - distance) % len(devices), i) for i in devices]
    return lax.ppermute(block, axis, route)


def shifted(array, axis, by):
    peers = lax.axis_size(axis)
    pairs = [(i, i + by) for i in range(peers) if 0 <= i + by < peers]
    return lax.ppermute(array, axis, pairs)


def block_rows(row_count):
    size_rows = min(row_count, block_limit)
    while row_count % size_rows != 0:
        size_rows = size_rows - 1
    return size_rows


def norm_forward(values_in, gain_row):
    inv_root = lax.rsqrt(jnp.mean(values_in * values_in, axis=-1, keepdims=True) + norm_eps)
    return (values_in * inv_root * gain_row, inv_root)


def norm_backward(values_in, inv_root, gain_row, grad_in):
    weighted = grad_in * gain_row
    inner_mean = jnp.mean(weighted * values_in, axis=-1, keepdims=True)
    grad_values = inv_root * weighted - values_in * inv_root * inv_root * inv_root * inner_mean
    grad_gain = jnp.sum(grad_in * values_in * inv_root, axis=(0, 1))
    return (grad_values, grad_gain)


def allowed_mask(query_pos, key_pos, lengths):
    causal = key_pos[None, :] <= query_pos[:, None]
    inside = key_pos[None, :] < lengths[:, None]
    return jnp.logical_and(causal[None, None], inside[:, None, None, :])


def block_scores(query_rows, key_rows, query_pos, key_pos, lengths):
    allowed = allowed_mask(query_pos, key_pos, lengths)
    raw_scores = jnp.einsum(
        "bqhe,bkhe->bhqk", query_rows, key_rows, preferred_element_type=jnp.float32
    ) * HEAD_DIM ** (-0.5)
    return (jnp.where(allowed, raw_scores, mask_fill), allowed)


def block_grads(
    query_rows, grad_rows, log_rows, delta_rows, key_rows, value_rows, query_pos, key_pos, lengths
):
    scores, allowed = block_scores(query_rows, key_rows, query_pos, key_pos, lengths)
    prob_rows = jnp.where(
        allowed, jnp.exp(scores - jnp.transpose(log_rows, (0, 2, 1))[..., None]), 0.0
    )
    grad_probs = jnp.einsum(
        "bqhe,bkhe->bhqk", grad_rows, value_rows, preferred_element_type=jnp.float32
    )
    grad_scores = (
        prob_rows * (grad_probs - jnp.transpose(delta_rows, (0, 2, 1))[..., None])
    ).astype(jnp.bfloat16)
    grad_query = jnp.einsum(
        "bhqk,bkhe->bqhe", grad_scores, key_rows, preferred_element_type=jnp.float32
    ) * HEAD_DIM ** (-0.5)
    grad_key = jnp.einsum(
        "bhqk,bqhe->bkhe", grad_scores, query_rows, preferred_element_type=jnp.float32
    ) * HEAD_DIM ** (-0.5)
    grad_value = jnp.einsum(
        "bhqk,bqhe->bkhe",
        prob_rows.astype(jnp.bfloat16),
        grad_rows,
        preferred_element_type=jnp.float32,
    )
    return (grad_query, grad_key, grad_value)


def attend_forward(queries, keys_here, values_here, query_pos, lengths):
    seq_count, span_rows, head_count, head_width = queries.shape
    initial = (
        jnp.full((seq_count, head_count, span_rows), mask_fill, jnp.float32),
        jnp.zeros((seq_count, head_count, span_rows), jnp.float32),
        jnp.zeros((seq_count, span_rows, head_count, head_width), jnp.float32),
    )
    key_piece = lax.all_gather(keys_here, "seq", axis=1, tiled=True)
    value_piece = lax.all_gather(values_here, "seq", axis=1, tiled=True)
    row_count = key_piece.shape[1]
    size_rows = block_rows(row_count)

    def one_block(block_index, carried_state):
        running_top, running_sum, acc_rows = carried_state
        offset = block_index * size_rows
        key_rows = lax.dynamic_slice_in_dim(key_piece, offset, size_rows, 1)
        value_rows = lax.dynamic_slice_in_dim(value_piece, offset, size_rows, 1)
        key_pos = offset + jnp.arange(size_rows, dtype=jnp.int32)
        scores, allowed = block_scores(queries, key_rows, query_pos, key_pos, lengths)
        new_top = jnp.maximum(running_top, jnp.max(scores, axis=-1))
        exp_terms = jnp.where(allowed, jnp.exp(scores - new_top[..., None]), 0.0)
        shrink = jnp.exp(running_top - new_top)
        running_sum = running_sum * shrink + jnp.sum(exp_terms, axis=-1)
        acc_rows = acc_rows * jnp.transpose(shrink, (0, 2, 1))[..., None] + jnp.einsum(
            "bhqk,bkhe->bqhe",
            exp_terms.astype(jnp.bfloat16),
            value_rows,
            preferred_element_type=jnp.float32,
        )
        return (new_top, running_sum, acc_rows)

    running_top, running_sum, acc_rows = lax.fori_loop(
        0, row_count // size_rows, one_block, initial
    )
    attention = acc_rows / jnp.transpose(running_sum, (0, 2, 1))[..., None]
    log_totals = jnp.transpose(running_top + jnp.log(running_sum), (0, 2, 1))
    return (attention, log_totals)


def pass_sums(grad_keys, grad_values):
    return (
        passed_along(grad_keys.astype(jnp.bfloat16), "seq", 1).astype(grad_keys.dtype),
        passed_along(grad_values.astype(jnp.bfloat16), "seq", 1).astype(grad_values.dtype),
    )


def attend_backward(
    queries, keys_here, values_here, grad_attention, log_totals, delta_rows, query_pos, lengths
):
    seq_count, span_rows, head_count, head_width = queries.shape
    zeros_local = jnp.zeros(queries.shape, jnp.float32)
    seq_size = lax.axis_size("seq")
    my_index = lax.axis_index("seq")
    local_pos = jnp.arange(span_rows, dtype=jnp.int32)

    def step_grads(step, key_piece, value_piece):
        anchor = jnp.mod(my_index - step, seq_size)
        key_pos = anchor * span_rows + local_pos
        return block_grads(
            queries,
            grad_attention,
            log_totals,
            delta_rows,
            key_piece,
            value_piece,
            query_pos,
            key_pos,
            lengths,
        )

    def cycle_step(step, state):
        key_piece, value_piece, grad_keys, grad_values, grad_query = state
        query_part, key_part, value_part = step_grads(step, key_piece, value_piece)
        key_piece, value_piece = shifted((key_piece, value_piece), "seq", 1)
        grad_keys, grad_values = pass_sums(grad_keys + key_part, grad_values + value_part)
        return (key_piece, value_piece, grad_keys, grad_values, grad_query + query_part)

    final_state = lax.fori_loop(
        0, seq_size - 1, cycle_step, (keys_here, values_here, zeros_local, zeros_local, zeros_local)
    )
    key_piece, value_piece, grad_keys, grad_values, grad_query = final_state
    query_part, key_part, value_part = step_grads(seq_size - 1, key_piece, value_piece)
    grad_key, grad_value = pass_sums(grad_keys + key_part, grad_values + value_part)
    grad_query = grad_query + query_part
    return (grad_query, grad_key, grad_value)


def micro_batch(inputs, cotangent, lengths, weights):
    proj_full, out_full, taps_full, attend_gain, up_full, down_full, ffn_gain = weights
    seq_count, span_rows, model_width = inputs.shape
    local_width = proj_full.shape[2]
    heads_here = local_width // HEAD_DIM
    query_pos = lax.axis_index("seq") * span_rows + jnp.arange(span_rows, dtype=jnp.int32)
    valid_rows = (query_pos[None, :] < lengths[:, None])[..., None]
    residual_in = inputs.astype(jnp.float32)
    normed, inv_first = norm_forward(residual_in, attend_gain)
    normed_low = normed.astype(jnp.bfloat16)
    mixed_qkv = jnp.einsum(
        "btd,cde->cbte", normed_low, proj_full, preferred_element_type=jnp.float32
    ).astype(jnp.bfloat16)
    borrowed = shifted(mixed_qkv[:, :, span_rows - 2 :, :], "seq", 1)
    extended = jnp.concatenate([borrowed, mixed_qkv], axis=2).astype(jnp.float32)
    tap_table = taps_full.astype(jnp.float32).reshape(3, 3, local_width)
    tap_now = tap_table[:, 0][:, None, None, :]
    tap_one = tap_table[:, 1][:, None, None, :]
    tap_two = tap_table[:, 2][:, None, None, :]
    conved = (
        tap_now * extended[:, :, 2:]
        + tap_one * extended[:, :, 1:-1]
        + tap_two * extended[:, :, :-2]
    )
    conv_out = conved.astype(jnp.bfloat16).reshape(3, seq_count, span_rows, heads_here, HEAD_DIM)
    queries, keys_here, values_here = (conv_out[0], conv_out[1], conv_out[2])
    attention, log_totals = attend_forward(queries, keys_here, values_here, query_pos, lengths)
    attention_low = attention.astype(jnp.bfloat16).reshape(seq_count, span_rows, local_width)
    attend_part = jnp.einsum(
        "bte,ed->btd", attention_low, out_full, preferred_element_type=jnp.float32
    )
    mid_residual = residual_in + lax.psum(attend_part.astype(jnp.bfloat16), "head").astype(
        jnp.float32
    )
    normed_ffn, inv_second = norm_forward(mid_residual, ffn_gain)
    normed_ffn_low = normed_ffn.astype(jnp.bfloat16)
    up_proj = jnp.einsum("btd,df->btf", normed_ffn_low, up_full, preferred_element_type=jnp.float32)
    relu_up = jnp.maximum(up_proj, 0.0)
    squared = (relu_up * relu_up).astype(jnp.bfloat16)
    ffn_part = jnp.einsum("btf,fd->btd", squared, down_full, preferred_element_type=jnp.float32)
    output = (
        mid_residual + lax.psum(ffn_part.astype(jnp.bfloat16), "head").astype(jnp.float32)
    ).astype(jnp.bfloat16)
    grad_out = jnp.where(valid_rows, cotangent.astype(jnp.float32), 0.0)
    grad_out_low = grad_out.astype(jnp.bfloat16)
    down_term = jnp.einsum("btf,btd->fd", squared, grad_out_low, preferred_element_type=jnp.float32)
    grad_squared = jnp.einsum(
        "btd,fd->btf", grad_out_low, down_full, preferred_element_type=jnp.float32
    )
    grad_up = (grad_squared * 2.0 * relu_up).astype(jnp.bfloat16)
    up_term = jnp.einsum("btd,btf->df", normed_ffn_low, grad_up, preferred_element_type=jnp.float32)
    grad_normed_ffn = lax.psum(
        jnp.einsum("btf,df->btd", grad_up, up_full, preferred_element_type=jnp.float32).astype(
            jnp.bfloat16
        ),
        "head",
    ).astype(jnp.float32)
    grad_through, feed_term = norm_backward(mid_residual, inv_second, ffn_gain, grad_normed_ffn)
    grad_mid = grad_out + grad_through
    grad_mid_low = grad_mid.astype(jnp.bfloat16)
    out_term = jnp.einsum(
        "bte,btd->ed", attention_low, grad_mid_low, preferred_element_type=jnp.float32
    )
    grad_attention = jnp.einsum(
        "btd,ed->bte", grad_mid_low, out_full, preferred_element_type=jnp.float32
    )
    grad_attention = grad_attention.astype(jnp.bfloat16).reshape(
        seq_count, span_rows, heads_here, HEAD_DIM
    )
    delta_rows = jnp.einsum("bqhe,bqhe->bqh", grad_attention.astype(jnp.float32), attention)
    grad_query, grad_key, grad_value = attend_backward(
        queries, keys_here, values_here, grad_attention, log_totals, delta_rows, query_pos, lengths
    )
    grad_conv = jnp.stack([grad_query, grad_key, grad_value]).reshape(
        3, seq_count, span_rows, local_width
    )
    taps_term = jnp.stack(
        [
            jnp.sum(grad_conv * extended[:, :, 2:], axis=(1, 2)),
            jnp.sum(grad_conv * extended[:, :, 1:-1], axis=(1, 2)),
            jnp.sum(grad_conv * extended[:, :, :-2], axis=(1, 2)),
        ],
        axis=1,
    ).reshape(9, local_width)
    full_grad = jnp.pad(grad_conv, ((0, 0), (0, 0), (2, 2), (0, 0)))
    grad_extended = (
        tap_now * full_grad[:, :, 0 : span_rows + 2]
        + tap_one * full_grad[:, :, 1 : span_rows + 3]
        + tap_two * full_grad[:, :, 2 : span_rows + 4]
    )
    returned = shifted(grad_extended[:, :, :2], "seq", -1)
    grad_mixed = jnp.concatenate(
        [grad_extended[:, :, 2:span_rows], grad_extended[:, :, span_rows:] + returned], axis=2
    ).astype(jnp.bfloat16)
    proj_term = jnp.einsum(
        "btd,cbte->cde", normed_low, grad_mixed, preferred_element_type=jnp.float32
    )
    grad_normed = lax.psum(
        jnp.einsum(
            "cbte,cde->btd", grad_mixed, proj_full, preferred_element_type=jnp.float32
        ).astype(jnp.bfloat16),
        "head",
    ).astype(jnp.float32)
    grad_first, attention_term = norm_backward(residual_in, inv_first, attend_gain, grad_normed)
    grad_input = grad_mid + grad_first
    return (
        output,
        grad_input,
        (proj_term, out_term, taps_term, attention_term, up_term, down_term, feed_term),
    )


def ring_shards(
    short_input,
    long_input,
    short_cotangent,
    long_cotangent,
    short_lengths,
    long_lengths,
    proj_weight,
    out_weight,
    conv_taps,
    attention_gain,
    up_weight,
    down_weight,
    feed_gain,
):
    proj_full, out_full, taps_full, attend_gain = (
        lax.all_gather(proj_weight, "seq", axis=1, tiled=True),
        lax.all_gather(out_weight, "seq", axis=1, tiled=True),
        lax.all_gather(conv_taps, "seq", axis=1, tiled=True),
        lax.all_gather(attention_gain, "seq", axis=0, tiled=True),
    )
    up_full, down_full, ffn_gain = (
        lax.all_gather(up_weight, "seq", axis=0, tiled=True),
        lax.all_gather(down_weight, "seq", axis=1, tiled=True),
        lax.all_gather(feed_gain, "seq", axis=0, tiled=True),
    )
    weights = (
        proj_full,
        out_full,
        taps_full,
        attend_gain.astype(jnp.float32),
        up_full,
        down_full,
        ffn_gain.astype(jnp.float32),
    )
    short_output, short_input_grad, short_terms = micro_batch(
        short_input, short_cotangent, short_lengths, weights
    )
    long_output, long_input_grad, long_terms = micro_batch(
        long_input, long_cotangent, long_lengths, weights
    )
    summed = tuple(
        (first_term + second_term for first_term, second_term in zip(short_terms, long_terms))
    )
    reduced = (
        lax.psum_scatter(summed[0], "seq", scatter_dimension=1, tiled=True),
        lax.psum_scatter(summed[1], "seq", scatter_dimension=1, tiled=True),
        lax.psum_scatter(summed[2], "seq", scatter_dimension=1, tiled=True),
        lax.psum_scatter(summed[3], "seq", scatter_dimension=0, tiled=True),
        lax.psum_scatter(summed[4], "seq", scatter_dimension=0, tiled=True),
        lax.psum_scatter(summed[5], "seq", scatter_dimension=1, tiled=True),
        lax.psum_scatter(summed[6], "seq", scatter_dimension=0, tiled=True),
    )
    return (
        short_output,
        long_output,
        short_input_grad,
        long_input_grad,
        reduced[0],
        reduced[1],
        reduced[2],
        reduced[3],
        reduced[4],
        reduced[5],
        reduced[6],
    )


LANES = 128
FENCE = 10**11
NT = (((1,), (1,)), ((), ()))
TN = (((0,), (0,)), ((), ()))
F32 = jnp.float32
BF16 = jnp.bfloat16


def dot(a, b, dims=(((1,), (0,)), ((), ()))):
    return lax.dot_general(a, b, dims, preferred_element_type=F32)


def in_vmem(body, outs, scalars, arrays, scratch=(), limit_mib=16, fence=False):
    return pl.pallas_call(
        body,
        out_shape=[
            pltpu.HBM(*out[:2]) if len(out) == 3 else jax.ShapeDtypeStruct(*out) for out in outs
        ],
        in_specs=[pl.BlockSpec(memory_space=pltpu.SMEM)] * len(scalars)
        + [pl.BlockSpec(memory_space=pltpu.VMEM)] * len(arrays),
        out_specs=[pl.BlockSpec(memory_space=pltpu.VMEM)] * len(outs),
        scratch_shapes=[pltpu.VMEM(shape, kind) for shape, kind in scratch],
        compiler_params=pltpu.CompilerParams(vmem_limit_bytes=limit_mib * 1024 * 1024),
        cost_estimate=pl.CostEstimate(
            flops=FENCE if fence else 0, bytes_accessed=0, transcendentals=0
        ),
    )(*scalars, *arrays)


def far(*arrays):
    return tuple(pltpu.with_memory_space_constraint(array, pltpu.HBM) for array in arrays)


def after(array, *others):
    return lax.optimization_barrier((array, *others))[0]


def marker(*arrays):
    def body(*refs):
        refs[-1][...] = jnp.zeros_like(refs[-1])

    return pl.pallas_call(
        body,
        out_shape=jax.ShapeDtypeStruct((8, LANES), F32),
        in_specs=[pl.BlockSpec(memory_space=pl.ANY)] * len(arrays),
        out_specs=pl.BlockSpec(memory_space=pltpu.VMEM),
        cost_estimate=pl.CostEstimate(flops=FENCE, bytes_accessed=0, transcendentals=0),
    )(*arrays)


def exchange(array, axis, mask):
    size = lax.axis_size(axis)
    return lax.ppermute(array, axis, [(i, i ^ mask) for i in range(size)])


def add_low(a, b):
    return (a.astype(F32) + b.astype(F32)).astype(BF16)


def shift_back(rows, by):
    index = lax.broadcasted_iota(jnp.int32, rows.shape, 0)
    return jnp.where(index >= by, pltpu.roll(rows, by, axis=0), 0.0)


def shift_ahead(rows, by):
    count = rows.shape[0]
    index = lax.broadcasted_iota(jnp.int32, rows.shape, 0)
    return jnp.where(index < count - by, pltpu.roll(rows, count - by, axis=0), 0.0)


def fold(rows):
    half = rows.shape[0] // 2
    return jnp.concatenate([rows[:half], rows[half:]], axis=1)


def unfold(rows):
    return jnp.concatenate([rows[:, :HEAD_DIM], rows[:, HEAD_DIM:]], axis=0)


def pack_proj_body(proj, gain, packed):
    rows = proj.shape[1]
    for c in range(3):
        packed[c * rows : (c + 1) * rows, :] = proj[c, :, :LANES]
    narrow = jnp.concatenate([proj[c, :, LANES:] for c in range(3)], axis=0)
    packed[3 * rows : 9 * rows // 2, :] = fold(narrow)
    gain_row = gain[...].astype(F32).reshape(1, rows)
    gain_row = jnp.concatenate([gain_row, jnp.zeros((1, LANES - rows), F32)], axis=1)
    packed[9 * rows // 2 :, :] = jnp.broadcast_to(gain_row, (16, LANES)).astype(BF16)


def unpack_blocks(packed, rows, count):
    narrow = unfold(packed[count * rows : 3 * count * rows // 2, :])
    return [
        (packed[i * rows : (i + 1) * rows, :], narrow[i * rows : (i + 1) * rows, :])
        for i in range(count)
    ]


def narrow_pack(block, store):
    groups = block.shape[0] // 16
    for g in range(groups):
        rows = block[16 * g : 16 * g + 16, :]
        store(0, LANES * g, rows[:, :LANES])
        tail = rows[:, LANES:]
        store(16, LANES * g, jnp.concatenate([tail, jnp.zeros_like(tail)], axis=1))


def pack_out_body(out, packed):
    def store(row, lane, value):
        packed[row : row + 16, lane : lane + LANES] = value

    narrow_pack(out[...].astype(F32).T.astype(BF16), store)


def pack_ffn_body(up, down, out, out_x, gain, packed):
    rows = up.shape[0]
    gain_column = gain[...].astype(F32).reshape(1, rows).T
    packed[:rows, :] = (up[...].astype(F32) * gain_column).astype(BF16)
    packed[rows : 2 * rows, :] = down[...]
    packed[2 * rows : 2 * rows + 16, :] = out[:16, :]
    packed[2 * rows + 16 : 2 * rows + 32, :] = out_x[:16, :]
    for g in range(rows // 16):
        lanes = slice(LANES * g, LANES * g + HEAD_DIM)
        packed[2 * rows + 32 :, LANES * g : LANES * (g + 1)] = jnp.concatenate(
            [out[16:, lanes], out_x[16:, lanes]], axis=1
        )


def place_ffn_body(place, *refs):
    up, down, out, out_now, out_x = refs[8:]
    rows = out.shape[0] // 8
    for i in range(8):
        owner = jnp.bitwise_xor(place[0], i)
        part = refs[i]
        first = pl.ds(pl.multiple_of(owner * rows, rows), rows)
        up[first, :] = part[:rows, :]
        down[first, :] = part[rows : 2 * rows, :]
        for g in range(rows // 16):
            at = pl.ds(pl.multiple_of(owner * rows + 16 * g, 16), 16)
            lanes = slice(LANES * g, LANES * (g + 1))
            narrow = part[2 * rows + 32 :, lanes]
            out[at, :LANES] = part[2 * rows : 2 * rows + 16, lanes]
            out[at, LANES:] = narrow[:, :HEAD_DIM]
            out_x[at, :LANES] = part[2 * rows + 16 : 2 * rows + 32, lanes]
            out_x[at, LANES:] = narrow[:, HEAD_DIM:]
    out_now[...] = out[...]


def project_body(place, *refs):
    parts = refs[:8]
    long_in, short_in, taps, send, normed, weight, gain, gain_rows = refs[8:]
    seqs, long_rows, _ = long_in.shape
    rows = long_rows + short_in.shape[1]
    for i in range(8):
        packed = parts[i][...]
        shard = weight.shape[1] // 8
        owner = jnp.bitwise_xor(place[0], i)
        gain_rows[pl.ds(owner, 1), :] = packed[9 * shard // 2 :, :].astype(F32)[:1]
        at = pl.ds(pl.multiple_of(owner * shard, shard), shard)
        for c, (wide, narrow) in enumerate(unpack_blocks(packed, shard, 3)):
            weight[c, at, :LANES] = wide
            weight[c, at, LANES:] = narrow
    gain[...] = jnp.concatenate([gain_rows[j : j + 1, :shard] for j in range(8)], axis=1)
    for b in range(seqs):
        values = jnp.concatenate([long_in[b], short_in[b]], axis=0).astype(F32)
        root = lax.rsqrt(jnp.mean(values * values, axis=-1, keepdims=True) + norm_eps)
        normed[b * rows : (b + 1) * rows, :] = (values * root * gain[...]).astype(BF16)
    mixed = [dot(normed[...], weight[c]).astype(BF16) for c in range(3)]
    tap_rows = jnp.concatenate(
        [taps[...], jnp.zeros((16 - taps.shape[0], taps.shape[1]), BF16)], axis=0
    )
    tap_rows = jnp.concatenate(
        [tap_rows, jnp.zeros((16, LANES - taps.shape[1]), BF16)], axis=1
    )
    half = rows // 2
    for dest in range(8):
        if dest < 3 * seqs:
            e, b = dest // seqs, dest % seqs
            lanes = slice(e * HEAD_DIM, (e + 1) * HEAD_DIM)
            q, k, v = [m[b * rows : (b + 1) * rows, lanes] for m in mixed]
            send[dest, :rows, :] = jnp.concatenate([k, v], axis=1)
            send[dest, rows : rows + half, :] = fold(q)
        else:
            send[dest, : rows + half, :] = jnp.zeros((rows + half, LANES), BF16)
        send[dest, rows + half :, :] = tap_rows


def head_taps(place, came, rows, seqs):
    first = rows + rows // 2
    width = 3 * HEAD_DIM // 8
    whole = jnp.concatenate(
        [came[j, first:, :].astype(F32)[:, :width] for j in range(8)], axis=1
    )
    e = place[0] // seqs
    mine = whole[:, :HEAD_DIM]
    for other in (1, 2):
        mine = jnp.where(
            e == other, whole[:, other * HEAD_DIM : (other + 1) * HEAD_DIM], mine
        )
    taps_q = [mine[m : m + 1, :] for m in range(3)]
    taps_kv = [
        jnp.concatenate([mine[3 + m : 4 + m, :], mine[6 + m : 7 + m, :]], axis=1) for m in range(3)
    ]
    return taps_q, taps_kv


def own_pair(came, long_rows, rows):
    q_rows = [unfold(came[j, rows : rows + rows // 2, :]) for j in range(8)]
    result = []
    for part in (slice(0, long_rows), slice(long_rows, rows)):
        q = jnp.concatenate([piece[part] for piece in q_rows], axis=0).astype(F32)
        kv = jnp.concatenate([came[j, part, :] for j in range(8)], axis=0).astype(F32)
        result.append((q, kv))
    return result


def convolve(rows, taps):
    return taps[0] * rows + taps[1] * shift_back(rows, 1) + taps[2] * shift_back(rows, 2)


def attend_body(
    long_rows, seqs, place, long_lengths, short_lengths, came, send, q_all, kv_all, att_t, log_row, kept
):
    rows = (came.shape[1] - 16) * 2 // 3
    kept[...] = came[...]
    taps_q, taps_kv = head_taps(place, came, rows, seqs)
    b = place[0] % seqs
    first = 0
    results = []
    for lengths, (q_mixed, kv_mixed) in zip(
        (long_lengths, short_lengths), own_pair(came, long_rows, rows)
    ):
        count = q_mixed.shape[0]
        block = min(256, count)
        length = lengths[b]
        q = (convolve(q_mixed, taps_q).astype(BF16).astype(F32) * HEAD_DIM ** (-0.5)).astype(BF16)
        kv = convolve(kv_mixed, taps_kv).astype(BF16)
        kv_t = kv.astype(F32).T.astype(BF16)
        q_all[first : first + count, :] = q
        kv_all[first : first + count, :] = kv
        k = kv[:, :HEAD_DIM]
        v_t = kv_t[HEAD_DIM:, :]
        pieces = []
        for start in range(0, count, block):
            stop = start + block
            scores = dot(k[:stop], q[start:stop], NT)
            key_pos = lax.broadcasted_iota(jnp.int32, scores.shape, 0)
            query_pos = lax.broadcasted_iota(jnp.int32, scores.shape, 1) + start
            allowed = jnp.logical_and(key_pos <= query_pos, key_pos < length)
            scores = jnp.where(allowed, scores, mask_fill)
            top = jnp.max(scores, axis=0, keepdims=True)
            terms = jnp.exp(scores - top)
            total = jnp.sum(terms, axis=0, keepdims=True)
            out_t = dot(v_t[:, :stop], terms.astype(BF16)) / total
            att_t[:, first + start : first + stop] = out_t
            log_row[:, first + start : first + stop] = top + jnp.log(total)
            pieces.append(out_t.T.astype(BF16))
        results.append(jnp.concatenate(pieces, axis=0))
        first += count
    short_rows = rows - long_rows
    for j in range(8):
        mine = jnp.concatenate(
            [
                results[0][j * long_rows : (j + 1) * long_rows],
                results[1][j * short_rows : (j + 1) * short_rows],
            ],
            axis=0,
        )
        send[j, :, :] = fold(mine)


def pair_rows(came, seqs):
    columns = []
    for e in range(3):
        columns.append(
            jnp.concatenate([unfold(came[seqs * e + b]) for b in range(seqs)], axis=0)
        )
    return jnp.concatenate(columns, axis=1)


def out_proj_body(came, came_x, out, out_x, att, part):
    att[...] = pair_rows(came, 2)
    total = dot(att[...], out[...], NT)
    part[...] = (total + dot(pair_rows(came_x, 2), out_x[...], NT)).astype(BF16)


def feed_body(
    long_rows,
    place,
    long_lengths,
    short_lengths,
    own,
    other,
    long_in,
    short_in,
    long_cot,
    short_cot,
    up,
    down,
    mid_ref,
    squared_ref,
    grad_out_ref,
    keep,
    send,
    normed_ref,
    grad_up_ref,
    scratch,
    attended,
):
    seqs = long_in.shape[0]
    rows = long_rows + short_in.shape[1]
    attended[...] = own[...].astype(F32) + other[...].astype(F32)
    for b in range(seqs):
        at = slice(b * rows, (b + 1) * rows)
        residual = jnp.concatenate([long_in[b], short_in[b]], axis=0).astype(F32)
        mid = residual + attended[at, :]
        mid_ref[at, :] = mid
        root = lax.rsqrt(jnp.mean(mid * mid, axis=-1, keepdims=True) + norm_eps)
        normed_ref[at, :] = (mid * root).astype(BF16)
        for cot, lengths, first, count in (
            (long_cot, long_lengths, b * rows, long_rows),
            (short_cot, short_lengths, b * rows + long_rows, rows - long_rows),
        ):
            value = cot[b]
            position = lax.broadcasted_iota(jnp.int32, value.shape, 0) + place[0] * count
            grad_out_ref[first : first + count, :] = jnp.where(
                position < lengths[b], value.astype(F32), 0.0
            ).astype(BF16)
    relu = jnp.maximum(dot(normed_ref[...], up[...]), 0.0)
    squared_ref[...] = (relu * relu).astype(BF16)
    grad_squared = dot(grad_out_ref[...], down[...])
    grad_up_ref[...] = (grad_squared * 2.0 * relu).astype(BF16)
    scratch[...] = dot(grad_up_ref[...], up[...], NT).astype(BF16)
    split_halves(place, scratch, keep, send)


def split_halves(place, whole, keep, send):
    half = whole.shape[0] // 2
    core = place[1] % 2
    keep[...] = whole[pl.ds(pl.multiple_of(core * half, half), half), :]
    send[...] = whole[pl.ds(pl.multiple_of((1 - core) * half, half), half), :]


def join_halves(place, whole, own, other):
    half = own.shape[0]
    core = place[1] % 2
    whole[pl.ds(pl.multiple_of(core * half, half), half), :] = own[...].astype(whole.dtype)
    whole[pl.ds(pl.multiple_of((1 - core) * half, half), half), :] = other[...].astype(whole.dtype)


def split_y(place, blocks, keep, send):
    y = place[0] % 2
    for z in range(4):
        keep[z] = blocks[2 * z + y]
        send[z] = blocks[2 * z + 1 - y]


def down_term_body(
    place,
    squared,
    grad_out,
    down,
    normed,
    grad_up,
    near,
    own,
    across,
    f_keep,
    f_send,
    up_keep,
    up_send,
    scratch,
    blocks,
):
    rows = blocks.shape[1]
    term = dot(normed[...], grad_up[...], TN).astype(BF16)
    for s in range(8):
        blocks[s] = term[s * rows : (s + 1) * rows]
    split_y(place, blocks, up_keep, up_send)
    term = dot(grad_out[...], squared[...], TN).astype(BF16)
    for s in range(8):
        blocks[s] = term[s * rows : (s + 1) * rows]
    z = place[0] // 2
    for i, target in ((0, own), (1, near.at[0]), (2, across), (3, near.at[1])):
        for y in range(2):
            target[y] = blocks[2 * jnp.bitwise_xor(z, i) + y]
    scratch[...] = dot(squared[...], down[...], NT).astype(BF16)
    split_halves(place, scratch, f_keep, f_send)


def down_across_body(across, near, out):
    out[...] = (across[...].astype(F32) + near[1].astype(F32)).astype(BF16)


def down_y_body(place, own, near, across, keep, send):
    y = place[0] % 2
    for target, block in ((keep, y), (send, 1 - y)):
        target[...] = (
            own[block].astype(F32) + near[0, block].astype(F32) + across[block].astype(F32)
        ).astype(BF16)


def middle_body(
    place, own, other, mid_ref, grad_out, out, att, grad_mid_ref, send, keep_out, send_out, scratch, low_ref, blocks
):
    join_halves(place, scratch, own, other)
    seqs = 2
    rows = mid_ref.shape[0] // seqs
    for b in range(seqs):
        at = slice(b * rows, (b + 1) * rows)
        mid = mid_ref[at, :]
        weighted = scratch[at, :]
        root = lax.rsqrt(jnp.mean(mid * mid, axis=-1, keepdims=True) + norm_eps)
        inner = jnp.mean(weighted * mid, axis=-1, keepdims=True)
        grad_mid = grad_out[at, :].astype(F32) + (
            root * weighted - mid * (root * root * root * inner)
        )
        grad_mid_ref[at, :] = grad_mid
        low_ref[at, :] = grad_mid.astype(BF16)
    grad_att = dot(low_ref[...], out[...]).astype(BF16)
    for dest in range(8):
        if dest < 3 * seqs:
            e, b = dest // seqs, dest % seqs
            send[dest] = fold(
                grad_att[b * rows : (b + 1) * rows, e * HEAD_DIM : (e + 1) * HEAD_DIM]
            )
        else:
            send[dest] = jnp.zeros_like(send[dest])
    term = dot(low_ref[...], att[...], TN).astype(BF16)
    shard = term.shape[0] // 8
    for s in range(8):

        def store(row, lane, value):
            blocks[s, row : row + 16, lane : lane + LANES] = value

        narrow_pack(term[s * shard : (s + 1) * shard], store)
    split_y(place, blocks, keep_out, send_out)


def attend_back_body(
    long_rows,
    seqs,
    place,
    long_lengths,
    short_lengths,
    came,
    q_all,
    kv_all,
    att_t,
    log_row,
    grad_came,
    send,
):
    rows = (came.shape[1] - 16) * 2 // 3
    short_rows = rows - long_rows
    taps_q, taps_kv = head_taps(place, came, rows, seqs)
    b = place[0] % seqs
    e = place[0] // seqs
    grads = [unfold(grad_came[j]) for j in range(8)]
    first = 0
    terms_q = [0.0, 0.0, 0.0]
    terms_kv = [0.0, 0.0, 0.0]
    results = []
    for lengths, part, (q_mixed, kv_mixed) in zip(
        (long_lengths, short_lengths),
        (slice(0, long_rows), slice(long_rows, rows)),
        own_pair(came, long_rows, rows),
    ):
        count = q_mixed.shape[0]
        block = min(256, count)
        length = lengths[b]
        at = slice(first, first + count)
        grad = jnp.concatenate([g[part] for g in grads], axis=0)
        q = q_all[at, :]
        kv = kv_all[at, :]
        kv_t = kv.astype(F32).T.astype(BF16)
        delta = jnp.sum(grad.astype(F32).T * att_t[:, at], axis=0, keepdims=True)
        log_total = log_row[:, at]
        k, v = kv[:, :HEAD_DIM], kv[:, HEAD_DIM:]
        k_t = kv_t[:HEAD_DIM, :]
        grad_q = None
        grad_kv = []
        for start in range(0, count, block):
            stop = start + block
            scores = dot(k[start:stop], q[start:], NT)
            key_pos = lax.broadcasted_iota(jnp.int32, scores.shape, 0)
            query_pos = lax.broadcasted_iota(jnp.int32, scores.shape, 1)
            allowed = jnp.logical_and(key_pos <= query_pos, key_pos + start < length)
            prob = jnp.where(allowed, jnp.exp(scores - log_total[:, start:]), 0.0)
            grad_prob = dot(v[start:stop], grad[start:], NT)
            grad_scores = (prob * (grad_prob - delta[:, start:])).astype(BF16)
            grad_k = dot(grad_scores, q[start:])
            grad_v = dot(prob.astype(BF16), grad[start:])
            grad_kv.append(jnp.concatenate([grad_k, grad_v], axis=1))
            part_q = dot(k_t[:, start:stop], grad_scores)
            if start == 0:
                grad_q = part_q
            else:
                grad_q = jnp.concatenate(
                    [grad_q[:, :start], grad_q[:, start:] + part_q], axis=1
                )
        grad_q = grad_q.T * HEAD_DIM ** (-0.5)
        grad_kv = jnp.concatenate(grad_kv, axis=0)
        pair = []
        for grad_conv, mixed, taps, terms in (
            (grad_q, q_mixed, taps_q, terms_q),
            (grad_kv, kv_mixed, taps_kv, terms_kv),
        ):
            grad_mixed = 0.0
            for m in range(3):
                ahead = grad_conv if m == 0 else shift_ahead(grad_conv, m)
                terms[m] = terms[m] + jnp.sum(ahead * mixed, axis=0, keepdims=True)
                grad_mixed = grad_mixed + taps[m] * ahead
            pair.append(grad_mixed.astype(BF16))
        results.append(pair)
        first += count
    table = jnp.concatenate(
        terms_q
        + [t[:, :HEAD_DIM] for t in terms_kv]
        + [t[:, HEAD_DIM:] for t in terms_kv]
        + [jnp.zeros((7, HEAD_DIM), F32)],
        axis=0,
    )
    table = jnp.concatenate([jnp.where(e == i, table, 0.0) for i in range(3)], axis=1)
    width = 3 * HEAD_DIM // 8
    for j in range(8):
        mine = [
            jnp.concatenate(
                [
                    results[0][i][j * long_rows : (j + 1) * long_rows],
                    results[1][i][j * short_rows : (j + 1) * short_rows],
                ],
                axis=0,
            )
            for i in range(2)
        ]
        send[j, :rows, :] = mine[1]
        send[j, rows : rows + rows // 2, :] = fold(mine[0])
        send[j, rows + rows // 2 :, :] = jnp.concatenate(
            [table[:, j * width : (j + 1) * width], jnp.zeros((16, LANES - width), F32)], axis=1
        ).astype(BF16)


def place_grad_mixed(came, grad_mixed):
    seqs = 2
    rows = (came.shape[1] - 16) * 2 // 3
    for e in range(3):
        for b in range(seqs):
            j = seqs * e + b
            at = slice(b * rows, (b + 1) * rows)
            lanes = slice(e * HEAD_DIM, (e + 1) * HEAD_DIM)
            grad_mixed[0, at, lanes] = unfold(came[j, rows : rows + rows // 2, :])
            grad_mixed[1, at, lanes] = came[j, :rows, :HEAD_DIM]
            grad_mixed[2, at, lanes] = came[j, :rows, HEAD_DIM:]


def project_back_body(
    place, came, normed, weight, keep_p, send_p, keep, send, taps, scratch, grad_mixed, blocks
):
    place_grad_mixed(came, grad_mixed)
    shard = normed.shape[1] // 8
    terms = [dot(normed[...], grad_mixed[c], TN).astype(BF16) for c in range(3)]
    for s in range(8):
        at = slice(s * shard, (s + 1) * shard)
        for c in range(3):
            blocks[s, c * shard : (c + 1) * shard, :] = terms[c][at, :LANES]
        blocks[s, 3 * shard :, :] = fold(
            jnp.concatenate([terms[c][at, LANES:] for c in range(3)], axis=0)
        )
    split_y(place, blocks, keep_p, send_p)
    rows = (came.shape[1] - 16) * 2 // 3
    total = came[0, rows + rows // 2 :, :].astype(F32)
    for j in range(1, 6):
        total = total + came[j, rows + rows // 2 :, :].astype(F32)
    taps[...] = total[: taps.shape[0], : taps.shape[1]]
    total = dot(grad_mixed[0], weight[0], NT)
    for c in (1, 2):
        total = total + dot(grad_mixed[c], weight[c], NT)
    scratch[...] = total.astype(BF16)
    split_halves(place, scratch, keep, send)


def input_grad_body(
    place, own, other, grad_mid, gain, long_in, short_in, long_out, short_out, scratch
):
    join_halves(place, scratch, own, other)
    seqs, long_rows, _ = long_in.shape
    rows = long_rows + short_in.shape[1]
    for b in range(seqs):
        at = slice(b * rows, (b + 1) * rows)
        values = jnp.concatenate([long_in[b], short_in[b]], axis=0).astype(F32)
        weighted = scratch[at, :] * gain[...]
        root = lax.rsqrt(jnp.mean(values * values, axis=-1, keepdims=True) + norm_eps)
        inner = jnp.mean(weighted * values, axis=-1, keepdims=True)
        grad = grad_mid[at, :] + (root * weighted - values * (root * root * root * inner))
        long_out[b] = grad[:long_rows]
        short_out[b] = grad[long_rows:]


def output_body(place, own, other, mid, long_out, short_out, scratch):
    join_halves(place, scratch, own, other)
    seqs, long_rows, _ = long_out.shape
    rows = long_rows + short_out.shape[1]
    for b in range(seqs):
        at = slice(b * rows, (b + 1) * rows)
        value = (mid[at, :] + scratch[at, :]).astype(BF16)
        long_out[b] = value[:long_rows]
        short_out[b] = value[long_rows:]


def scatter_z_body(place, *refs):
    count = (len(refs) - 4) // 2
    outs = refs[2 * count :]
    z = place[0] // 2
    for i in range(4):
        block = jnp.bitwise_xor(z, i)
        first = 0
        for a in range(count):
            keep, came = refs[2 * a], refs[2 * a + 1]
            rows = keep.shape[1]
            outs[i][first : first + rows, :] = (
                keep[block].astype(F32) + came[block].astype(F32)
            ).astype(BF16)
            first += rows


def near_body(place, *refs):
    pairs = len(refs[:-3]) // 2
    near, own, across = refs[-3:]
    z = place[0] // 2
    for i, target in ((0, own), (1, near.at[0]), (2, across), (3, near.at[1])):
        block = jnp.bitwise_xor(z, i)
        first = 0
        for p in range(pairs):
            keep, came = refs[2 * p], refs[2 * p + 1]
            rows = keep.shape[1]
            target[first : first + rows, :] = (
                keep[block].astype(F32) + came[block].astype(F32)
            ).astype(BF16)
            first += rows


def across_body(across, near, out):
    out[...] = (across[...].astype(F32) + near[1].astype(F32)).astype(BF16)


def sum_blocks(blocks):
    return (blocks[0][...].astype(F32) + blocks[1][...].astype(F32)) + (
        blocks[2][...].astype(F32) + blocks[3][...].astype(F32)
    )


def proj_grad_body(b0, b1, b2, b3, proj, gain, grad, gain_grad):
    total = sum_blocks((b0, b1, b2, b3))
    rows = proj.shape[1]
    column = 0.0
    for c, (wide, narrow) in enumerate(unpack_blocks(total, rows, 3)):
        term = jnp.concatenate([wide, narrow], axis=1)
        column = column + jnp.sum(term * proj[c].astype(F32), axis=1, keepdims=True)
        grad[c] = term
    gain_grad[...] = column.T / gain[...].astype(F32).reshape(1, rows)


def ffn_grad_body(
    own, near, across, down_keep, down_came, up, gain, up_grad, down_grad, out_grad, gain_grad
):
    rows = up.shape[0]
    total = own[...].astype(F32) + near[0].astype(F32) + across[...].astype(F32)
    raw = total[:rows]
    gain_grad[...] = jnp.sum(raw * up[...].astype(F32), axis=1, keepdims=True).T
    up_grad[...] = raw * gain[...].astype(F32).reshape(1, rows).T
    down_grad[...] = down_keep[...].astype(F32) + down_came[...].astype(F32)
    wide = total[rows : rows + 16]
    narrow = total[rows + 16 :]
    out = jnp.concatenate(
        [
            jnp.concatenate(
                [
                    wide[:, LANES * g : LANES * (g + 1)],
                    narrow[:, LANES * g : LANES * g + HEAD_DIM],
                ],
                axis=1,
            )
            for g in range(rows // 16)
        ],
        axis=0,
    )
    out_grad[...] = out.T


def pair_shards(
    short_input,
    long_input,
    short_cotangent,
    long_cotangent,
    short_lengths,
    long_lengths,
    proj_weight,
    out_weight,
    conv_taps,
    attention_gain,
    up_weight,
    down_weight,
    feed_gain,
):
    seqs, long_rows, width = long_input.shape
    short_rows = short_input.shape[1]
    rows = long_rows + short_rows
    tokens = seqs * rows
    shard = proj_weight.shape[1]
    local = proj_weight.shape[2]
    hidden = up_weight.shape[1]
    long_len, short_len = 8 * long_rows, 8 * short_rows
    total_len = long_len + short_len
    place = jnp.stack([lax.axis_index("seq"), lax.axis_index("head")]).astype(jnp.int32)
    packed_rows = shard * 9 // 2
    chunk = rows + rows // 2 + 16
    down_t = down_weight.T

    (proj_packed,) = in_vmem(
        pack_proj_body,
        [((packed_rows + 16, LANES), BF16)],
        (),
        far(proj_weight, attention_gain),
    )
    (out_packed,) = in_vmem(pack_out_body, [((32, hidden), BF16)], (), far(out_weight))
    out_packed_x = exchange(out_packed, "head", 2)
    (ffn_packed,) = in_vmem(
        pack_ffn_body,
        [((2 * shard + 48, hidden), BF16)],
        (),
        far(up_weight, down_t) + (out_packed, out_packed_x) + far(feed_gain),
    )
    proj_z = [proj_packed] + [exchange(proj_packed, "seq", mask) for mask in (2, 4, 6)]
    proj_parts = [proj_packed, exchange(after(proj_packed, ffn_packed), "seq", 1)]
    proj_parts += [proj_z[1], exchange(proj_z[1], "seq", 1)]
    proj_parts += [proj_z[2], exchange(proj_z[2], "seq", 1)]
    proj_parts += [proj_z[3], exchange(proj_z[3], "seq", 1)]
    ffn_0 = after(ffn_packed, *proj_z)
    ffn_1 = exchange(ffn_packed, "seq", 1)
    ffn_2 = exchange(ffn_0, "seq", 2)
    ffn_4 = exchange(ffn_0, "seq", 4)
    send, normed, proj_full, gain = in_vmem(
        project_body,
        [
            ((8, chunk, LANES), BF16),
            ((tokens, width), BF16, "far"),
            ((3, width, local), BF16, "far"),
            ((1, width), F32, "far"),
        ],
        (place,),
        (*proj_parts, *far(long_input, short_input, conv_taps)),
        scratch=[((8, LANES), F32)],
        fence=True,
    )
    came = lax.all_to_all(send, "seq", 0, 0, tiled=True)
    across_z = marker(ffn_4, ffn_1, send)
    ffn_2 = after(ffn_2, across_z)
    ffn_4 = after(ffn_4, across_z)
    ffn_6 = exchange(ffn_4, "seq", 2)
    ffn_3 = exchange(ffn_2, "seq", 1)
    ffn_5 = exchange(ffn_4, "seq", 1)
    att_send, q_all, kv_all, att_t, log_row, mixed = in_vmem(
        functools.partial(attend_body, long_rows, seqs),
        [
            ((8, rows // 2, LANES), BF16),
            ((total_len, HEAD_DIM), BF16, "far"),
            ((total_len, 2 * HEAD_DIM), BF16, "far"),
            ((HEAD_DIM, total_len), F32, "far"),
            ((1, total_len), F32, "far"),
            ((8, chunk, LANES), BF16, "far"),
        ],
        (place, long_lengths, short_lengths),
        (came,),
        fence=True,
    )
    att_0 = lax.all_to_all(att_send, "seq", 0, 0, tiled=True)
    ffn_7 = exchange(ffn_6, "seq", 1)
    up_full, down_full, out_full, out_now, out_x = in_vmem(
        place_ffn_body,
        [((width, hidden), BF16, "far")] * 2
        + [((width, local), BF16, "far"), ((width, local), BF16), ((width, local), BF16)],
        (place,),
        far(after(ffn_packed, att_send), ffn_1, ffn_2, ffn_3, ffn_4, ffn_5, ffn_6, ffn_7),
    )
    att_0 = after(att_0, out_full)
    att_x = exchange(after(att_0, ffn_7), "head", 2)
    att, own = in_vmem(
        out_proj_body,
        [((tokens, local), BF16, "far"), ((tokens, width), BF16)],
        (),
        (att_0, att_x, out_now, out_x),
    )
    other = exchange(own, "head", 1)
    mid, squared, grad_out, keep, send, normed_ffn, grad_up = in_vmem(
        functools.partial(feed_body, long_rows),
        [
            ((tokens, width), F32, "far"),
            ((tokens, hidden), BF16, "far"),
            ((tokens, width), BF16, "far"),
            ((tokens // 2, width), BF16),
            ((tokens // 2, width), BF16),
            ((tokens, width), BF16, "far"),
            ((tokens, hidden), BF16, "far"),
        ],
        (place, long_lengths, short_lengths),
        (own, other)
        + far(long_input, short_input, long_cotangent, short_cotangent, up_full, down_full),
        scratch=[
            ((tokens, width), BF16),
            ((tokens, width), F32),
        ],
        limit_mib=32,
    )
    half = add_low(keep, exchange(send, "head", 1))
    down_near, down_own, down_across, f_keep, f_send, up_keep, up_send = in_vmem(
        down_term_body,
        [((2, 2, shard, hidden), BF16, "far")]
        + [((2, shard, hidden), BF16, "far")] * 2
        + [((tokens // 2, width), BF16, "far")] * 2
        + [((4, shard, hidden), BF16, "far")] * 2,
        (place,),
        far(after(squared, half), grad_out, down_full, normed_ffn, grad_up),
        scratch=[
            ((tokens, width), BF16),
            ((8, shard, hidden), BF16),
        ],
        limit_mib=32,
        fence=True,
    )
    down_near = exchange(down_near, "seq", 2)
    up_came = exchange(up_send, "seq", 1)
    own = add_low(half, after(exchange(half, "head", 2), f_send))
    other = exchange(own, "head", 1)
    grad_mid, send, out_keep, out_send = in_vmem(
        middle_body,
        [
            ((tokens, width), F32, "far"),
            ((8, rows // 2, LANES), BF16),
            ((4, 32, hidden), BF16, "far"),
            ((4, 32, hidden), BF16, "far"),
        ],
        (place,),
        (own, other) + far(mid, grad_out, out_full, att),
        scratch=[((tokens, width), F32), ((tokens, width), BF16), ((8, 32, hidden), BF16)],
    )
    grad_came = lax.all_to_all(send, "seq", 0, 0, tiled=True)
    out_came = exchange(out_send, "seq", 1)
    (down_across,) = in_vmem(
        down_across_body,
        [((2, shard, hidden), BF16, "far")],
        (),
        far(after(down_across, send, up_came), down_near),
        fence=True,
    )
    grad_came = after(grad_came, down_across)
    down_across = exchange(down_across, "seq", 4)
    f_half = add_low(f_keep, exchange(after(f_send, send), "head", 1))
    f_own = add_low(f_half, exchange(f_half, "head", 2))
    f_other = exchange(f_own, "head", 1)
    long_output, short_output = in_vmem(
        output_body,
        [(long_input.shape, BF16), (short_input.shape, BF16)],
        (place,),
        (f_own, f_other) + far(mid),
        scratch=[((tokens, width), F32)],
    )
    (send,) = in_vmem(
        functools.partial(attend_back_body, long_rows, seqs),
        [((8, chunk, LANES), BF16)],
        (place, long_lengths, short_lengths),
        far(mixed, q_all, kv_all, att_t, log_row) + (grad_came,),
        fence=True,
    )
    mixed_came = lax.all_to_all(send, "seq", 0, 0, tiled=True)
    near, ffn_own, across = in_vmem(
        near_body,
        [((2, shard + 32, hidden), BF16, "far")] + [((shard + 32, hidden), BF16, "far")] * 2,
        (place,),
        far(up_keep, after(up_came, send), out_keep, out_came),
        fence=True,
    )
    near = exchange(near, "seq", 2)
    down_keep, down_send = in_vmem(
        down_y_body,
        [((shard, hidden), BF16, "far")] * 2,
        (place,),
        far(after(down_own, ffn_own), down_near, down_across),
    )
    down_came = exchange(down_send, "seq", 1)
    mixed_came = after(mixed_came, long_output, down_send)
    proj_keep, proj_send, keep, send, taps_grad = in_vmem(
        project_back_body,
        [
            ((4, packed_rows, LANES), BF16, "far"),
            ((4, packed_rows, LANES), BF16),
            ((tokens // 2, width), BF16),
            ((tokens // 2, width), BF16),
            (conv_taps.shape, F32),
        ],
        (place,),
        (mixed_came,) + far(normed, proj_full),
        scratch=[
            ((tokens, width), BF16),
            ((3, tokens, local), BF16),
            ((8, packed_rows, LANES), BF16),
        ],
        fence=True,
    )
    proj_came = exchange(proj_send, "seq", 1)
    half = add_low(keep, exchange(send, "head", 1))
    (across,) = in_vmem(
        across_body, [((shard + 32, hidden), BF16, "far")], (), far(across, near)
    )
    across = exchange(across, "seq", 4)
    own = add_low(half, after(exchange(half, "head", 2), proj_came))
    other = exchange(own, "head", 1)
    proj_blocks = in_vmem(
        scatter_z_body,
        [((packed_rows, LANES), BF16)] * 4,
        (place,),
        far(proj_keep) + (proj_came,),
        fence=True,
    )
    proj_blocks = [proj_blocks[0]] + [exchange(proj_blocks[i], "seq", 2 * i) for i in (1, 2, 3)]
    up_grad, down_grad, out_grad, feed_part = in_vmem(
        ffn_grad_body,
        [
            (up_weight.shape, F32),
            (down_t.shape, F32),
            (out_weight.shape, F32),
            ((1, shard), F32),
        ],
        (),
        far(after(ffn_own, proj_blocks[0]), near, across, down_keep, down_came, up_weight)
        + (feed_gain,),
    )
    proj_blocks[3] = after(proj_blocks[3], up_grad)
    proj_grad, attention_part = in_vmem(
        proj_grad_body,
        [(proj_weight.shape, F32), ((1, shard), F32)],
        (),
        (*proj_blocks, *far(proj_weight), attention_gain),
    )
    long_input_grad, short_input_grad = in_vmem(
        input_grad_body,
        [(long_input.shape, F32), (short_input.shape, F32)],
        (place,),
        (own, other) + far(after(grad_mid, attention_part), gain, long_input, short_input),
        scratch=[((tokens, width), F32)],
    )
    gains = jnp.concatenate([attention_part, feed_part], axis=0)
    gains = gains + exchange(gains, "head", 1)
    gains = gains + after(exchange(gains, "head", 2), long_input_grad)

    return (
        short_output,
        long_output,
        short_input_grad,
        long_input_grad,
        proj_grad,
        out_grad,
        taps_grad,
        gains[0],
        up_grad,
        down_grad.T,
        gains[1],
    )


def fits_pairs(short_input, long_input, proj_weight):
    seqs, long_rows, _ = long_input.shape
    short_seqs, short_rows, _ = short_input.shape
    return (
        lax.axis_size("seq") == 8
        and lax.axis_size("head") == 4
        and seqs == 2
        and short_seqs == 2
        and proj_weight.shape[2] == 3 * HEAD_DIM
        and proj_weight.shape[1] % 32 == 0
        and long_rows % 32 == 0
        and short_rows % 32 == 0
        and 8 * long_rows <= 2048
    )


def shards(short_input, long_input, *rest):
    proj_weight = rest[4]
    if fits_pairs(short_input, long_input, proj_weight):
        return pair_shards(short_input, long_input, *rest)
    return ring_shards(short_input, long_input, *rest)


def solution(mesh):
    placed = (
        P(None, "seq", None),
        P(None, "seq", None),
        P(None, "seq", None),
        P(None, "seq", None),
        P(),
        P(),
        P(None, "seq", "head"),
        P("head", "seq"),
        P(None, ("head", "seq")),
        P("seq"),
        P("seq", "head"),
        P("head", "seq"),
        P("seq"),
    )
    return jax.shard_map(
        shards,
        mesh=mesh,
        in_specs=placed,
        out_specs=(
            P(None, "seq", None),
            P(None, "seq", None),
            P(None, "seq", None),
            P(None, "seq", None),
            P(None, "seq", "head"),
            P("head", "seq"),
            P(None, ("head", "seq")),
            P("seq"),
            P("seq", "head"),
            P("head", "seq"),
            P("seq"),
        ),
        check_vma=False,
    )
```
